32 devices in a mesh: fsdp: 4 (over y, x), ctx: 2 (over core), tp: 4 (over z).
Axes of the slice: x: 2, y: 2, z: 4, core: 2. Of those that a mesh axis runs over, the one named last changes fastest.
Arguments:
- tokens: bfloat16 [8192, 2560], P(('fsdp', 'ctx'), 'tp'), may hold values from -6 to 6
- cotangent: bfloat16 [8192, 2560], P(('fsdp', 'ctx')), may hold values from -6 to 6
- lengths: int32 [4, 1], P('fsdp'), may hold values from 1024 to 2048, as said below
- w_qdown: float32 [2560, 768], P('tp', ('fsdp', 'ctx')), may hold values from -0.125 to 0.125
- w_kvdown: float32 [2560, 288], P('tp', ('fsdp', 'ctx')), may hold values from -0.125 to 0.125
- w_qup: float32 [768, 3840], P(('fsdp', 'ctx'), 'tp'), may hold values from -0.21875 to 0.21875
- w_kvup: float32 [256, 5120], P(('fsdp', 'ctx'), 'tp'), may hold values from -0.375 to 0.375
- w_out: float32 [2560, 2560], P('tp', ('fsdp', 'ctx')), may hold values from -1 to 1
- w_gateup: float32 [2, 2560, 6400], P(None, ('fsdp', 'ctx'), 'tp'), may hold values from -0.125 to 0.125
- w_down: float32 [6400, 2560], P('tp', ('fsdp', 'ctx')), may hold values from -0.625 to 0.625
- g_norms: float32 [2, 2560], P(None, 'tp'), may hold values from 0.5 to 1.5
- g_latent: float32 [1024], P(('fsdp', 'ctx')), may hold values from 0.5 to 1.5
- m_qdown: float32 [2560, 768], P('tp', ('fsdp', 'ctx')), may hold values from -0.00012207031 to 0.00012207031
- m_kvdown: float32 [2560, 288], P('tp', ('fsdp', 'ctx')), may hold values from -0.00012207031 to 0.00012207031
- m_qup: float32 [768, 3840], P(('fsdp', 'ctx'), 'tp'), may hold values from -0.00012207031 to 0.00012207031
- m_kvup: float32 [256, 5120], P(('fsdp', 'ctx'), 'tp'), may hold values from -0.00012207031 to 0.00012207031
- m_out: float32 [2560, 2560], P('tp', ('fsdp', 'ctx')), may hold values from -0.00012207031 to 0.00012207031
- m_gateup: float32 [2, 2560, 6400], P(None, ('fsdp', 'ctx'), 'tp'), may hold values from -0.00012207031 to 0.00012207031
- m_down: float32 [6400, 2560], P('tp', ('fsdp', 'ctx')), may hold values from -0.00012207031 to 0.00012207031
- m_norms: float32 [2, 2560], P(None, 'tp'), may hold values from -0.00012207031 to 0.00012207031
- m_latent: float32 [1024], P(('fsdp', 'ctx')), may hold values from -0.00012207031 to 0.00012207031
- v_qdown: float32 [2560, 768], P('tp', ('fsdp', 'ctx')), may hold values from 2e-09 to 8e-09
- v_kvdown: float32 [2560, 288], P('tp', ('fsdp', 'ctx')), may hold values from 2e-09 to 8e-09
- v_qup: float32 [768, 3840], P(('fsdp', 'ctx'), 'tp'), may hold values from 2e-09 to 8e-09
- v_kvup: float32 [256, 5120], P(('fsdp', 'ctx'), 'tp'), may hold values from 2e-09 to 8e-09
- v_out: float32 [2560, 2560], P('tp', ('fsdp', 'ctx')), may hold values from 2e-09 to 8e-09
- v_gateup: float32 [2, 2560, 6400], P(None, ('fsdp', 'ctx'), 'tp'), may hold values from 2e-09 to 8e-09
- v_down: float32 [6400, 2560], P('tp', ('fsdp', 'ctx')), may hold values from 2e-09 to 8e-09
- v_norms: float32 [2, 2560], P(None, 'tp'), may hold values from 2e-09 to 8e-09
- v_latent: float32 [1024], P(('fsdp', 'ctx')), may hold values from 2e-09 to 8e-09
Outputs:
- layer_out: bfloat16 [8192, 2560], P(('fsdp', 'ctx'), 'tp')
- grad_input: bfloat16 [8192, 2560], P(('fsdp', 'ctx'), 'tp')
- grad_qdown: float32 [2560, 768], P('tp', ('fsdp', 'ctx'))
- grad_kvdown: float32 [2560, 288], P('tp', ('fsdp', 'ctx'))
- grad_qup: float32 [768, 3840], P(('fsdp', 'ctx'), 'tp')
- grad_kvup: float32 [256, 5120], P(('fsdp', 'ctx'), 'tp')
- grad_out: float32 [2560, 2560], P('tp', ('fsdp', 'ctx'))
- grad_gateup: float32 [2, 2560, 6400], P(None, ('fsdp', 'ctx'), 'tp')
- grad_down: float32 [6400, 2560], P('tp', ('fsdp', 'ctx'))
- grad_norms: float32 [2, 2560], P(None, 'tp')
- grad_latent: float32 [1024], P(('fsdp', 'ctx'))
- new_qdown: float32 [2560, 768], P('tp', ('fsdp', 'ctx'))
- new_kvdown: float32 [2560, 288], P('tp', ('fsdp', 'ctx'))
- new_qup: float32 [768, 3840], P(('fsdp', 'ctx'), 'tp')
- new_kvup: float32 [256, 5120], P(('fsdp', 'ctx'), 'tp')
- new_out: float32 [2560, 2560], P('tp', ('fsdp', 'ctx'))
- new_gateup: float32 [2, 2560, 6400], P(None, ('fsdp', 'ctx'), 'tp')
- new_down: float32 [6400, 2560], P('tp', ('fsdp', 'ctx'))
- first_qdown: float32 [2560, 768], P('tp', ('fsdp', 'ctx'))
- first_kvdown: float32 [2560, 288], P('tp', ('fsdp', 'ctx'))
- first_qup: float32 [768, 3840], P(('fsdp', 'ctx'), 'tp')
- first_kvup: float32 [256, 5120], P(('fsdp', 'ctx'), 'tp')
- first_out: float32 [2560, 2560], P('tp', ('fsdp', 'ctx'))
- first_gateup: float32 [2, 2560, 6400], P(None, ('fsdp', 'ctx'), 'tp')
- first_down: float32 [6400, 2560], P('tp', ('fsdp', 'ctx'))
- first_norms: float32 [2, 2560], P(None, 'tp')
- first_latent: float32 [1024], P(('fsdp', 'ctx'))
- second_qdown: float32 [2560, 768], P('tp', ('fsdp', 'ctx'))
- second_kvdown: float32 [2560, 288], P('tp', ('fsdp', 'ctx'))
- second_qup: float32 [768, 3840], P(('fsdp', 'ctx'), 'tp')
- second_kvup: float32 [256, 5120], P(('fsdp', 'ctx'), 'tp')
- second_out: float32 [2560, 2560], P('tp', ('fsdp', 'ctx'))
- second_gateup: float32 [2, 2560, 6400], P(None, ('fsdp', 'ctx'), 'tp')
- second_down: float32 [6400, 2560], P('tp', ('fsdp', 'ctx'))
- second_norms: float32 [2, 2560], P(None, 'tp')
- second_latent: float32 [1024], P(('fsdp', 'ctx'))
The draws below stay inside these ranges and needn't reach their ends.
Inputs may be any that keep to these rules, and one draw needn't show every extreme that they name: `lengths`: entry g is the length of the one sequence at the start of slot g; the rest of the slot is padding. Some slot is full and some slot is half full in every draw.
All inputs are finite; a program needn't handle non-finite values.
Results may differ from the reference program's by a relative error of at most 0.035.
Values may be sent and summed in bfloat16 or wider, within the bound.
A program may use at most 448 MiB of HBM per device.

```python
import math
import jax
import jax.numpy as jnp
from jax import lax

D = 2560
H = 40
NOPE = 64
ROPE = 32
VD = 64
QR = 768
KVR = 256
FF = 6400
BLOCK_TOK = 1024
STEP = 3
GROUP = 2048
TOKENS = 8192
N_FSDP = 4
N_CTX = 2
N_TP = 4


def draw_lengths(key, part):
    key_values = jax.random.fold_in(key, 11)
    key_order = jax.random.fold_in(key, 12)
    values = jax.random.randint(key_values, (N_FSDP, 1), GROUP // 2, GROUP + 1).astype(jnp.int32)
    order = jax.random.permutation(key_order, N_FSDP).astype(jnp.int32)[:, None]
    values = jnp.where(order == 0, GROUP, values)
    values = jnp.where(order == 1, GROUP // 2, values)
    return values.astype(jnp.int32)


def level_of(stream_key, dims, split, smallest, high):
    loudness, own = 1.0, jax.random.fold_in(stream_key, 6)
    for dim, parts in split:
        steps = jnp.exp(jax.random.uniform(jax.random.fold_in(own, dim), (parts,), jnp.float32, smallest / len(split), high / len(split)))
        loudness = loudness * jnp.repeat(steps, dims[dim] // parts).reshape([-1 if axis == dim else 1 for axis in range(len(dims))])
    return loudness


def gaussian(stream_key, dims, scale, bound, cuts=(), held_as=jnp.bfloat16):
    level = level_of(stream_key, dims, cuts, -0.22, 0.18) if cuts else 1.0
    drawn = jax.random.normal(stream_key, dims, jnp.float32) * scale * level
    return jnp.minimum(jnp.maximum(drawn, -bound), bound).astype(held_as)


def setup_inputs(seed: int = 0) -> dict:
    seeds = jax.random.split(jax.random.key(seed), 31)
    return {
        "tokens": gaussian(seeds[0], (TOKENS, D), 1.0, 6.0, ((0, 8), (1, 4))),
        "cotangent": gaussian(seeds[1], (TOKENS, D), 1.0, 6.0, ((0, 8),)),
        "lengths": draw_lengths(jax.random.fold_in(seeds[30], 71), 0),
        "w_qdown": gaussian(seeds[3], (D, QR), D ** -0.5, 0.125, ((0, 4), (1, 8)), jnp.float32),
        "w_kvdown": gaussian(seeds[4], (D, KVR + ROPE), D ** -0.5, 0.125, ((0, 4), (1, 8)), jnp.float32),
        "w_qup": gaussian(seeds[5], (QR, H * (NOPE + ROPE)), QR ** -0.5, 0.21875, ((0, 8), (1, 4)), jnp.float32),
        "w_kvup": gaussian(seeds[6], (KVR, H * (NOPE + VD)), KVR ** -0.5, 0.375, ((0, 8), (1, 4)), jnp.float32),
        "w_out": gaussian(seeds[7], (H * VD, D), (H * VD // 64) ** -0.5, 1.0, ((0, 4), (1, 8)), jnp.float32),
        "w_gateup": gaussian(seeds[8], (2, D, FF), D ** -0.5, 0.125, ((1, 8), (2, 4)), jnp.float32),
        "w_down": gaussian(seeds[9], (FF, D), (FF // 64) ** -0.5, 0.625, ((0, 4), (1, 8)), jnp.float32),
        "g_norms": jnp.clip(1.0 + 0.1 * jax.random.normal(seeds[10], (2, D), jnp.float32), 0.5, 1.5),
        "g_latent": jnp.clip(1.0 + 0.1 * jax.random.normal(seeds[11], (QR + KVR,), jnp.float32), 0.5, 1.5),
        "m_qdown": gaussian(seeds[12], (D, QR), (2e-5), 0.00012207031, ((0, 4), (1, 8)), jnp.float32),
        "m_kvdown": gaussian(seeds[13], (D, KVR + ROPE), (2e-5), 0.00012207031, ((0, 4), (1, 8)), jnp.float32),
        "m_qup": gaussian(seeds[14], (QR, H * (NOPE + ROPE)), (2e-5), 0.00012207031, ((0, 8), (1, 4)), jnp.float32),
        "m_kvup": gaussian(seeds[15], (KVR, H * (NOPE + VD)), (2e-5), 0.00012207031, ((0, 8), (1, 4)), jnp.float32),
        "m_out": gaussian(seeds[16], (H * VD, D), (2e-5), 0.00012207031, ((0, 4), (1, 8)), jnp.float32),
        "m_gateup": gaussian(seeds[17], (2, D, FF), (2e-5), 0.00012207031, ((1, 8), (2, 4)), jnp.float32),
        "m_down": gaussian(seeds[18], (FF, D), (2e-5), 0.00012207031, ((0, 4), (1, 8)), jnp.float32),
        "m_norms": gaussian(seeds[19], (2, D), (2e-5), 0.00012207031, ((1, 4),), jnp.float32),
        "m_latent": gaussian(seeds[20], (QR + KVR,), (2e-5), 0.00012207031, ((0, 8),), jnp.float32),
        "v_qdown": jnp.clip(jnp.exp(math.log(7.999999773744548e-09) - 1.3862944 * jax.random.uniform(seeds[21], (D, QR), jnp.float32) ** level_of(seeds[21], (D, QR), ((0, 4), (1, 8)), -0.2, 0.2)), 1.999999943436137e-09, 7.999999773744548e-09),
        "v_kvdown": jnp.clip(jnp.exp(math.log(7.999999773744548e-09) - 1.3862944 * jax.random.uniform(seeds[22], (D, KVR + ROPE), jnp.float32) ** level_of(seeds[22], (D, KVR + ROPE), ((0, 4), (1, 8)), -0.2, 0.2)), 1.999999943436137e-09, 7.999999773744548e-09),
        "v_qup": jnp.clip(jnp.exp(math.log(7.999999773744548e-09) - 1.3862944 * jax.random.uniform(seeds[23], (QR, H * (NOPE + ROPE)), jnp.float32) ** level_of(seeds[23], (QR, H * (NOPE + ROPE)), ((0, 8), (1, 4)), -0.2, 0.2)), 1.999999943436137e-09, 7.999999773744548e-09),
        "v_kvup": jnp.clip(jnp.exp(math.log(7.999999773744548e-09) - 1.3862944 * jax.random.uniform(seeds[24], (KVR, H * (NOPE + VD)), jnp.float32) ** level_of(seeds[24], (KVR, H * (NOPE + VD)), ((0, 8), (1, 4)), -0.2, 0.2)), 1.999999943436137e-09, 7.999999773744548e-09),
        "v_out": jnp.clip(jnp.exp(math.log(7.999999773744548e-09) - 1.3862944 * jax.random.uniform(seeds[25], (H * VD, D), jnp.float32) ** level_of(seeds[25], (H * VD, D), ((0, 4), (1, 8)), -0.2, 0.2)), 1.999999943436137e-09, 7.999999773744548e-09),
        "v_gateup": jnp.clip(jnp.exp(math.log(7.999999773744548e-09) - 1.3862944 * jax.random.uniform(seeds[26], (2, D, FF), jnp.float32) ** level_of(seeds[26], (2, D, FF), ((1, 8), (2, 4)), -0.2, 0.2)), 1.999999943436137e-09, 7.999999773744548e-09),
        "v_down": jnp.clip(jnp.exp(math.log(7.999999773744548e-09) - 1.3862944 * jax.random.uniform(seeds[27], (FF, D), jnp.float32) ** level_of(seeds[27], (FF, D), ((0, 4), (1, 8)), -0.2, 0.2)), 1.999999943436137e-09, 7.999999773744548e-09),
        "v_norms": jnp.clip(jnp.exp(math.log(7.999999773744548e-09) - 1.3862944 * jax.random.uniform(seeds[28], (2, D), jnp.float32) ** level_of(seeds[28], (2, D), ((1, 4),), -0.2, 0.2)), 1.999999943436137e-09, 7.999999773744548e-09),
        "v_latent": jnp.clip(jnp.exp(math.log(7.999999773744548e-09) - 1.3862944 * jax.random.uniform(seeds[29], (QR + KVR,), jnp.float32) ** level_of(seeds[29], (QR + KVR,), ((0, 8),), -0.2, 0.2)), 1.999999943436137e-09, 7.999999773744548e-09),
    }


EPS_NORM = 1e-05
RESIDUAL_SCALE = 1.4 / 62 ** 0.5
ROPE_BASE = 10000.0
MASK_VALUE = -1e+30
BETA_ONE = 0.9
BETA_TWO = 0.95
ADAM_EPS = 1e-08
LEARN_RATE = 0.1
WEIGHT_DECAY = 0.1
CLIP_RMS = 0.0002

def rounded(values):
    return lax.optimization_barrier(values.astype(jnp.bfloat16)).astype(jnp.float32)

def rotary_tables(positions, rope_width):
    half_width = rope_width // 2
    frequency = ROPE_BASE ** (-2.0 * jnp.arange(half_width, dtype=jnp.float32) / rope_width)
    angles = positions.astype(jnp.float32)[:, None] * frequency[None, :]
    cosine = jnp.cos(angles)
    sine_table = jnp.sin(angles)
    return (jnp.concatenate([cosine, cosine], axis=1), jnp.concatenate([sine_table, sine_table], axis=1))

def rotate_forward(values, cosine, sine_table):
    half_width = values.shape[-1] // 2
    turned = jnp.concatenate([-values[..., half_width:], values[..., :half_width]], axis=-1)
    return values * cosine + turned * sine_table

def rotate_backward(incoming, cosine, sine_table):
    half_width = incoming.shape[-1] // 2
    scaled = incoming * sine_table
    turned = jnp.concatenate([scaled[..., half_width:], -scaled[..., :half_width]], axis=-1)
    return incoming * cosine + turned

def group_layout(seq_length, indices):
    segment = (indices >= seq_length).astype(jnp.int32)
    return (segment, indices - segment * seq_length)

def block_mask(index_block, segment_block, key_index, key_segment):
    return (key_index[None, :] >= 0) & (key_index[None, :] <= index_block[:, None]) & (key_segment[None, :] == segment_block[:, None])

def product(spec, left_side, right_side):
    return jnp.einsum(spec, left_side.astype(jnp.float32), right_side.astype(jnp.float32))

def contract_last(left_side, right_side):
    return lax.dot_general(left_side, right_side, (((1,), (1,)), ((), ())), preferred_element_type=jnp.float32)

def contract_first(left_side, right_side):
    return lax.dot_general(left_side, right_side, (((0,), (0,)), ((), ())), preferred_element_type=jnp.float32)

def norm_forward(values, gain):
    factor = lax.rsqrt(lax.optimization_barrier(jnp.mean(values * values, axis=1, keepdims=True)) + EPS_NORM)
    return (values * factor * gain, factor)

def norm_backward(incoming, values, factor, gain):
    scaled = incoming * gain
    gain_grad = lax.optimization_barrier(jnp.sum(incoming * values * factor, axis=0))
    result = factor * scaled - values * factor ** 3 * lax.optimization_barrier(jnp.mean(scaled * values, axis=1, keepdims=True))
    return (result, gain_grad)

def expand_keys(key_latent, key_rope, kv_up):
    row_count = key_latent.shape[0]
    head_count = kv_up.shape[1] // (NOPE + VD)
    expanded = jnp.dot(key_latent, kv_up, preferred_element_type=jnp.float32).reshape(row_count, head_count, NOPE + VD)
    rope_part = jnp.broadcast_to(key_rope[:, None, :], (row_count, head_count, ROPE))
    key_full = jnp.concatenate([expanded[..., :NOPE].astype(jnp.bfloat16), rope_part], axis=2)
    return (key_full, expanded[..., NOPE:].astype(jnp.bfloat16))

def sliced_product(pair_list, part_count):
    row_count = pair_list[0][0].shape[0]
    col_count = pair_list[0][1].shape[1]

    def add_part(part_total, part_index):
        part_term = jnp.zeros((row_count, col_count), jnp.float32)
        for left_side, right_side in pair_list:
            span_width = left_side.shape[1] // part_count
            piece_left = lax.dynamic_slice_in_dim(left_side, part_index * span_width, span_width, 1)
            piece_right = lax.dynamic_slice_in_dim(right_side, part_index * span_width, span_width, 0)
            part_term = part_term + jnp.dot(piece_left, piece_right, preferred_element_type=jnp.float32)
        return (part_total + rounded(part_term), None)
    part_total, _ = lax.scan(add_part, jnp.zeros((row_count, col_count), jnp.float32), jnp.arange(part_count, dtype=jnp.int32))
    return part_total

def attend_forward(queries, key_full, values, query_index, query_segment, key_index, key_segment):
    row_count, head_count, head_depth = queries.shape
    block_rows = min(512, row_count)
    block_count = row_count // block_rows
    score_scale = head_depth ** (-0.5)

    def one_block(carried, pieces):
        query_block, index_block, segment_block = pieces
        allowed = block_mask(index_block, segment_block, key_index, key_segment)
        scores = jnp.where(allowed[None], product('qhd,khd->hqk', query_block, key_full) * score_scale, MASK_VALUE)
        largest = lax.optimization_barrier(jnp.max(scores, axis=2, keepdims=True))
        exp_scores = jnp.exp(scores - largest)
        denominator = lax.optimization_barrier(jnp.sum(exp_scores, axis=2, keepdims=True))
        prob_block = (exp_scores / denominator).astype(jnp.bfloat16)
        result = product('hqk,khd->qhd', prob_block, values).astype(jnp.bfloat16)
        return (carried, (result, (largest + jnp.log(denominator))[:, :, 0]))
    _, (results, log_totals) = lax.scan(one_block, None, (queries.reshape(block_count, block_rows, head_count, head_depth), query_index.reshape(block_count, block_rows), query_segment.reshape(block_count, block_rows)))
    return (results.reshape(row_count, head_count, values.shape[2]), log_totals)

def attend_backward(queries, key_full, values, results, d_results, log_totals, query_index, query_segment, key_index, key_segment):
    row_count, head_count, head_depth = queries.shape
    block_rows = min(512, row_count)
    block_count = row_count // block_rows
    score_scale = head_depth ** (-0.5)
    value_depth = values.shape[2]

    def one_block(carried, pieces):
        key_sum, value_sum = carried
        query_block, result_block, grad_block, log_block, index_block, segment_block = pieces
        allowed = block_mask(index_block, segment_block, key_index, key_segment)
        scores = jnp.where(allowed[None], product('qhd,khd->hqk', query_block, key_full) * score_scale, MASK_VALUE)
        prob_full = jnp.exp(scores - log_block[:, :, None])
        prob_block = prob_full.astype(jnp.bfloat16)
        d_prob = product('qhd,khd->hqk', grad_block, values)
        row_inner = jnp.transpose(lax.optimization_barrier(jnp.sum(grad_block.astype(jnp.float32) * result_block.astype(jnp.float32), axis=2)))
        d_score = (prob_full * (d_prob - row_inner[:, :, None]) * score_scale).astype(jnp.bfloat16)
        d_query = product('hqk,khd->qhd', d_score, key_full)
        key_sum = key_sum + product('hqk,qhd->khd', d_score, query_block)
        value_sum = value_sum + product('hqk,qhd->khd', prob_block, grad_block)
        return ((key_sum, value_sum), d_query)
    initial = (jnp.zeros(key_full.shape, jnp.float32), jnp.zeros(values.shape, jnp.float32))
    pieces = (queries.reshape(block_count, block_rows, head_count, head_depth), results.reshape(block_count, block_rows, head_count, value_depth), d_results.reshape(block_count, block_rows, head_count, value_depth), log_totals, query_index.reshape(block_count, block_rows), query_segment.reshape(block_count, block_rows))
    (key_sum, value_sum), d_queries = lax.scan(one_block, initial, pieces)
    return (d_queries.reshape(row_count, head_count, head_depth), key_sum, value_sum)

def layer_group(used, tokens_group, cotangent_group, lengths_row):
    q_down, kv_down, q_up, kv_up, out_weight, gate_up, down_weight, gain_attn, gain_mlp, gain_query, gain_latent = used
    block_rows = BLOCK_TOK
    group_rows = tokens_group.shape[0]
    head_width = NOPE + ROPE
    seq_length = lengths_row[0]
    inputs = tokens_group.astype(jnp.float32)
    normed_raw, factor_one = norm_forward(inputs, gain_attn)
    normed_one = normed_raw.astype(jnp.bfloat16)
    down_both = jnp.concatenate([q_down, kv_down], axis=1)
    latents = jnp.dot(normed_one, down_both, preferred_element_type=jnp.float32)
    query_latent = latents[:, :QR]
    kv_latent = latents[:, QR:QR + KVR]
    rope_raw = latents[:, QR + KVR:]
    query_raw, factor_query = norm_forward(query_latent, gain_query)
    query_normed = query_raw.astype(jnp.bfloat16)
    kv_raw, factor_kv = norm_forward(kv_latent, gain_latent)
    kv_normed = kv_raw.astype(jnp.bfloat16)
    own_index = jnp.arange(group_rows, dtype=jnp.int32)
    own_segment, own_position = group_layout(seq_length, own_index)
    cosine, sine_table = rotary_tables(own_position, ROPE)
    rope_key = rotate_forward(rope_raw, cosine, sine_table).astype(jnp.bfloat16)
    query_all = jnp.dot(query_normed, q_up, preferred_element_type=jnp.float32).reshape(group_rows, -1, head_width)
    queries = jnp.concatenate([query_all[..., :NOPE], rotate_forward(query_all[..., NOPE:], cosine[:, None], sine_table[:, None])], axis=2).astype(jnp.bfloat16)
    padded_kv = jnp.concatenate([jnp.zeros((block_rows, KVR), jnp.bfloat16), kv_normed], axis=0)
    padded_rope = jnp.concatenate([jnp.zeros((block_rows, ROPE), jnp.bfloat16), rope_key], axis=0)
    key_sets = []
    attended_parts = []
    log_parts = []
    for index_ctx in range(N_CTX):
        row_start = index_ctx * block_rows
        row_stop = row_start + block_rows
        key_latent = padded_kv[row_start:row_start + 2 * block_rows]
        key_rope = padded_rope[row_start:row_start + 2 * block_rows]
        key_index = jnp.arange(2 * block_rows, dtype=jnp.int32) + (index_ctx - 1) * block_rows
        key_segment, _ = group_layout(seq_length, key_index)
        key_full, key_values = expand_keys(key_latent, key_rope, kv_up)
        attended_block, log_block = attend_forward(queries[row_start:row_stop], key_full, key_values, own_index[row_start:row_stop], own_segment[row_start:row_stop], key_index, key_segment)
        key_sets.append((key_latent, key_full, key_values, key_index, key_segment))
        attended_parts.append(attended_block)
        log_parts.append(log_block)
    attended = jnp.concatenate(attended_parts, axis=0)
    attended_flat = attended.reshape(group_rows, -1)
    attn_part = sliced_product([(attended_flat, out_weight)], N_TP)
    hidden = inputs + RESIDUAL_SCALE * attn_part
    normed_raw_two, factor_two = norm_forward(hidden, gain_mlp)
    normed_two = normed_raw_two.astype(jnp.bfloat16)
    gate_proj = jnp.dot(normed_two, gate_up[0], preferred_element_type=jnp.float32)
    up_proj = jnp.dot(normed_two, gate_up[1], preferred_element_type=jnp.float32)
    sigmoid_gate = jax.nn.sigmoid(gate_proj)
    activation = (gate_proj * sigmoid_gate * up_proj).astype(jnp.bfloat16)
    mlp_part = sliced_product([(activation, down_weight)], N_TP)
    layer_rows = (hidden + RESIDUAL_SCALE * mlp_part).astype(jnp.bfloat16)
    live_rows = (own_segment == 0).astype(jnp.float32)[:, None]
    upstream = cotangent_group.astype(jnp.float32) * live_rows
    mlp_seed = (RESIDUAL_SCALE * upstream).astype(jnp.bfloat16)
    d_activation = contract_last(mlp_seed, down_weight)
    grad_down = contract_first(activation, mlp_seed)
    d_gate = (d_activation * up_proj * sigmoid_gate * (1.0 + gate_proj * (1.0 - sigmoid_gate))).astype(jnp.bfloat16)
    d_up = (d_activation * gate_proj * sigmoid_gate).astype(jnp.bfloat16)
    grad_gateup = jnp.stack([contract_first(normed_two, d_gate), contract_first(normed_two, d_up)])
    d_normed_two = sliced_product([(d_gate, jnp.transpose(gate_up[0])), (d_up, jnp.transpose(gate_up[1]))], N_TP)
    d_hidden_norm, grad_gain_mlp = norm_backward(d_normed_two, hidden, factor_two, gain_mlp)
    d_hidden = upstream + d_hidden_norm
    attn_seed = (RESIDUAL_SCALE * d_hidden).astype(jnp.bfloat16)
    d_attended = contract_last(attn_seed, out_weight).astype(jnp.bfloat16).reshape(group_rows, -1, VD)
    grad_out = contract_first(attended_flat, attn_seed)
    grad_kvup = jnp.zeros(kv_up.shape, jnp.float32)
    d_kv_pad = jnp.zeros((group_rows + block_rows, KVR), jnp.float32)
    d_rope_pad = jnp.zeros((group_rows + block_rows, ROPE), jnp.float32)
    d_query_parts = []
    for index_ctx in range(N_CTX):
        row_start = index_ctx * block_rows
        row_stop = row_start + block_rows
        key_latent, key_full, key_values, key_index, key_segment = key_sets[index_ctx]
        d_query, d_key, d_value = attend_backward(queries[row_start:row_stop], key_full, key_values, attended[row_start:row_stop], d_attended[row_start:row_stop], log_parts[index_ctx], own_index[row_start:row_stop], own_segment[row_start:row_stop], key_index, key_segment)
        d_expanded = jnp.concatenate([d_key[..., :NOPE], d_value], axis=2).reshape(2 * block_rows, -1).astype(jnp.bfloat16)
        grad_kvup = grad_kvup + contract_first(key_latent, d_expanded)
        d_kv_pad = d_kv_pad.at[row_start:row_start + 2 * block_rows].add(contract_last(d_expanded, kv_up))
        d_rope_pad = d_rope_pad.at[row_start:row_start + 2 * block_rows].add(lax.optimization_barrier(jnp.sum(d_key[..., NOPE:], axis=1)))
        d_query_parts.append(d_query)
    d_kv_normed = d_kv_pad[block_rows:]
    d_rope_key = rotate_backward(d_rope_pad[block_rows:], cosine, sine_table)
    d_query = jnp.concatenate(d_query_parts, axis=0)
    d_query_rope = rotate_backward(d_query[..., NOPE:], cosine[:, None], sine_table[:, None])
    d_query_flat = jnp.concatenate([d_query[..., :NOPE], d_query_rope], axis=2).reshape(group_rows, -1).astype(jnp.bfloat16)
    grad_qup = contract_first(query_normed, d_query_flat)
    d_query_normed = contract_last(d_query_flat, q_up)
    d_query_latent, grad_gain_query = norm_backward(d_query_normed, query_latent, factor_query, gain_query)
    d_kv_latent, grad_gain_latent = norm_backward(d_kv_normed, kv_latent, factor_kv, gain_latent)
    d_latents = jnp.concatenate([d_query_latent, d_kv_latent, d_rope_key], axis=1).astype(jnp.bfloat16)
    grad_both = contract_first(normed_one, d_latents)
    d_normed_one = contract_last(d_latents, down_both)
    d_input_norm, grad_gain_attn = norm_backward(d_normed_one, inputs, factor_one, gain_attn)
    input_rows = (d_hidden + d_input_norm).astype(jnp.bfloat16)
    grads = (grad_both[:, :QR], grad_both[:, QR:], grad_qup, grad_kvup, grad_out, grad_gateup, grad_down, jnp.stack([grad_gain_attn, grad_gain_mlp]), jnp.concatenate([grad_gain_query, grad_gain_latent]))
    return (layer_rows, input_rows, grads)

def adamw_update(parameter, gradient, first_moment, second_moment, decay_rate):
    first_new = BETA_ONE * first_moment + (1.0 - BETA_ONE) * gradient
    second_new = BETA_TWO * second_moment + (1.0 - BETA_TWO) * gradient * gradient
    first_hat = first_new / (1.0 - BETA_ONE ** STEP)
    second_hat = second_new / (1.0 - BETA_TWO ** STEP)
    updated = parameter - LEARN_RATE * (first_hat / (jnp.sqrt(second_hat) + ADAM_EPS) + decay_rate * parameter)
    return (updated, first_new, second_new)

def reference(tokens, cotangent, lengths, w_qdown, w_kvdown, w_qup, w_kvup, w_out, w_gateup, w_down, g_norms, g_latent, m_qdown, m_kvdown, m_qup, m_kvup, m_out, m_gateup, m_down, m_norms, m_latent, v_qdown, v_kvdown, v_qup, v_kvup, v_out, v_gateup, v_down, v_norms, v_latent):
    params = (w_qdown, w_kvdown, w_qup, w_kvup, w_out, w_gateup, w_down, g_norms, g_latent)
    firsts = (m_qdown, m_kvdown, m_qup, m_kvup, m_out, m_gateup, m_down, m_norms, m_latent)
    seconds = (v_qdown, v_kvdown, v_qup, v_kvup, v_out, v_gateup, v_down, v_norms, v_latent)
    gains_norm = rounded(g_norms)
    gains_latent = rounded(g_latent)
    used = (w_qdown.astype(jnp.bfloat16), w_kvdown.astype(jnp.bfloat16), w_qup.astype(jnp.bfloat16), w_kvup.astype(jnp.bfloat16), w_out.astype(jnp.bfloat16), w_gateup.astype(jnp.bfloat16), w_down.astype(jnp.bfloat16), gains_norm[0], gains_norm[1], gains_latent[:QR], gains_latent[QR:])
    group_rows = BLOCK_TOK * N_CTX

    def scan_group(totals, pieces):
        layer_rows, input_rows, grads = layer_group(used, pieces[0], pieces[1], pieces[2])
        return (tuple((total_one + grad_one for total_one, grad_one in zip(totals, grads))), (layer_rows, input_rows))
    initial = tuple((jnp.zeros(parameter.shape, jnp.float32) for parameter in params))
    grad_totals, (layer_rows, input_rows) = lax.scan(scan_group, initial, (tokens.reshape(N_FSDP, group_rows, D), cotangent.reshape(N_FSDP, group_rows, D), lengths))
    layer_out = layer_rows.reshape(TOKENS, D)
    grad_input = input_rows.reshape(TOKENS, D)
    new_params = []
    new_firsts = []
    new_seconds = []
    for param_index in range(9):
        decay_rate = WEIGHT_DECAY if param_index < 7 else 0.0
        gradient = grad_totals[param_index]
        limit = CLIP_RMS * gradient.size ** 0.5
        clipped = gradient * (limit / jnp.maximum(jnp.sqrt(jnp.sum(gradient * gradient)), limit))
        updated, first_new, second_new = adamw_update(params[param_index], clipped, firsts[param_index], seconds[param_index], decay_rate)
        new_params.append(updated)
        new_firsts.append(first_new)
        new_seconds.append(second_new)
    return (layer_out, grad_input, grad_totals[0], grad_totals[1], grad_totals[2], grad_totals[3], grad_totals[4], grad_totals[5], grad_totals[6], grad_totals[7], grad_totals[8], new_params[0], new_params[1], new_params[2], new_params[3], new_params[4], new_params[5], new_params[6], new_firsts[0], new_firsts[1], new_firsts[2], new_firsts[3], new_firsts[4], new_firsts[5], new_firsts[6], new_firsts[7], new_firsts[8], new_seconds[0], new_seconds[1], new_seconds[2], new_seconds[3], new_seconds[4], new_seconds[5], new_seconds[6], new_seconds[7], new_seconds[8])
```

```python
import functools

import jax
import jax.numpy as jnp
from jax import lax
from jax.experimental import pallas as pl
from jax.experimental.pallas import tpu as pltpu
from jax.sharding import PartitionSpec as P

D = 2560
H = 40
NOPE = 64
ROPE = 32
VD = 64
QR = 768
KVR = 256
FF = 6400
STEP = 3
HEAD = NOPE + ROPE
LAT = QR + KVR + ROPE

EPS_NORM = 1e-05
RESIDUAL_SCALE = 1.4 / 62**0.5
ROPE_BASE = 10000.0
MASK_VALUE = -1e30
BETA_ONE = 0.9
BETA_TWO = 0.95
ADAM_EPS = 1e-08
LEARN_RATE = 0.1
WEIGHT_DECAY = 0.1
CLIP_RMS = 0.0002
LOG2E = 1.4426950408889634
LN2 = 0.6931471805599453

BF = jnp.bfloat16
F32 = jnp.float32
MESH = pl.DeviceIdType.MESH
MIB = 1024 * 1024


def dot_nn(a, b):
    return lax.dot_general(a, b, (((1,), (0,)), ((), ())), preferred_element_type=F32)


def dot_nt(a, b):
    return lax.dot_general(a, b, (((1,), (1,)), ((), ())), preferred_element_type=F32)


def dot_tn(a, b):
    return lax.dot_general(a, b, (((0,), (0,)), ((), ())), preferred_element_type=F32)


def line_reduce_kernel(chunks, x_ref, o_ref, near, cross, part, in_send, in_recv, mid_send, mid_recv, out_send, out_recv):
    z = lax.axis_index("tp")
    rows = x_ref.shape[0] // chunks
    is_end = jnp.logical_or(z == 0, z == 3)
    is_mid = jnp.logical_not(is_end)
    partner = jnp.where(z == 0, 1, jnp.where(z == 3, 2, jnp.where(z == 1, 0, 3)))
    across = jnp.where(z == 1, 2, 1)

    barrier = pltpu.get_barrier_semaphore()
    pl.semaphore_signal(barrier, inc=1, device_id={"tp": partner}, device_id_type=MESH)

    @pl.when(is_mid)
    def _():
        pl.semaphore_signal(barrier, inc=1, device_id={"tp": across}, device_id_type=MESH)
        pl.semaphore_wait(barrier, 2)

    @pl.when(is_end)
    def _():
        pl.semaphore_wait(barrier, 1)

    def piece(k):
        return pl.ds(pl.multiple_of(k * rows, rows), rows)

    def to_mid(k):
        return pltpu.make_async_remote_copy(
            src_ref=x_ref.at[piece(k)], dst_ref=near.at[piece(k)], send_sem=in_send.at[k], recv_sem=in_recv.at[k],
            device_id={"tp": partner}, device_id_type=MESH,
        )

    def over(k):
        return pltpu.make_async_remote_copy(
            src_ref=part.at[piece(k)], dst_ref=cross.at[piece(k)], send_sem=mid_send.at[k], recv_sem=mid_recv.at[k],
            device_id={"tp": across}, device_id_type=MESH,
        )

    def to_end(k):
        return pltpu.make_async_remote_copy(
            src_ref=o_ref.at[piece(k)], dst_ref=o_ref.at[piece(k)], send_sem=out_send.at[k], recv_sem=out_recv.at[k],
            device_id={"tp": partner}, device_id_type=MESH,
        )

    @pl.when(is_end)
    def _():
        def begin(k, carry):
            to_mid(k).start()
            return carry

        def finish(k, carry):
            to_mid(k).wait_send()
            to_end(k).wait_recv()
            return carry

        lax.fori_loop(0, chunks, begin, 0)
        lax.fori_loop(0, chunks, finish, 0)

    @pl.when(is_mid)
    def _():
        def first(k):
            to_mid(k).wait_recv()
            part[piece(k)] = (x_ref[piece(k)].astype(F32) + near[piece(k)].astype(F32)).astype(BF)
            over(k).start()

        def second(k):
            over(k).wait_recv()
            o_ref[piece(k)] = (part[piece(k)].astype(F32) + cross[piece(k)].astype(F32)).astype(BF)
            to_end(k).start()

        first(0)

        def step(k, carry):
            first(k)
            second(k - 1)
            return carry

        lax.fori_loop(1, chunks, step, 0)
        second(chunks - 1)

        def finish(k, carry):
            over(k).wait_send()
            to_end(k).wait_send()
            return carry

        lax.fori_loop(0, chunks, finish, 0)


def line_reduce(x, chunks, collective_id):
    if lax.axis_size("tp") != 4:
        return lax.psum(x, "tp")
    rows, cols = x.shape
    dma = pltpu.SemaphoreType.DMA((chunks,))
    return pl.pallas_call(
        functools.partial(line_reduce_kernel, chunks),
        out_shape=jax.ShapeDtypeStruct((rows, cols), BF),
        in_specs=[pl.BlockSpec(memory_space=pltpu.VMEM)],
        out_specs=pl.BlockSpec(memory_space=pltpu.VMEM),
        scratch_shapes=[pltpu.VMEM((rows, cols), BF)] * 3 + [dma] * 6,
        compiler_params=pltpu.CompilerParams(
            collective_id=collective_id, has_side_effects=True, vmem_limit_bytes=40 * MIB
        ),
        cost_estimate=pl.CostEstimate(flops=rows * cols * 2, bytes_accessed=rows * cols * 40, transcendentals=0),
        name="line_reduce",
    )(x)


BQ = 512


def attend_forward_kernel(
    qn_ref, kn_ref, krx_ref, cos_ref, sin_ref, segq_ref, wq_ref, wk_ref, wv_ref, o_ref, lse_ref, q_ref, k_ref, v_ref
):
    i = pl.program_id(1)
    rows = qn_ref.shape[0]

    @pl.when(i == 0)
    def _():
        for r in range(rows // BQ):
            part = pl.ds(r * BQ, BQ)
            qf = dot_nt(wq_ref[0], qn_ref[part, :]) * (LOG2E * HEAD**-0.5)
            cos = cos_ref[:, part]
            sin = sin_ref[:, part]
            one, two = qf[NOPE : NOPE + 16], qf[NOPE + 16 : HEAD]
            q_ref[0, 0:NOPE, part] = qf[:NOPE].astype(BF)
            q_ref[0, NOPE : NOPE + 16, part] = (one * cos - two * sin).astype(BF)
            q_ref[0, NOPE + 16 : HEAD, part] = (two * cos + one * sin).astype(BF)
            q_ref[0, HEAD : HEAD + 16, part] = segq_ref[:, part]
            q_ref[0, HEAD + 16 : 128, part] = jnp.zeros((16, BQ), BF)
            k_ref[0, part, :] = (dot_nn(kn_ref[part, :], wk_ref[0]) + krx_ref[part, :].astype(F32)).astype(BF)
            vt = dot_nt(wv_ref[0], kn_ref[part, :])
            row = lax.broadcasted_iota(jnp.int32, vt.shape, 0)
            v_ref[0, :, part] = jnp.where(row == VD, 1.0, vt).astype(BF)

    here = pl.ds(pl.multiple_of(i * BQ, BQ), BQ)
    q = q_ref[0, :, here]

    def block(j, carried, masked):
        m, acc = carried
        there = pl.ds(pl.multiple_of(j * BQ, BQ), BQ)
        s = dot_nn(k_ref[0, there, :], q)
        if masked:
            krow = lax.broadcasted_iota(jnp.int32, s.shape, 0)
            qcol = lax.broadcasted_iota(jnp.int32, s.shape, 1)
            s = jnp.where(krow <= qcol, s, MASK_VALUE)
        top = jnp.maximum(m, jnp.max(s, axis=0, keepdims=True))
        p = jnp.exp2(s - top).astype(BF)
        acc = acc * jnp.exp2(m - top) + dot_nn(v_ref[0, :, there], p)
        return top, acc

    start = (jnp.full((1, BQ), -3e38, F32), jnp.zeros((80, BQ), F32))
    carried = lax.fori_loop(0, i, lambda j, c: block(j, c, False), start)
    m, acc = block(i, carried, True)
    total = acc[VD : VD + 1]
    o_ref[0, :, here] = (acc[:VD] / total).astype(BF)
    lse_ref[0, :, here] = m + jnp.log2(total)


def attend_forward(qn, kn, krx, cos, sin, segq, wq, wk, wv):
    heads = wq.shape[0]
    rows = qn.shape[0]
    whole = lambda a: pl.BlockSpec(a.shape, lambda h, i: (0,) * a.ndim)
    per_head = lambda a, b: pl.BlockSpec((1, a, b), lambda h, i: (h, 0, 0))
    return pl.pallas_call(
        attend_forward_kernel,
        grid=(heads, rows // BQ),
        in_specs=[whole(qn), whole(kn), whole(krx), whole(cos), whole(sin), whole(segq)]
        + [per_head(*w.shape[1:]) for w in (wq, wk, wv)],
        out_specs=[per_head(VD, rows), per_head(1, rows), per_head(128, rows), per_head(rows, 128), per_head(80, rows)],
        out_shape=[
            jax.ShapeDtypeStruct((heads, VD, rows), BF),
            jax.ShapeDtypeStruct((heads, 1, rows), F32),
            jax.ShapeDtypeStruct((heads, 128, rows), BF),
            jax.ShapeDtypeStruct((heads, rows, 128), BF),
            jax.ShapeDtypeStruct((heads, 80, rows), BF),
        ],
        compiler_params=pltpu.CompilerParams(vmem_limit_bytes=40 * MIB),
        cost_estimate=pl.CostEstimate(flops=heads * rows * rows * 320, bytes_accessed=30 * MIB, transcendentals=0),
        name="attend_forward",
    )(qn, kn, krx, cos, sin, segq, wq, wk, wv)


def attend_backward_kernel(q_ref, k_ref, v_ref, o_ref, do_ref, lse_ref, cos_ref, sin_ref, dq_ref, de_ref, dkr_ref, dq_acc, delta):
    h, j = pl.program_id(0), pl.program_id(1)
    rows = k_ref.shape[1]
    blocks = rows // BQ

    @pl.when(j == 0)
    def _():
        dq_acc[...] = jnp.zeros_like(dq_acc)
        delta[...] = jnp.sum(o_ref[0].astype(F32) * do_ref[0].astype(F32), axis=0, keepdims=True)

    there = pl.ds(pl.multiple_of(j * BQ, BQ), BQ)
    k = k_ref[0, there, :]
    kt = k.astype(F32).T.astype(BF)
    v = v_ref[0, 0:VD, there].astype(F32).T.astype(BF)

    def block(i, carried, masked):
        dk, dv = carried
        here = pl.ds(pl.multiple_of(i * BQ, BQ), BQ)
        q = q_ref[0, :, here]
        do = do_ref[0, :, here]
        s = dot_nn(k, q)
        if masked:
            krow = lax.broadcasted_iota(jnp.int32, s.shape, 0)
            qcol = lax.broadcasted_iota(jnp.int32, s.shape, 1)
            s = jnp.where(krow <= qcol, s, MASK_VALUE)
        p = jnp.exp2(s - lse_ref[0, :, here])
        dp = dot_nn(v, do)
        ds = (p * (dp - delta[:, here])).astype(BF)
        dv = dv + dot_nt(p.astype(BF), do)
        dk = dk + dot_nt(ds, q)
        dq_acc[:, here] = dq_acc[:, here] + dot_nn(kt, ds)
        return dk, dv

    start = (jnp.zeros((BQ, 128), F32), jnp.zeros((BQ, VD), F32))
    carried = block(j, start, True)
    dk, dv = lax.fori_loop(j + 1, blocks, lambda i, c: block(i, c, False), carried)
    dk = dk * LN2
    de_ref[there, 0:NOPE] = dk[:, :NOPE].astype(BF)
    de_ref[there, NOPE:128] = dv.astype(BF)

    @pl.when(h == 0)
    def _():
        dkr_ref[there, :] = dk

    @pl.when(h > 0)
    def _():
        dkr_ref[there, :] = dkr_ref[there, :] + dk

    @pl.when(j == blocks - 1)
    def _():
        dq = dq_acc[...] * HEAD**-0.5
        cos, sin = cos_ref[...], sin_ref[...]
        one, two = dq[NOPE : NOPE + 16], dq[NOPE + 16 : HEAD]
        dq_ref[0:NOPE, :] = dq[:NOPE].astype(BF)
        dq_ref[NOPE : NOPE + 16, :] = (one * cos + two * sin).astype(BF)
        dq_ref[NOPE + 16 : HEAD, :] = (two * cos - one * sin).astype(BF)


def attend_backward(q, k, v, o, do, lse, cos, sin):
    heads = q.shape[0]
    rows = k.shape[1]
    whole = lambda a: pl.BlockSpec(a.shape, lambda h, i: (0,) * a.ndim)
    per_head = lambda a: pl.BlockSpec((1,) + a.shape[1:], lambda h, i: (h, 0, 0))
    return pl.pallas_call(
        attend_backward_kernel,
        grid=(heads, rows // BQ),
        in_specs=[per_head(a) for a in (q, k, v, o, do, lse)] + [whole(cos), whole(sin)],
        out_specs=[
            pl.BlockSpec((HEAD, rows), lambda h, i: (h, 0)),
            pl.BlockSpec((rows, 128), lambda h, i: (0, h)),
            pl.BlockSpec((rows, 128), lambda h, i: (0, 0)),
        ],
        out_shape=[
            jax.ShapeDtypeStruct((heads * HEAD, rows), BF),
            jax.ShapeDtypeStruct((rows, heads * 128), BF),
            jax.ShapeDtypeStruct((rows, 128), F32),
        ],
        scratch_shapes=[pltpu.VMEM((128, rows), F32), pltpu.VMEM((1, rows), F32)],
        compiler_params=pltpu.CompilerParams(vmem_limit_bytes=40 * MIB),
        cost_estimate=pl.CostEstimate(flops=heads * rows * rows * 900, bytes_accessed=30 * MIB, transcendentals=0),
        name="attend_backward",
    )(q, k, v, o, do, lse, cos, sin)


LINE = 32
MLP_ROWS = 256
TILES = ((0, 384), (384, 384), (768, 384), (1152, 448))


def line_places(z):
    is_end = jnp.logical_or(z == 0, z == 3)
    partner = jnp.where(z == 0, 1, jnp.where(z == 3, 2, jnp.where(z == 1, 0, 3)))
    return is_end, jnp.logical_not(is_end), partner, jnp.where(z == 1, 2, 1)


def line_barrier(is_mid, is_end, partner, across):
    barrier = pltpu.get_barrier_semaphore()
    pl.semaphore_signal(barrier, inc=1, device_id={"tp": partner}, device_id_type=MESH)

    @pl.when(is_mid)
    def _():
        pl.semaphore_signal(barrier, inc=1, device_id={"tp": across}, device_id_type=MESH)
        pl.semaphore_wait(barrier, 2)

    @pl.when(is_end)
    def _():
        pl.semaphore_wait(barrier, 1)


def line_copies(source, near, cross, total, sems, partner, across):
    in_send, in_recv, mid_send, mid_recv, out_send, out_recv = sems

    def piece(k):
        return pl.ds(pl.multiple_of(k * LINE, LINE), LINE)

    def copy(src, dst, send, recv, k, to):
        return pltpu.make_async_remote_copy(
            src_ref=src.at[piece(k)], dst_ref=dst.at[piece(k)], send_sem=send.at[k], recv_sem=recv.at[k],
            device_id={"tp": to}, device_id_type=MESH,
        )

    to_mid = lambda k: copy(source, near, in_send, in_recv, k, partner)
    over = lambda k: copy(near, cross, mid_send, mid_recv, k, across)
    to_end = lambda k: copy(total, total, out_send, out_recv, k, partner)

    def first(k):
        to_mid(k).wait_recv()
        near[piece(k)] = (source[piece(k)].astype(F32) + near[piece(k)].astype(F32)).astype(BF)
        over(k).start()

    def second(k):
        over(k).wait_recv()
        total[piece(k)] = (near[piece(k)].astype(F32) + cross[piece(k)].astype(F32)).astype(BF)
        to_end(k).start()

    return to_mid, over, to_end, first, second


def each(count, body):
    def step(k, carry):
        body(k)
        return carry

    lax.fori_loop(0, count, step, 0)


def block_kernel(
    att_ref, x_ref, out_ref, gain_ref, seed_any, gu_any, down_any,
    hid_any, dn_any, mo_any, n2t_any, act_any, dg_any, du_any,
    xb, near, cross, total, gu, down, n2, n2t, seed, act, dg, du,
    load_sem, seed_sem, hid_sem, dn_sem, mo_sem, n2t_sem, act_sem, dg_sem, du_sem, *sems,
):
    z = lax.axis_index("tp")
    is_end, is_mid, partner, across = line_places(z)
    to_mid, over, to_end, first, second = line_copies(xb, near, cross, total, sems, partner, across)
    count = xb.shape[0] // LINE
    group = MLP_ROWS // LINE
    groups = count // group
    width = x_ref.shape[1]

    def rows_of(m):
        return pl.ds(pl.multiple_of(m * MLP_ROWS, MLP_ROWS), MLP_ROWS)

    load_gu = pltpu.make_async_copy(gu_any, gu, load_sem.at[0])
    load_down = pltpu.make_async_copy(down_any, down, load_sem.at[1])
    load_seed = lambda m: pltpu.make_async_copy(seed_any.at[rows_of(m)], seed, seed_sem.at[m])
    save_hid = lambda m: pltpu.make_async_copy(total.at[rows_of(m)], hid_any.at[rows_of(m)], hid_sem.at[m])
    save_dn = lambda m: pltpu.make_async_copy(xb.at[rows_of(m)], dn_any.at[rows_of(m)], dn_sem.at[m])
    save_mo = lambda m: pltpu.make_async_copy(cross.at[rows_of(m)], mo_any.at[rows_of(m)], mo_sem.at[m])
    save_n2t = lambda m: pltpu.make_async_copy(n2t, n2t_any.at[:, rows_of(m)], n2t_sem.at[m])
    save_act = lambda m: pltpu.make_async_copy(act, act_any.at[rows_of(m)], act_sem.at[m])
    save_dg = lambda m: pltpu.make_async_copy(dg, dg_any.at[rows_of(m)], dg_sem.at[m])
    save_du = lambda m: pltpu.make_async_copy(du, du_any.at[rows_of(m)], du_sem.at[m])

    load_seed(0).start()
    load_gu.start()
    load_down.start()
    line_barrier(is_mid, is_end, partner, across)

    mine = pl.ds(pl.multiple_of(z * width, 128), width)
    per = 128

    def project(p):
        rows = pl.ds(pl.multiple_of(p * per, per), per)
        part = dot_nt(att_ref[rows, :], out_ref[...]) * RESIDUAL_SCALE
        xb[rows, :] = part.astype(BF)
        xb[rows, mine] = (xb[rows, mine].astype(F32) + x_ref[rows, :].astype(F32)).astype(BF)

        @pl.when(is_end)
        def _():
            for n in range(per // LINE):
                to_mid(p * (per // LINE) + n).start()

    each(xb.shape[0] // per, project)

    @pl.when(is_mid)
    def _():
        first(0)

        def both(k):
            first(k + 1)
            second(k)

        each(group, both)

    def mlp(m):
        rows = rows_of(m)

        @pl.when(is_end)
        def _():
            def arrive(n):
                to_mid(m * group + n).wait_send()
                to_end(m * group + n).wait_recv()

            each(group, arrive)

        def serve(n):
            k = (m + 1) * group + 1 + n

            @pl.when(jnp.logical_and(is_mid, k < count))
            def _():
                first(k)

            @pl.when(jnp.logical_and(is_mid, k <= count))
            def _():
                second(k - 1)

        save_hid(m).start()

        @pl.when(m > 0)
        def _():
            save_n2t(m - 1).wait()
            save_act(m - 1).wait()
            save_dg(m - 1).wait()
            save_du(m - 1).wait()

        def normalize(r):
            here = pl.ds(pl.multiple_of(r * 32, 32), 32)
            h = total[pl.ds(pl.multiple_of(m * MLP_ROWS + r * 32, 32), 32), :].astype(F32)
            factor = lax.rsqrt(jnp.mean(h * h, axis=1, keepdims=True) + EPS_NORM)
            n2[here, :] = (h * factor * gain_ref[...]).astype(BF)

        each(MLP_ROWS // 32, normalize)

        def turn(c):
            cols = pl.ds(pl.multiple_of(c * 256, 256), 256)
            n2t[cols, :] = n2[:, cols].astype(F32).T.astype(BF)

        each(D // 256, turn)
        save_n2t(m).start()
        load_seed(m).wait()

        @pl.when(m == 0)
        def _():
            load_gu.wait()
            load_down.wait()

        for t, (at, size) in enumerate(TILES):
            cols = pl.ds(at, size)
            g = dot_nn(n2[...], gu[0, :, cols])
            u = dot_nn(n2[...], gu[1, :, cols])
            d = dot_nn(seed[...], down[:, cols])
            sig = jax.nn.sigmoid(g)
            act[:, cols] = (g * sig * u).astype(BF)
            dg[:, cols] = (d * u * sig * (1.0 + g * (1.0 - sig))).astype(BF)
            du[:, cols] = (d * g * sig).astype(BF)
            serve(t)
        save_act(m).start()
        save_dg(m).start()
        save_du(m).start()

        @pl.when(m + 1 < groups)
        def _():
            load_seed(m + 1).start()

        for n in range(4):
            cols = pl.ds(n * 640, 640)
            xb[rows, cols] = (dot_nt(dg[...], gu[0, cols, :]) + dot_nt(du[...], gu[1, cols, :])).astype(BF)
            cross[rows, cols] = dot_nt(act[...], down[cols, :]).astype(BF)
            serve(4 + n)
        save_dn(m).start()
        save_mo(m).start()

    each(groups, mlp)

    def finish(m):
        save_hid(m).wait()
        save_dn(m).wait()
        save_mo(m).wait()

    each(groups, finish)
    save_n2t(groups - 1).wait()
    save_act(groups - 1).wait()
    save_dg(groups - 1).wait()
    save_du(groups - 1).wait()

    @pl.when(is_mid)
    def _():
        def sent(k):
            over(k).wait_send()
            to_end(k).wait_send()

        each(count, sent)


def block_forward(att, x, out_t, gain, seed, gate_up, down_t):
    rows = att.shape[0]
    hidden_units = down_t.shape[1]
    count, groups = rows // LINE, rows // MLP_ROWS
    vmem = pl.BlockSpec(memory_space=pltpu.VMEM)
    anywhere = pl.BlockSpec(memory_space=pl.ANY)
    wide = jax.ShapeDtypeStruct((rows, D), BF)
    units = jax.ShapeDtypeStruct((rows, hidden_units), BF)
    dma = pltpu.SemaphoreType.DMA
    return pl.pallas_call(
        block_kernel,
        out_shape=[wide, wide, wide, jax.ShapeDtypeStruct((D, rows), BF), units, units, units],
        in_specs=[vmem] * 4 + [anywhere] * 3,
        out_specs=[anywhere] * 7,
        scratch_shapes=[pltpu.VMEM((rows, D), BF)] * 4
        + [
            pltpu.VMEM(gate_up.shape, BF),
            pltpu.VMEM(down_t.shape, BF),
            pltpu.VMEM((MLP_ROWS, D), BF),
            pltpu.VMEM((D, MLP_ROWS), BF),
            pltpu.VMEM((MLP_ROWS, D), BF),
        ]
        + [pltpu.VMEM((MLP_ROWS, hidden_units), BF)] * 3
        + [dma((2,))]
        + [dma((groups,))] * 8
        + [dma((count,))] * 6,
        compiler_params=pltpu.CompilerParams(collective_id=3, has_side_effects=True, vmem_limit_bytes=63 * MIB),
        cost_estimate=pl.CostEstimate(flops=rows * D * hidden_units * 12, bytes_accessed=400 * MIB, transcendentals=0),
        name="block_forward",
    )(att, x, out_t, gain, seed, gate_up, down_t)


def swap_cores(v):
    return lax.ppermute(v, "ctx", [(0, 1), (1, 0)])


def in_core_order(mine, other, core, axis):
    return jnp.where(
        core == 0, jnp.concatenate([mine, other], axis=axis), jnp.concatenate([other, mine], axis=axis)
    )


def gather_shards(v):
    return lax.all_gather(v, ("fsdp", "ctx"), axis=0, tiled=True)


X_SWAP = [(0, 1), (1, 0), (2, 3), (3, 2)]
Y_SWAP = [(0, 2), (2, 0), (1, 3), (3, 1)]


def take(v, which, axis):
    return lax.dynamic_index_in_dim(v, which, axis, keepdims=False)


def add_up(a, b):
    return (a.astype(F32) + b.astype(F32)).astype(BF)


def keep_half(v, axis, which, name, pairs):
    other = lax.ppermute(take(v, 1 - which, axis), name, pairs)
    return add_up(take(v, which, axis), other)


def scatter_fsdp(v):
    if lax.axis_size("fsdp") != 4:
        return lax.psum_scatter(v, "fsdp", scatter_dimension=0, tiled=False)
    place = lax.axis_index("fsdp")
    y, x = place // 2, place % 2
    _, rows, cols = v.shape
    v = v.reshape(2, 2, 2, rows // 2, cols)
    first = keep_half(v[:, :, 0], 1, x, "fsdp", X_SWAP)
    second = keep_half(v[:, :, 1], 0, y, "fsdp", Y_SWAP)
    first = keep_half(first, 0, y, "fsdp", Y_SWAP)
    second = keep_half(second, 0, x, "fsdp", X_SWAP)
    return jnp.concatenate([first, second], axis=0)


def scatter_grads(v):
    fsdp, ctx = lax.axis_size("fsdp"), lax.axis_size("ctx")
    rows, cols = v.shape
    v = v.reshape(fsdp, ctx, rows // (fsdp * ctx), cols)
    return scatter_fsdp(keep_half(v, 1, lax.axis_index("ctx"), "ctx", [(0, 1), (1, 0)]))


def split_two(v):
    high = v.astype(BF)
    return high, (v - high.astype(F32)).astype(BF)


def adamw_update(parameter, gradient, first_moment, second_moment, decay_rate):
    first_new = BETA_ONE * first_moment + (1.0 - BETA_ONE) * gradient
    second_new = BETA_TWO * second_moment + (1.0 - BETA_TWO) * gradient * gradient
    first_hat = first_new / (1.0 - BETA_ONE**STEP)
    second_hat = second_new / (1.0 - BETA_TWO**STEP)
    updated = parameter - LEARN_RATE * (
        first_hat / (jnp.sqrt(second_hat) + ADAM_EPS) + decay_rate * parameter
    )
    return (updated, first_new, second_new)


def norm_backward(incoming, values, factor, gain):
    scaled = incoming * gain
    gain_grad = jnp.sum(incoming * values * factor, axis=0)
    result = factor * scaled - values * factor**3 * jnp.mean(scaled * values, axis=1, keepdims=True)
    return (result, gain_grad)


def local(*args):
    tokens, cotangent, lengths = args[:3]
    params, firsts, seconds = args[3:12], args[12:21], args[21:30]
    w_qdown, w_kvdown, w_qup, w_kvup, w_out, w_gateup, w_down, g_norms, g_latent = params
    n_tp, n_ctx, n_fsdp = lax.axis_size("tp"), lax.axis_size("ctx"), lax.axis_size("fsdp")
    tp, core = lax.axis_index("tp"), lax.axis_index("ctx")
    rows, width = tokens.shape
    slot = rows * n_ctx
    heads_all = H // n_tp
    by_head = heads_all % n_ctx == 0
    heads = heads_all // n_ctx if by_head else heads_all

    down_t = jnp.concatenate(
        [gather_shards(w_qdown.T.astype(BF)), gather_shards(w_kvdown.T.astype(BF))], axis=0
    )
    q_up = gather_shards(w_qup.astype(BF))
    kv_up = gather_shards(w_kvup.astype(BF))
    gain_lat = lax.all_gather(g_latent.astype(BF), ("fsdp", "ctx"), axis=0, tiled=True).astype(F32)
    out_t = gather_shards(w_out.T.astype(BF))
    gate_up = lax.all_gather(w_gateup.astype(BF), ("fsdp", "ctx"), axis=1, tiled=True)
    ff_down_t = gather_shards(w_down.T.astype(BF))
    if by_head:
        q_up_here = lax.dynamic_slice_in_dim(q_up, core * heads * HEAD, heads * HEAD, 1)
        kv_up_here = lax.dynamic_slice_in_dim(kv_up, core * heads * 128, heads * 128, 1)
    else:
        q_up_here, kv_up_here = q_up, kv_up
    wq = q_up_here.T.reshape(heads, HEAD, QR)
    kv3 = kv_up_here.reshape(KVR, heads, 128)
    wk = jnp.pad(jnp.transpose(kv3[:, :, :NOPE], (1, 0, 2)), ((0, 0), (0, 0), (0, 128 - NOPE)))
    wv = jnp.pad(jnp.transpose(kv3[:, :, NOPE:], (1, 2, 0)), ((0, 0), (0, 80 - VD), (0, 0)))

    gains_norm = g_norms.astype(BF)
    gain_attn = gains_norm[0].astype(F32)
    gain_query, gain_kv = gain_lat[:QR], gain_lat[QR:]

    seq_length = lengths[0, 0]
    index = jnp.arange(slot, dtype=jnp.int32)
    segment = (index >= seq_length).astype(jnp.int32)
    position = (index - segment * seq_length).astype(F32)
    frequency = ROPE_BASE ** (-2.0 * jnp.arange(ROPE // 2, dtype=F32) / ROPE)
    angles = frequency[:, None] * position[None, :]
    cos_t, sin_t = jnp.cos(angles), jnp.sin(angles)
    own_cos = lax.dynamic_slice_in_dim(cos_t, core * rows, rows, 1).T
    own_sin = lax.dynamic_slice_in_dim(sin_t, core * rows, rows, 1).T
    own_segment = lax.dynamic_slice_in_dim(segment, core * rows, rows, 0)
    live = (own_segment == 0).astype(F32)[:, None]
    seg_f = segment.astype(F32)
    seg_q = jnp.concatenate([seg_f[None], 1.0 - seg_f[None], jnp.zeros((14, slot), F32)], axis=0).astype(BF)
    seg_k = (MASK_VALUE * jnp.concatenate([1.0 - seg_f[:, None], seg_f[:, None]], axis=1)).astype(BF)

    inputs = tokens.astype(F32)
    scaled_in = (inputs * gain_attn).astype(BF)
    lat_part = dot_nt(scaled_in, down_t)
    squares_high, squares_low = split_two(jnp.sum(inputs * inputs, axis=1))
    column = jnp.arange(2 * n_tp)
    stats = jnp.where(
        column[None] == 2 * tp, squares_high[:, None], jnp.where(column[None] == 2 * tp + 1, squares_low[:, None], 0)
    ).astype(BF)
    lat_wide = 1152
    payload = jnp.concatenate(
        [lat_part.astype(BF), stats, jnp.zeros((rows, lat_wide - LAT - 2 * n_tp), BF)], axis=1
    )
    gain_rows = jnp.where((jnp.arange(64) == tp)[:, None], gains_norm[1][None], 0).astype(BF)
    gain_rows = jnp.pad(gain_rows, ((0, 0), (0, lat_wide - width)))
    reduced = line_reduce(jnp.concatenate([payload, gain_rows], axis=0), 17, 0)
    gain_mlp = reduced[rows : rows + n_tp, :width].reshape(n_tp * width).astype(F32)
    lat_sum = reduced[:rows].astype(F32)
    factor_one = lax.rsqrt(jnp.sum(lat_sum[:, LAT : LAT + 2 * n_tp], axis=1) / D + EPS_NORM)[:, None]
    latents = lat_sum[:, :LAT] * factor_one
    query_latent = latents[:, :QR]
    kv_latent = latents[:, QR : QR + KVR]
    rope_raw = latents[:, QR + KVR :]
    factor_query = lax.rsqrt(jnp.mean(query_latent * query_latent, axis=1, keepdims=True) + EPS_NORM)
    factor_kv = lax.rsqrt(jnp.mean(kv_latent * kv_latent, axis=1, keepdims=True) + EPS_NORM)
    query_normed = (query_latent * factor_query * gain_query).astype(BF)
    kv_normed = (kv_latent * factor_kv * gain_kv).astype(BF)
    r_one, r_two = rope_raw[:, : ROPE // 2], rope_raw[:, ROPE // 2 :]
    rope_key = jnp.concatenate(
        [r_one * own_cos - r_two * own_sin, r_two * own_cos + r_one * own_sin], axis=1
    ).astype(BF)
    normed_lat = jnp.concatenate([query_normed, kv_normed, rope_key], axis=1)
    lat_both = in_core_order(normed_lat, swap_cores(normed_lat), core, 0)
    qn, kn, kr = lat_both[:, :QR], lat_both[:, QR : QR + KVR], lat_both[:, QR + KVR :]
    krx = jnp.concatenate(
        [jnp.zeros((slot, NOPE), BF), kr, seg_k, jnp.zeros((slot, 128 - HEAD - 2), BF)], axis=1
    )

    att_heads, lse, q_t, k_rows, v_t = attend_forward(qn, kn, krx, cos_t, sin_t, seg_q, wq, wk, wv)
    att_flat = att_heads.reshape(heads * VD, slot)
    own_cols = lambda v: lax.dynamic_slice_in_dim(v, core * rows, rows, 1)
    if by_head:
        other = swap_cores(lax.dynamic_slice_in_dim(att_flat, (1 - core) * rows, rows, 1))
        att_t = in_core_order(own_cols(att_flat), other, core, 0)
    else:
        att_t = own_cols(att_flat)

    feature_owner = jnp.arange(D) // width
    dy = cotangent.astype(F32) * live
    mlp_seed = (RESIDUAL_SCALE * dy).astype(BF)
    if n_tp == 4:
        hidden, d_normed_part, mlp_part, normed_two_t, activation, d_gate, d_up = block_forward(
            att_t.T, tokens, out_t, gain_mlp[None], mlp_seed, gate_up, ff_down_t
        )
        hidden_f = hidden.astype(F32)
        factor_two = lax.rsqrt(jnp.mean(hidden_f * hidden_f, axis=1, keepdims=True) + EPS_NORM)
    else:
        h_part = RESIDUAL_SCALE * dot_nt(att_t.T, out_t)
        h_part = h_part + jnp.where(
            (feature_owner == tp)[None], jnp.concatenate([inputs] * n_tp, axis=1), 0.0
        )
        hidden = lax.psum(h_part.astype(BF), "tp")
        hidden_f = hidden.astype(F32)
        factor_two = lax.rsqrt(jnp.mean(hidden_f * hidden_f, axis=1, keepdims=True) + EPS_NORM)
        normed_two = (hidden_f * factor_two * gain_mlp).astype(BF)
        normed_two_t = normed_two.T
        gate_proj = dot_nn(normed_two, gate_up[0])
        up_proj = dot_nn(normed_two, gate_up[1])
        sigmoid_gate = jax.nn.sigmoid(gate_proj)
        activation = (gate_proj * sigmoid_gate * up_proj).astype(BF)
        mlp_part = dot_nt(activation, ff_down_t).astype(BF)
        d_activation = dot_nn(mlp_seed, ff_down_t)
        d_gate = (
            d_activation * up_proj * sigmoid_gate * (1.0 + gate_proj * (1.0 - sigmoid_gate))
        ).astype(BF)
        d_up = (d_activation * gate_proj * sigmoid_gate).astype(BF)
        d_normed_part = (dot_nt(d_gate, gate_up[0]) + dot_nt(d_up, gate_up[1])).astype(BF)
    mlp_out = lax.psum_scatter(mlp_part, "tp", scatter_dimension=1, tiled=True).astype(F32)
    grads = (
        dot_nn(mlp_seed.T, activation).astype(BF),
        dot_nn(normed_two_t, d_gate).astype(BF),
        dot_nn(normed_two_t, d_up).astype(BF),
    )
    d_normed_part, grads = lax.optimization_barrier((d_normed_part, grads))
    d_normed = line_reduce(d_normed_part, 32, 1).astype(F32)
    own_features = lambda v: lax.dynamic_slice_in_dim(v, tp * width, width, 1)
    layer_out = (own_features(hidden).astype(F32) + RESIDUAL_SCALE * mlp_out).astype(BF)

    grad_down, grad_gate, grad_up = (scatter_grads(g) for g in grads)

    row_inner = jnp.sum(d_normed * gain_mlp * hidden_f, axis=1, keepdims=True) / D
    d_hidden_full = dy + factor_two * d_normed * gain_mlp - hidden_f * (factor_two**3 * row_inner)
    attn_seed = (RESIDUAL_SCALE * d_hidden_full).astype(BF)
    own_dn, own_h = own_features(d_normed), own_features(hidden).astype(F32)
    d_hidden = (
        own_features(cotangent).astype(F32) * live
        + factor_two * own_dn * own_features(gain_mlp[None])
        - own_h * (factor_two**3 * row_inner)
    )
    grad_gain_mlp = jnp.sum(own_dn * own_h * factor_two, axis=0)
    d_att_t = lax.dot_general(out_t, attn_seed, (((0,), (1,)), ((), ())), preferred_element_type=F32).astype(BF)
    grad_out = scatter_grads(dot_tn(attn_seed, att_t.T).astype(BF))

    if by_head:
        pick = lambda v, which: lax.dynamic_slice_in_dim(v, which * heads * VD, heads * VD, 0)
        d_att = in_core_order(pick(d_att_t, core), swap_cores(pick(d_att_t, 1 - core)), core, 1)
    else:
        d_att = lax.dynamic_update_slice(jnp.zeros((heads * VD, slot), BF), d_att_t, (0, core * rows))
    dq_t, d_e, d_kr = attend_backward(
        q_t, k_rows, v_t, att_heads, d_att.reshape(heads, VD, slot), lse, cos_t, sin_t
    )

    d_qn = lax.dot_general(dq_t, q_up_here, (((0,), (1,)), ((), ())), preferred_element_type=F32)
    d_kn = dot_nt(d_e, kv_up_here)
    d_lat_part = jnp.concatenate([d_qn, d_kn, d_kr[:, NOPE:HEAD]], axis=1)
    own_rows = lambda v, which: lax.dynamic_slice_in_dim(v, which * rows, rows, 0)
    from_other = swap_cores(own_rows(d_lat_part, 1 - core).astype(BF)).astype(F32)
    d_lat_sum = (own_rows(d_lat_part, core) + from_other).astype(BF)
    d_lat = line_reduce(jnp.pad(d_lat_sum, ((0, 0), (0, lat_wide - LAT))), 16, 2).astype(F32)
    d_rope = d_lat[:, QR + KVR : LAT]
    k_one, k_two = d_rope[:, : ROPE // 2], d_rope[:, ROPE // 2 :]
    d_rope_raw = jnp.concatenate([k_one * own_cos + k_two * own_sin, k_two * own_cos - k_one * own_sin], axis=1)
    d_query_latent, grad_gain_query = norm_backward(d_lat[:, :QR], query_latent, factor_query, gain_query)
    d_kv_latent, grad_gain_kv = norm_backward(d_lat[:, QR : QR + KVR], kv_latent, factor_kv, gain_kv)
    d_latents = jnp.concatenate([d_query_latent, d_kv_latent, d_rope_raw], axis=1)
    in_inner = jnp.sum(d_latents * latents, axis=1, keepdims=True) / D
    d_latents = (d_latents * factor_one).astype(BF)
    grad_both = dot_tn(d_latents, scaled_in).astype(BF)
    grad_qdown = scatter_grads(grad_both[:QR])
    grad_kvdown = scatter_grads(grad_both[QR:])
    d_in = dot_nn(d_latents, down_t)
    grad_gain_attn = jnp.sum(d_in * inputs, axis=0)
    grad_input = (d_hidden + d_in * gain_attn - inputs * (factor_one**2 * in_inner)).astype(BF)

    grad_qup = dot_nt(qn.T, dq_t).astype(BF)
    grad_kvup = dot_tn(kn, d_e).astype(BF)

    def scatter_up(g):
        if not by_head:
            return scatter_grads(g)
        n_rows, n_cols = g.shape
        g = g.reshape(n_fsdp, n_ctx, n_rows // (n_fsdp * n_ctx), n_cols)
        mine = lax.dynamic_index_in_dim(g, core, 1, keepdims=False)
        other = swap_cores(lax.dynamic_index_in_dim(g, 1 - core, 1, keepdims=False))
        return scatter_fsdp(in_core_order(mine, other, core, 2))

    grad_qup, grad_kvup = scatter_up(grad_qup), scatter_up(grad_kvup)

    owned = [
        grad_qdown.astype(F32).T,
        grad_kvdown.astype(F32).T,
        grad_qup.astype(F32),
        grad_kvup.astype(F32),
        grad_out.astype(F32).T,
        jnp.stack([grad_gate, grad_up]).astype(F32),
        grad_down.astype(F32).T,
    ]
    both_gains = jnp.stack([grad_gain_attn, grad_gain_mlp])
    placed_gains = jnp.where((feature_owner == tp)[None], jnp.concatenate([both_gains] * n_tp, axis=1), 0.0)
    latent_gains = jnp.concatenate([grad_gain_query, grad_gain_kv]) * (tp == 0)
    squares = jnp.stack([jnp.sum(g * g) for g in owned])
    small = lax.psum(
        jnp.concatenate([placed_gains.reshape(-1), latent_gains, squares]), ("fsdp", "ctx", "tp")
    )
    all_gains = small[: 2 * D].reshape(2, D)
    all_latent = small[2 * D : 2 * D + QR + KVR]
    share = g_latent.shape[0]
    place = lax.axis_index("fsdp") * n_ctx + core
    owned.append(own_features(all_gains))
    owned.append(lax.dynamic_slice_in_dim(all_latent, place * share, share, 0))
    totals = [small[2 * D + QR + KVR + n] for n in range(7)]
    totals += [jnp.sum(all_gains * all_gains), jnp.sum(all_latent * all_latent)]
    entry_counts = (
        D * QR,
        D * (KVR + ROPE),
        QR * H * HEAD,
        KVR * H * (NOPE + VD),
        H * VD * D,
        2 * D * FF,
        FF * D,
        2 * D,
        QR + KVR,
    )
    new_params, new_firsts, new_seconds = [], [], []
    for n in range(9):
        limit = CLIP_RMS * entry_counts[n] ** 0.5
        clipped = owned[n] * (limit / jnp.maximum(jnp.sqrt(totals[n]), limit))
        updated, first_new, second_new = adamw_update(
            params[n], clipped, firsts[n], seconds[n], WEIGHT_DECAY if n < 7 else 0.0
        )
        new_params.append(updated)
        new_firsts.append(first_new)
        new_seconds.append(second_new)
    return (layer_out, grad_input, *owned, *new_params[:7], *new_firsts, *new_seconds)


def solution(mesh):
    sharded = ("fsdp", "ctx")
    weights = (
        P("tp", sharded),
        P("tp", sharded),
        P(sharded, "tp"),
        P(sharded, "tp"),
        P("tp", sharded),
        P(None, sharded, "tp"),
        P("tp", sharded),
    )
    gains = (P(None, "tp"), P(sharded))
    tokens = P(sharded, "tp")
    return jax.shard_map(
        local,
        mesh=mesh,
        in_specs=(tokens, P(sharded, None), P("fsdp", None)) + (weights + gains) * 3,
        out_specs=(tokens, tokens) + weights + gains + weights + (weights + gains) * 2,
        check_vma=False,
    )
```

```python
import functools

import jax
import jax.numpy as jnp
from jax import lax
from jax.experimental import pallas as pl
from jax.experimental.pallas import tpu as pltpu
from jax.sharding import PartitionSpec as P

D = 2560
H = 40
NOPE = 64
ROPE = 32
VD = 64
QR = 768
KVR = 256
FF = 6400
STEP = 3
HEAD = NOPE + ROPE
LAT = QR + KVR + ROPE

EPS_NORM = 1e-05
RESIDUAL_SCALE = 1.4 / 62**0.5
ROPE_BASE = 10000.0
MASK_VALUE = -1e30
BETA_ONE = 0.9
BETA_TWO = 0.95
ADAM_EPS = 1e-08
LEARN_RATE = 0.1
WEIGHT_DECAY = 0.1
CLIP_RMS = 0.0002
LOG2E = 1.4426950408889634
LN2 = 0.6931471805599453

BF = jnp.bfloat16
F32 = jnp.float32
MESH = pl.DeviceIdType.MESH
MIB = 1024 * 1024


def dot_nn(a, b):
    return lax.dot_general(a, b, (((1,), (0,)), ((), ())), preferred_element_type=F32)


def dot_nt(a, b):
    return lax.dot_general(a, b, (((1,), (1,)), ((), ())), preferred_element_type=F32)


def dot_tn(a, b):
    return lax.dot_general(a, b, (((0,), (0,)), ((), ())), preferred_element_type=F32)


def line_reduce_kernel(chunks, x_ref, o_ref, near, cross, part, in_send, in_recv, mid_send, mid_recv, out_send, out_recv):
    z = lax.axis_index("tp")
    rows = x_ref.shape[0] // chunks
    is_end = jnp.logical_or(z == 0, z == 3)
    is_mid = jnp.logical_not(is_end)
    partner = jnp.where(z == 0, 1, jnp.where(z == 3, 2, jnp.where(z == 1, 0, 3)))
    across = jnp.where(z == 1, 2, 1)

    barrier = pltpu.get_barrier_semaphore()
    pl.semaphore_signal(barrier, inc=1, device_id={"tp": partner}, device_id_type=MESH)

    @pl.when(is_mid)
    def _():
        pl.semaphore_signal(barrier, inc=1, device_id={"tp": across}, device_id_type=MESH)
        pl.semaphore_wait(barrier, 2)

    @pl.when(is_end)
    def _():
        pl.semaphore_wait(barrier, 1)

    def piece(k):
        return pl.ds(pl.multiple_of(k * rows, rows), rows)

    def to_mid(k):
        return pltpu.make_async_remote_copy(
            src_ref=x_ref.at[piece(k)], dst_ref=near.at[piece(k)], send_sem=in_send.at[k], recv_sem=in_recv.at[k],
            device_id={"tp": partner}, device_id_type=MESH,
        )

    def over(k):
        return pltpu.make_async_remote_copy(
            src_ref=part.at[piece(k)], dst_ref=cross.at[piece(k)], send_sem=mid_send.at[k], recv_sem=mid_recv.at[k],
            device_id={"tp": across}, device_id_type=MESH,
        )

    def to_end(k):
        return pltpu.make_async_remote_copy(
            src_ref=o_ref.at[piece(k)], dst_ref=o_ref.at[piece(k)], send_sem=out_send.at[k], recv_sem=out_recv.at[k],
            device_id={"tp": partner}, device_id_type=MESH,
        )

    @pl.when(is_end)
    def _():
        def begin(k, carry):
            to_mid(k).start()
            return carry

        def finish(k, carry):
            to_mid(k).wait_send()
            to_end(k).wait_recv()
            return carry

        lax.fori_loop(0, chunks, begin, 0)
        lax.fori_loop(0, chunks, finish, 0)

    @pl.when(is_mid)
    def _():
        def first(k):
            to_mid(k).wait_recv()
            part[piece(k)] = (x_ref[piece(k)].astype(F32) + near[piece(k)].astype(F32)).astype(BF)
            over(k).start()

        def second(k):
            over(k).wait_recv()
            o_ref[piece(k)] = (part[piece(k)].astype(F32) + cross[piece(k)].astype(F32)).astype(BF)
            to_end(k).start()

        first(0)

        def step(k, carry):
            first(k)
            second(k - 1)
            return carry

        lax.fori_loop(1, chunks, step, 0)
        second(chunks - 1)

        def finish(k, carry):
            over(k).wait_send()
            to_end(k).wait_send()
            return carry

        lax.fori_loop(0, chunks, finish, 0)


def line_reduce(x, chunks, collective_id):
    if lax.axis_size("tp") != 4:
        return lax.psum(x, "tp")
    rows, cols = x.shape
    dma = pltpu.SemaphoreType.DMA((chunks,))
    return pl.pallas_call(
        functools.partial(line_reduce_kernel, chunks),
        out_shape=jax.ShapeDtypeStruct((rows, cols), BF),
        in_specs=[pl.BlockSpec(memory_space=pltpu.VMEM)],
        out_specs=pl.BlockSpec(memory_space=pltpu.VMEM),
        scratch_shapes=[pltpu.VMEM((rows, cols), BF)] * 3 + [dma] * 6,
        compiler_params=pltpu.CompilerParams(
            collective_id=collective_id, has_side_effects=True, vmem_limit_bytes=40 * MIB
        ),
        cost_estimate=pl.CostEstimate(flops=rows * cols * 2, bytes_accessed=rows * cols * 40, transcendentals=0),
        name="line_reduce",
    )(x)


BQ = 512


def attend_forward_kernel(
    qn_ref, kn_ref, krx_ref, cos_ref, sin_ref, segq_ref, wq_ref, wk_ref, wv_ref, o_ref, lse_ref, q_ref, k_ref, v_ref
):
    i = pl.program_id(1)
    rows = qn_ref.shape[0]

    @pl.when(i == 0)
    def _():
        for r in range(rows // BQ):
            part = pl.ds(r * BQ, BQ)
            qf = dot_nt(wq_ref[0], qn_ref[part, :]) * (LOG2E * HEAD**-0.5)
            cos = cos_ref[:, part]
            sin = sin_ref[:, part]
            one, two = qf[NOPE : NOPE + 16], qf[NOPE + 16 : HEAD]
            q_ref[0, 0:NOPE, part] = qf[:NOPE].astype(BF)
            q_ref[0, NOPE : NOPE + 16, part] = (one * cos - two * sin).astype(BF)
            q_ref[0, NOPE + 16 : HEAD, part] = (two * cos + one * sin).astype(BF)
            q_ref[0, HEAD : HEAD + 16, part] = segq_ref[:, part]
            q_ref[0, HEAD + 16 : 128, part] = jnp.zeros((16, BQ), BF)
            k_ref[0, part, :] = (dot_nn(kn_ref[part, :], wk_ref[0]) + krx_ref[part, :].astype(F32)).astype(BF)
            vt = dot_nt(wv_ref[0], kn_ref[part, :])
            row = lax.broadcasted_iota(jnp.int32, vt.shape, 0)
            v_ref[0, :, part] = jnp.where(row == VD, 1.0, vt).astype(BF)

    here = pl.ds(pl.multiple_of(i * BQ, BQ), BQ)
    q = q_ref[0, :, here]

    def block(j, carried, masked):
        m, acc = carried
        there = pl.ds(pl.multiple_of(j * BQ, BQ), BQ)
        s = dot_nn(k_ref[0, there, :], q)
        if masked:
            krow = lax.broadcasted_iota(jnp.int32, s.shape, 0)
            qcol = lax.broadcasted_iota(jnp.int32, s.shape, 1)
            s = jnp.where(krow <= qcol, s, MASK_VALUE)
        top = jnp.maximum(m, jnp.max(s, axis=0, keepdims=True))
        p = jnp.exp2(s - top).astype(BF)
        acc = acc * jnp.exp2(m - top) + dot_nn(v_ref[0, :, there], p)
        return top, acc

    start = (jnp.full((1, BQ), -3e38, F32), jnp.zeros((80, BQ), F32))
    carried = lax.fori_loop(0, i, lambda j, c: block(j, c, False), start)
    m, acc = block(i, carried, True)
    total = acc[VD : VD + 1]
    o_ref[0, :, here] = (acc[:VD] / total).astype(BF)
    lse_ref[0, :, here] = m + jnp.log2(total)


def attend_forward(qn, kn, krx, cos, sin, segq, wq, wk, wv):
    heads = wq.shape[0]
    rows = qn.shape[0]
    whole = lambda a: pl.BlockSpec(a.shape, lambda h, i: (0,) * a.ndim)
    per_head = lambda a, b: pl.BlockSpec((1, a, b), lambda h, i: (h, 0, 0))
    return pl.pallas_call(
        attend_forward_kernel,
        grid=(heads, rows // BQ),
        in_specs=[whole(qn), whole(kn), whole(krx), whole(cos), whole(sin), whole(segq)]
        + [per_head(*w.shape[1:]) for w in (wq, wk, wv)],
        out_specs=[per_head(VD, rows), per_head(1, rows), per_head(128, rows), per_head(rows, 128), per_head(80, rows)],
        out_shape=[
            jax.ShapeDtypeStruct((heads, VD, rows), BF),
            jax.ShapeDtypeStruct((heads, 1, rows), F32),
            jax.ShapeDtypeStruct((heads, 128, rows), BF),
            jax.ShapeDtypeStruct((heads, rows, 128), BF),
            jax.ShapeDtypeStruct((heads, 80, rows), BF),
        ],
        compiler_params=pltpu.CompilerParams(vmem_limit_bytes=40 * MIB),
        cost_estimate=pl.CostEstimate(flops=heads * rows * rows * 320, bytes_accessed=30 * MIB, transcendentals=0),
        name="attend_forward",
    )(qn, kn, krx, cos, sin, segq, wq, wk, wv)


def attend_backward_kernel(q_ref, k_ref, v_ref, o_ref, do_ref, lse_ref, cos_ref, sin_ref, dq_ref, de_ref, dkr_ref, dq_acc, delta):
    h, j = pl.program_id(0), pl.program_id(1)
    rows = k_ref.shape[1]
    blocks = rows // BQ

    @pl.when(j == 0)
    def _():
        dq_acc[...] = jnp.zeros_like(dq_acc)
        delta[...] = jnp.sum(o_ref[0].astype(F32) * do_ref[0].astype(F32), axis=0, keepdims=True)

    there = pl.ds(pl.multiple_of(j * BQ, BQ), BQ)
    k = k_ref[0, there, :]
    kt = k.astype(F32).T.astype(BF)
    v = v_ref[0, 0:VD, there].astype(F32).T.astype(BF)

    def block(i, carried, masked):
        dk, dv = carried
        here = pl.ds(pl.multiple_of(i * BQ, BQ), BQ)
        q = q_ref[0, :, here]
        do = do_ref[0, :, here]
        s = dot_nn(k, q)
        if masked:
            krow = lax.broadcasted_iota(jnp.int32, s.shape, 0)
            qcol = lax.broadcasted_iota(jnp.int32, s.shape, 1)
            s = jnp.where(krow <= qcol, s, MASK_VALUE)
        p = jnp.exp2(s - lse_ref[0, :, here])
        dp = dot_nn(v, do)
        ds = (p * (dp - delta[:, here])).astype(BF)
        dv = dv + dot_nt(p.astype(BF), do)
        dk = dk + dot_nt(ds, q)
        dq_acc[:, here] = dq_acc[:, here] + dot_nn(kt, ds)
        return dk, dv

    start = (jnp.zeros((BQ, 128), F32), jnp.zeros((BQ, VD), F32))
    carried = block(j, start, True)
    dk, dv = lax.fori_loop(j + 1, blocks, lambda i, c: block(i, c, False), carried)
    dk = dk * LN2
    de_ref[there, 0:NOPE] = dk[:, :NOPE].astype(BF)
    de_ref[there, NOPE:128] = dv.astype(BF)

    @pl.when(h == 0)
    def _():
        dkr_ref[there, :] = dk

    @pl.when(h > 0)
    def _():
        dkr_ref[there, :] = dkr_ref[there, :] + dk

    @pl.when(j == blocks - 1)
    def _():
        dq = dq_acc[...] * HEAD**-0.5
        cos, sin = cos_ref[...], sin_ref[...]
        one, two = dq[NOPE : NOPE + 16], dq[NOPE + 16 : HEAD]
        dq_ref[0:NOPE, :] = dq[:NOPE].astype(BF)
        dq_ref[NOPE : NOPE + 16, :] = (one * cos + two * sin).astype(BF)
        dq_ref[NOPE + 16 : HEAD, :] = (two * cos - one * sin).astype(BF)


def attend_backward(q, k, v, o, do, lse, cos, sin):
    heads = q.shape[0]
    rows = k.shape[1]
    whole = lambda a: pl.BlockSpec(a.shape, lambda h, i: (0,) * a.ndim)
    per_head = lambda a: pl.BlockSpec((1,) + a.shape[1:], lambda h, i: (h, 0, 0))
    return pl.pallas_call(
        attend_backward_kernel,
        grid=(heads, rows // BQ),
        in_specs=[per_head(a) for a in (q, k, v, o, do, lse)] + [whole(cos), whole(sin)],
        out_specs=[
            pl.BlockSpec((HEAD, rows), lambda h, i: (h, 0)),
            pl.BlockSpec((rows, 128), lambda h, i: (0, h)),
            pl.BlockSpec((rows, 128), lambda h, i: (0, 0)),
        ],
        out_shape=[
            jax.ShapeDtypeStruct((heads * HEAD, rows), BF),
            jax.ShapeDtypeStruct((rows, heads * 128), BF),
            jax.ShapeDtypeStruct((rows, 128), F32),
        ],
        scratch_shapes=[pltpu.VMEM((128, rows), F32), pltpu.VMEM((1, rows), F32)],
        compiler_params=pltpu.CompilerParams(vmem_limit_bytes=40 * MIB),
        cost_estimate=pl.CostEstimate(flops=heads * rows * rows * 900, bytes_accessed=30 * MIB, transcendentals=0),
        name="attend_backward",
    )(q, k, v, o, do, lse, cos, sin)


LINE = 32
MLP_ROWS = 256
TILES = ((0, 384), (384, 384), (768, 384), (1152, 448))


def line_places(z):
    is_end = jnp.logical_or(z == 0, z == 3)
    partner = jnp.where(z == 0, 1, jnp.where(z == 3, 2, jnp.where(z == 1, 0, 3)))
    return is_end, jnp.logical_not(is_end), partner, jnp.where(z == 1, 2, 1)


def line_barrier(is_mid, is_end, partner, across):
    barrier = pltpu.get_barrier_semaphore()
    pl.semaphore_signal(barrier, inc=1, device_id={"tp": partner}, device_id_type=MESH)

    @pl.when(is_mid)
    def _():
        pl.semaphore_signal(barrier, inc=1, device_id={"tp": across}, device_id_type=MESH)
        pl.semaphore_wait(barrier, 2)

    @pl.when(is_end)
    def _():
        pl.semaphore_wait(barrier, 1)


def line_copies(source, near, cross, total, sems, partner, across):
    in_send, in_recv, mid_send, mid_recv, out_send, out_recv = sems

    def piece(k):
        return pl.ds(pl.multiple_of(k * LINE, LINE), LINE)

    def copy(src, dst, send, recv, k, to):
        return pltpu.make_async_remote_copy(
            src_ref=src.at[piece(k)], dst_ref=dst.at[piece(k)], send_sem=send.at[k], recv_sem=recv.at[k],
            device_id={"tp": to}, device_id_type=MESH,
        )

    to_mid = lambda k: copy(source, near, in_send, in_recv, k, partner)
    over = lambda k: copy(near, cross, mid_send, mid_recv, k, across)
    to_end = lambda k: copy(total, total, out_send, out_recv, k, partner)

    def first(k):
        to_mid(k).wait_recv()
        near[piece(k)] = (source[piece(k)].astype(F32) + near[piece(k)].astype(F32)).astype(BF)
        over(k).start()

    def second(k):
        over(k).wait_recv()
        total[piece(k)] = (near[piece(k)].astype(F32) + cross[piece(k)].astype(F32)).astype(BF)
        to_end(k).start()

    return to_mid, over, to_end, first, second


def each(count, body):
    def step(k, carry):
        body(k)
        return carry

    lax.fori_loop(0, count, step, 0)


def block_kernel(
    att_ref, x_ref, out_ref, gain_ref, live_ref, seed_any, gu_any, down_any,
    hid_any, dn_any, mo_any, n2t_any, act_any, dg_any, du_any,
    xb, near, cross, total, gu, down, n2, n2t, seed, act, dg, du,
    load_sem, seed_sem, hid_sem, dn_sem, mo_sem, n2t_sem, act_sem, dg_sem, du_sem, *sems,
):
    z = lax.axis_index("tp")
    is_end, is_mid, partner, across = line_places(z)
    to_mid, over, to_end, first, second = line_copies(xb, near, cross, total, sems, partner, across)
    count = xb.shape[0] // LINE
    group = MLP_ROWS // LINE
    groups = count // group
    width = x_ref.shape[1]

    def rows_of(m):
        return pl.ds(pl.multiple_of(m * MLP_ROWS, MLP_ROWS), MLP_ROWS)

    load_gu = pltpu.make_async_copy(gu_any, gu, load_sem.at[0])
    load_down = pltpu.make_async_copy(down_any, down, load_sem.at[1])
    load_seed = lambda m: pltpu.make_async_copy(seed_any.at[rows_of(m)], seed, seed_sem.at[m])
    save_hid = lambda m: pltpu.make_async_copy(total.at[rows_of(m)], hid_any.at[rows_of(m)], hid_sem.at[m])
    save_dn = lambda m: pltpu.make_async_copy(xb.at[rows_of(m)], dn_any.at[rows_of(m)], dn_sem.at[m])
    save_mo = lambda m: pltpu.make_async_copy(cross.at[rows_of(m)], mo_any.at[rows_of(m)], mo_sem.at[m])
    save_n2t = lambda m: pltpu.make_async_copy(n2t, n2t_any.at[:, rows_of(m)], n2t_sem.at[m])
    save_act = lambda m: pltpu.make_async_copy(act, act_any.at[rows_of(m)], act_sem.at[m])
    save_dg = lambda m: pltpu.make_async_copy(dg, dg_any.at[rows_of(m)], dg_sem.at[m])
    save_du = lambda m: pltpu.make_async_copy(du, du_any.at[rows_of(m)], du_sem.at[m])

    load_seed(0).start()
    load_gu.start()
    load_down.start()
    line_barrier(is_mid, is_end, partner, across)

    mine = pl.ds(pl.multiple_of(z * width, 128), width)
    per = 128

    def project(p):
        rows = pl.ds(pl.multiple_of(p * per, per), per)
        part = dot_nt(att_ref[rows, :], out_ref[...]) * RESIDUAL_SCALE
        xb[rows, :] = part.astype(BF)
        xb[rows, mine] = (xb[rows, mine].astype(F32) + x_ref[rows, :].astype(F32)).astype(BF)

        @pl.when(is_end)
        def _():
            for n in range(per // LINE):
                to_mid(p * (per // LINE) + n).start()

    each(xb.shape[0] // per, project)

    @pl.when(is_mid)
    def _():
        first(0)

        def both(k):
            first(k + 1)
            second(k)

        each(group, both)

    def mlp(m):
        rows = rows_of(m)

        @pl.when(is_end)
        def _():
            def arrive(n):
                to_mid(m * group + n).wait_send()
                to_end(m * group + n).wait_recv()

            each(group, arrive)

        def serve(n):
            k = (m + 1) * group + 1 + n

            @pl.when(jnp.logical_and(is_mid, k < count))
            def _():
                first(k)

            @pl.when(jnp.logical_and(is_mid, k <= count))
            def _():
                second(k - 1)

        save_hid(m).start()

        @pl.when(m > 0)
        def _():
            save_n2t(m - 1).wait()
            save_act(m - 1).wait()
            save_dg(m - 1).wait()
            save_du(m - 1).wait()

        def normalize(r):
            here = pl.ds(pl.multiple_of(r * 32, 32), 32)
            h = total[pl.ds(pl.multiple_of(m * MLP_ROWS + r * 32, 32), 32), :].astype(F32)
            factor = lax.rsqrt(jnp.mean(h * h, axis=1, keepdims=True) + EPS_NORM)
            n2[here, :] = (h * factor * gain_ref[...]).astype(BF)

        each(MLP_ROWS // 32, normalize)

        def turn(c):
            cols = pl.ds(pl.multiple_of(c * 256, 256), 256)
            n2t[cols, :] = n2[:, cols].astype(F32).T.astype(BF)

        each(D // 256, turn)
        save_n2t(m).start()
        load_seed(m).wait()

        def weigh(r):
            here = pl.ds(pl.multiple_of(r * 32, 32), 32)
            live = live_ref[pl.ds(pl.multiple_of(m * MLP_ROWS + r * 32, 32), 32), :]
            seed[here, :] = (seed[here, :].astype(F32) * (live * RESIDUAL_SCALE)).astype(BF)

        each(MLP_ROWS // 32, weigh)

        @pl.when(m == 0)
        def _():
            load_gu.wait()
            load_down.wait()

        for t, (at, size) in enumerate(TILES):
            cols = pl.ds(at, size)
            g = dot_nn(n2[...], gu[0, :, cols])
            u = dot_nn(n2[...], gu[1, :, cols])
            d = dot_nn(seed[...], down[:, cols])
            sig = jax.nn.sigmoid(g)
            act[:, cols] = (g * sig * u).astype(BF)
            dg[:, cols] = (d * u * sig * (1.0 + g * (1.0 - sig))).astype(BF)
            du[:, cols] = (d * g * sig).astype(BF)
            serve(t)
        save_act(m).start()
        save_dg(m).start()
        save_du(m).start()

        @pl.when(m + 1 < groups)
        def _():
            load_seed(m + 1).start()

        for n in range(4):
            cols = pl.ds(n * 640, 640)
            xb[rows, cols] = (dot_nt(dg[...], gu[0, cols, :]) + dot_nt(du[...], gu[1, cols, :])).astype(BF)
            cross[rows, cols] = dot_nt(act[...], down[cols, :]).astype(BF)
            serve(4 + n)
        save_dn(m).start()
        save_mo(m).start()

    each(groups, mlp)

    def finish(m):
        save_hid(m).wait()
        save_dn(m).wait()
        save_mo(m).wait()

    each(groups, finish)
    save_n2t(groups - 1).wait()
    save_act(groups - 1).wait()
    save_dg(groups - 1).wait()
    save_du(groups - 1).wait()

    @pl.when(is_mid)
    def _():
        def sent(k):
            over(k).wait_send()
            to_end(k).wait_send()

        each(count, sent)


def block_forward(att, x, out_t, gain, live, seed, gate_up, down_t):
    rows = att.shape[0]
    hidden_units = down_t.shape[1]
    count, groups = rows // LINE, rows // MLP_ROWS
    vmem = pl.BlockSpec(memory_space=pltpu.VMEM)
    anywhere = pl.BlockSpec(memory_space=pl.ANY)
    wide = jax.ShapeDtypeStruct((rows, D), BF)
    units = jax.ShapeDtypeStruct((rows, hidden_units), BF)
    dma = pltpu.SemaphoreType.DMA
    return pl.pallas_call(
        block_kernel,
        out_shape=[wide, wide, wide, jax.ShapeDtypeStruct((D, rows), BF), units, units, units],
        in_specs=[vmem] * 5 + [anywhere] * 3,
        out_specs=[anywhere] * 7,
        scratch_shapes=[pltpu.VMEM((rows, D), BF)] * 4
        + [
            pltpu.VMEM(gate_up.shape, BF),
            pltpu.VMEM(down_t.shape, BF),
            pltpu.VMEM((MLP_ROWS, D), BF),
            pltpu.VMEM((D, MLP_ROWS), BF),
            pltpu.VMEM((MLP_ROWS, D), BF),
        ]
        + [pltpu.VMEM((MLP_ROWS, hidden_units), BF)] * 3
        + [dma((2,))]
        + [dma((groups,))] * 8
        + [dma((count,))] * 6,
        compiler_params=pltpu.CompilerParams(collective_id=3, has_side_effects=True, vmem_limit_bytes=63 * MIB),
        cost_estimate=pl.CostEstimate(flops=rows * D * hidden_units * 12, bytes_accessed=400 * MIB, transcendentals=0),
        name="block_forward",
    )(att, x, out_t, gain, live, seed, gate_up, down_t)


LAG = 3
LOAD = 128


def grad_kernel(
    live_ref, gain_ref, dnp_any, hid_any, cot_any, n2t_any, dg_any, du_any, act_any,
    sa_any, dh_any, gain_out, grad_any,
    near, cross, total, cin, stage, xin, yin2, yin, xin2, lhs, rhs, hbuf, cbuf, sbuf, dbuf, prep,
    total_sem, lhs_sem, rhs_sem, h_sem, c_sem, sa_sem, dh_sem, prep_sem, out_sem,
    core_send, core_recv, x_send, x_recv, y2_send, y2_recv, y_send, y_recv, x2_send, x2_recv, *sems,
):
    z, core, place = lax.axis_index("tp"), lax.axis_index("ctx"), lax.axis_index("fsdp")
    y, x = place // 2, place % 2
    is_end, is_mid, partner, across = line_places(z)
    to_mid, over, to_end, _, _ = line_copies(dnp_any, near, cross, total, sems, partner, across)
    count = total.shape[0] // LINE
    width = dh_any.shape[1]
    half = yin.shape[1]
    block = 2 * half
    mine = pl.ds(pl.multiple_of(z * width, 128), width)
    to_core, to_x, to_y = {"ctx": 1 - core}, {"fsdp": y * 2 + 1 - x}, {"fsdp": (1 - y) * 2 + x}

    def piece(k):
        return pl.ds(pl.multiple_of(k * LINE, LINE), LINE)

    def remote(src, dst, send, recv, to):
        return pltpu.make_async_remote_copy(
            src_ref=src, dst_ref=dst, send_sem=send, recv_sem=recv, device_id=to, device_id_type=MESH
        )

    local = pltpu.make_async_copy
    load_total = local(dnp_any, total, total_sem)
    load_lhs = local(n2t_any, lhs, lhs_sem)
    right = (dg_any, du_any, act_any)
    load_rhs = lambda i: local(right[i], rhs.at[i % 2], rhs_sem.at[i])
    rows_of = lambda g: pl.ds(pl.multiple_of(g * LOAD, LOAD), LOAD)
    load_h = lambda g: local(hid_any.at[rows_of(g)], hbuf.at[g % 2], h_sem.at[g])
    load_c = lambda g: local(cot_any.at[rows_of(g)], cbuf.at[g % 2], c_sem.at[g])
    save_sa = lambda e: local(sbuf.at[e % 2], sa_any.at[piece(e)], sa_sem.at[e])
    save_dh = lambda e: local(dbuf.at[e % 2], dh_any.at[piece(e)], dh_sem.at[e])

    load_lhs.start()
    load_rhs(0).start()
    load_rhs(1).start()
    load_h(0).start()
    load_c(0).start()

    @pl.when(is_mid)
    def _():
        load_total.start()

    barrier = pltpu.get_barrier_semaphore()
    for to in (to_core, to_x, to_y, {"tp": partner}):
        pl.semaphore_signal(barrier, inc=1, device_id=to, device_id_type=MESH)

    @pl.when(is_mid)
    def _():
        pl.semaphore_signal(barrier, inc=1, device_id={"tp": across}, device_id_type=MESH)
        pl.semaphore_wait(barrier, 5)

    @pl.when(is_end)
    def _():
        pl.semaphore_wait(barrier, 4)
        each(count, lambda k: to_mid(k).start())

    gain_out[...] = jnp.zeros_like(gain_out)

    @pl.when(is_mid)
    def _():
        load_total.wait()

    def finish_rows(e):
        per = LOAD // LINE
        g = e // per

        @pl.when(e % per == 0)
        def _():
            load_h(g).wait()
            load_c(g).wait()

            @pl.when(g + 1 < count // per)
            def _():
                load_h(g + 1).start()
                load_c(g + 1).start()

        @pl.when(e >= 2)
        def _():
            save_sa(e - 2).wait()
            save_dh(e - 2).wait()

        here = pl.ds(pl.multiple_of((e % per) * LINE, LINE), LINE)
        live = live_ref[piece(e), :]

        def grads_of(dn, h, dy, gain, factor, inner):
            return dy * live + factor * (dn * gain) - h * (factor * factor * factor * inner)

        dn = total[piece(e), :].astype(F32)
        h = hbuf[g % 2, here, :].astype(F32)
        factor = lax.rsqrt(jnp.mean(h * h, axis=1, keepdims=True) + EPS_NORM)
        inner = jnp.mean(dn * gain_ref[...] * h, axis=1, keepdims=True)
        dy = cbuf[g % 2, here, :].astype(F32)
        sbuf[e % 2] = (RESIDUAL_SCALE * grads_of(dn, h, dy, gain_ref[...], factor, inner)).astype(BF)
        own_dn = total[piece(e), mine].astype(F32)
        own_h = hbuf[g % 2, here, mine].astype(F32)
        own_dy = cbuf[g % 2, here, mine].astype(F32)
        dbuf[e % 2] = grads_of(own_dn, own_h, own_dy, gain_ref[:, mine], factor, inner)
        gain_out[...] += jnp.sum(own_dn * own_h * factor, axis=0, keepdims=True)
        save_sa(e).start()
        save_dh(e).start()

    def serve(n):
        @pl.when(jnp.logical_and(is_mid, n < count))
        def _():
            to_mid(n).wait_recv()
            near[piece(n)] = (total[piece(n)].astype(F32) + near[piece(n)].astype(F32)).astype(BF)
            over(n).start()

        @pl.when(jnp.logical_and(is_mid, jnp.logical_and(n >= 1, n <= count)))
        def _():
            over(n - 1).wait_recv()
            total[piece(n - 1)] = (near[piece(n - 1)].astype(F32) + cross[piece(n - 1)].astype(F32)).astype(BF)
            to_end(n - 1).start()
            finish_rows(n - 1)

        @pl.when(jnp.logical_and(is_end, jnp.logical_and(n >= LAG, n < count + LAG)))
        def _():
            to_mid(n - LAG).wait_send()
            to_end(n - LAG).wait_recv()
            finish_rows(n - LAG)

    def flip(v, by):
        return v + by - 2 * v * by

    def spot(j):
        down, over_x = 1 - j // 2, 1 - j % 2
        return down, over_x, flip(y, down), flip(x, over_x)

    def tile(i, f, parity):
        rows = pl.ds(pl.multiple_of((2 * f + parity) * block, 16), block)
        return dot_nn(lhs[rows, :], rhs[i % 2])

    upper, lower = pl.ds(0, half), pl.ds(half, half)
    core_copy = lambda i, j, f: remote(stage.at[j % 2], cin.at[i, f], core_send.at[i, j], core_recv.at[i, f], to_core)
    x_copy = lambda i, f, yy: remote(cin.at[i, f, upper], xin.at[i, yy], x_send.at[i, yy], x_recv.at[i, yy], to_x)
    y2_copy = lambda i, f, xx: remote(cin.at[i, f, lower], yin2.at[i, xx], y2_send.at[i, xx], y2_recv.at[i, xx], to_y)
    y_copy = lambda i: remote(xin.at[i, 1 - y], yin.at[i], y_send.at[i], y_recv.at[i], to_y)
    x2_copy = lambda i: remote(yin2.at[i, 1 - x], xin2.at[i], x2_send.at[i], x2_recv.at[i], to_x)
    save_upper = lambda i: local(yin.at[i], grad_any.at[i, upper], out_sem.at[i, 0])
    save_lower = lambda i: local(xin2.at[i], grad_any.at[i, lower], out_sem.at[i, 1])

    def plus(a, b):
        return (a.astype(F32) + b.astype(F32)).astype(BF)

    def products(i, n0):
        def for_other(j):
            _, _, yy, xx = spot(j)
            f = yy * 2 + xx

            @pl.when(j >= 2)
            def _():
                core_copy(i, j - 2, f).wait_send()

            stage[j % 2] = tile(i, f, 1 - core).astype(BF)
            core_copy(i, j, f).start()
            serve(n0 + j)

        each(4, for_other)

        def for_own(j):
            down, over_x, yy, xx = spot(j)
            f = yy * 2 + xx
            own = tile(i, f, core)
            core_copy(i, j, f).wait_recv()
            cin[i, f] = (own + cin[i, f].astype(F32)).astype(BF)

            @pl.when(over_x == 1)
            def _():
                x_copy(i, f, yy).start()

            @pl.when(down == 1)
            def _():
                y2_copy(i, f, xx).start()

            serve(n0 + 4 + j)

        each(4, for_own)
        for j in (2, 3):
            core_copy(i, j, 0).wait_send()

    def first_stage(i):
        x_copy(i, 0, 1 - y).wait_recv()
        xin[i, 1 - y] = plus(xin[i, 1 - y], cin[i, (1 - y) * 2 + x, upper])
        y_copy(i).start()
        y2_copy(i, 0, 1 - x).wait_recv()
        yin2[i, 1 - x] = plus(yin2[i, 1 - x], cin[i, y * 2 + 1 - x, lower])
        x2_copy(i).start()
        x_copy(i, 0, y).wait_recv()
        xin[i, y] = plus(xin[i, y], cin[i, y * 2 + x, upper])
        y2_copy(i, 0, x).wait_recv()
        yin2[i, x] = plus(yin2[i, x], cin[i, y * 2 + x, lower])

    def second_stage(i):
        y_copy(i).wait_recv()
        yin[i] = plus(yin[i], xin[i, y])
        save_upper(i).start()
        x2_copy(i).wait_recv()
        xin2[i] = plus(xin2[i], yin2[i, x])
        save_lower(i).start()

    load_lhs.wait()
    load_rhs(0).wait()
    products(0, 0)
    load_rhs(2).start()
    load_rhs(1).wait()
    products(1, 8)

    cols_of = lambda c: pl.ds(pl.multiple_of(c * 256, 256), 256)
    load_prep = lambda c: local(cot_any.at[:, cols_of(c)], prep.at[c % 2], prep_sem.at[c])
    load_prep(0).start()
    groups = D // 256

    def turn(c):
        load_prep(c).wait()

        @pl.when(c + 1 < groups)
        def _():
            load_prep(c + 1).start()

        seed = prep[c % 2].astype(F32) * (live_ref[...] * RESIDUAL_SCALE)
        lhs[cols_of(c), :] = seed.T.astype(BF)
        serve(16 + c)

    each(groups, turn)
    first_stage(0)
    load_rhs(2).wait()
    products(2, 16 + groups)
    first_stage(1)
    second_stage(0)
    for n in range(24 + groups, count + LAG):
        serve(n)
    first_stage(2)
    second_stage(1)
    second_stage(2)
    for i in range(3):
        for v in range(2):
            x_copy(i, 0, v).wait_send()
            y2_copy(i, 0, v).wait_send()
        y_copy(i).wait_send()
        x2_copy(i).wait_send()
        save_upper(i).wait()
        save_lower(i).wait()
    for e in (count - 2, count - 1):
        save_sa(e).wait()
        save_dh(e).wait()

    @pl.when(is_mid)
    def _():
        def sent(k):
            over(k).wait_send()
            to_end(k).wait_send()

        each(count, sent)


def grad_reduce(live, gain, d_normed_part, hidden, cotangent, normed_t, d_gate, d_up, activation):
    rows = hidden.shape[0]
    units = d_gate.shape[1]
    width = D // lax.axis_size("tp")
    shard = D // (lax.axis_size("fsdp") * lax.axis_size("ctx"))
    count = rows // LINE
    vmem = pl.BlockSpec(memory_space=pltpu.VMEM)
    anywhere = pl.BlockSpec(memory_space=pl.ANY)
    dma = pltpu.SemaphoreType.DMA
    scratch = lambda *shape: pltpu.VMEM(shape, BF)
    return pl.pallas_call(
        grad_kernel,
        out_shape=[
            jax.ShapeDtypeStruct((rows, D), BF),
            jax.ShapeDtypeStruct((rows, width), F32),
            jax.ShapeDtypeStruct((1, width), F32),
            jax.ShapeDtypeStruct((3, shard, units), BF),
        ],
        in_specs=[vmem] * 2 + [anywhere] * 7,
        out_specs=[anywhere, anywhere, vmem, anywhere],
        scratch_shapes=[scratch(rows, D)] * 3
        + [
            scratch(3, 4, shard, units),
            scratch(2, shard, units),
            scratch(3, 2, shard // 2, units),
            scratch(3, 2, shard // 2, units),
            scratch(3, shard // 2, units),
            scratch(3, shard // 2, units),
            scratch(D, rows),
            scratch(2, rows, units),
            scratch(2, LOAD, D),
            scratch(2, LOAD, D),
            scratch(2, LINE, D),
            pltpu.VMEM((2, LINE, width), F32),
            scratch(2, rows, 256),
        ]
        + [dma, dma, dma((3,)), dma((rows // LOAD,)), dma((rows // LOAD,)), dma((count,)), dma((count,)), dma((D // 256,)), dma((3, 2))]
        + [dma((3, 4))] * 2
        + [dma((3, 2))] * 4
        + [dma((3,))] * 4
        + [dma((count,))] * 6,
        compiler_params=pltpu.CompilerParams(collective_id=4, has_side_effects=True, vmem_limit_bytes=63 * MIB),
        cost_estimate=pl.CostEstimate(flops=rows * D * units * 6, bytes_accessed=400 * MIB, transcendentals=0),
        name="grad_reduce",
    )(live, gain, d_normed_part, hidden, cotangent, normed_t, d_gate, d_up, activation)


def swap_cores(v):
    return lax.ppermute(v, "ctx", [(0, 1), (1, 0)])


def in_core_order(mine, other, core, axis):
    return jnp.where(
        core == 0, jnp.concatenate([mine, other], axis=axis), jnp.concatenate([other, mine], axis=axis)
    )


def gather_shards(v):
    return lax.all_gather(v, ("fsdp", "ctx"), axis=0, tiled=True)


X_SWAP = [(0, 1), (1, 0), (2, 3), (3, 2)]
Y_SWAP = [(0, 2), (2, 0), (1, 3), (3, 1)]


def take(v, which, axis):
    return lax.dynamic_index_in_dim(v, which, axis, keepdims=False)


def add_up(a, b):
    return (a.astype(F32) + b.astype(F32)).astype(BF)


def keep_half(v, axis, which, name, pairs):
    other = lax.ppermute(take(v, 1 - which, axis), name, pairs)
    return add_up(take(v, which, axis), other)


def scatter_fsdp(v):
    if lax.axis_size("fsdp") != 4:
        return lax.psum_scatter(v, "fsdp", scatter_dimension=0, tiled=False)
    place = lax.axis_index("fsdp")
    y, x = place // 2, place % 2
    _, rows, cols = v.shape
    v = v.reshape(2, 2, 2, rows // 2, cols)
    first = keep_half(v[:, :, 0], 1, x, "fsdp", X_SWAP)
    second = keep_half(v[:, :, 1], 0, y, "fsdp", Y_SWAP)
    first = keep_half(first, 0, y, "fsdp", Y_SWAP)
    second = keep_half(second, 0, x, "fsdp", X_SWAP)
    return jnp.concatenate([first, second], axis=0)


def scatter_grads(v):
    fsdp, ctx = lax.axis_size("fsdp"), lax.axis_size("ctx")
    rows, cols = v.shape
    v = v.reshape(fsdp, ctx, rows // (fsdp * ctx), cols)
    return scatter_fsdp(keep_half(v, 1, lax.axis_index("ctx"), "ctx", [(0, 1), (1, 0)]))


def split_two(v):
    high = v.astype(BF)
    return high, (v - high.astype(F32)).astype(BF)


def adamw_update(parameter, gradient, first_moment, second_moment, decay_rate):
    first_new = BETA_ONE * first_moment + (1.0 - BETA_ONE) * gradient
    second_new = BETA_TWO * second_moment + (1.0 - BETA_TWO) * gradient * gradient
    first_hat = first_new / (1.0 - BETA_ONE**STEP)
    second_hat = second_new / (1.0 - BETA_TWO**STEP)
    updated = parameter - LEARN_RATE * (
        first_hat / (jnp.sqrt(second_hat) + ADAM_EPS) + decay_rate * parameter
    )
    return (updated, first_new, second_new)


def norm_backward(incoming, values, factor, gain):
    scaled = incoming * gain
    gain_grad = jnp.sum(incoming * values * factor, axis=0)
    result = factor * scaled - values * factor**3 * jnp.mean(scaled * values, axis=1, keepdims=True)
    return (result, gain_grad)


def local(*args):
    tokens, cotangent, lengths = args[:3]
    params, firsts, seconds = args[3:12], args[12:21], args[21:30]
    w_qdown, w_kvdown, w_qup, w_kvup, w_out, w_gateup, w_down, g_norms, g_latent = params
    n_tp, n_ctx, n_fsdp = lax.axis_size("tp"), lax.axis_size("ctx"), lax.axis_size("fsdp")
    tp, core = lax.axis_index("tp"), lax.axis_index("ctx")
    rows, width = tokens.shape
    slot = rows * n_ctx
    heads_all = H // n_tp
    by_head = heads_all % n_ctx == 0
    heads = heads_all // n_ctx if by_head else heads_all

    down_t = jnp.concatenate(
        [gather_shards(w_qdown.T.astype(BF)), gather_shards(w_kvdown.T.astype(BF))], axis=0
    )
    q_up = gather_shards(w_qup.astype(BF))
    kv_up = gather_shards(w_kvup.astype(BF))
    gain_lat = lax.all_gather(g_latent.astype(BF), ("fsdp", "ctx"), axis=0, tiled=True).astype(F32)
    out_t = gather_shards(w_out.T.astype(BF))
    gate_up = lax.all_gather(w_gateup.astype(BF), ("fsdp", "ctx"), axis=1, tiled=True)
    ff_down_t = gather_shards(w_down.T.astype(BF))
    if by_head:
        q_up_here = lax.dynamic_slice_in_dim(q_up, core * heads * HEAD, heads * HEAD, 1)
        kv_up_here = lax.dynamic_slice_in_dim(kv_up, core * heads * 128, heads * 128, 1)
    else:
        q_up_here, kv_up_here = q_up, kv_up
    wq = q_up_here.T.reshape(heads, HEAD, QR)
    kv3 = kv_up_here.reshape(KVR, heads, 128)
    wk = jnp.pad(jnp.transpose(kv3[:, :, :NOPE], (1, 0, 2)), ((0, 0), (0, 0), (0, 128 - NOPE)))
    wv = jnp.pad(jnp.transpose(kv3[:, :, NOPE:], (1, 2, 0)), ((0, 0), (0, 80 - VD), (0, 0)))

    gains_norm = g_norms.astype(BF)
    gain_attn = gains_norm[0].astype(F32)
    gain_query, gain_kv = gain_lat[:QR], gain_lat[QR:]

    seq_length = lengths[0, 0]
    index = jnp.arange(slot, dtype=jnp.int32)
    segment = (index >= seq_length).astype(jnp.int32)
    position = (index - segment * seq_length).astype(F32)
    frequency = ROPE_BASE ** (-2.0 * jnp.arange(ROPE // 2, dtype=F32) / ROPE)
    angles = frequency[:, None] * position[None, :]
    cos_t, sin_t = jnp.cos(angles), jnp.sin(angles)
    own_cos = lax.dynamic_slice_in_dim(cos_t, core * rows, rows, 1).T
    own_sin = lax.dynamic_slice_in_dim(sin_t, core * rows, rows, 1).T
    own_segment = lax.dynamic_slice_in_dim(segment, core * rows, rows, 0)
    live = (own_segment == 0).astype(F32)[:, None]
    seg_f = segment.astype(F32)
    seg_q = jnp.concatenate([seg_f[None], 1.0 - seg_f[None], jnp.zeros((14, slot), F32)], axis=0).astype(BF)
    seg_k = (MASK_VALUE * jnp.concatenate([1.0 - seg_f[:, None], seg_f[:, None]], axis=1)).astype(BF)

    inputs = tokens.astype(F32)
    scaled_in = (inputs * gain_attn).astype(BF)
    lat_part = dot_nt(scaled_in, down_t)
    squares_high, squares_low = split_two(jnp.sum(inputs * inputs, axis=1))
    column = jnp.arange(2 * n_tp)
    stats = jnp.where(
        column[None] == 2 * tp, squares_high[:, None], jnp.where(column[None] == 2 * tp + 1, squares_low[:, None], 0)
    ).astype(BF)
    lat_wide = 1152
    payload = jnp.concatenate(
        [lat_part.astype(BF), stats, jnp.zeros((rows, lat_wide - LAT - 2 * n_tp), BF)], axis=1
    )
    gain_rows = jnp.where((jnp.arange(64) == tp)[:, None], gains_norm[1][None], 0).astype(BF)
    gain_rows = jnp.pad(gain_rows, ((0, 0), (0, lat_wide - width)))
    reduced = line_reduce(jnp.concatenate([payload, gain_rows], axis=0), 17, 0)
    gain_mlp = reduced[rows : rows + n_tp, :width].reshape(n_tp * width).astype(F32)
    lat_sum = reduced[:rows].astype(F32)
    factor_one = lax.rsqrt(jnp.sum(lat_sum[:, LAT : LAT + 2 * n_tp], axis=1) / D + EPS_NORM)[:, None]
    latents = lat_sum[:, :LAT] * factor_one
    query_latent = latents[:, :QR]
    kv_latent = latents[:, QR : QR + KVR]
    rope_raw = latents[:, QR + KVR :]
    factor_query = lax.rsqrt(jnp.mean(query_latent * query_latent, axis=1, keepdims=True) + EPS_NORM)
    factor_kv = lax.rsqrt(jnp.mean(kv_latent * kv_latent, axis=1, keepdims=True) + EPS_NORM)
    query_normed = (query_latent * factor_query * gain_query).astype(BF)
    kv_normed = (kv_latent * factor_kv * gain_kv).astype(BF)
    r_one, r_two = rope_raw[:, : ROPE // 2], rope_raw[:, ROPE // 2 :]
    rope_key = jnp.concatenate(
        [r_one * own_cos - r_two * own_sin, r_two * own_cos + r_one * own_sin], axis=1
    ).astype(BF)
    normed_lat = jnp.concatenate([query_normed, kv_normed, rope_key], axis=1)
    lat_both = in_core_order(normed_lat, swap_cores(normed_lat), core, 0)
    qn, kn, kr = lat_both[:, :QR], lat_both[:, QR : QR + KVR], lat_both[:, QR + KVR :]
    krx = jnp.concatenate(
        [jnp.zeros((slot, NOPE), BF), kr, seg_k, jnp.zeros((slot, 128 - HEAD - 2), BF)], axis=1
    )

    att_heads, lse, q_t, k_rows, v_t = attend_forward(qn, kn, krx, cos_t, sin_t, seg_q, wq, wk, wv)
    att_flat = att_heads.reshape(heads * VD, slot)
    own_cols = lambda v: lax.dynamic_slice_in_dim(v, core * rows, rows, 1)
    if by_head:
        other = swap_cores(lax.dynamic_slice_in_dim(att_flat, (1 - core) * rows, rows, 1))
        att_t = in_core_order(own_cols(att_flat), other, core, 0)
    else:
        att_t = own_cols(att_flat)

    feature_owner = jnp.arange(D) // width
    own_features = lambda v: lax.dynamic_slice_in_dim(v, tp * width, width, 1)
    if n_tp == 4 and n_fsdp == 4:
        hidden, d_normed_part, mlp_part, normed_two_t, activation, d_gate, d_up = block_forward(
            att_t.T, tokens, out_t, gain_mlp[None], live, cotangent, gate_up, ff_down_t
        )
        attn_seed, d_hidden, grad_gain_mlp, grads = grad_reduce(
            live, gain_mlp[None], d_normed_part, hidden, cotangent, normed_two_t, d_gate, d_up, activation
        )
        grad_gain_mlp = grad_gain_mlp[0]
        grad_gate, grad_up, grad_down = grads[0], grads[1], grads[2]
    else:
        dy = cotangent.astype(F32) * live
        mlp_seed = (RESIDUAL_SCALE * dy).astype(BF)
        h_part = RESIDUAL_SCALE * dot_nt(att_t.T, out_t)
        h_part = h_part + jnp.where(
            (feature_owner == tp)[None], jnp.concatenate([inputs] * n_tp, axis=1), 0.0
        )
        hidden = lax.psum(h_part.astype(BF), "tp")
        hidden_f = hidden.astype(F32)
        factor_two = lax.rsqrt(jnp.mean(hidden_f * hidden_f, axis=1, keepdims=True) + EPS_NORM)
        normed_two = (hidden_f * factor_two * gain_mlp).astype(BF)
        gate_proj = dot_nn(normed_two, gate_up[0])
        up_proj = dot_nn(normed_two, gate_up[1])
        sigmoid_gate = jax.nn.sigmoid(gate_proj)
        activation = (gate_proj * sigmoid_gate * up_proj).astype(BF)
        mlp_part = dot_nt(activation, ff_down_t).astype(BF)
        d_activation = dot_nn(mlp_seed, ff_down_t)
        d_gate = (
            d_activation * up_proj * sigmoid_gate * (1.0 + gate_proj * (1.0 - sigmoid_gate))
        ).astype(BF)
        d_up = (d_activation * gate_proj * sigmoid_gate).astype(BF)
        d_normed_part = (dot_nt(d_gate, gate_up[0]) + dot_nt(d_up, gate_up[1])).astype(BF)
        grad_down = scatter_grads(dot_tn(mlp_seed, activation).astype(BF))
        grad_gate = scatter_grads(dot_tn(normed_two, d_gate).astype(BF))
        grad_up = scatter_grads(dot_tn(normed_two, d_up).astype(BF))
        d_normed = lax.psum(d_normed_part, "tp").astype(F32)
        row_inner = jnp.mean(d_normed * gain_mlp * hidden_f, axis=1, keepdims=True)
        d_hidden_full = dy + factor_two * d_normed * gain_mlp - hidden_f * (factor_two**3 * row_inner)
        attn_seed = (RESIDUAL_SCALE * d_hidden_full).astype(BF)
        d_hidden = own_features(d_hidden_full)
        grad_gain_mlp = jnp.sum(own_features(d_normed * hidden_f) * factor_two, axis=0)
    mlp_part, attn_seed = lax.optimization_barrier((mlp_part, attn_seed))
    mlp_out = lax.psum_scatter(mlp_part, "tp", scatter_dimension=1, tiled=True).astype(F32)
    layer_out = (own_features(hidden).astype(F32) + RESIDUAL_SCALE * mlp_out).astype(BF)
    d_att_t = lax.dot_general(out_t, attn_seed, (((0,), (1,)), ((), ())), preferred_element_type=F32).astype(BF)
    grad_out = scatter_grads(dot_tn(attn_seed, att_t.T).astype(BF))

    if by_head:
        pick = lambda v, which: lax.dynamic_slice_in_dim(v, which * heads * VD, heads * VD, 0)
        d_att = in_core_order(pick(d_att_t, core), swap_cores(pick(d_att_t, 1 - core)), core, 1)
    else:
        d_att = lax.dynamic_update_slice(jnp.zeros((heads * VD, slot), BF), d_att_t, (0, core * rows))
    dq_t, d_e, d_kr = attend_backward(
        q_t, k_rows, v_t, att_heads, d_att.reshape(heads, VD, slot), lse, cos_t, sin_t
    )

    d_qn = lax.dot_general(dq_t, q_up_here, (((0,), (1,)), ((), ())), preferred_element_type=F32)
    d_kn = dot_nt(d_e, kv_up_here)
    d_lat_part = jnp.concatenate([d_qn, d_kn, d_kr[:, NOPE:HEAD]], axis=1)
    own_rows = lambda v, which: lax.dynamic_slice_in_dim(v, which * rows, rows, 0)
    from_other = swap_cores(own_rows(d_lat_part, 1 - core).astype(BF)).astype(F32)
    d_lat_sum = (own_rows(d_lat_part, core) + from_other).astype(BF)
    d_lat = line_reduce(jnp.pad(d_lat_sum, ((0, 0), (0, lat_wide - LAT))), 16, 2).astype(F32)
    d_rope = d_lat[:, QR + KVR : LAT]
    k_one, k_two = d_rope[:, : ROPE // 2], d_rope[:, ROPE // 2 :]
    d_rope_raw = jnp.concatenate([k_one * own_cos + k_two * own_sin, k_two * own_cos - k_one * own_sin], axis=1)
    d_query_latent, grad_gain_query = norm_backward(d_lat[:, :QR], query_latent, factor_query, gain_query)
    d_kv_latent, grad_gain_kv = norm_backward(d_lat[:, QR : QR + KVR], kv_latent, factor_kv, gain_kv)
    d_latents = jnp.concatenate([d_query_latent, d_kv_latent, d_rope_raw], axis=1)
    in_inner = jnp.sum(d_latents * latents, axis=1, keepdims=True) / D
    d_latents = (d_latents * factor_one).astype(BF)
    grad_both = dot_tn(d_latents, scaled_in).astype(BF)
    grad_qdown = scatter_grads(grad_both[:QR])
    grad_kvdown = scatter_grads(grad_both[QR:])
    d_in = dot_nn(d_latents, down_t)
    grad_gain_attn = jnp.sum(d_in * inputs, axis=0)
    grad_input = (d_hidden + d_in * gain_attn - inputs * (factor_one**2 * in_inner)).astype(BF)

    grad_qup = dot_nt(qn.T, dq_t).astype(BF)
    grad_kvup = dot_tn(kn, d_e).astype(BF)

    def scatter_up(g):
        if not by_head:
            return scatter_grads(g)
        n_rows, n_cols = g.shape
        g = g.reshape(n_fsdp, n_ctx, n_rows // (n_fsdp * n_ctx), n_cols)
        mine = lax.dynamic_index_in_dim(g, core, 1, keepdims=False)
        other = swap_cores(lax.dynamic_index_in_dim(g, 1 - core, 1, keepdims=False))
        return scatter_fsdp(in_core_order(mine, other, core, 2))

    grad_qup, grad_kvup = scatter_up(grad_qup), scatter_up(grad_kvup)

    owned = [
        grad_qdown.astype(F32).T,
        grad_kvdown.astype(F32).T,
        grad_qup.astype(F32),
        grad_kvup.astype(F32),
        grad_out.astype(F32).T,
        jnp.stack([grad_gate, grad_up]).astype(F32),
        grad_down.astype(F32).T,
    ]
    both_gains = jnp.stack([grad_gain_attn, grad_gain_mlp])
    placed_gains = jnp.where((feature_owner == tp)[None], jnp.concatenate([both_gains] * n_tp, axis=1), 0.0)
    latent_gains = jnp.concatenate([grad_gain_query, grad_gain_kv]) * (tp == 0)
    squares = jnp.stack([jnp.sum(g * g) for g in owned])
    small = lax.psum(
        jnp.concatenate([placed_gains.reshape(-1), latent_gains, squares]), ("fsdp", "ctx", "tp")
    )
    all_gains = small[: 2 * D].reshape(2, D)
    all_latent = small[2 * D : 2 * D + QR + KVR]
    share = g_latent.shape[0]
    place = lax.axis_index("fsdp") * n_ctx + core
    owned.append(own_features(all_gains))
    owned.append(lax.dynamic_slice_in_dim(all_latent, place * share, share, 0))
    totals = [small[2 * D + QR + KVR + n] for n in range(7)]
    totals += [jnp.sum(all_gains * all_gains), jnp.sum(all_latent * all_latent)]
    entry_counts = (
        D * QR,
        D * (KVR + ROPE),
        QR * H * HEAD,
        KVR * H * (NOPE + VD),
        H * VD * D,
        2 * D * FF,
        FF * D,
        2 * D,
        QR + KVR,
    )
    new_params, new_firsts, new_seconds = [], [], []
    for n in range(9):
        limit = CLIP_RMS * entry_counts[n] ** 0.5
        clipped = owned[n] * (limit / jnp.maximum(jnp.sqrt(totals[n]), limit))
        updated, first_new, second_new = adamw_update(
            params[n], clipped, firsts[n], seconds[n], WEIGHT_DECAY if n < 7 else 0.0
        )
        new_params.append(updated)
        new_firsts.append(first_new)
        new_seconds.append(second_new)
    return (layer_out, grad_input, *owned, *new_params[:7], *new_firsts, *new_seconds)


def solution(mesh):
    sharded = ("fsdp", "ctx")
    weights = (
        P("tp", sharded),
        P("tp", sharded),
        P(sharded, "tp"),
        P(sharded, "tp"),
        P("tp", sharded),
        P(None, sharded, "tp"),
        P("tp", sharded),
    )
    gains = (P(None, "tp"), P(sharded))
    tokens = P(sharded, "tp")
    return jax.shard_map(
        local,
        mesh=mesh,
        in_specs=(tokens, P(sharded, None), P("fsdp", None)) + (weights + gains) * 3,
        out_specs=(tokens, tokens) + weights + gains + weights + (weights + gains) * 2,
        check_vma=False,
    )
```

```python
import functools

import jax
import jax.numpy as jnp
from jax import lax
from jax.experimental import pallas as pl
from jax.experimental.pallas import tpu as pltpu
from jax.sharding import PartitionSpec as P

D = 2560
H = 40
NOPE = 64
ROPE = 32
VD = 64
QR = 768
KVR = 256
FF = 6400
STEP = 3
HEAD = NOPE + ROPE
LAT = QR + KVR + ROPE
LAT_WIDE = 1152

EPS_NORM = 1e-05
RESIDUAL_SCALE = 1.4 / 62**0.5
ROPE_BASE = 10000.0
MASK_VALUE = -1e30
BETA_ONE = 0.9
BETA_TWO = 0.95
ADAM_EPS = 1e-08
LEARN_RATE = 0.1
WEIGHT_DECAY = 0.1
CLIP_RMS = 0.0002
LOG2E = 1.4426950408889634
LN2 = 0.6931471805599453

BF = jnp.bfloat16
F32 = jnp.float32
MESH = pl.DeviceIdType.MESH
MIB = 1024 * 1024


def dot_nn(a, b):
    return lax.dot_general(a, b, (((1,), (0,)), ((), ())), preferred_element_type=F32)


def dot_nt(a, b):
    return lax.dot_general(a, b, (((1,), (1,)), ((), ())), preferred_element_type=F32)


def dot_tn(a, b):
    return lax.dot_general(a, b, (((0,), (0,)), ((), ())), preferred_element_type=F32)


BQ = 512


def attend_forward_kernel(
    lat_ref, cos_ref, sin_ref, segq_ref, up_ref, o_ref, lse_ref, q_ref, k_ref, v_ref, stack_q, stack_kv, wq_t
):
    i = pl.program_id(1)
    rows = lat_ref.shape[0]
    pieces = up_ref.shape[0]
    nq, nk = QR // pieces, KVR // pieces

    @pl.when(i == 0)
    def _():
        for p in range(pieces):
            stack_q[p * nq : (p + 1) * nq, :] = up_ref[p, 0:nq, :].astype(F32)
            stack_kv[p * nk : (p + 1) * nk, :] = up_ref[p, nq : nq + nk, :].astype(F32)
        wq_t[...] = stack_q[...].T.astype(BF)
        kv = stack_kv[...]
        wk = jnp.where(lax.broadcasted_iota(jnp.int32, kv.shape, 1) < NOPE, kv, 0.0).astype(BF)
        wv_t = kv.T[NOPE:128].astype(BF)
        for r in range(rows // BQ):
            part = pl.ds(r * BQ, BQ)
            kn = lat_ref[part, QR : QR + KVR]
            qf = dot_nt(wq_t[...], lat_ref[part, 0:QR]) * (LOG2E * HEAD**-0.5)
            cos = cos_ref[:, part]
            sin = sin_ref[:, part]
            one, two = qf[NOPE : NOPE + 16], qf[NOPE + 16 : HEAD]
            q_ref[0, 0:NOPE, part] = qf[:NOPE].astype(BF)
            q_ref[0, NOPE : NOPE + 16, part] = (one * cos - two * sin).astype(BF)
            q_ref[0, NOPE + 16 : HEAD, part] = (two * cos + one * sin).astype(BF)
            q_ref[0, HEAD : HEAD + 16, part] = segq_ref[:, part]
            q_ref[0, HEAD + 16 : 128, part] = jnp.zeros((16, BQ), BF)
            k_ref[0, part, :] = (dot_nn(kn, wk) + lat_ref[part, QR + KVR : LAT_WIDE].astype(F32)).astype(BF)
            v_ref[0, 0:VD, part] = dot_nt(wv_t, kn).astype(BF)
            ones = lax.broadcasted_iota(jnp.int32, (16, BQ), 0) == 0
            v_ref[0, VD : VD + 16, part] = ones.astype(F32).astype(BF)

    here = pl.ds(pl.multiple_of(i * BQ, BQ), BQ)
    q = q_ref[0, :, here]

    def block(j, carried, masked):
        m, acc = carried
        there = pl.ds(pl.multiple_of(j * BQ, BQ), BQ)
        s = dot_nn(k_ref[0, there, :], q)
        if masked:
            krow = lax.broadcasted_iota(jnp.int32, s.shape, 0)
            qcol = lax.broadcasted_iota(jnp.int32, s.shape, 1)
            s = jnp.where(krow <= qcol, s, MASK_VALUE)
        top = jnp.maximum(m, jnp.max(s, axis=0, keepdims=True))
        p = jnp.exp2(s - top).astype(BF)
        acc = acc * jnp.exp2(m - top) + dot_nn(v_ref[0, :, there], p)
        return top, acc

    start = (jnp.full((1, BQ), -3e38, F32), jnp.zeros((80, BQ), F32))
    carried = lax.fori_loop(0, i, lambda j, c: block(j, c, False), start)
    m, acc = block(i, carried, True)
    total = acc[VD : VD + 1]
    o_ref[0, :, here] = (acc[:VD] / total).astype(BF)
    lse_ref[0, :, here] = m + jnp.log2(total)


def attend_forward(lat, cos, sin, segq, up):
    heads = up.shape[2] // 128
    rows = lat.shape[0]
    whole = lambda a: pl.BlockSpec(a.shape, lambda h, i: (0,) * a.ndim)
    per_head = lambda a, b: pl.BlockSpec((1, a, b), lambda h, i: (h, 0, 0))
    return pl.pallas_call(
        attend_forward_kernel,
        grid=(heads, rows // BQ),
        in_specs=[whole(lat), whole(cos), whole(sin), whole(segq)]
        + [pl.BlockSpec((up.shape[0], up.shape[1], 128), lambda h, i: (0, 0, h))],
        out_specs=[per_head(VD, rows), per_head(1, rows), per_head(128, rows), per_head(rows, 128), per_head(80, rows)],
        out_shape=[
            jax.ShapeDtypeStruct((heads, VD, rows), BF),
            jax.ShapeDtypeStruct((heads, 1, rows), F32),
            jax.ShapeDtypeStruct((heads, 128, rows), BF),
            jax.ShapeDtypeStruct((heads, rows, 128), BF),
            jax.ShapeDtypeStruct((heads, 80, rows), BF),
        ],
        scratch_shapes=[pltpu.VMEM((QR, 128), F32), pltpu.VMEM((KVR, 128), F32), pltpu.VMEM((128, QR), BF)],
        compiler_params=pltpu.CompilerParams(vmem_limit_bytes=40 * MIB),
        cost_estimate=pl.CostEstimate(flops=heads * rows * rows * 320, bytes_accessed=30 * MIB, transcendentals=0),
        name="attend_forward",
    )(lat, cos, sin, segq, up)


def attend_backward_kernel(q_ref, k_ref, v_ref, o_ref, do_ref, lse_ref, cos_ref, sin_ref, dq_ref, de_ref, dkr_ref, dq_acc, delta):
    h, j = pl.program_id(0), pl.program_id(1)
    rows = k_ref.shape[1]
    blocks = rows // BQ

    @pl.when(j == 0)
    def _():
        dq_acc[...] = jnp.zeros_like(dq_acc)
        delta[...] = jnp.sum(o_ref[0].astype(F32) * do_ref[0].astype(F32), axis=0, keepdims=True)

    there = pl.ds(pl.multiple_of(j * BQ, BQ), BQ)
    k = k_ref[0, there, :]
    kt = k.astype(F32).T.astype(BF)
    v = v_ref[0, 0:VD, there].astype(F32).T.astype(BF)

    def block(i, carried, masked):
        dk, dv = carried
        here = pl.ds(pl.multiple_of(i * BQ, BQ), BQ)
        q = q_ref[0, :, here]
        do = do_ref[0, :, here]
        s = dot_nn(k, q)
        if masked:
            krow = lax.broadcasted_iota(jnp.int32, s.shape, 0)
            qcol = lax.broadcasted_iota(jnp.int32, s.shape, 1)
            s = jnp.where(krow <= qcol, s, MASK_VALUE)
        p = jnp.exp2(s - lse_ref[0, :, here])
        dp = dot_nn(v, do)
        ds = (p * (dp - delta[:, here])).astype(BF)
        dv = dv + dot_nt(p.astype(BF), do)
        dk = dk + dot_nt(ds, q)
        dq_acc[:, here] = dq_acc[:, here] + dot_nn(kt, ds)
        return dk, dv

    start = (jnp.zeros((BQ, 128), F32), jnp.zeros((BQ, VD), F32))
    carried = block(j, start, True)
    dk, dv = lax.fori_loop(j + 1, blocks, lambda i, c: block(i, c, False), carried)
    dk = dk * LN2
    de_ref[there, 0:NOPE] = dk[:, :NOPE].astype(BF)
    de_ref[there, NOPE:128] = dv.astype(BF)

    @pl.when(h == 0)
    def _():
        dkr_ref[there, :] = dk

    @pl.when(h > 0)
    def _():
        dkr_ref[there, :] = dkr_ref[there, :] + dk

    @pl.when(j == blocks - 1)
    def _():
        for r in range(blocks):
            part = pl.ds(r * BQ, BQ)
            dq = dq_acc[:, part] * HEAD**-0.5
            cos, sin = cos_ref[:, part], sin_ref[:, part]
            one, two = dq[NOPE : NOPE + 16], dq[NOPE + 16 : HEAD]
            dq = jnp.concatenate(
                [dq[:NOPE], one * cos + two * sin, two * cos - one * sin, jnp.zeros((128 - HEAD, BQ), F32)], axis=0
            )
            dq_ref[part, :] = dq.T.astype(BF)


def attend_backward(q, k, v, o, do, lse, cos, sin):
    heads = q.shape[0]
    rows = k.shape[1]
    whole = lambda a: pl.BlockSpec(a.shape, lambda h, i: (0,) * a.ndim)
    per_head = lambda a: pl.BlockSpec((1,) + a.shape[1:], lambda h, i: (h, 0, 0))
    return pl.pallas_call(
        attend_backward_kernel,
        grid=(heads, rows // BQ),
        in_specs=[per_head(a) for a in (q, k, v, o, do, lse)] + [whole(cos), whole(sin)],
        out_specs=[
            pl.BlockSpec((rows, 128), lambda h, i: (0, h)),
            pl.BlockSpec((rows, 128), lambda h, i: (0, h)),
            pl.BlockSpec((rows, 128), lambda h, i: (0, 0)),
        ],
        out_shape=[
            jax.ShapeDtypeStruct((rows, heads * 128), BF),
            jax.ShapeDtypeStruct((rows, heads * 128), BF),
            jax.ShapeDtypeStruct((rows, 128), F32),
        ],
        scratch_shapes=[pltpu.VMEM((128, rows), F32), pltpu.VMEM((1, rows), F32)],
        compiler_params=pltpu.CompilerParams(vmem_limit_bytes=40 * MIB),
        cost_estimate=pl.CostEstimate(flops=heads * rows * rows * 900, bytes_accessed=30 * MIB, transcendentals=0),
        name="attend_backward",
    )(q, k, v, o, do, lse, cos, sin)


LAT_LINE = 64
PIECE = 160


def latent_kernel(
    x_ref, gain_ref, gain2_ref, piece_ref, up_ref, sel_ref, freq_col, freq_lane, len_ref,
    w_ref, total, lat_ref, cos_ref, sin_ref, segq_ref, upg_ref, tcos, tsin, gains,
    gat, xb, near, cross, kvg,
    w_send, w_recv, u_send, u_recv, c_send, c_recv, *sems,
):
    z, core, place = lax.axis_index("tp"), lax.axis_index("ctx"), lax.axis_index("fsdp")
    is_end, is_mid, partner, across = line_places(z)
    to_mid, over, to_end, first, second = line_copies(xb, near, cross, total, sems, partner, across, LAT_LINE)
    count = xb.shape[0] // LAT_LINE
    rows = x_ref.shape[0]
    peers = gat.shape[0]
    me = place * 2 + core

    def remote(src, dst, send, recv, to):
        return pltpu.make_async_remote_copy(
            src_ref=src, dst_ref=dst, send_sem=send, recv_sem=recv, device_id=to, device_id_type=MESH
        )

    def peer(d):
        to = lax.rem(me + d, peers)
        return {"fsdp": to // 2, "ctx": lax.rem(to, 2)}

    barrier = pltpu.get_barrier_semaphore()
    for d in range(1, peers):
        pl.semaphore_signal(barrier, inc=1, device_id=peer(d), device_id_type=MESH)
    pl.semaphore_signal(barrier, inc=1, device_id={"tp": partner}, device_id_type=MESH)

    @pl.when(is_mid)
    def _():
        pl.semaphore_signal(barrier, inc=1, device_id={"tp": across}, device_id_type=MESH)
        pl.semaphore_wait(barrier, peers + 1)

    @pl.when(is_end)
    def _():
        pl.semaphore_wait(barrier, peers)

    def w_copy(d, source):
        return remote(piece_ref, gat.at[source], w_send.at[d], w_recv.at[source], peer(d))

    def u_copy(d, source):
        return remote(up_ref.at[lax.rem(me + d, 2)], upg_ref.at[source], u_send.at[d], u_recv.at[source], peer(d))

    for d in range(1, peers):
        w_copy(d, me).start()
    for d in range(1, peers):
        u_copy(d, me).start()
    gat[me] = piece_ref[...]
    upg_ref[me] = up_ref[core]

    length = len_ref[0, 0]
    slot = cos_ref.shape[1]
    index = lax.broadcasted_iota(jnp.int32, (1, slot), 1)
    segment = (index >= length).astype(jnp.int32)
    angle = freq_col[...] * (index - segment * length).astype(F32)
    cos_ref[...] = jnp.cos(angle)
    sin_ref[...] = jnp.sin(angle)
    row16 = lax.broadcasted_iota(jnp.int32, (16, slot), 0)
    seg_f = segment.astype(F32)
    segq_ref[...] = jnp.where(row16 == 0, seg_f, jnp.where(row16 == 1, 1.0 - seg_f, 0.0)).astype(BF)
    lane = lax.broadcasted_iota(jnp.int32, (1, 128), 1)
    in_rope = jnp.logical_and(lane >= NOPE, lane < HEAD)

    def own_index(e):
        at = core * rows + e * LAT_LINE
        return at + lax.broadcasted_iota(jnp.int32, (LAT_LINE, 1), 0)

    def table(e):
        here = pl.ds(pl.multiple_of(e * LAT_LINE, LAT_LINE), LAT_LINE)
        at = own_index(e)
        seg = (at >= length).astype(jnp.int32)
        turn = (at - seg * length).astype(F32) * freq_lane[...]
        tcos[here, :] = jnp.where(in_rope, jnp.cos(turn), 0.0)
        tsin[here, :] = jnp.where(in_rope, jnp.sin(turn), 0.0)

    each(rows // LAT_LINE, table)

    for d in range(1, peers):
        w_copy(d, lax.rem(me + peers - d, peers)).wait_recv()
    for p in range(peers):
        w_ref[p * 96 : (p + 1) * 96, :] = gat[p, 0:96, :]
        kvg[p * 48 : (p + 1) * 48, :] = gat[p, 96:144, :]
        gains[:, p * 128 : (p + 1) * 128] = gat[p, 144:160, 0:128].astype(F32)
    w_ref[QR:LAT, :] = dot_nn(sel_ref[...], kvg[...]).astype(BF)
    w_ref[LAT:LAT_WIDE, :] = jnp.zeros((LAT_WIDE - LAT, w_ref.shape[1]), BF)

    wide_lane = lax.broadcasted_iota(jnp.int32, (1, LAT_WIDE), 1)
    per = 128

    def project(r):
        here = pl.ds(pl.multiple_of(r * per, per), per)
        x = x_ref[here, :].astype(F32)
        square = jnp.sum(x * x, axis=1, keepdims=True)
        high = square.astype(BF).astype(F32)
        part = dot_nt((x * gain_ref[...]).astype(BF), w_ref[...])
        part = jnp.where(wide_lane == LAT + 2 * z, high, jnp.where(wide_lane == LAT + 2 * z + 1, square - high, part))
        xb[here, :] = part.astype(BF)

        @pl.when(is_end)
        def _():
            for n in range(per // LAT_LINE):
                to_mid(r * (per // LAT_LINE) + n).start()

    each(rows // per, project)
    gain_row = lax.broadcasted_iota(jnp.int32, (LAT_LINE, LAT_WIDE), 0) == z
    xb[rows : rows + LAT_LINE, :] = jnp.where(gain_row, gain2_ref[...], 0.0).astype(BF)

    @pl.when(is_end)
    def _():
        to_mid(count - 1).start()

    def handover(e):
        here = pl.ds(pl.multiple_of(core * rows + e * LAT_LINE, LAT_LINE), LAT_LINE)
        return remote(lat_ref.at[here], lat_ref.at[here], c_send.at[e], c_recv.at[e], {"ctx": 1 - core})

    stat_lane = jnp.logical_and(wide_lane >= LAT, wide_lane < LAT + 8)

    def finish_rows(e):
        @pl.when(e < rows // LAT_LINE)
        def _():
            here = pl.ds(pl.multiple_of(e * LAT_LINE, LAT_LINE), LAT_LINE)
            there = pl.ds(pl.multiple_of(core * rows + e * LAT_LINE, LAT_LINE), LAT_LINE)
            v = total[here, :].astype(F32)
            square = jnp.sum(jnp.where(stat_lane, v, 0.0), axis=1, keepdims=True)
            v = v * lax.rsqrt(square / D + EPS_NORM)
            ql, kl, raw = v[:, :QR], v[:, QR : QR + KVR], v[:, QR + KVR :]
            ql = ql * lax.rsqrt(jnp.mean(ql * ql, axis=1, keepdims=True) + EPS_NORM)
            kl = kl * lax.rsqrt(jnp.mean(kl * kl, axis=1, keepdims=True) + EPS_NORM)
            lat_ref[there, 0:QR] = (ql * gains[0:1, 0:QR]).astype(BF)
            lat_ref[there, QR : QR + KVR] = (kl * gains[0:1, QR : QR + KVR]).astype(BF)
            moved = pltpu.roll(jnp.where(lane < ROPE, raw, 0.0), NOPE, 1)
            turned = jnp.where(lane < NOPE + 16, -pltpu.roll(moved, 128 - 16, 1), pltpu.roll(moved, 16, 1))
            seg = (own_index(e) >= length).astype(F32)
            mask = jnp.where(lane == HEAD, 1.0 - seg, jnp.where(lane == HEAD + 1, seg, 0.0)) * MASK_VALUE
            lat_ref[there, QR + KVR : LAT_WIDE] = (moved * tcos[here, :] + turned * tsin[here, :] + mask).astype(BF)
            handover(e).start()

    def serve(n):
        @pl.when(jnp.logical_and(is_mid, n < count))
        def _():
            first(n)

        @pl.when(jnp.logical_and(is_mid, jnp.logical_and(n >= 1, n <= count)))
        def _():
            second(n - 1)
            finish_rows(n - 1)

        @pl.when(jnp.logical_and(is_end, n < count))
        def _():
            to_mid(n).wait_send()
            to_end(n).wait_recv()
            finish_rows(n)

    each(count + 1, serve)

    @pl.when(is_mid)
    def _():
        def sent(k):
            over(k).wait_send()
            to_end(k).wait_send()

        each(count, sent)

    for d in range(1, peers):
        w_copy(d, me).wait_send()
        u_copy(d, me).wait_send()
        u_copy(d, lax.rem(me + peers - d, peers)).wait_recv()

    def passed(e):
        handover(e).wait_send()
        here = pl.ds(pl.multiple_of((1 - core) * rows + e * LAT_LINE, LAT_LINE), LAT_LINE)
        remote(lat_ref.at[here], lat_ref.at[here], c_send.at[e], c_recv.at[e], {"ctx": 1 - core}).wait_recv()

    each(rows // LAT_LINE, passed)


def spread(peers):
    index = jnp.arange(KVR + ROPE)
    return jnp.equal((index // 36 * 48 + index % 36)[:, None], jnp.arange(peers * 48)[None]).astype(BF)


def latent_forward(x, gain, gain2, piece, up, length):
    rows, width = x.shape
    peers = lax.axis_size("fsdp") * lax.axis_size("ctx")
    slot = rows * lax.axis_size("ctx")
    wide = rows + LAT_LINE
    count = wide // LAT_LINE
    sel = spread(peers)
    frequency = ROPE_BASE ** (-2.0 * jnp.arange(ROPE // 2, dtype=F32) / ROPE)
    vmem = pl.BlockSpec(memory_space=pltpu.VMEM)
    dma = pltpu.SemaphoreType.DMA
    return pl.pallas_call(
        latent_kernel,
        out_shape=[
            jax.ShapeDtypeStruct((LAT_WIDE, width), BF),
            jax.ShapeDtypeStruct((wide, LAT_WIDE), BF),
            jax.ShapeDtypeStruct((slot, LAT_WIDE), BF),
            jax.ShapeDtypeStruct((ROPE // 2, slot), F32),
            jax.ShapeDtypeStruct((ROPE // 2, slot), F32),
            jax.ShapeDtypeStruct((16, slot), BF),
            jax.ShapeDtypeStruct((peers,) + up.shape[1:], BF),
            jax.ShapeDtypeStruct((rows, 128), F32),
            jax.ShapeDtypeStruct((rows, 128), F32),
            jax.ShapeDtypeStruct((16, QR + KVR), F32),
        ],
        in_specs=[vmem] * 8 + [pl.BlockSpec(memory_space=pltpu.SMEM)],
        out_specs=[vmem] * 10,
        scratch_shapes=[
            pltpu.VMEM((peers, PIECE, width), BF),
            pltpu.VMEM((wide, LAT_WIDE), BF),
            pltpu.VMEM((wide, LAT_WIDE), BF),
            pltpu.VMEM((wide, LAT_WIDE), BF),
            pltpu.VMEM((peers * 48, width), BF),
        ]
        + [dma((peers,))] * 4
        + [dma((rows // LAT_LINE,))] * 2
        + [dma((count,))] * 6,
        compiler_params=pltpu.CompilerParams(collective_id=0, has_side_effects=True, vmem_limit_bytes=48 * MIB),
        cost_estimate=pl.CostEstimate(flops=rows * LAT_WIDE * width * 2, bytes_accessed=150 * MIB, transcendentals=0),
        name="latent_forward",
    )(x, gain, gain2, piece, up, sel, frequency[:, None], jnp.tile(frequency, 8)[None], length)


LINE = 32
MLP_ROWS = 256
TILES = ((0, 384), (384, 384), (768, 384), (1152, 448))


def line_places(z):
    is_end = jnp.logical_or(z == 0, z == 3)
    partner = jnp.where(z == 0, 1, jnp.where(z == 3, 2, jnp.where(z == 1, 0, 3)))
    return is_end, jnp.logical_not(is_end), partner, jnp.where(z == 1, 2, 1)


def line_barrier(is_mid, is_end, partner, across):
    barrier = pltpu.get_barrier_semaphore()
    pl.semaphore_signal(barrier, inc=1, device_id={"tp": partner}, device_id_type=MESH)

    @pl.when(is_mid)
    def _():
        pl.semaphore_signal(barrier, inc=1, device_id={"tp": across}, device_id_type=MESH)
        pl.semaphore_wait(barrier, 2)

    @pl.when(is_end)
    def _():
        pl.semaphore_wait(barrier, 1)


def line_copies(source, near, cross, total, sems, partner, across, line=LINE):
    in_send, in_recv, mid_send, mid_recv, out_send, out_recv = sems

    def piece(k):
        return pl.ds(pl.multiple_of(k * line, line), line)

    def copy(src, dst, send, recv, k, to):
        return pltpu.make_async_remote_copy(
            src_ref=src.at[piece(k)], dst_ref=dst.at[piece(k)], send_sem=send.at[k], recv_sem=recv.at[k],
            device_id={"tp": to}, device_id_type=MESH,
        )

    to_mid = lambda k: copy(source, near, in_send, in_recv, k, partner)
    over = lambda k: copy(near, cross, mid_send, mid_recv, k, across)
    to_end = lambda k: copy(total, total, out_send, out_recv, k, partner)

    def first(k):
        to_mid(k).wait_recv()
        near[piece(k)] = (source[piece(k)].astype(F32) + near[piece(k)].astype(F32)).astype(BF)
        over(k).start()

    def second(k):
        over(k).wait_recv()
        total[piece(k)] = (near[piece(k)].astype(F32) + cross[piece(k)].astype(F32)).astype(BF)
        to_end(k).start()

    return to_mid, over, to_end, first, second


def each(count, body):
    def step(k, carry):
        body(k)
        return carry

    lax.fori_loop(0, count, step, 0)


def block_kernel(
    att_ref, x_ref, out_ref, gain_ref, live_ref, seed_any, gu_any, down_any,
    hid_any, dn_any, mo_any, n2t_any, act_any, dg_any, du_any,
    xb, near, cross, total, gu, down, n2, n2t, seed, act, dg, du,
    load_sem, seed_sem, hid_sem, dn_sem, mo_sem, n2t_sem, act_sem, dg_sem, du_sem, *sems,
):
    z = lax.axis_index("tp")
    is_end, is_mid, partner, across = line_places(z)
    to_mid, over, to_end, first, second = line_copies(xb, near, cross, total, sems, partner, across)
    count = xb.shape[0] // LINE
    group = MLP_ROWS // LINE
    groups = count // group
    width = x_ref.shape[1]

    def rows_of(m):
        return pl.ds(pl.multiple_of(m * MLP_ROWS, MLP_ROWS), MLP_ROWS)

    load_gu = pltpu.make_async_copy(gu_any, gu, load_sem.at[0])
    load_down = pltpu.make_async_copy(down_any, down, load_sem.at[1])
    load_seed = lambda m: pltpu.make_async_copy(seed_any.at[rows_of(m)], seed, seed_sem.at[m])
    save_hid = lambda m: pltpu.make_async_copy(total.at[rows_of(m)], hid_any.at[rows_of(m)], hid_sem.at[m])
    save_dn = lambda m: pltpu.make_async_copy(xb.at[rows_of(m)], dn_any.at[rows_of(m)], dn_sem.at[m])
    save_mo = lambda m: pltpu.make_async_copy(cross.at[rows_of(m)], mo_any.at[rows_of(m)], mo_sem.at[m])
    save_n2t = lambda m: pltpu.make_async_copy(n2t, n2t_any.at[:, rows_of(m)], n2t_sem.at[m])
    save_act = lambda m: pltpu.make_async_copy(act, act_any.at[rows_of(m)], act_sem.at[m])
    save_dg = lambda m: pltpu.make_async_copy(dg, dg_any.at[rows_of(m)], dg_sem.at[m])
    save_du = lambda m: pltpu.make_async_copy(du, du_any.at[rows_of(m)], du_sem.at[m])

    load_seed(0).start()
    load_gu.start()
    load_down.start()
    line_barrier(is_mid, is_end, partner, across)

    mine = pl.ds(pl.multiple_of(z * width, 128), width)
    per = 128

    def project(p):
        rows = pl.ds(pl.multiple_of(p * per, per), per)
        part = dot_nt(att_ref[rows, :], out_ref[...]) * RESIDUAL_SCALE
        xb[rows, :] = part.astype(BF)
        xb[rows, mine] = (xb[rows, mine].astype(F32) + x_ref[rows, :].astype(F32)).astype(BF)

        @pl.when(is_end)
        def _():
            for n in range(per // LINE):
                to_mid(p * (per // LINE) + n).start()

    each(xb.shape[0] // per, project)

    @pl.when(is_mid)
    def _():
        first(0)

        def both(k):
            first(k + 1)
            second(k)

        each(group, both)

    def mlp(m):
        rows = rows_of(m)

        @pl.when(is_end)
        def _():
            def arrive(n):
                to_mid(m * group + n).wait_send()
                to_end(m * group + n).wait_recv()

            each(group, arrive)

        def serve(n):
            k = (m + 1) * group + 1 + n

            @pl.when(jnp.logical_and(is_mid, k < count))
            def _():
                first(k)

            @pl.when(jnp.logical_and(is_mid, k <= count))
            def _():
                second(k - 1)

        save_hid(m).start()

        @pl.when(m > 0)
        def _():
            save_n2t(m - 1).wait()
            save_act(m - 1).wait()
            save_dg(m - 1).wait()
            save_du(m - 1).wait()

        def normalize(r):
            here = pl.ds(pl.multiple_of(r * 32, 32), 32)
            h = total[pl.ds(pl.multiple_of(m * MLP_ROWS + r * 32, 32), 32), :].astype(F32)
            factor = lax.rsqrt(jnp.mean(h * h, axis=1, keepdims=True) + EPS_NORM)
            n2[here, :] = (h * factor * gain_ref[...]).astype(BF)

        each(MLP_ROWS // 32, normalize)

        def turn(c):
            cols = pl.ds(pl.multiple_of(c * 256, 256), 256)
            n2t[cols, :] = n2[:, cols].astype(F32).T.astype(BF)

        each(D // 256, turn)
        save_n2t(m).start()
        load_seed(m).wait()

        def weigh(r):
            here = pl.ds(pl.multiple_of(r * 32, 32), 32)
            live = live_ref[pl.ds(pl.multiple_of(m * MLP_ROWS + r * 32, 32), 32), :]
            seed[here, :] = (seed[here, :].astype(F32) * (live * RESIDUAL_SCALE)).astype(BF)

        each(MLP_ROWS // 32, weigh)

        @pl.when(m == 0)
        def _():
            load_gu.wait()
            load_down.wait()

        for t, (at, size) in enumerate(TILES):
            cols = pl.ds(at, size)
            g = dot_nn(n2[...], gu[0, :, cols])
            u = dot_nn(n2[...], gu[1, :, cols])
            d = dot_nn(seed[...], down[:, cols])
            sig = jax.nn.sigmoid(g)
            act[:, cols] = (g * sig * u).astype(BF)
            dg[:, cols] = (d * u * sig * (1.0 + g * (1.0 - sig))).astype(BF)
            du[:, cols] = (d * g * sig).astype(BF)
            serve(t)
        save_act(m).start()
        save_dg(m).start()
        save_du(m).start()

        @pl.when(m + 1 < groups)
        def _():
            load_seed(m + 1).start()

        for n in range(4):
            cols = pl.ds(n * 640, 640)
            xb[rows, cols] = (dot_nt(dg[...], gu[0, cols, :]) + dot_nt(du[...], gu[1, cols, :])).astype(BF)
            cross[rows, cols] = dot_nt(act[...], down[cols, :]).astype(BF)
            serve(4 + n)
        save_dn(m).start()
        save_mo(m).start()

    each(groups, mlp)

    def finish(m):
        save_hid(m).wait()
        save_dn(m).wait()
        save_mo(m).wait()

    each(groups, finish)
    save_n2t(groups - 1).wait()
    save_act(groups - 1).wait()
    save_dg(groups - 1).wait()
    save_du(groups - 1).wait()

    @pl.when(is_mid)
    def _():
        def sent(k):
            over(k).wait_send()
            to_end(k).wait_send()

        each(count, sent)


def block_forward(att, x, out_t, gain, live, seed, gate_up, down_t):
    rows = att.shape[0]
    hidden_units = down_t.shape[1]
    count, groups = rows // LINE, rows // MLP_ROWS
    vmem = pl.BlockSpec(memory_space=pltpu.VMEM)
    anywhere = pl.BlockSpec(memory_space=pl.ANY)
    wide = jax.ShapeDtypeStruct((rows, D), BF)
    units = jax.ShapeDtypeStruct((rows, hidden_units), BF)
    dma = pltpu.SemaphoreType.DMA
    return pl.pallas_call(
        block_kernel,
        out_shape=[wide, wide, wide, jax.ShapeDtypeStruct((D, rows), BF), units, units, units],
        in_specs=[vmem] * 5 + [anywhere] * 3,
        out_specs=[anywhere] * 7,
        scratch_shapes=[pltpu.VMEM((rows, D), BF)] * 4
        + [
            pltpu.VMEM(gate_up.shape, BF),
            pltpu.VMEM(down_t.shape, BF),
            pltpu.VMEM((MLP_ROWS, D), BF),
            pltpu.VMEM((D, MLP_ROWS), BF),
            pltpu.VMEM((MLP_ROWS, D), BF),
        ]
        + [pltpu.VMEM((MLP_ROWS, hidden_units), BF)] * 3
        + [dma((2,))]
        + [dma((groups,))] * 8
        + [dma((count,))] * 6,
        compiler_params=pltpu.CompilerParams(collective_id=3, has_side_effects=True, vmem_limit_bytes=63 * MIB),
        cost_estimate=pl.CostEstimate(flops=rows * D * hidden_units * 12, bytes_accessed=400 * MIB, transcendentals=0),
        name="block_forward",
    )(att, x, out_t, gain, live, seed, gate_up, down_t)


LAG = 3
LOAD = 128


def total_square(v):
    v = v.astype(F32)
    return jnp.sum(jnp.sum(v * v, axis=0, keepdims=True), axis=1, keepdims=True)


def grad_kernel(
    live_ref, gain_ref, dnp_any, hid_any, cot_any, n2t_any, dg_any, du_any, act_any,
    sa_any, dh_any, gain_out, grad_any, square_out,
    near, cross, total, cin, stage, xin, yin2, yin, xin2, lhs, rhs, hbuf, cbuf, sbuf, dbuf, prep,
    total_sem, lhs_sem, rhs_sem, h_sem, c_sem, sa_sem, dh_sem, prep_sem, out_sem,
    core_send, core_recv, x_send, x_recv, y2_send, y2_recv, y_send, y_recv, x2_send, x2_recv, *sems,
):
    z, core, place = lax.axis_index("tp"), lax.axis_index("ctx"), lax.axis_index("fsdp")
    y, x = place // 2, place % 2
    is_end, is_mid, partner, across = line_places(z)
    to_mid, over, to_end, _, _ = line_copies(dnp_any, near, cross, total, sems, partner, across)
    count = total.shape[0] // LINE
    width = dh_any.shape[1]
    half = yin.shape[1]
    block = 2 * half
    mine = pl.ds(pl.multiple_of(z * width, 128), width)
    to_core, to_x, to_y = {"ctx": 1 - core}, {"fsdp": y * 2 + 1 - x}, {"fsdp": (1 - y) * 2 + x}

    def piece(k):
        return pl.ds(pl.multiple_of(k * LINE, LINE), LINE)

    def remote(src, dst, send, recv, to):
        return pltpu.make_async_remote_copy(
            src_ref=src, dst_ref=dst, send_sem=send, recv_sem=recv, device_id=to, device_id_type=MESH
        )

    local = pltpu.make_async_copy
    load_total = local(dnp_any, total, total_sem)
    load_lhs = local(n2t_any, lhs, lhs_sem)
    right = (dg_any, du_any, act_any)
    load_rhs = lambda i: local(right[i], rhs.at[i % 2], rhs_sem.at[i])
    rows_of = lambda g: pl.ds(pl.multiple_of(g * LOAD, LOAD), LOAD)
    load_h = lambda g: local(hid_any.at[rows_of(g)], hbuf.at[g % 2], h_sem.at[g])
    load_c = lambda g: local(cot_any.at[rows_of(g)], cbuf.at[g % 2], c_sem.at[g])
    save_sa = lambda e: local(sbuf.at[e % 2], sa_any.at[piece(e)], sa_sem.at[e])
    save_dh = lambda e: local(dbuf.at[e % 2], dh_any.at[piece(e)], dh_sem.at[e])

    load_lhs.start()
    load_rhs(0).start()
    load_rhs(1).start()
    load_h(0).start()
    load_c(0).start()

    @pl.when(is_mid)
    def _():
        load_total.start()

    barrier = pltpu.get_barrier_semaphore()
    for to in (to_core, to_x, to_y, {"tp": partner}):
        pl.semaphore_signal(barrier, inc=1, device_id=to, device_id_type=MESH)

    @pl.when(is_mid)
    def _():
        pl.semaphore_signal(barrier, inc=1, device_id={"tp": across}, device_id_type=MESH)
        pl.semaphore_wait(barrier, 5)

    @pl.when(is_end)
    def _():
        pl.semaphore_wait(barrier, 4)
        each(count, lambda k: to_mid(k).start())

    gain_out[...] = jnp.zeros_like(gain_out)

    @pl.when(is_mid)
    def _():
        load_total.wait()

    def finish_rows(e):
        per = LOAD // LINE
        g = e // per

        @pl.when(e % per == 0)
        def _():
            load_h(g).wait()
            load_c(g).wait()

            @pl.when(g + 1 < count // per)
            def _():
                load_h(g + 1).start()
                load_c(g + 1).start()

        @pl.when(e >= 2)
        def _():
            save_sa(e - 2).wait()
            save_dh(e - 2).wait()

        here = pl.ds(pl.multiple_of((e % per) * LINE, LINE), LINE)
        live = live_ref[piece(e), :]

        def grads_of(dn, h, dy, gain, factor, inner):
            return dy * live + factor * (dn * gain) - h * (factor * factor * factor * inner)

        dn = total[piece(e), :].astype(F32)
        h = hbuf[g % 2, here, :].astype(F32)
        factor = lax.rsqrt(jnp.mean(h * h, axis=1, keepdims=True) + EPS_NORM)
        inner = jnp.mean(dn * gain_ref[...] * h, axis=1, keepdims=True)
        dy = cbuf[g % 2, here, :].astype(F32)
        sbuf[e % 2] = (RESIDUAL_SCALE * grads_of(dn, h, dy, gain_ref[...], factor, inner)).astype(BF)
        own_dn = total[piece(e), mine].astype(F32)
        own_h = hbuf[g % 2, here, mine].astype(F32)
        own_dy = cbuf[g % 2, here, mine].astype(F32)
        dbuf[e % 2] = grads_of(own_dn, own_h, own_dy, gain_ref[:, mine], factor, inner)
        gain_out[...] += jnp.sum(own_dn * own_h * factor, axis=0, keepdims=True)
        save_sa(e).start()
        save_dh(e).start()

    def serve(n):
        @pl.when(jnp.logical_and(is_mid, n < count))
        def _():
            to_mid(n).wait_recv()
            near[piece(n)] = (total[piece(n)].astype(F32) + near[piece(n)].astype(F32)).astype(BF)
            over(n).start()

        @pl.when(jnp.logical_and(is_mid, jnp.logical_and(n >= 1, n <= count)))
        def _():
            over(n - 1).wait_recv()
            total[piece(n - 1)] = (near[piece(n - 1)].astype(F32) + cross[piece(n - 1)].astype(F32)).astype(BF)
            to_end(n - 1).start()
            finish_rows(n - 1)

        @pl.when(jnp.logical_and(is_end, jnp.logical_and(n >= LAG, n < count + LAG)))
        def _():
            to_mid(n - LAG).wait_send()
            to_end(n - LAG).wait_recv()
            finish_rows(n - LAG)

    def flip(v, by):
        return v + by - 2 * v * by

    def spot(j):
        down, over_x = 1 - j // 2, 1 - j % 2
        return down, over_x, flip(y, down), flip(x, over_x)

    def tile(i, f, parity):
        rows = pl.ds(pl.multiple_of((2 * f + parity) * block, 16), block)
        return dot_nn(lhs[rows, :], rhs[i % 2])

    upper, lower = pl.ds(0, half), pl.ds(half, half)
    core_copy = lambda i, j, f: remote(stage.at[j % 2], cin.at[i, f], core_send.at[i, j], core_recv.at[i, f], to_core)
    x_copy = lambda i, f, yy: remote(cin.at[i, f, upper], xin.at[i, yy], x_send.at[i, yy], x_recv.at[i, yy], to_x)
    y2_copy = lambda i, f, xx: remote(cin.at[i, f, lower], yin2.at[i, xx], y2_send.at[i, xx], y2_recv.at[i, xx], to_y)
    y_copy = lambda i: remote(xin.at[i, 1 - y], yin.at[i], y_send.at[i], y_recv.at[i], to_y)
    x2_copy = lambda i: remote(yin2.at[i, 1 - x], xin2.at[i], x2_send.at[i], x2_recv.at[i], to_x)
    save_upper = lambda i: local(yin.at[i], grad_any.at[i, upper], out_sem.at[i, 0])
    save_lower = lambda i: local(xin2.at[i], grad_any.at[i, lower], out_sem.at[i, 1])

    def plus(a, b):
        return (a.astype(F32) + b.astype(F32)).astype(BF)

    def products(i, n0):
        def for_other(j):
            _, _, yy, xx = spot(j)
            f = yy * 2 + xx

            @pl.when(j >= 2)
            def _():
                core_copy(i, j - 2, f).wait_send()

            stage[j % 2] = tile(i, f, 1 - core).astype(BF)
            core_copy(i, j, f).start()
            serve(n0 + j)

        each(4, for_other)

        def for_own(j):
            down, over_x, yy, xx = spot(j)
            f = yy * 2 + xx
            own = tile(i, f, core)
            core_copy(i, j, f).wait_recv()
            cin[i, f] = (own + cin[i, f].astype(F32)).astype(BF)

            @pl.when(over_x == 1)
            def _():
                x_copy(i, f, yy).start()

            @pl.when(down == 1)
            def _():
                y2_copy(i, f, xx).start()

            serve(n0 + 4 + j)

        each(4, for_own)
        for j in (2, 3):
            core_copy(i, j, 0).wait_send()

    def first_stage(i):
        x_copy(i, 0, 1 - y).wait_recv()
        xin[i, 1 - y] = plus(xin[i, 1 - y], cin[i, (1 - y) * 2 + x, upper])
        y_copy(i).start()
        y2_copy(i, 0, 1 - x).wait_recv()
        yin2[i, 1 - x] = plus(yin2[i, 1 - x], cin[i, y * 2 + 1 - x, lower])
        x2_copy(i).start()
        x_copy(i, 0, y).wait_recv()
        xin[i, y] = plus(xin[i, y], cin[i, y * 2 + x, upper])
        y2_copy(i, 0, x).wait_recv()
        yin2[i, x] = plus(yin2[i, x], cin[i, y * 2 + x, lower])

    def second_stage(i):
        y_copy(i).wait_recv()
        yin[i] = plus(yin[i], xin[i, y])
        save_upper(i).start()
        x2_copy(i).wait_recv()
        xin2[i] = plus(xin2[i], yin2[i, x])
        save_lower(i).start()
        square = total_square(yin[i]) + total_square(xin2[i])
        square_out[i : i + 1, :] = jnp.broadcast_to(square, (1, 128))

    square_out[...] = jnp.zeros_like(square_out)
    load_lhs.wait()
    load_rhs(0).wait()
    products(0, 0)
    load_rhs(2).start()
    load_rhs(1).wait()
    products(1, 8)

    cols_of = lambda c: pl.ds(pl.multiple_of(c * 256, 256), 256)
    load_prep = lambda c: local(cot_any.at[:, cols_of(c)], prep.at[c % 2], prep_sem.at[c])
    load_prep(0).start()
    groups = D // 256

    def turn(c):
        load_prep(c).wait()

        @pl.when(c + 1 < groups)
        def _():
            load_prep(c + 1).start()

        seed = prep[c % 2].astype(F32) * (live_ref[...] * RESIDUAL_SCALE)
        lhs[cols_of(c), :] = seed.T.astype(BF)
        serve(16 + c)

    each(groups, turn)
    first_stage(0)
    load_rhs(2).wait()
    products(2, 16 + groups)
    first_stage(1)
    second_stage(0)
    for n in range(24 + groups, count + LAG):
        serve(n)
    first_stage(2)
    second_stage(1)
    second_stage(2)
    for i in range(3):
        for v in range(2):
            x_copy(i, 0, v).wait_send()
            y2_copy(i, 0, v).wait_send()
        y_copy(i).wait_send()
        x2_copy(i).wait_send()
        save_upper(i).wait()
        save_lower(i).wait()
    for e in (count - 2, count - 1):
        save_sa(e).wait()
        save_dh(e).wait()

    @pl.when(is_mid)
    def _():
        def sent(k):
            over(k).wait_send()
            to_end(k).wait_send()

        each(count, sent)


def grad_reduce(live, gain, d_normed_part, hidden, cotangent, normed_t, d_gate, d_up, activation):
    rows = hidden.shape[0]
    units = d_gate.shape[1]
    width = D // lax.axis_size("tp")
    shard = D // (lax.axis_size("fsdp") * lax.axis_size("ctx"))
    count = rows // LINE
    vmem = pl.BlockSpec(memory_space=pltpu.VMEM)
    anywhere = pl.BlockSpec(memory_space=pl.ANY)
    dma = pltpu.SemaphoreType.DMA
    scratch = lambda *shape: pltpu.VMEM(shape, BF)
    return pl.pallas_call(
        grad_kernel,
        out_shape=[
            jax.ShapeDtypeStruct((rows, D), BF),
            jax.ShapeDtypeStruct((rows, width), F32),
            jax.ShapeDtypeStruct((1, width), F32),
            jax.ShapeDtypeStruct((3, shard, units), BF),
            jax.ShapeDtypeStruct((8, 128), F32),
        ],
        in_specs=[vmem] * 2 + [anywhere] * 7,
        out_specs=[anywhere, anywhere, vmem, anywhere, vmem],
        scratch_shapes=[scratch(rows, D)] * 3
        + [
            scratch(3, 4, shard, units),
            scratch(2, shard, units),
            scratch(3, 2, shard // 2, units),
            scratch(3, 2, shard // 2, units),
            scratch(3, shard // 2, units),
            scratch(3, shard // 2, units),
            scratch(D, rows),
            scratch(2, rows, units),
            scratch(2, LOAD, D),
            scratch(2, LOAD, D),
            scratch(2, LINE, D),
            pltpu.VMEM((2, LINE, width), F32),
            scratch(2, rows, 256),
        ]
        + [dma, dma, dma((3,)), dma((rows // LOAD,)), dma((rows // LOAD,)), dma((count,)), dma((count,)), dma((D // 256,)), dma((3, 2))]
        + [dma((3, 4))] * 2
        + [dma((3, 2))] * 4
        + [dma((3,))] * 4
        + [dma((count,))] * 6,
        compiler_params=pltpu.CompilerParams(collective_id=4, has_side_effects=True, vmem_limit_bytes=63 * MIB),
        cost_estimate=pl.CostEstimate(flops=rows * D * units * 6, bytes_accessed=400 * MIB, transcendentals=0),
        name="grad_reduce",
    )(live, gain, d_normed_part, hidden, cotangent, normed_t, d_gate, d_up, activation)


PACK = 576
HALF = PACK // 2


def torus(s1, xin, yin2, yin, xin2, sems, x, y, to_x, to_y):
    x_send, x_recv, y2_send, y2_recv, y_send, y_recv, x2_send, x2_recv = sems
    half = yin.shape[0]
    upper, lower = pl.ds(0, half), pl.ds(half, half)

    def remote(src, dst, send, recv, to):
        return pltpu.make_async_remote_copy(
            src_ref=src, dst_ref=dst, send_sem=send, recv_sem=recv, device_id=to, device_id_type=MESH
        )

    def plus(a, b):
        return (a.astype(F32) + b.astype(F32)).astype(BF)

    x_copy = lambda v: remote(s1.at[v * 2 + 1 - x, upper], xin.at[v], x_send.at[v], x_recv.at[v], to_x)
    y2_copy = lambda v: remote(s1.at[(1 - y) * 2 + v, lower], yin2.at[v], y2_send.at[v], y2_recv.at[v], to_y)
    y_copy = remote(xin.at[1 - y], yin, y_send.at[0], y_recv.at[0], to_y)
    x2_copy = remote(yin2.at[1 - x], xin2, x2_send.at[0], x2_recv.at[0], to_x)

    def begin():
        x_copy(1 - y).start()
        y2_copy(1 - x).start()
        x_copy(y).start()
        y2_copy(x).start()

    def middle():
        x_copy(1 - y).wait_recv()
        xin[1 - y] = plus(xin[1 - y], s1[(1 - y) * 2 + x, upper])
        y_copy.start()
        y2_copy(1 - x).wait_recv()
        yin2[1 - x] = plus(yin2[1 - x], s1[y * 2 + 1 - x, lower])
        x2_copy.start()
        x_copy(y).wait_recv()
        xin[y] = plus(xin[y], s1[y * 2 + x, upper])
        y2_copy(x).wait_recv()
        yin2[x] = plus(yin2[x], s1[y * 2 + x, lower])

    def last(out):
        y_copy.wait_recv()
        out[upper, :] = plus(yin[...], xin[y])
        x2_copy.wait_recv()
        out[lower, :] = plus(xin2[...], yin2[x])

    def drain():
        for v in range(2):
            x_copy(v).wait_send()
            y2_copy(v).wait_send()
        y_copy.wait_send()
        x2_copy.wait_send()

    return begin, middle, last, drain


def latent_back_kernel(
    dq_ref, de_ref, dkr_ref, up_ref, sum_ref, w_ref, x_ref, gain_ref, dh_ref, tcos, tsin, gains, gout_ref, gq_ref, gkv_ref,
    sel_ref, b2_ref, square_ref,
    gin_ref, pack_out, wd_out, small_out, scalar_out,
    uq, ukv, away, arrived, xb, near, cross, total, dl, dlt, xg, w_pack, small, small_in, scal_in,
    s1, cin, xin, yin2, yin, xin2, s1w, cinw, xinw, yin2w, yinw, xin2w,
    lat_send, lat_recv, out_send, out_recv, q_send, q_recv, kv_send, kv_recv, w_send, w_recv,
    small_send, small_recv, scal_send, scal_recv, *sems,
):
    z, core, place = lax.axis_index("tp"), lax.axis_index("ctx"), lax.axis_index("fsdp")
    y, x = place // 2, place % 2
    is_end, is_mid, partner, across = line_places(z)
    line_sems, pack_sems, w_sems = sems[:6], sems[6:14], sems[14:22]
    to_mid, over, to_end, first, second = line_copies(xb, near, cross, total, line_sems, partner, across, LAT_LINE)
    count = xb.shape[0] // LAT_LINE
    rows = xb.shape[0]
    peers = up_ref.shape[0]
    me = place * 2 + core
    to_core, to_x, to_y = {"ctx": 1 - core}, {"fsdp": y * 2 + 1 - x}, {"fsdp": (1 - y) * 2 + x}

    def remote(src, dst, send, recv, to):
        return pltpu.make_async_remote_copy(
            src_ref=src, dst_ref=dst, send_sem=send, recv_sem=recv, device_id=to, device_id_type=MESH
        )

    def peer(d):
        to = lax.rem(me + d, peers)
        return {"fsdp": to // 2, "ctx": lax.rem(to, 2)}

    barrier = pltpu.get_barrier_semaphore()
    for d in range(1, peers):
        pl.semaphore_signal(barrier, inc=1, device_id=peer(d), device_id_type=MESH)
    for d in range(1, 4):
        pl.semaphore_signal(barrier, inc=1, device_id={"tp": lax.rem(z + d, 4)}, device_id_type=MESH)
    pl.semaphore_wait(barrier, peers + 2)

    def piece(e):
        return pl.ds(pl.multiple_of(e * LAT_LINE, LAT_LINE), LAT_LINE)

    def span(f, parity, size):
        return pl.ds(pl.multiple_of((2 * f + parity) * size, size), size)

    slot_q, slot_kv = pl.ds(320 + 96 * core, 96), pl.ds(512 + 32 * core, 32)
    other_q, other_kv = pl.ds(320 + 96 * (1 - core), 96), pl.ds(512 + 32 * (1 - core), 32)
    out_copy = lambda f: remote(gout_ref.at[span(f, 1 - core, 320)], cin.at[f], out_send.at[f], out_recv.at[f], to_core)
    q_copy = lambda f: remote(gq_ref.at[span(f, 1 - core, 96)], s1.at[f, slot_q], q_send.at[f], q_recv.at[f], to_core)
    kv_copy = lambda f: remote(gkv_ref.at[span(f, 1 - core, 32)], s1.at[f, slot_kv], kv_send.at[f], kv_recv.at[f], to_core)
    q_got = lambda f: remote(gq_ref.at[span(f, 1 - core, 96)], s1.at[f, other_q], q_send.at[f], q_recv.at[f], to_core)
    kv_got = lambda f: remote(gkv_ref.at[span(f, 1 - core, 32)], s1.at[f, other_kv], kv_send.at[f], kv_recv.at[f], to_core)

    for p in range(peers):
        uq[p * 96 : (p + 1) * 96, :] = up_ref[p, 0:96, :]
        ukv[p * 32 : (p + 1) * 32, :] = up_ref[p, 96:128, :]

    lane = lax.broadcasted_iota(jnp.int32, (1, 128), 1)
    hand = lambda e: remote(away.at[piece(e)], arrived.at[piece(e)], lat_send.at[e], lat_recv.at[e], to_core)

    def share(at):
        here = pl.ds(pl.multiple_of(at, LAT_LINE), LAT_LINE)
        q = dot_nt(dq_ref[here, :], uq[...])
        kv = dot_nt(de_ref[here, :], ukv[...])
        rope = jnp.where(lane < ROPE, pltpu.roll(dkr_ref[here, :], NOPE, 1), 0.0)
        return q, kv, rope

    def send_away(e):
        q, kv, rope = share((1 - core) * rows + e * LAT_LINE)
        away[piece(e), 0:QR] = q.astype(BF)
        away[piece(e), QR : QR + KVR] = kv.astype(BF)
        away[piece(e), QR + KVR : LAT_WIDE] = rope.astype(BF)
        hand(e).start()

    each(count, send_away)
    for f in range(4):
        out_copy(f).start()
        q_copy(f).start()
        kv_copy(f).start()

    def keep(e):
        q, kv, rope = share(core * rows + e * LAT_LINE)
        hand(e).wait_recv()
        got = arrived[piece(e), :].astype(F32)
        xb[piece(e), 0:QR] = (q + got[:, 0:QR]).astype(BF)
        xb[piece(e), QR : QR + KVR] = (kv + got[:, QR : QR + KVR]).astype(BF)
        xb[piece(e), QR + KVR : LAT_WIDE] = (rope + got[:, QR + KVR :]).astype(BF)

        @pl.when(is_end)
        def _():
            to_mid(e).start()

    each(count, keep)

    small[...] = jnp.zeros_like(small)
    small[2:3, 0 : b2_ref.shape[1]] = b2_ref[...]
    stat_lane = lax.broadcasted_iota(jnp.int32, (1, LAT_WIDE), 1)
    stat_lane = jnp.logical_and(stat_lane >= LAT, stat_lane < LAT + 8)
    gain_q, gain_kv = gains[0:1, 0:QR], gains[0:1, QR : QR + KVR]

    def through(d, v, gain):
        factor = lax.rsqrt(jnp.mean(v * v, axis=1, keepdims=True) + EPS_NORM)
        scaled = d * gain
        gain_grad = jnp.sum(d * v * factor, axis=0, keepdims=True)
        return factor * scaled - v * (factor * factor * factor * jnp.mean(scaled * v, axis=1, keepdims=True)), gain_grad

    def finish_rows(e):
        v = sum_ref[piece(e), :].astype(F32)
        square = jnp.sum(jnp.where(stat_lane, v, 0.0), axis=1, keepdims=True)
        factor = lax.rsqrt(square / D + EPS_NORM)
        v = v * factor
        d = total[piece(e), :].astype(F32)
        ql, kl, raw = v[:, :QR], v[:, QR : QR + KVR], jnp.where(lane < ROPE, v[:, QR + KVR :], 0.0)
        dql, grad_q = through(d[:, :QR], ql, gain_q)
        dkl, grad_kv = through(d[:, QR : QR + KVR], kl, gain_kv)
        moved = pltpu.roll(d[:, QR + KVR :], NOPE, 1)
        turned = jnp.where(lane < NOPE + 16, pltpu.roll(moved, 128 - 16, 1), -pltpu.roll(moved, 16, 1))
        rope = pltpu.roll(moved * tcos[piece(e), :] + turned * tsin[piece(e), :], NOPE, 1)
        inner = (
            jnp.sum(dql * ql, axis=1, keepdims=True)
            + jnp.sum(dkl * kl, axis=1, keepdims=True)
            + jnp.sum(rope * raw, axis=1, keepdims=True)
        ) / D
        small[0:1, 0:QR] += grad_q
        small[0:1, QR : QR + KVR] += grad_kv
        dl[piece(e), 0:QR] = (dql * factor).astype(BF)
        dl[piece(e), QR : QR + KVR] = (dkl * factor).astype(BF)
        dl[piece(e), QR + KVR : LAT_WIDE] = (rope * factor).astype(BF)
        d_in = dot_nn(dl[piece(e), :], w_ref[...])
        xin_rows = x_ref[piece(e), :].astype(F32)
        gin_ref[piece(e), :] = (
            dh_ref[piece(e), :] + d_in * gain_ref[...] - xin_rows * (factor * factor * inner)
        ).astype(BF)
        small[1:2, 0 : d_in.shape[1]] += jnp.sum(d_in * xin_rows, axis=0, keepdims=True)
        xg[piece(e), :] = (xin_rows * gain_ref[...]).astype(BF)

        @pl.when(e % 2 == 1)
        def _():
            pair = pl.ds(pl.multiple_of((e - 1) * LAT_LINE, 128), 128)
            dlt[:, pair] = dl[pair, :].astype(F32).T.astype(BF)

    def serve(n):
        @pl.when(jnp.logical_and(is_mid, n < count))
        def _():
            first(n)

        @pl.when(jnp.logical_and(is_mid, jnp.logical_and(n >= 1, n <= count)))
        def _():
            second(n - 1)
            finish_rows(n - 1)

        @pl.when(jnp.logical_and(is_end, jnp.logical_and(n >= 2, n < count + 2)))
        def _():
            to_mid(n - 2).wait_send()
            to_end(n - 2).wait_recv()
            finish_rows(n - 2)

    begin, middle, last, drain = torus(s1, xin, yin2, yin, xin2, pack_sems, x, y, to_x, to_y)
    begin_w, middle_w, last_w, drain_w = torus(s1w, xinw, yin2w, yinw, xin2w, w_sems, x, y, to_x, to_y)

    serve(0)
    for f in range(4):
        out_copy(f).wait_recv()
        s1[f, 0:320] = (gout_ref[span(f, core, 320), :].astype(F32) + cin[f].astype(F32)).astype(BF)
        s1[f, slot_q] = gq_ref[span(f, core, 96), :]
        s1[f, slot_kv] = gkv_ref[span(f, core, 32), :]
        q_got(f).wait_recv()
        kv_got(f).wait_recv()
    begin()
    each(6, lambda n: serve(n + 1))
    middle()
    each(4, lambda n: serve(n + 7))
    last(pack_out)
    each(count + 2 - 11, lambda n: serve(n + 11))

    both = dot_nn(dlt[0:QR, :], xg[...])
    for p in range(peers):
        w_pack[p, 0:96, :] = both[p * 96 : (p + 1) * 96].astype(BF)
    tail = dot_nn(dlt[QR:LAT, :], xg[...]).astype(BF)
    wide = lax.dot_general(sel_ref[...], tail, (((0,), (0,)), ((), ())), preferred_element_type=F32)
    for p in range(peers):
        w_pack[p, 96:144, :] = wide[p * 48 : (p + 1) * 48].astype(BF)
        w_pack[p, 144:160, :] = jnp.zeros((16, wide.shape[1]), BF)
    w_copy = lambda f: remote(w_pack.at[2 * f + 1 - core], cinw.at[f], w_send.at[f], w_recv.at[f], to_core)
    for f in range(4):
        w_copy(f).start()
    for f in range(4):
        w_copy(f).wait_recv()
        s1w[f] = (w_pack[2 * f + core].astype(F32) + cinw[f].astype(F32)).astype(BF)
    begin_w()
    middle_w()
    last_w(wd_out)

    squares = (
        total_square(wd_out[0:96, :]),
        total_square(wd_out[96:144, :]),
        total_square(pack_out[320:512, :]),
        total_square(pack_out[512:576, :]),
        total_square(pack_out[0:320, :]),
        square_ref[0:1, 0:1] + square_ref[1:2, 0:1],
        square_ref[2:3, 0:1],
    )
    line = jnp.zeros((1, 128), F32)
    for n, v in enumerate(squares):
        line = jnp.where(lane == n, v, line)
    small[3:4, 0:128] = line
    small_copy = lambda d, source: remote(small, small_in.at[source], small_send.at[d], small_recv.at[source], peer(d))
    for d in range(1, peers):
        small_copy(d, me).start()
    small_in[me] = small[...]
    for d in range(1, peers):
        small_copy(d, lax.rem(me + peers - d, peers)).wait_recv()
    whole = small_in[0]
    for p in range(1, peers):
        whole = whole + small_in[p]
    small_out[...] = whole
    norms = total_square(whole[1:2]) + total_square(whole[2:3])
    scal_in[z] = jnp.broadcast_to(jnp.where(lane == 7, norms, whole[3:4, 0:128]), (8, 128))
    scal_copy = lambda d, source: remote(
        scal_in.at[z], scal_in.at[source], scal_send.at[d], scal_recv.at[source], {"tp": lax.rem(z + d, 4)}
    )
    for d in range(1, 4):
        scal_copy(d, z).start()
    for d in range(1, 4):
        scal_copy(d, lax.rem(z + 4 - d, 4)).wait_recv()
    scalars = (scal_in[0] + scal_in[1]) + (scal_in[2] + scal_in[3])
    scalar_out[...] = jnp.where(lane == 8, total_square(whole[0:1]), scalars)

    for d in range(1, peers):
        small_copy(d, me).wait_send()
    for d in range(1, 4):
        scal_copy(d, z).wait_send()
    drain()
    drain_w()
    for f in range(4):
        out_copy(f).wait_send()
        q_copy(f).wait_send()
        kv_copy(f).wait_send()
        w_copy(f).wait_send()
    each(count, lambda e: hand(e).wait_send())

    @pl.when(is_mid)
    def _():
        def sent(k):
            over(k).wait_send()
            to_end(k).wait_send()

        each(count, sent)


def latent_backward(*args):
    dq, up, x = args[0], args[3], args[6]
    rows, width = x.shape
    lanes = dq.shape[1]
    peers = up.shape[0]
    count = rows // LAT_LINE
    vmem = pl.BlockSpec(memory_space=pltpu.VMEM)
    dma = pltpu.SemaphoreType.DMA
    scratch = lambda *shape: pltpu.VMEM(shape, BF)
    halves = lambda half: [scratch(2, half, width), scratch(2, half, width), scratch(half, width), scratch(half, width)]
    torus_sems = [dma((2,))] * 4 + [dma((1,))] * 4
    return pl.pallas_call(
        latent_back_kernel,
        out_shape=[
            jax.ShapeDtypeStruct((rows, width), BF),
            jax.ShapeDtypeStruct((PACK, width), BF),
            jax.ShapeDtypeStruct((PIECE, width), BF),
            jax.ShapeDtypeStruct((8, QR + KVR), F32),
            jax.ShapeDtypeStruct((8, 128), F32),
        ],
        in_specs=[vmem] * len(args),
        out_specs=[vmem] * 5,
        scratch_shapes=[scratch(QR, lanes), scratch(KVR, lanes)]
        + [scratch(rows, LAT_WIDE)] * 7
        + [
            scratch(LAT_WIDE, rows),
            scratch(rows, width),
            scratch(peers, PIECE, width),
            pltpu.VMEM((8, QR + KVR), F32),
            pltpu.VMEM((peers, 8, QR + KVR), F32),
            pltpu.VMEM((4, 8, 128), F32),
            scratch(4, PACK, width),
            scratch(4, 320, width),
        ]
        + halves(HALF)
        + [scratch(4, PIECE, width), scratch(4, PIECE, width)]
        + halves(PIECE // 2)
        + [dma((count,))] * 2
        + [dma((4,))] * 8
        + [dma((peers,))] * 2
        + [dma((4,))] * 2
        + [dma((count,))] * 6
        + torus_sems * 2,
        compiler_params=pltpu.CompilerParams(collective_id=5, has_side_effects=True, vmem_limit_bytes=62 * MIB),
        cost_estimate=pl.CostEstimate(flops=rows * LAT_WIDE * width * 6, bytes_accessed=200 * MIB, transcendentals=0),
        name="latent_backward",
    )(*args)


def swap_cores(v):
    return lax.ppermute(v, "ctx", [(0, 1), (1, 0)])


def in_core_order(mine, other, core, axis):
    return jnp.where(
        core == 0, jnp.concatenate([mine, other], axis=axis), jnp.concatenate([other, mine], axis=axis)
    )


def gather_shards(v):
    return lax.all_gather(v, ("fsdp", "ctx"), axis=0, tiled=True)


X_SWAP = [(0, 1), (1, 0), (2, 3), (3, 2)]
Y_SWAP = [(0, 2), (2, 0), (1, 3), (3, 1)]


def take(v, which, axis):
    return lax.dynamic_index_in_dim(v, which, axis, keepdims=False)


def add_up(a, b):
    return (a.astype(F32) + b.astype(F32)).astype(BF)


def keep_half(v, axis, which, name, pairs):
    other = lax.ppermute(take(v, 1 - which, axis), name, pairs)
    return add_up(take(v, which, axis), other)


def scatter_fsdp(v):
    if lax.axis_size("fsdp") != 4:
        return lax.psum_scatter(v, "fsdp", scatter_dimension=0, tiled=False)
    place = lax.axis_index("fsdp")
    y, x = place // 2, place % 2
    _, rows, cols = v.shape
    v = v.reshape(2, 2, 2, rows // 2, cols)
    first = keep_half(v[:, :, 0], 1, x, "fsdp", X_SWAP)
    second = keep_half(v[:, :, 1], 0, y, "fsdp", Y_SWAP)
    first = keep_half(first, 0, y, "fsdp", Y_SWAP)
    second = keep_half(second, 0, x, "fsdp", X_SWAP)
    return jnp.concatenate([first, second], axis=0)


def scatter_grads(v):
    fsdp, ctx = lax.axis_size("fsdp"), lax.axis_size("ctx")
    rows, cols = v.shape
    v = v.reshape(fsdp, ctx, rows // (fsdp * ctx), cols)
    return scatter_fsdp(keep_half(v, 1, lax.axis_index("ctx"), "ctx", [(0, 1), (1, 0)]))


def split_two(v):
    high = v.astype(BF)
    return high, (v - high.astype(F32)).astype(BF)


def adamw_update(parameter, gradient, first_moment, second_moment, decay_rate):
    first_new = BETA_ONE * first_moment + (1.0 - BETA_ONE) * gradient
    second_new = BETA_TWO * second_moment + (1.0 - BETA_TWO) * gradient * gradient
    first_hat = first_new / (1.0 - BETA_ONE**STEP)
    second_hat = second_new / (1.0 - BETA_TWO**STEP)
    updated = parameter - LEARN_RATE * (
        first_hat / (jnp.sqrt(second_hat) + ADAM_EPS) + decay_rate * parameter
    )
    return (updated, first_new, second_new)


def norm_backward(incoming, values, factor, gain):
    scaled = incoming * gain
    gain_grad = jnp.sum(incoming * values * factor, axis=0)
    result = factor * scaled - values * factor**3 * jnp.mean(scaled * values, axis=1, keepdims=True)
    return (result, gain_grad)


def local(*args):
    tokens, cotangent, lengths = args[:3]
    params, firsts, seconds = args[3:12], args[12:21], args[21:30]
    w_qdown, w_kvdown, w_qup, w_kvup, w_out, w_gateup, w_down, g_norms, g_latent = params
    n_tp, n_ctx, n_fsdp = lax.axis_size("tp"), lax.axis_size("ctx"), lax.axis_size("fsdp")
    tp, core = lax.axis_index("tp"), lax.axis_index("ctx")
    rows, width = tokens.shape
    slot = rows * n_ctx
    heads_all = H // n_tp
    by_head = heads_all % n_ctx == 0
    heads = heads_all // n_ctx if by_head else heads_all

    fused = n_tp == 4 and n_fsdp == 4 and n_ctx == 2
    gains_norm = g_norms.astype(BF)
    gain_attn = gains_norm[0].astype(F32)
    inputs = tokens.astype(F32)
    seq_length = lengths[0, 0]
    own_index = core * rows + jnp.arange(rows, dtype=jnp.int32)
    own_segment = (own_index >= seq_length).astype(jnp.int32)
    live = (own_segment == 0).astype(F32)[:, None]

    out_t = gather_shards(w_out.T.astype(BF))
    gate_up = lax.all_gather(w_gateup.astype(BF), ("fsdp", "ctx"), axis=1, tiled=True)
    ff_down_t = gather_shards(w_down.T.astype(BF))
    q_shard = jnp.pad(
        w_qup.astype(BF).reshape(w_qup.shape[0], heads_all, HEAD), ((0, 0), (0, 0), (0, 128 - HEAD))
    ).reshape(w_qup.shape[0], heads_all * 128)
    up_shard = jnp.concatenate([q_shard, w_kvup.astype(BF)], axis=0)

    if fused:
        piece = jnp.concatenate(
            [
                w_qdown.T.astype(BF),
                jnp.pad(w_kvdown.T.astype(BF), ((0, 12), (0, 0))),
                jnp.broadcast_to(jnp.pad(g_latent.astype(BF), (0, width - g_latent.shape[0])), (16, width)),
            ],
            axis=0,
        )
        up_pair = jnp.stack([up_shard[:, : heads * 128], up_shard[:, heads * 128 :]])
        gain_wide = jnp.pad(gains_norm[1].astype(F32), (0, LAT_WIDE - width))[None]
        down_t, lat_sum, lat_all, cos_t, sin_t, seg_q, up, tcos, tsin, gains_lat = latent_forward(
            tokens, gain_attn[None], gain_wide, piece, up_pair, lengths
        )
        gain_mlp = lat_sum[rows : rows + n_tp, :width].reshape(D).astype(F32)
    else:
        index = jnp.arange(slot, dtype=jnp.int32)
        segment = (index >= seq_length).astype(jnp.int32)
        position = (index - segment * seq_length).astype(F32)
        frequency = ROPE_BASE ** (-2.0 * jnp.arange(ROPE // 2, dtype=F32) / ROPE)
        angles = frequency[:, None] * position[None, :]
        cos_t, sin_t = jnp.cos(angles), jnp.sin(angles)
        own_cos = lax.dynamic_slice_in_dim(cos_t, core * rows, rows, 1).T
        own_sin = lax.dynamic_slice_in_dim(sin_t, core * rows, rows, 1).T
        seg_f = segment.astype(F32)
        seg_q = jnp.concatenate([seg_f[None], 1.0 - seg_f[None], jnp.zeros((14, slot), F32)], axis=0).astype(BF)
        seg_k = (MASK_VALUE * jnp.concatenate([1.0 - seg_f[:, None], seg_f[:, None]], axis=1)).astype(BF)
        down_t = jnp.concatenate(
            [gather_shards(w_qdown.T.astype(BF)), gather_shards(w_kvdown.T.astype(BF)), jnp.zeros((LAT_WIDE - LAT, width), BF)]
        )
        gain_lat = lax.all_gather(g_latent.astype(BF), ("fsdp", "ctx"), axis=0, tiled=True).astype(F32)
        gain_mlp = lax.all_gather(gains_norm[1], "tp", axis=0, tiled=True).astype(F32)
        up = gather_shards(up_shard).reshape(n_fsdp * n_ctx, up_shard.shape[0], heads_all * 128)
        if by_head:
            up = lax.dynamic_slice_in_dim(up, core * heads * 128, heads * 128, 2)
        scaled_in = (inputs * gain_attn).astype(BF)
        lat_sum = lax.psum(dot_nt(scaled_in, down_t).astype(BF), "tp").astype(F32)
        square_sum = lax.psum(jnp.sum(inputs * inputs, axis=1), "tp")
    if not fused:
        factor_one = lax.rsqrt(square_sum / D + EPS_NORM)[:, None]
        latents = lat_sum[:, :LAT] * factor_one
        query_latent = latents[:, :QR]
        kv_latent = latents[:, QR : QR + KVR]
        gain_query, gain_kv = gain_lat[:QR], gain_lat[QR:]
        factor_query = lax.rsqrt(jnp.mean(query_latent * query_latent, axis=1, keepdims=True) + EPS_NORM)
        factor_kv = lax.rsqrt(jnp.mean(kv_latent * kv_latent, axis=1, keepdims=True) + EPS_NORM)
        rope_raw = latents[:, QR + KVR :]
        query_normed = (query_latent * factor_query * gain_query).astype(BF)
        kv_normed = (kv_latent * factor_kv * gain_kv).astype(BF)
        r_one, r_two = rope_raw[:, : ROPE // 2], rope_raw[:, ROPE // 2 :]
        rope_key = jnp.concatenate(
            [r_one * own_cos - r_two * own_sin, r_two * own_cos + r_one * own_sin], axis=1
        ).astype(BF)
        normed_lat = jnp.concatenate([query_normed, kv_normed, jnp.zeros((rows, NOPE), BF), rope_key], axis=1)
        lat_both = in_core_order(normed_lat, swap_cores(normed_lat), core, 0)
        lat_all = jnp.concatenate([lat_both, seg_k, jnp.zeros((slot, 128 - HEAD - 2), BF)], axis=1)
    qn, kn = lat_all[:, :QR], lat_all[:, QR : QR + KVR]

    att_heads, lse, q_t, k_rows, v_t = attend_forward(lat_all, cos_t, sin_t, seg_q, up)
    att_flat = att_heads.reshape(heads * VD, slot)
    own_cols = lambda v: lax.dynamic_slice_in_dim(v, core * rows, rows, 1)
    if by_head:
        other = swap_cores(lax.dynamic_slice_in_dim(att_flat, (1 - core) * rows, rows, 1))
        att_t = in_core_order(own_cols(att_flat), other, core, 0)
    else:
        att_t = own_cols(att_flat)

    feature_owner = jnp.arange(D) // width
    own_features = lambda v: lax.dynamic_slice_in_dim(v, tp * width, width, 1)
    if fused:
        hidden, d_normed_part, mlp_part, normed_two_t, activation, d_gate, d_up = block_forward(
            att_t.T, tokens, out_t, gain_mlp[None], live, cotangent, gate_up, ff_down_t
        )
        attn_seed, d_hidden, grad_gain_mlp, grads, grad_squares = grad_reduce(
            live, gain_mlp[None], d_normed_part, hidden, cotangent, normed_two_t, d_gate, d_up, activation
        )
    else:
        dy = cotangent.astype(F32) * live
        mlp_seed = (RESIDUAL_SCALE * dy).astype(BF)
        h_part = RESIDUAL_SCALE * dot_nt(att_t.T, out_t)
        h_part = h_part + jnp.where(
            (feature_owner == tp)[None], jnp.concatenate([inputs] * n_tp, axis=1), 0.0
        )
        hidden = lax.psum(h_part.astype(BF), "tp")
        hidden_f = hidden.astype(F32)
        factor_two = lax.rsqrt(jnp.mean(hidden_f * hidden_f, axis=1, keepdims=True) + EPS_NORM)
        normed_two = (hidden_f * factor_two * gain_mlp).astype(BF)
        gate_proj = dot_nn(normed_two, gate_up[0])
        up_proj = dot_nn(normed_two, gate_up[1])
        sigmoid_gate = jax.nn.sigmoid(gate_proj)
        activation = (gate_proj * sigmoid_gate * up_proj).astype(BF)
        mlp_part = dot_nt(activation, ff_down_t).astype(BF)
        d_activation = dot_nn(mlp_seed, ff_down_t)
        d_gate = (
            d_activation * up_proj * sigmoid_gate * (1.0 + gate_proj * (1.0 - sigmoid_gate))
        ).astype(BF)
        d_up = (d_activation * gate_proj * sigmoid_gate).astype(BF)
        d_normed_part = (dot_nt(d_gate, gate_up[0]) + dot_nt(d_up, gate_up[1])).astype(BF)
        grad_down = scatter_grads(dot_tn(mlp_seed, activation).astype(BF))
        grad_gate = scatter_grads(dot_tn(normed_two, d_gate).astype(BF))
        grad_up = scatter_grads(dot_tn(normed_two, d_up).astype(BF))
        d_normed = lax.psum(d_normed_part, "tp").astype(F32)
        row_inner = jnp.mean(d_normed * gain_mlp * hidden_f, axis=1, keepdims=True)
        d_hidden_full = dy + factor_two * d_normed * gain_mlp - hidden_f * (factor_two**3 * row_inner)
        attn_seed = (RESIDUAL_SCALE * d_hidden_full).astype(BF)
        d_hidden = own_features(d_hidden_full)
        grad_gain_mlp = jnp.sum(own_features(d_normed * hidden_f) * factor_two, axis=0)
    mlp_part, attn_seed = lax.optimization_barrier((mlp_part, attn_seed))
    mlp_out = lax.psum_scatter(mlp_part, "tp", scatter_dimension=1, tiled=True).astype(F32)
    layer_out = (own_features(hidden).astype(F32) + RESIDUAL_SCALE * mlp_out).astype(BF)
    d_att_t = lax.dot_general(out_t, attn_seed, (((0,), (1,)), ((), ())), preferred_element_type=F32).astype(BF)
    grad_out = dot_tn(attn_seed, att_t.T).astype(BF)

    if by_head:
        pick = lambda v, which: lax.dynamic_slice_in_dim(v, which * heads * VD, heads * VD, 0)
        d_att = in_core_order(pick(d_att_t, core), swap_cores(pick(d_att_t, 1 - core)), core, 1)
    else:
        d_att = lax.dynamic_update_slice(jnp.zeros((heads * VD, slot), BF), d_att_t, (0, core * rows))
    d_q, d_e, d_kr = attend_backward(
        q_t, k_rows, v_t, att_heads, d_att.reshape(heads, VD, slot), lse, cos_t, sin_t
    )
    grad_qup = dot_tn(qn, d_q).astype(BF)
    grad_kvup = dot_tn(kn, d_e).astype(BF)

    def heads_only(g):
        return g.reshape(g.shape[0], heads_all, 128)[:, :, :HEAD].reshape(g.shape[0], heads_all * HEAD)

    share = g_latent.shape[0]
    my_share = (lax.axis_index("fsdp") * n_ctx + core) * share
    if fused:
        grad_input, pack, wd_grad, small, scalars = latent_backward(
            d_q, d_e, d_kr, up, lat_sum, down_t, tokens, gain_attn[None], d_hidden, tcos, tsin, gains_lat,
            grad_out, grad_qup, grad_kvup, spread(n_fsdp * n_ctx), grad_gain_mlp, grad_squares,
        )
        lanes = heads * 128
        owned = [
            wd_grad[:96].astype(F32).T,
            wd_grad[96:132].astype(F32).T,
            heads_only(jnp.concatenate([pack[320:416], pack[416:512]], axis=1)).astype(F32),
            jnp.concatenate([pack[512:544], pack[544:576]], axis=1).astype(F32),
            pack[:320].astype(F32).T,
            grads[:2].astype(F32),
            grads[2].astype(F32).T,
            small[1:3, :width],
            lax.dynamic_slice_in_dim(small[0], my_share, share, 0),
        ]
        totals = [scalars[0, n] for n in range(9)]
    else:
        q_up_here = up[:, : w_qup.shape[0]].reshape(QR, heads * 128)
        kv_up_here = up[:, w_qup.shape[0] :].reshape(KVR, heads * 128)
        d_lat_part = jnp.concatenate([dot_nt(d_q, q_up_here), dot_nt(d_e, kv_up_here), d_kr[:, NOPE:HEAD]], axis=1)
        own_rows = lambda v, which: lax.dynamic_slice_in_dim(v, which * rows, rows, 0)
        from_other = swap_cores(own_rows(d_lat_part, 1 - core).astype(BF)).astype(F32)
        d_lat = lax.psum((own_rows(d_lat_part, core) + from_other).astype(BF), "tp").astype(F32)
        d_rope = d_lat[:, QR + KVR : LAT]
        k_one, k_two = d_rope[:, : ROPE // 2], d_rope[:, ROPE // 2 :]
        d_rope_raw = jnp.concatenate([k_one * own_cos + k_two * own_sin, k_two * own_cos - k_one * own_sin], axis=1)
        d_query_latent, grad_gain_query = norm_backward(d_lat[:, :QR], query_latent, factor_query, gain_query)
        d_kv_latent, grad_gain_kv = norm_backward(d_lat[:, QR : QR + KVR], kv_latent, factor_kv, gain_kv)
        d_latents = jnp.concatenate([d_query_latent, d_kv_latent, d_rope_raw], axis=1)
        in_inner = jnp.sum(d_latents * latents, axis=1, keepdims=True) / D
        d_latents = (d_latents * factor_one).astype(BF)
        grad_both = dot_tn(d_latents, scaled_in).astype(BF)
        d_in = dot_nn(d_latents, down_t[:LAT])
        grad_gain_attn = jnp.sum(d_in * inputs, axis=0)
        grad_input = (d_hidden + d_in * gain_attn - inputs * (factor_one**2 * in_inner)).astype(BF)

        def scatter_up(g):
            if not by_head:
                return scatter_grads(g)
            n_rows, n_cols = g.shape
            g = g.reshape(n_fsdp, n_ctx, n_rows // (n_fsdp * n_ctx), n_cols)
            other = swap_cores(take(g, 1 - core, 1))
            return scatter_fsdp(in_core_order(take(g, core, 1), other, core, 2))

        owned = [
            scatter_grads(grad_both[:QR]).astype(F32).T,
            scatter_grads(grad_both[QR:]).astype(F32).T,
            heads_only(scatter_up(grad_qup)).astype(F32),
            scatter_up(grad_kvup).astype(F32),
            scatter_grads(grad_out).astype(F32).T,
            jnp.stack([grad_gate, grad_up]).astype(F32),
            grad_down.astype(F32).T,
        ]
        both_gains = jnp.stack([grad_gain_attn, grad_gain_mlp])
        placed_gains = jnp.where((feature_owner == tp)[None], jnp.concatenate([both_gains] * n_tp, axis=1), 0.0)
        latent_gains = jnp.concatenate([grad_gain_query, grad_gain_kv]) * (tp == 0)
        squares = jnp.stack([jnp.sum(g * g) for g in owned])
        small = lax.psum(
            jnp.concatenate([placed_gains.reshape(-1), latent_gains, squares]), ("fsdp", "ctx", "tp")
        )
        all_gains = small[: 2 * D].reshape(2, D)
        all_latent = small[2 * D : 2 * D + QR + KVR]
        owned.append(own_features(all_gains))
        owned.append(lax.dynamic_slice_in_dim(all_latent, my_share, share, 0))
        totals = [small[2 * D + QR + KVR + n] for n in range(7)]
        totals += [jnp.sum(all_gains * all_gains), jnp.sum(all_latent * all_latent)]
    entry_counts = (
        D * QR,
        D * (KVR + ROPE),
        QR * H * HEAD,
        KVR * H * (NOPE + VD),
        H * VD * D,
        2 * D * FF,
        FF * D,
        2 * D,
        QR + KVR,
    )
    new_params, new_firsts, new_seconds = [], [], []
    for n in range(9):
        limit = CLIP_RMS * entry_counts[n] ** 0.5
        clipped = owned[n] * (limit / jnp.maximum(jnp.sqrt(totals[n]), limit))
        updated, first_new, second_new = adamw_update(
            params[n], clipped, firsts[n], seconds[n], WEIGHT_DECAY if n < 7 else 0.0
        )
        new_params.append(updated)
        new_firsts.append(first_new)
        new_seconds.append(second_new)
    return (layer_out, grad_input, *owned, *new_params[:7], *new_firsts, *new_seconds)


def solution(mesh):
    sharded = ("fsdp", "ctx")
    weights = (
        P("tp", sharded),
        P("tp", sharded),
        P(sharded, "tp"),
        P(sharded, "tp"),
        P("tp", sharded),
        P(None, sharded, "tp"),
        P("tp", sharded),
    )
    gains = (P(None, "tp"), P(sharded))
    tokens = P(sharded, "tp")
    return jax.shard_map(
        local,
        mesh=mesh,
        in_specs=(tokens, P(sharded, None), P("fsdp", None)) + (weights + gains) * 3,
        out_specs=(tokens, tokens) + weights + gains + weights + (weights + gains) * 2,
        check_vma=False,
    )
```

```python
import functools

import jax
import jax.numpy as jnp
from jax import lax
from jax.experimental import pallas as pl
from jax.experimental.pallas import tpu as pltpu
from jax.sharding import PartitionSpec as P

D = 2560
H = 40
NOPE = 64
ROPE = 32
VD = 64
QR = 768
KVR = 256
FF = 6400
STEP = 3
HEAD = NOPE + ROPE
LAT = QR + KVR + ROPE
LAT_WIDE = 1152

EPS_NORM = 1e-05
RESIDUAL_SCALE = 1.4 / 62**0.5
ROPE_BASE = 10000.0
MASK_VALUE = -1e30
BETA_ONE = 0.9
BETA_TWO = 0.95
ADAM_EPS = 1e-08
LEARN_RATE = 0.1
WEIGHT_DECAY = 0.1
CLIP_RMS = 0.0002
LOG2E = 1.4426950408889634
LN2 = 0.6931471805599453

BF = jnp.bfloat16
F32 = jnp.float32
MESH = pl.DeviceIdType.MESH
MIB = 1024 * 1024


def dot_nn(a, b):
    return lax.dot_general(a, b, (((1,), (0,)), ((), ())), preferred_element_type=F32)


def dot_nt(a, b):
    return lax.dot_general(a, b, (((1,), (1,)), ((), ())), preferred_element_type=F32)


def dot_tn(a, b):
    return lax.dot_general(a, b, (((0,), (0,)), ((), ())), preferred_element_type=F32)


def torus_gather(piece, whole, sems, place, core):
    x1s, x1r, y1s, y1r, c1s, c1r, x2s, x2r, y2s, y2r, cxs, cxr, cys, cyr, cds, cdr, own = sems
    y, x = place // 2, place % 2
    half = piece.shape[1] // 2
    upper, lower = pl.ds(0, half), pl.ds(half, half)
    to_core, to_x, to_y = {"ctx": 1 - core}, {"fsdp": y * 2 + 1 - x}, {"fsdp": (1 - y) * 2 + x}

    def owner(yy, xx, cc):
        return (yy * 2 + xx) * 2 + cc

    me, px, py = owner(y, x, core), owner(y, 1 - x, core), owner(1 - y, x, core)
    pd = owner(1 - y, 1 - x, core)

    def remote(src, dst, send, recv, i, to):
        return pltpu.make_async_remote_copy(
            src_ref=src, dst_ref=dst, send_sem=send.at[i], recv_sem=recv.at[i], device_id=to, device_id_type=MESH
        )

    first = lambda i, p, send, recv, to: remote(piece.at[i], whole.at[p, i], send, recv, i, to)
    part = lambda i, p, rows, send, recv, to: remote(whole.at[p, i, rows], whole.at[p, i, rows], send, recv, i, to)
    full = lambda i, p, send, recv: remote(whole.at[p, i], whole.at[p, i], send, recv, i, to_core)
    keep = lambda i: pltpu.make_async_copy(piece.at[i], whole.at[me, i], own.at[i])

    def begin(i):
        first(i, me, x1s, x1r, to_x).start()
        first(i, me, y1s, y1r, to_y).start()
        first(i, me, c1s, c1r, to_core).start()
        keep(i).start()

    def forward(i):
        first(i, px, x1s, x1r, to_x).wait_recv()
        part(i, px, upper, y2s, y2r, to_y).start()
        full(i, px, cxs, cxr).start()
        first(i, py, y1s, y1r, to_y).wait_recv()
        part(i, py, lower, x2s, x2r, to_x).start()
        full(i, py, cys, cyr).start()

    def final(i):
        part(i, pd, upper, y2s, y2r, to_y).wait_recv()
        part(i, pd, lower, x2s, x2r, to_x).wait_recv()
        full(i, pd, cds, cdr).start()

    def drain(i):
        first(i, owner(y, x, 1 - core), c1s, c1r, to_core).wait_recv()
        full(i, owner(y, 1 - x, 1 - core), cxs, cxr).wait_recv()
        full(i, owner(1 - y, x, 1 - core), cys, cyr).wait_recv()
        full(i, owner(1 - y, 1 - x, 1 - core), cds, cdr).wait_recv()
        first(i, me, x1s, x1r, to_x).wait_send()
        first(i, me, y1s, y1r, to_y).wait_send()
        first(i, me, c1s, c1r, to_core).wait_send()
        part(i, px, upper, y2s, y2r, to_y).wait_send()
        part(i, py, lower, x2s, x2r, to_x).wait_send()
        full(i, px, cxs, cxr).wait_send()
        full(i, py, cys, cyr).wait_send()
        full(i, pd, cds, cdr).wait_send()
        keep(i).wait()

    return begin, forward, final, drain


GATHER_SEMS = 17


BQ = 512


def attend_forward_kernel(fused, *refs):
    lat_ref, cos_ref, sin_ref, segq_ref, up_ref, *refs = refs
    if fused:
        down_any, out_any, *refs = refs
    o_ref, lse_ref, q_ref, k_ref, v_ref, *refs = refs
    if fused:
        att_any, down_all, out_all, *refs = refs
    stack_q, stack_kv, wq_t, *refs = refs
    h, i = pl.program_id(0), pl.program_id(1)
    rows = lat_ref.shape[0]
    heads, blocks = pl.num_programs(0), rows // BQ
    if fused:
        place, core = lax.axis_index("fsdp"), lax.axis_index("ctx")
        stage, att_send, att_recv, *sems = refs
        at = h * blocks + i
        gathers = (
            torus_gather(out_any, out_all, sems[:GATHER_SEMS], place, core),
            torus_gather(down_any, down_all, sems[GATHER_SEMS:], place, core),
        )

        @pl.when(at == 0)
        def _():
            y, x = place // 2, place % 2
            barrier = pltpu.get_barrier_semaphore()
            for to in ({"ctx": 1 - core}, {"fsdp": y * 2 + 1 - x}, {"fsdp": (1 - y) * 2 + x}):
                pl.semaphore_signal(barrier, inc=1, device_id=to, device_id_type=MESH)
            pl.semaphore_wait(barrier, 3)
            for begin, _, _, _ in gathers:
                begin(0)

        for n in range(2):

            @pl.when(at == 8 + 3 * n)
            def _():
                gathers[n][1](0)

            @pl.when(at == 15 + 3 * n)
            def _():
                gathers[n][2](0)
    pieces = up_ref.shape[0]
    nq, nk = QR // pieces, KVR // pieces

    @pl.when(i == 0)
    def _():
        for p in range(pieces):
            stack_q[p * nq : (p + 1) * nq, :] = up_ref[p, 0:nq, :].astype(F32)
            stack_kv[p * nk : (p + 1) * nk, :] = up_ref[p, nq : nq + nk, :].astype(F32)
        wq_t[...] = stack_q[...].T.astype(BF)
        kv = stack_kv[...]
        wk = jnp.where(lax.broadcasted_iota(jnp.int32, kv.shape, 1) < NOPE, kv, 0.0).astype(BF)
        wv_t = kv.T[NOPE:128].astype(BF)
        for r in range(rows // BQ):
            part = pl.ds(r * BQ, BQ)
            kn = lat_ref[part, QR : QR + KVR]
            qf = dot_nt(wq_t[...], lat_ref[part, 0:QR]) * (LOG2E * HEAD**-0.5)
            cos = cos_ref[:, part]
            sin = sin_ref[:, part]
            one, two = qf[NOPE : NOPE + 16], qf[NOPE + 16 : HEAD]
            q_ref[0, 0:NOPE, part] = qf[:NOPE].astype(BF)
            q_ref[0, NOPE : NOPE + 16, part] = (one * cos - two * sin).astype(BF)
            q_ref[0, NOPE + 16 : HEAD, part] = (two * cos + one * sin).astype(BF)
            q_ref[0, HEAD : HEAD + 16, part] = segq_ref[:, part]
            q_ref[0, HEAD + 16 : 128, part] = jnp.zeros((16, BQ), BF)
            k_ref[0, part, :] = (dot_nn(kn, wk) + lat_ref[part, QR + KVR : LAT_WIDE].astype(F32)).astype(BF)
            v_ref[0, 0:VD, part] = dot_nt(wv_t, kn).astype(BF)
            ones = lax.broadcasted_iota(jnp.int32, (16, BQ), 0) == 0
            v_ref[0, VD : VD + 16, part] = ones.astype(F32).astype(BF)

    here = pl.ds(pl.multiple_of(i * BQ, BQ), BQ)
    q = q_ref[0, :, here]

    def block(j, carried, masked):
        m, acc = carried
        there = pl.ds(pl.multiple_of(j * BQ, BQ), BQ)
        s = dot_nn(k_ref[0, there, :], q)
        if masked:
            krow = lax.broadcasted_iota(jnp.int32, s.shape, 0)
            qcol = lax.broadcasted_iota(jnp.int32, s.shape, 1)
            s = jnp.where(krow <= qcol, s, MASK_VALUE)
        top = jnp.maximum(m, jnp.max(s, axis=0, keepdims=True))
        p = jnp.exp2(s - top).astype(BF)
        acc = acc * jnp.exp2(m - top) + dot_nn(v_ref[0, :, there], p)
        return top, acc

    start = (jnp.full((1, BQ), -3e38, F32), jnp.zeros((80, BQ), F32))
    carried = lax.fori_loop(0, i, lambda j, c: block(j, c, False), start)
    m, acc = block(i, carried, True)
    total = acc[VD : VD + 1]
    o = (acc[:VD] / total).astype(BF)
    o_ref[0, :, here] = o
    lse_ref[0, :, here] = m + jnp.log2(total)
    if fused:
        count = blocks // 2

        def spot(owner, hh, b):
            return (
                pl.ds(pl.multiple_of((owner * heads + hh) * VD, VD), VD),
                pl.ds(pl.multiple_of(lax.rem(b, count) * BQ, BQ), BQ),
            )

        stage[h, i] = o
        keep = lambda hh, b: pltpu.make_async_copy(stage.at[hh, b], att_any.at[spot(core, hh, b)], att_send.at[hh, b])
        give = lambda hh, b, owner: pltpu.make_async_remote_copy(
            src_ref=stage.at[hh, b], dst_ref=att_any.at[spot(owner, hh, b)], send_sem=att_send.at[hh, b],
            recv_sem=att_recv.at[hh, lax.rem(b, count)], device_id={"ctx": 1 - core}, device_id_type=MESH,
        )

        @pl.when(i // count == core)
        def _():
            keep(h, i).start()

        @pl.when(i // count != core)
        def _():
            give(h, i, core).start()

        @pl.when(at == heads * blocks - 1)
        def _():
            def done(n):
                hh, b = n // count, lax.rem(n, count)
                keep(hh, core * count + b).wait()
                give(hh, (1 - core) * count + b, core).wait_send()
                give(hh, core * count + b, 1 - core).wait_recv()

            each(heads * count, done)
            for _, _, _, drain in gathers:
                drain(0)


def attend_forward(lat, cos, sin, segq, up, *pieces):
    heads = up.shape[2] // 128
    rows = lat.shape[0]
    fused = len(pieces) > 0
    anywhere = pl.BlockSpec(memory_space=pl.ANY)
    dma = pltpu.SemaphoreType.DMA
    more_out, more_scratch, params = [], [], {}
    if fused:
        more_out = [jax.ShapeDtypeStruct((2 * heads * VD, rows // 2), BF)]
        more_out += [jax.ShapeDtypeStruct((up.shape[0],) + p.shape, BF) for p in pieces]
        more_scratch = [pltpu.VMEM((heads, rows // BQ, VD, BQ), BF), dma((heads, rows // BQ)), dma((heads, rows // BQ // 2))]
        more_scratch += [dma((1,))] * (2 * GATHER_SEMS)
        params = {"collective_id": 6, "has_side_effects": True}
    whole = lambda a: pl.BlockSpec(a.shape, lambda h, i: (0,) * a.ndim)
    per_head = lambda a, b: pl.BlockSpec((1, a, b), lambda h, i: (h, 0, 0))
    return pl.pallas_call(
        functools.partial(attend_forward_kernel, fused),
        grid=(heads, rows // BQ),
        in_specs=[whole(lat), whole(cos), whole(sin), whole(segq)]
        + [pl.BlockSpec((up.shape[0], up.shape[1], 128), lambda h, i: (0, 0, h))]
        + [anywhere] * len(pieces),
        out_specs=[per_head(VD, rows), per_head(1, rows), per_head(128, rows), per_head(rows, 128), per_head(80, rows)]
        + [anywhere] * len(more_out),
        out_shape=[
            jax.ShapeDtypeStruct((heads, VD, rows), BF),
            jax.ShapeDtypeStruct((heads, 1, rows), F32),
            jax.ShapeDtypeStruct((heads, 128, rows), BF),
            jax.ShapeDtypeStruct((heads, rows, 128), BF),
            jax.ShapeDtypeStruct((heads, 80, rows), BF),
        ]
        + more_out,
        scratch_shapes=[pltpu.VMEM((QR, 128), F32), pltpu.VMEM((KVR, 128), F32), pltpu.VMEM((128, QR), BF)] + more_scratch,
        compiler_params=pltpu.CompilerParams(vmem_limit_bytes=40 * MIB, **params),
        cost_estimate=pl.CostEstimate(flops=heads * rows * rows * 320, bytes_accessed=30 * MIB, transcendentals=0),
        name="attend_forward",
    )(lat, cos, sin, segq, up, *pieces)


def attend_backward_kernel(q_ref, k_ref, v_ref, o_ref, do_ref, lse_ref, cos_ref, sin_ref, dq_ref, de_ref, dkr_ref, dq_acc, delta):
    h, j = pl.program_id(0), pl.program_id(1)
    rows = k_ref.shape[1]
    blocks = rows // BQ

    @pl.when(j == 0)
    def _():
        dq_acc[...] = jnp.zeros_like(dq_acc)
        delta[...] = jnp.sum(o_ref[0].astype(F32) * do_ref[0].astype(F32), axis=0, keepdims=True)

    there = pl.ds(pl.multiple_of(j * BQ, BQ), BQ)
    k = k_ref[0, there, :]
    kt = k.astype(F32).T.astype(BF)
    v = v_ref[0, 0:VD, there].astype(F32).T.astype(BF)

    def block(i, carried, masked):
        dk, dv = carried
        here = pl.ds(pl.multiple_of(i * BQ, BQ), BQ)
        q = q_ref[0, :, here]
        do = do_ref[0, :, here]
        s = dot_nn(k, q)
        if masked:
            krow = lax.broadcasted_iota(jnp.int32, s.shape, 0)
            qcol = lax.broadcasted_iota(jnp.int32, s.shape, 1)
            s = jnp.where(krow <= qcol, s, MASK_VALUE)
        p = jnp.exp2(s - lse_ref[0, :, here])
        dp = dot_nn(v, do)
        ds = (p * (dp - delta[:, here])).astype(BF)
        dv = dv + dot_nt(p.astype(BF), do)
        dk = dk + dot_nt(ds, q)
        dq_acc[:, here] = dq_acc[:, here] + dot_nn(kt, ds)
        return dk, dv

    start = (jnp.zeros((BQ, 128), F32), jnp.zeros((BQ, VD), F32))
    carried = block(j, start, True)
    dk, dv = lax.fori_loop(j + 1, blocks, lambda i, c: block(i, c, False), carried)
    dk = dk * LN2
    de_ref[there, 0:NOPE] = dk[:, :NOPE].astype(BF)
    de_ref[there, NOPE:128] = dv.astype(BF)

    @pl.when(h == 0)
    def _():
        dkr_ref[there, :] = dk

    @pl.when(h > 0)
    def _():
        dkr_ref[there, :] = dkr_ref[there, :] + dk

    @pl.when(j == blocks - 1)
    def _():
        for r in range(blocks):
            part = pl.ds(r * BQ, BQ)
            dq = dq_acc[:, part] * HEAD**-0.5
            cos, sin = cos_ref[:, part], sin_ref[:, part]
            one, two = dq[NOPE : NOPE + 16], dq[NOPE + 16 : HEAD]
            dq = jnp.concatenate(
                [dq[:NOPE], one * cos + two * sin, two * cos - one * sin, jnp.zeros((128 - HEAD, BQ), F32)], axis=0
            )
            dq_ref[part, :] = dq.T.astype(BF)


def attend_backward(q, k, v, o, do, lse, cos, sin):
    heads = q.shape[0]
    rows = k.shape[1]
    whole = lambda a: pl.BlockSpec(a.shape, lambda h, i: (0,) * a.ndim)
    per_head = lambda a: pl.BlockSpec((1,) + a.shape[1:], lambda h, i: (h, 0, 0))
    return pl.pallas_call(
        attend_backward_kernel,
        grid=(heads, rows // BQ),
        in_specs=[per_head(a) for a in (q, k, v, o, do, lse)] + [whole(cos), whole(sin)],
        out_specs=[
            pl.BlockSpec((rows, 128), lambda h, i: (0, h)),
            pl.BlockSpec((rows, 128), lambda h, i: (0, h)),
            pl.BlockSpec((rows, 128), lambda h, i: (0, 0)),
        ],
        out_shape=[
            jax.ShapeDtypeStruct((rows, heads * 128), BF),
            jax.ShapeDtypeStruct((rows, heads * 128), BF),
            jax.ShapeDtypeStruct((rows, 128), F32),
        ],
        scratch_shapes=[pltpu.VMEM((128, rows), F32), pltpu.VMEM((1, rows), F32)],
        compiler_params=pltpu.CompilerParams(vmem_limit_bytes=40 * MIB),
        cost_estimate=pl.CostEstimate(flops=heads * rows * rows * 900, bytes_accessed=30 * MIB, transcendentals=0),
        name="attend_backward",
    )(q, k, v, o, do, lse, cos, sin)


LAT_LINE = 64
PIECE = 160


def latent_kernel(
    x_ref, gain_ref, gain2_ref, piece_ref, up_ref, sel_ref, freq_col, freq_lane, len_ref, gu_any,
    w_ref, total, lat_ref, cos_ref, sin_ref, segq_ref, upg_ref, tcos, tsin, gains, gu_all,
    gat, xb, near, cross, kvg,
    w_send, w_recv, u_send, u_recv, c_send, c_recv, *sems,
):
    gather_sems, sems = sems[6:], sems[:6]
    z, core, place = lax.axis_index("tp"), lax.axis_index("ctx"), lax.axis_index("fsdp")
    is_end, is_mid, partner, across = line_places(z)
    to_mid, over, to_end, first, second = line_copies(xb, near, cross, total, sems, partner, across, LAT_LINE)
    count = xb.shape[0] // LAT_LINE
    rows = x_ref.shape[0]
    peers = gat.shape[0]
    me = place * 2 + core

    def remote(src, dst, send, recv, to):
        return pltpu.make_async_remote_copy(
            src_ref=src, dst_ref=dst, send_sem=send, recv_sem=recv, device_id=to, device_id_type=MESH
        )

    def peer(d):
        to = lax.rem(me + d, peers)
        return {"fsdp": to // 2, "ctx": lax.rem(to, 2)}

    barrier = pltpu.get_barrier_semaphore()
    for d in range(1, peers):
        pl.semaphore_signal(barrier, inc=1, device_id=peer(d), device_id_type=MESH)
    pl.semaphore_signal(barrier, inc=1, device_id={"tp": partner}, device_id_type=MESH)

    @pl.when(is_mid)
    def _():
        pl.semaphore_signal(barrier, inc=1, device_id={"tp": across}, device_id_type=MESH)
        pl.semaphore_wait(barrier, peers + 1)

    @pl.when(is_end)
    def _():
        pl.semaphore_wait(barrier, peers)

    def w_copy(d, source):
        return remote(piece_ref, gat.at[source], w_send.at[d], w_recv.at[source], peer(d))

    def u_copy(d, source):
        return remote(up_ref.at[lax.rem(me + d, 2)], upg_ref.at[source], u_send.at[d], u_recv.at[source], peer(d))

    begin, forward, final, drain = torus_gather(gu_any, gu_all, gather_sems, place, core)
    for d in range(1, peers):
        w_copy(d, me).start()
    begin(0)
    for d in range(1, peers):
        u_copy(d, me).start()
    begin(1)
    gat[me] = piece_ref[...]
    upg_ref[me] = up_ref[core]

    length = len_ref[0, 0]
    slot = cos_ref.shape[1]
    index = lax.broadcasted_iota(jnp.int32, (1, slot), 1)
    segment = (index >= length).astype(jnp.int32)
    angle = freq_col[...] * (index - segment * length).astype(F32)
    cos_ref[...] = jnp.cos(angle)
    sin_ref[...] = jnp.sin(angle)
    row16 = lax.broadcasted_iota(jnp.int32, (16, slot), 0)
    seg_f = segment.astype(F32)
    segq_ref[...] = jnp.where(row16 == 0, seg_f, jnp.where(row16 == 1, 1.0 - seg_f, 0.0)).astype(BF)
    lane = lax.broadcasted_iota(jnp.int32, (1, 128), 1)
    in_rope = jnp.logical_and(lane >= NOPE, lane < HEAD)

    def own_index(e):
        at = core * rows + e * LAT_LINE
        return at + lax.broadcasted_iota(jnp.int32, (LAT_LINE, 1), 0)

    def table(e):
        here = pl.ds(pl.multiple_of(e * LAT_LINE, LAT_LINE), LAT_LINE)
        at = own_index(e)
        seg = (at >= length).astype(jnp.int32)
        turn = (at - seg * length).astype(F32) * freq_lane[...]
        tcos[here, :] = jnp.where(in_rope, jnp.cos(turn), 0.0)
        tsin[here, :] = jnp.where(in_rope, jnp.sin(turn), 0.0)

    each(rows // LAT_LINE, table)

    for d in range(1, peers):
        w_copy(d, lax.rem(me + peers - d, peers)).wait_recv()
    for p in range(peers):
        w_ref[p * 96 : (p + 1) * 96, :] = gat[p, 0:96, :]
        kvg[p * 48 : (p + 1) * 48, :] = gat[p, 96:144, :]
        gains[:, p * 128 : (p + 1) * 128] = gat[p, 144:160, 0:128].astype(F32)
    w_ref[QR:LAT, :] = dot_nn(sel_ref[...], kvg[...]).astype(BF)
    w_ref[LAT:LAT_WIDE, :] = jnp.zeros((LAT_WIDE - LAT, w_ref.shape[1]), BF)

    wide_lane = lax.broadcasted_iota(jnp.int32, (1, LAT_WIDE), 1)
    per = 128

    def project(r):
        here = pl.ds(pl.multiple_of(r * per, per), per)
        x = x_ref[here, :].astype(F32)
        square = jnp.sum(x * x, axis=1, keepdims=True)
        high = square.astype(BF).astype(F32)
        part = dot_nt((x * gain_ref[...]).astype(BF), w_ref[...])
        part = jnp.where(wide_lane == LAT + 2 * z, high, jnp.where(wide_lane == LAT + 2 * z + 1, square - high, part))
        xb[here, :] = part.astype(BF)

        @pl.when(is_end)
        def _():
            for n in range(per // LAT_LINE):
                to_mid(r * (per // LAT_LINE) + n).start()

    each(rows // per, project)
    gain_row = lax.broadcasted_iota(jnp.int32, (LAT_LINE, LAT_WIDE), 0) == z
    xb[rows : rows + LAT_LINE, :] = jnp.where(gain_row, gain2_ref[...], 0.0).astype(BF)

    @pl.when(is_end)
    def _():
        to_mid(count - 1).start()

    def handover(e):
        here = pl.ds(pl.multiple_of(core * rows + e * LAT_LINE, LAT_LINE), LAT_LINE)
        return remote(lat_ref.at[here], lat_ref.at[here], c_send.at[e], c_recv.at[e], {"ctx": 1 - core})

    stat_lane = jnp.logical_and(wide_lane >= LAT, wide_lane < LAT + 8)

    def finish_rows(e):
        @pl.when(e < rows // LAT_LINE)
        def _():
            here = pl.ds(pl.multiple_of(e * LAT_LINE, LAT_LINE), LAT_LINE)
            there = pl.ds(pl.multiple_of(core * rows + e * LAT_LINE, LAT_LINE), LAT_LINE)
            v = total[here, :].astype(F32)
            square = jnp.sum(jnp.where(stat_lane, v, 0.0), axis=1, keepdims=True)
            v = v * lax.rsqrt(square / D + EPS_NORM)
            ql, kl, raw = v[:, :QR], v[:, QR : QR + KVR], v[:, QR + KVR :]
            ql = ql * lax.rsqrt(jnp.mean(ql * ql, axis=1, keepdims=True) + EPS_NORM)
            kl = kl * lax.rsqrt(jnp.mean(kl * kl, axis=1, keepdims=True) + EPS_NORM)
            lat_ref[there, 0:QR] = (ql * gains[0:1, 0:QR]).astype(BF)
            lat_ref[there, QR : QR + KVR] = (kl * gains[0:1, QR : QR + KVR]).astype(BF)
            moved = pltpu.roll(jnp.where(lane < ROPE, raw, 0.0), NOPE, 1)
            turned = jnp.where(lane < NOPE + 16, -pltpu.roll(moved, 128 - 16, 1), pltpu.roll(moved, 16, 1))
            seg = (own_index(e) >= length).astype(F32)
            mask = jnp.where(lane == HEAD, 1.0 - seg, jnp.where(lane == HEAD + 1, seg, 0.0)) * MASK_VALUE
            lat_ref[there, QR + KVR : LAT_WIDE] = (moved * tcos[here, :] + turned * tsin[here, :] + mask).astype(BF)
            handover(e).start()

    def serve(n):
        @pl.when(jnp.logical_and(is_mid, n < count))
        def _():
            first(n)

        @pl.when(jnp.logical_and(is_mid, jnp.logical_and(n >= DEPTH, n < count + DEPTH)))
        def _():
            second(n - DEPTH)
            finish_rows(n - DEPTH)

        @pl.when(jnp.logical_and(is_end, n < count))
        def _():
            to_mid(n).wait_send()
            to_end(n).wait_recv()
            finish_rows(n)

    each(7, serve)
    forward(0)
    each(4, lambda n: serve(n + 7))
    forward(1)
    each(count + DEPTH - 11, lambda n: serve(n + 11))
    final(0)
    final(1)

    @pl.when(is_mid)
    def _():
        def sent(k):
            over(k).wait_send()
            to_end(k).wait_send()

        each(count, sent)

    drain(0)
    drain(1)
    for d in range(1, peers):
        w_copy(d, me).wait_send()
        u_copy(d, me).wait_send()
        u_copy(d, lax.rem(me + peers - d, peers)).wait_recv()

    def passed(e):
        handover(e).wait_send()
        here = pl.ds(pl.multiple_of((1 - core) * rows + e * LAT_LINE, LAT_LINE), LAT_LINE)
        remote(lat_ref.at[here], lat_ref.at[here], c_send.at[e], c_recv.at[e], {"ctx": 1 - core}).wait_recv()

    each(rows // LAT_LINE, passed)


def spread(peers):
    index = jnp.arange(KVR + ROPE)
    return jnp.equal((index // 36 * 48 + index % 36)[:, None], jnp.arange(peers * 48)[None]).astype(BF)


def latent_forward(x, gain, gain2, piece, up, length, gate_up):
    rows, width = x.shape
    peers = lax.axis_size("fsdp") * lax.axis_size("ctx")
    slot = rows * lax.axis_size("ctx")
    wide = rows + LAT_LINE
    count = wide // LAT_LINE
    sel = spread(peers)
    frequency = ROPE_BASE ** (-2.0 * jnp.arange(ROPE // 2, dtype=F32) / ROPE)
    vmem = pl.BlockSpec(memory_space=pltpu.VMEM)
    dma = pltpu.SemaphoreType.DMA
    return pl.pallas_call(
        latent_kernel,
        out_shape=[
            jax.ShapeDtypeStruct((LAT_WIDE, width), BF),
            jax.ShapeDtypeStruct((wide, LAT_WIDE), BF),
            jax.ShapeDtypeStruct((slot, LAT_WIDE), BF),
            jax.ShapeDtypeStruct((ROPE // 2, slot), F32),
            jax.ShapeDtypeStruct((ROPE // 2, slot), F32),
            jax.ShapeDtypeStruct((16, slot), BF),
            jax.ShapeDtypeStruct((peers,) + up.shape[1:], BF),
            jax.ShapeDtypeStruct((rows, 128), F32),
            jax.ShapeDtypeStruct((rows, 128), F32),
            jax.ShapeDtypeStruct((16, QR + KVR), F32),
            jax.ShapeDtypeStruct((peers,) + gate_up.shape, BF),
        ],
        in_specs=[vmem] * 8 + [pl.BlockSpec(memory_space=pltpu.SMEM), pl.BlockSpec(memory_space=pl.ANY)],
        out_specs=[vmem] * 10 + [pl.BlockSpec(memory_space=pl.ANY)],
        scratch_shapes=[
            pltpu.VMEM((peers, PIECE, width), BF),
            pltpu.VMEM((wide, LAT_WIDE), BF),
            pltpu.VMEM((wide, LAT_WIDE), BF),
            pltpu.VMEM((wide, LAT_WIDE), BF),
            pltpu.VMEM((peers * 48, width), BF),
        ]
        + [dma((peers,))] * 4
        + [dma((rows // LAT_LINE,))] * 2
        + [dma((count,))] * 6
        + [dma((2,))] * GATHER_SEMS,
        compiler_params=pltpu.CompilerParams(collective_id=0, has_side_effects=True, vmem_limit_bytes=48 * MIB),
        cost_estimate=pl.CostEstimate(flops=rows * LAT_WIDE * width * 2, bytes_accessed=150 * MIB, transcendentals=0),
        name="latent_forward",
    )(x, gain, gain2, piece, up, sel, frequency[:, None], jnp.tile(frequency, 8)[None], length, gate_up)


LINE = 16
DEPTH = 4
MLP_ROWS = 256
TILES = ((0, 384), (384, 384), (768, 384), (1152, 448))


def line_places(z):
    is_end = jnp.logical_or(z == 0, z == 3)
    partner = jnp.where(z == 0, 1, jnp.where(z == 3, 2, jnp.where(z == 1, 0, 3)))
    return is_end, jnp.logical_not(is_end), partner, jnp.where(z == 1, 2, 1)


def line_barrier(is_mid, is_end, partner, across):
    barrier = pltpu.get_barrier_semaphore()
    pl.semaphore_signal(barrier, inc=1, device_id={"tp": partner}, device_id_type=MESH)

    @pl.when(is_mid)
    def _():
        pl.semaphore_signal(barrier, inc=1, device_id={"tp": across}, device_id_type=MESH)
        pl.semaphore_wait(barrier, 2)

    @pl.when(is_end)
    def _():
        pl.semaphore_wait(barrier, 1)


def line_copies(source, near, cross, total, sems, partner, across, line=LINE):
    in_send, in_recv, mid_send, mid_recv, out_send, out_recv = sems

    def piece(k):
        return pl.ds(pl.multiple_of(k * line, line), line)

    def copy(src, dst, send, recv, k, to):
        return pltpu.make_async_remote_copy(
            src_ref=src.at[piece(k)], dst_ref=dst.at[piece(k)], send_sem=send.at[k], recv_sem=recv.at[k],
            device_id={"tp": to}, device_id_type=MESH,
        )

    to_mid = lambda k: copy(source, near, in_send, in_recv, k, partner)
    over = lambda k: copy(near, cross, mid_send, mid_recv, k, across)
    to_end = lambda k: copy(total, total, out_send, out_recv, k, partner)

    def first(k):
        to_mid(k).wait_recv()
        near[piece(k)] = source[piece(k)] + near[piece(k)]
        over(k).start()

    def second(k):
        over(k).wait_recv()
        total[piece(k)] = near[piece(k)] + cross[piece(k)]
        to_end(k).start()

    return to_mid, over, to_end, first, second


def each(count, body):
    def step(k, carry):
        body(k)
        return carry

    lax.fori_loop(0, count, step, 0)


def block_kernel(
    att_ref, x_ref, out_ref, gain_ref, live_ref, seed_any, gu_any, down_any,
    hid_any, dn_any, mo_any, n2t_any, act_any, dg_any, du_any,
    xb, near, cross, total, gu, down, n2, n2t, seed, d_all, act, dg, du,
    load_sem, down_sem, seed_sem, hid_sem, dn_sem, mo_sem, n2t_sem, act_sem, dg_sem, du_sem, *sems,
):
    z = lax.axis_index("tp")
    is_end, is_mid, partner, across = line_places(z)
    to_mid, over, to_end, first, second = line_copies(xb, near, cross, total, sems, partner, across)
    count = xb.shape[0] // LINE
    group = MLP_ROWS // LINE
    groups = count // group
    width = x_ref.shape[1]

    def rows_of(m):
        return pl.ds(pl.multiple_of(m * MLP_ROWS, MLP_ROWS), MLP_ROWS)

    peers, shard = gu_any.shape[0], gu_any.shape[2]
    load_gu = lambda p, i: pltpu.make_async_copy(gu_any.at[p, i], gu.at[i, pl.ds(p * shard, shard)], load_sem.at[p, i])
    load_down = pltpu.make_async_copy(down_any, down, down_sem)
    load_seed = lambda m: pltpu.make_async_copy(seed_any.at[rows_of(m)], seed, seed_sem.at[m])
    save_hid = lambda m: pltpu.make_async_copy(total.at[rows_of(m)], hid_any.at[rows_of(m)], hid_sem.at[m])
    save_dn = lambda m: pltpu.make_async_copy(xb.at[rows_of(m)], dn_any.at[rows_of(m)], dn_sem.at[m])
    save_mo = lambda m, n: pltpu.make_async_copy(
        cross.at[rows_of(m), pl.ds(n * width, width)], mo_any.at[n, rows_of(m)], mo_sem.at[m, n]
    )
    save_n2t = lambda m: pltpu.make_async_copy(n2t, n2t_any.at[:, rows_of(m)], n2t_sem.at[m])
    save_act = lambda m: pltpu.make_async_copy(act, act_any.at[rows_of(m)], act_sem.at[m])
    save_dg = lambda m: pltpu.make_async_copy(dg, dg_any.at[rows_of(m)], dg_sem.at[m])
    save_du = lambda m: pltpu.make_async_copy(du, du_any.at[rows_of(m)], du_sem.at[m])

    load_seed(0).start()
    load_down.start()
    for p in range(peers):
        load_gu(p, 0).start()
        load_gu(p, 1).start()
    line_barrier(is_mid, is_end, partner, across)

    mine = pl.ds(pl.multiple_of(z * width, 128), width)
    per = 128

    def project(p):
        rows = pl.ds(pl.multiple_of(p * per, per), per)
        part = dot_nt(att_ref[:, rows].astype(F32).T.astype(BF), out_ref[...]) * RESIDUAL_SCALE
        xb[rows, :] = part.astype(BF)
        xb[rows, mine] = (xb[rows, mine].astype(F32) + x_ref[rows, :].astype(F32)).astype(BF)

        @pl.when(is_end)
        def _():
            each(per // LINE, lambda n: to_mid(p * (per // LINE) + n).start())

    each(xb.shape[0] // per, project)

    @pl.when(is_mid)
    def _():
        each(DEPTH, first)

    load_down.wait()
    ahead = group // len(TILES) // groups

    def seed_product(m):
        load_seed(m).wait()

        def weigh(r):
            here = pl.ds(pl.multiple_of(r * 32, 32), 32)
            live = live_ref[pl.ds(pl.multiple_of(m * MLP_ROWS + r * 32, 32), 32), :]
            seed[here, :] = (seed[here, :].astype(F32) * (live * RESIDUAL_SCALE)).astype(BF)

        each(MLP_ROWS // 32, weigh)
        for t, (at, size) in enumerate(TILES):
            d_all[rows_of(m), pl.ds(at, size)] = dot_nn(seed[...], down[:, pl.ds(at, size)]).astype(BF)

            @pl.when(is_mid)
            def _():
                def both(v):
                    k = (m * len(TILES) + t) * ahead + v
                    first(k + DEPTH)
                    second(k)

                each(ahead, both)

        @pl.when(m + 1 < groups)
        def _():
            load_seed(m + 1).start()

    each(groups, seed_product)

    def mlp(m):
        rows = rows_of(m)

        @pl.when(is_end)
        def _():
            def arrive(n):
                to_mid(m * group + n).wait_send()
                to_end(m * group + n).wait_recv()

            each(group, arrive)

        def serve(n):
            def one(v):
                k = (m + 1) * group + DEPTH + n * (group // 8) + v

                @pl.when(jnp.logical_and(is_mid, k < count))
                def _():
                    first(k)

                @pl.when(jnp.logical_and(is_mid, k < count + DEPTH))
                def _():
                    second(k - DEPTH)

            each(group // 8, one)

        save_hid(m).start()

        @pl.when(m > 0)
        def _():
            save_n2t(m - 1).wait()
            save_act(m - 1).wait()
            save_dg(m - 1).wait()
            save_du(m - 1).wait()

        def normalize(r):
            here = pl.ds(pl.multiple_of(r * 32, 32), 32)
            h = total[pl.ds(pl.multiple_of(m * MLP_ROWS + r * 32, 32), 32), :].astype(F32)
            factor = lax.rsqrt(jnp.mean(h * h, axis=1, keepdims=True) + EPS_NORM)
            n2[here, :] = (h * factor * gain_ref[...]).astype(BF)

        each(MLP_ROWS // 32, normalize)

        def turn(c):
            cols = pl.ds(pl.multiple_of(c * 256, 256), 256)
            n2t[cols, :] = n2[:, cols].astype(F32).T.astype(BF)

        each(D // 256, turn)
        save_n2t(m).start()
        @pl.when(m == 0)
        def _():
            for p in range(peers):
                load_gu(p, 0).wait()
                load_gu(p, 1).wait()

        for t, (at, size) in enumerate(TILES):
            cols = pl.ds(at, size)
            g = dot_nn(n2[...], gu[0, :, cols])
            u = dot_nn(n2[...], gu[1, :, cols])
            d = d_all[rows, cols].astype(F32)
            sig = jax.nn.sigmoid(g)
            act[:, cols] = (g * sig * u).astype(BF)
            dg[:, cols] = (d * u * sig * (1.0 + g * (1.0 - sig))).astype(BF)
            du[:, cols] = (d * g * sig).astype(BF)
            serve(t)
        save_act(m).start()
        save_dg(m).start()
        save_du(m).start()

        for n in range(4):
            cols = pl.ds(n * 640, 640)
            xb[rows, cols] = (dot_nt(dg[...], gu[0, cols, :]) + dot_nt(du[...], gu[1, cols, :])).astype(BF)
            cross[rows, cols] = dot_nt(act[...], down[cols, :]).astype(BF)
            serve(4 + n)
        save_dn(m).start()
        for n in range(4):
            save_mo(m, n).start()

    each(groups, mlp)

    def finish(m):
        save_hid(m).wait()
        save_dn(m).wait()
        for n in range(4):
            save_mo(m, n).wait()

    each(groups, finish)
    save_n2t(groups - 1).wait()
    save_act(groups - 1).wait()
    save_dg(groups - 1).wait()
    save_du(groups - 1).wait()

    @pl.when(is_mid)
    def _():
        def sent(k):
            over(k).wait_send()
            to_end(k).wait_send()

        each(count, sent)


def block_forward(att, x, out_t, gain, live, seed, gate_up, down_t):
    rows, width = x.shape
    hidden_units = down_t.shape[1]
    count, groups = rows // LINE, rows // MLP_ROWS
    vmem = pl.BlockSpec(memory_space=pltpu.VMEM)
    anywhere = pl.BlockSpec(memory_space=pl.ANY)
    wide = jax.ShapeDtypeStruct((rows, D), BF)
    units = jax.ShapeDtypeStruct((rows, hidden_units), BF)
    dma = pltpu.SemaphoreType.DMA
    return pl.pallas_call(
        block_kernel,
        out_shape=[wide, wide, jax.ShapeDtypeStruct((4, rows, width), BF), jax.ShapeDtypeStruct((D, rows), BF), units, units, units],
        in_specs=[vmem] * 5 + [anywhere] * 3,
        out_specs=[anywhere] * 7,
        scratch_shapes=[pltpu.VMEM((rows, D), BF)] * 4
        + [
            pltpu.VMEM((2, D, hidden_units), BF),
            pltpu.VMEM(down_t.shape, BF),
            pltpu.VMEM((MLP_ROWS, D), BF),
            pltpu.VMEM((D, MLP_ROWS), BF),
            pltpu.VMEM((MLP_ROWS, D), BF),
            pltpu.VMEM((rows, hidden_units), BF),
        ]
        + [pltpu.VMEM((MLP_ROWS, hidden_units), BF)] * 3
        + [dma(gate_up.shape[:2]), dma]
        + [dma((groups,))] * 3
        + [dma((groups, 4))]
        + [dma((groups,))] * 4
        + [dma((count,))] * 6,
        compiler_params=pltpu.CompilerParams(collective_id=3, has_side_effects=True, vmem_limit_bytes=63 * MIB),
        cost_estimate=pl.CostEstimate(flops=rows * D * hidden_units * 12, bytes_accessed=400 * MIB, transcendentals=0),
        name="block_forward",
    )(att, x, out_t, gain, live, seed, gate_up, down_t)


LAG = 8
ROWS = 32
LOAD = 128


def total_square(v):
    v = v.astype(F32)
    return jnp.sum(jnp.sum(v * v, axis=0, keepdims=True), axis=1, keepdims=True)


def grad_kernel(
    live_ref, gain_ref, dnp_any, hid_any, cot_any, n2t_any, dg_any, du_any, act_any,
    sa_any, dh_any, gain_out, grad_any, square_out,
    near, cross, total, cin, stage, xin, yin2, yin, xin2, lhs, rhs, hbuf, cbuf, sbuf, dbuf, prep,
    total_sem, lhs_sem, rhs_sem, h_sem, c_sem, sa_sem, dh_sem, prep_sem, out_sem,
    core_send, core_recv, x_send, x_recv, y2_send, y2_recv, y_send, y_recv, x2_send, x2_recv, *sems,
):
    z, core, place = lax.axis_index("tp"), lax.axis_index("ctx"), lax.axis_index("fsdp")
    y, x = place // 2, place % 2
    is_end, is_mid, partner, across = line_places(z)
    to_mid, over, to_end, _, _ = line_copies(dnp_any, near, cross, total, sems, partner, across)
    count = total.shape[0] // LINE
    width = dh_any.shape[1]
    half = yin.shape[1]
    block = 2 * half
    mine = pl.ds(pl.multiple_of(z * width, 128), width)
    to_core, to_x, to_y = {"ctx": 1 - core}, {"fsdp": y * 2 + 1 - x}, {"fsdp": (1 - y) * 2 + x}

    def piece(k):
        return pl.ds(pl.multiple_of(k * LINE, LINE), LINE)

    def band(e):
        return pl.ds(pl.multiple_of(e * ROWS, ROWS), ROWS)

    bands = total.shape[0] // ROWS
    twice = ROWS // LINE

    def remote(src, dst, send, recv, to):
        return pltpu.make_async_remote_copy(
            src_ref=src, dst_ref=dst, send_sem=send, recv_sem=recv, device_id=to, device_id_type=MESH
        )

    local = pltpu.make_async_copy
    load_total = local(dnp_any, total, total_sem)
    load_lhs = local(n2t_any, lhs, lhs_sem)
    right = (dg_any, du_any, act_any)
    load_rhs = lambda i: local(right[i], rhs.at[i % 2], rhs_sem.at[i])
    rows_of = lambda g: pl.ds(pl.multiple_of(g * LOAD, LOAD), LOAD)
    load_h = lambda g: local(hid_any.at[rows_of(g)], hbuf.at[g % 2], h_sem.at[g])
    load_c = lambda g: local(cot_any.at[rows_of(g)], cbuf.at[g % 2], c_sem.at[g])
    save_sa = lambda e: local(sbuf.at[e % 2], sa_any.at[band(e)], sa_sem.at[e])
    save_dh = lambda e: local(dbuf.at[e % 2], dh_any.at[band(e)], dh_sem.at[e])

    load_lhs.start()
    load_rhs(0).start()
    load_rhs(1).start()
    load_h(0).start()
    load_c(0).start()

    @pl.when(is_mid)
    def _():
        load_total.start()

    barrier = pltpu.get_barrier_semaphore()
    for to in (to_core, to_x, to_y, {"tp": partner}):
        pl.semaphore_signal(barrier, inc=1, device_id=to, device_id_type=MESH)

    @pl.when(is_mid)
    def _():
        pl.semaphore_signal(barrier, inc=1, device_id={"tp": across}, device_id_type=MESH)
        pl.semaphore_wait(barrier, 5)

    @pl.when(is_end)
    def _():
        pl.semaphore_wait(barrier, 4)
        each(count, lambda k: to_mid(k).start())

    gain_out[...] = jnp.zeros_like(gain_out)

    @pl.when(is_mid)
    def _():
        load_total.wait()

    def finish_rows(e):
        per = LOAD // ROWS
        g = e // per

        @pl.when(e % per == 0)
        def _():
            load_h(g).wait()
            load_c(g).wait()

            @pl.when(g + 1 < bands // per)
            def _():
                load_h(g + 1).start()
                load_c(g + 1).start()

        @pl.when(e >= 2)
        def _():
            save_sa(e - 2).wait()
            save_dh(e - 2).wait()

        here = pl.ds(pl.multiple_of((e % per) * ROWS, ROWS), ROWS)
        live = live_ref[band(e), :]

        def grads_of(dn, h, dy, gain, factor, inner):
            return dy * live + factor * (dn * gain) - h * (factor * factor * factor * inner)

        dn = total[band(e), :].astype(F32)
        h = hbuf[g % 2, here, :].astype(F32)
        factor = lax.rsqrt(jnp.mean(h * h, axis=1, keepdims=True) + EPS_NORM)
        inner = jnp.mean(dn * gain_ref[...] * h, axis=1, keepdims=True)
        dy = cbuf[g % 2, here, :].astype(F32)
        sbuf[e % 2] = (RESIDUAL_SCALE * grads_of(dn, h, dy, gain_ref[...], factor, inner)).astype(BF)
        own_dn = total[band(e), mine].astype(F32)
        own_h = hbuf[g % 2, here, mine].astype(F32)
        own_dy = cbuf[g % 2, here, mine].astype(F32)
        dbuf[e % 2] = grads_of(own_dn, own_h, own_dy, gain_ref[:, mine], factor, inner)
        gain_out[...] += jnp.sum(own_dn * own_h * factor, axis=0, keepdims=True)
        save_sa(e).start()
        save_dh(e).start()

    def serve(n):
        @pl.when(jnp.logical_and(is_mid, n < count))
        def _():
            to_mid(n).wait_recv()
            near[piece(n)] = total[piece(n)] + near[piece(n)]
            over(n).start()

        @pl.when(jnp.logical_and(is_mid, jnp.logical_and(n >= DEPTH, n < count + DEPTH)))
        def _():
            k = n - DEPTH
            over(k).wait_recv()
            total[piece(k)] = near[piece(k)] + cross[piece(k)]
            to_end(k).start()

            @pl.when(k % twice == twice - 1)
            def _():
                finish_rows(k // twice)

        @pl.when(jnp.logical_and(is_end, jnp.logical_and(n >= LAG, n < count + LAG)))
        def _():
            k = n - LAG
            to_mid(k).wait_send()
            to_end(k).wait_recv()

            @pl.when(k % twice == twice - 1)
            def _():
                finish_rows(k // twice)

    def flip(v, by):
        return v + by - 2 * v * by

    def spot(j):
        down, over_x = 1 - j // 2, 1 - j % 2
        return down, over_x, flip(y, down), flip(x, over_x)

    def tile(i, f, parity):
        rows = pl.ds(pl.multiple_of((2 * f + parity) * block, 16), block)
        return dot_nn(lhs[rows, :], rhs[i % 2])

    upper, lower = pl.ds(0, half), pl.ds(half, half)
    core_copy = lambda i, j, f: remote(stage.at[j % 2], cin.at[i, f], core_send.at[i, j], core_recv.at[i, f], to_core)
    x_copy = lambda i, f, yy: remote(cin.at[i, f, upper], xin.at[i, yy], x_send.at[i, yy], x_recv.at[i, yy], to_x)
    y2_copy = lambda i, f, xx: remote(cin.at[i, f, lower], yin2.at[i, xx], y2_send.at[i, xx], y2_recv.at[i, xx], to_y)
    y_copy = lambda i: remote(xin.at[i, 1 - y], yin.at[i], y_send.at[i], y_recv.at[i], to_y)
    x2_copy = lambda i: remote(yin2.at[i, 1 - x], xin2.at[i], x2_send.at[i], x2_recv.at[i], to_x)
    save_upper = lambda i: local(yin.at[i], grad_any.at[i, upper], out_sem.at[i, 0])
    save_lower = lambda i: local(xin2.at[i], grad_any.at[i, lower], out_sem.at[i, 1])

    def plus(a, b):
        return (a.astype(F32) + b.astype(F32)).astype(BF)

    def products(i, n0):
        def for_other(j):
            _, _, yy, xx = spot(j)
            f = yy * 2 + xx

            @pl.when(j >= 2)
            def _():
                core_copy(i, j - 2, f).wait_send()

            stage[j % 2] = tile(i, f, 1 - core).astype(BF)
            core_copy(i, j, f).start()
            serve(n0 + j)

        each(4, for_other)

        def for_own(j):
            down, over_x, yy, xx = spot(j)
            f = yy * 2 + xx
            own = tile(i, f, core)
            core_copy(i, j, f).wait_recv()
            cin[i, f] = (own + cin[i, f].astype(F32)).astype(BF)

            @pl.when(over_x == 1)
            def _():
                x_copy(i, f, yy).start()

            @pl.when(down == 1)
            def _():
                y2_copy(i, f, xx).start()

            serve(n0 + 4 + j)

        each(4, for_own)
        for j in (2, 3):
            core_copy(i, j, 0).wait_send()

    def first_stage(i):
        x_copy(i, 0, 1 - y).wait_recv()
        xin[i, 1 - y] = plus(xin[i, 1 - y], cin[i, (1 - y) * 2 + x, upper])
        y_copy(i).start()
        y2_copy(i, 0, 1 - x).wait_recv()
        yin2[i, 1 - x] = plus(yin2[i, 1 - x], cin[i, y * 2 + 1 - x, lower])
        x2_copy(i).start()
        x_copy(i, 0, y).wait_recv()
        xin[i, y] = plus(xin[i, y], cin[i, y * 2 + x, upper])
        y2_copy(i, 0, x).wait_recv()
        yin2[i, x] = plus(yin2[i, x], cin[i, y * 2 + x, lower])

    def second_stage(i):
        y_copy(i).wait_recv()
        yin[i] = plus(yin[i], xin[i, y])
        save_upper(i).start()
        x2_copy(i).wait_recv()
        xin2[i] = plus(xin2[i], yin2[i, x])
        save_lower(i).start()
        square = total_square(yin[i]) + total_square(xin2[i])
        square_out[i : i + 1, :] = jnp.broadcast_to(square, (1, 128))

    square_out[...] = jnp.zeros_like(square_out)
    load_lhs.wait()
    load_rhs(0).wait()
    products(0, 0)
    load_rhs(2).start()
    load_rhs(1).wait()
    products(1, 8)

    cols_of = lambda c: pl.ds(pl.multiple_of(c * 256, 256), 256)
    load_prep = lambda c: local(cot_any.at[:, cols_of(c)], prep.at[c % 2], prep_sem.at[c])
    load_prep(0).start()
    groups = D // 256

    def turn(c):
        load_prep(c).wait()

        @pl.when(c + 1 < groups)
        def _():
            load_prep(c + 1).start()

        seed = prep[c % 2].astype(F32) * (live_ref[...] * RESIDUAL_SCALE)
        lhs[cols_of(c), :] = seed.T.astype(BF)
        serve(16 + c)

    each(groups, turn)
    first_stage(0)
    load_rhs(2).wait()
    products(2, 16 + groups)
    served = 24 + groups

    def serve_until(stop, served):
        each(stop - served, lambda n: serve(n + served))
        return stop

    first_stage(1)
    served = serve_until(42, served)
    second_stage(0)
    served = serve_until(50, served)
    first_stage(2)
    served = serve_until(58, served)
    second_stage(1)
    serve_until(count + LAG, served)
    second_stage(2)
    for i in range(3):
        for v in range(2):
            x_copy(i, 0, v).wait_send()
            y2_copy(i, 0, v).wait_send()
        y_copy(i).wait_send()
        x2_copy(i).wait_send()
        save_upper(i).wait()
        save_lower(i).wait()
    for e in (bands - 2, bands - 1):
        save_sa(e).wait()
        save_dh(e).wait()

    @pl.when(is_mid)
    def _():
        def sent(k):
            over(k).wait_send()
            to_end(k).wait_send()

        each(count, sent)


def grad_reduce(live, gain, d_normed_part, hidden, cotangent, normed_t, d_gate, d_up, activation):
    rows = hidden.shape[0]
    units = d_gate.shape[1]
    width = D // lax.axis_size("tp")
    shard = D // (lax.axis_size("fsdp") * lax.axis_size("ctx"))
    count = rows // LINE
    vmem = pl.BlockSpec(memory_space=pltpu.VMEM)
    anywhere = pl.BlockSpec(memory_space=pl.ANY)
    dma = pltpu.SemaphoreType.DMA
    scratch = lambda *shape: pltpu.VMEM(shape, BF)
    return pl.pallas_call(
        grad_kernel,
        out_shape=[
            jax.ShapeDtypeStruct((rows, D), BF),
            jax.ShapeDtypeStruct((rows, width), F32),
            jax.ShapeDtypeStruct((1, width), F32),
            jax.ShapeDtypeStruct((3, shard, units), BF),
            jax.ShapeDtypeStruct((8, 128), F32),
        ],
        in_specs=[vmem] * 2 + [anywhere] * 7,
        out_specs=[anywhere, anywhere, vmem, anywhere, vmem],
        scratch_shapes=[scratch(rows, D)] * 3
        + [
            scratch(3, 4, shard, units),
            scratch(2, shard, units),
            scratch(3, 2, shard // 2, units),
            scratch(3, 2, shard // 2, units),
            scratch(3, shard // 2, units),
            scratch(3, shard // 2, units),
            scratch(D, rows),
            scratch(2, rows, units),
            scratch(2, LOAD, D),
            scratch(2, LOAD, D),
            scratch(2, ROWS, D),
            pltpu.VMEM((2, ROWS, width), F32),
            scratch(2, rows, 256),
        ]
        + [dma, dma, dma((3,)), dma((rows // LOAD,)), dma((rows // LOAD,)), dma((rows // ROWS,)), dma((rows // ROWS,)), dma((D // 256,)), dma((3, 2))]
        + [dma((3, 4))] * 2
        + [dma((3, 2))] * 4
        + [dma((3,))] * 4
        + [dma((count,))] * 6,
        compiler_params=pltpu.CompilerParams(collective_id=4, has_side_effects=True, vmem_limit_bytes=63 * MIB),
        cost_estimate=pl.CostEstimate(flops=rows * D * units * 6, bytes_accessed=400 * MIB, transcendentals=0),
        name="grad_reduce",
    )(live, gain, d_normed_part, hidden, cotangent, normed_t, d_gate, d_up, activation)


PACK = 576
HALF = PACK // 2
SHARE = 256


def torus(s1, xin, yin2, yin, xin2, sems, x, y, to_x, to_y):
    x_send, x_recv, y2_send, y2_recv, y_send, y_recv, x2_send, x2_recv = sems
    half = yin.shape[0]
    upper, lower = pl.ds(0, half), pl.ds(half, half)

    def remote(src, dst, send, recv, to):
        return pltpu.make_async_remote_copy(
            src_ref=src, dst_ref=dst, send_sem=send, recv_sem=recv, device_id=to, device_id_type=MESH
        )

    def plus(a, b):
        return (a.astype(F32) + b.astype(F32)).astype(BF)

    x_copy = lambda v: remote(s1.at[v * 2 + 1 - x, upper], xin.at[v], x_send.at[v], x_recv.at[v], to_x)
    y2_copy = lambda v: remote(s1.at[(1 - y) * 2 + v, lower], yin2.at[v], y2_send.at[v], y2_recv.at[v], to_y)
    y_copy = remote(xin.at[1 - y], yin, y_send.at[0], y_recv.at[0], to_y)
    x2_copy = remote(yin2.at[1 - x], xin2, x2_send.at[0], x2_recv.at[0], to_x)

    def begin():
        x_copy(1 - y).start()
        y2_copy(1 - x).start()
        x_copy(y).start()
        y2_copy(x).start()

    def middle():
        x_copy(1 - y).wait_recv()
        xin[1 - y] = plus(xin[1 - y], s1[(1 - y) * 2 + x, upper])
        y_copy.start()
        y2_copy(1 - x).wait_recv()
        yin2[1 - x] = plus(yin2[1 - x], s1[y * 2 + 1 - x, lower])
        x2_copy.start()
        x_copy(y).wait_recv()
        xin[y] = plus(xin[y], s1[y * 2 + x, upper])
        y2_copy(x).wait_recv()
        yin2[x] = plus(yin2[x], s1[y * 2 + x, lower])

    def last(out):
        y_copy.wait_recv()
        out[upper, :] = plus(yin[...], xin[y])
        x2_copy.wait_recv()
        out[lower, :] = plus(xin2[...], yin2[x])

    def drain():
        for v in range(2):
            x_copy(v).wait_send()
            y2_copy(v).wait_send()
        y_copy.wait_send()
        x2_copy.wait_send()

    return begin, middle, last, drain


def latent_back_kernel(
    dq_ref, de_ref, dkr_ref, up_ref, sum_ref, w_ref, x_ref, gain_ref, dh_ref, tcos, tsin, gains, gout_ref, gq_ref, gkv_ref,
    sel_ref, b2_ref, square_ref, fold_ref,
    gin_ref, pack_out, wd_out, small_out, scalar_out, gq_out, gkv_out,
    uq, ukv, away, arrived, xb, near, cross, total, dl, dlt, xg, weight, w_pack, small, small_in, scal_in,
    s1, cin, xin, yin2, yin, xin2, s1w, cinw, xinw, yin2w, yinw, xin2w,
    lat_send, lat_recv, out_send, out_recv, q_send, q_recv, kv_send, kv_recv, w_send, w_recv,
    small_send, small_recv, scal_send, scal_recv, *sems,
):
    z, core, place = lax.axis_index("tp"), lax.axis_index("ctx"), lax.axis_index("fsdp")
    y, x = place // 2, place % 2
    is_end, is_mid, partner, across = line_places(z)
    line_sems, pack_sems, w_sems = sems[:6], sems[6:14], sems[14:22]
    to_mid, over, to_end, first, second = line_copies(xb, near, cross, total, line_sems, partner, across, LAT_LINE)
    count = xb.shape[0] // LAT_LINE
    rows = xb.shape[0]
    peers = up_ref.shape[0]
    me = place * 2 + core
    to_core, to_x, to_y = {"ctx": 1 - core}, {"fsdp": y * 2 + 1 - x}, {"fsdp": (1 - y) * 2 + x}

    def remote(src, dst, send, recv, to):
        return pltpu.make_async_remote_copy(
            src_ref=src, dst_ref=dst, send_sem=send, recv_sem=recv, device_id=to, device_id_type=MESH
        )

    def peer(d):
        to = lax.rem(me + d, peers)
        return {"fsdp": to // 2, "ctx": lax.rem(to, 2)}

    barrier = pltpu.get_barrier_semaphore()
    for d in range(1, peers):
        pl.semaphore_signal(barrier, inc=1, device_id=peer(d), device_id_type=MESH)
    for d in range(1, 4):
        pl.semaphore_signal(barrier, inc=1, device_id={"tp": lax.rem(z + d, 4)}, device_id_type=MESH)
    pl.semaphore_wait(barrier, peers + 2)

    def piece(e):
        return pl.ds(pl.multiple_of(e * LAT_LINE, LAT_LINE), LAT_LINE)

    def span(f, parity, size):
        return pl.ds(pl.multiple_of((2 * f + parity) * size, size), size)

    slot_q, slot_kv = pl.ds(320 + 96 * core, 96), pl.ds(512 + 32 * core, 32)
    other_q, other_kv = pl.ds(320 + 96 * (1 - core), 96), pl.ds(512 + 32 * (1 - core), 32)
    out_copy = lambda f: remote(gout_ref.at[span(f, 1 - core, 320)], cin.at[f], out_send.at[f], out_recv.at[f], to_core)
    q_copy = lambda f: remote(gq_ref.at[span(f, 1 - core, 96)], s1.at[f, slot_q], q_send.at[f], q_recv.at[f], to_core)
    kv_copy = lambda f: remote(gkv_ref.at[span(f, 1 - core, 32)], s1.at[f, slot_kv], kv_send.at[f], kv_recv.at[f], to_core)
    q_got = lambda f: remote(gq_ref.at[span(f, 1 - core, 96)], s1.at[f, other_q], q_send.at[f], q_recv.at[f], to_core)
    kv_got = lambda f: remote(gkv_ref.at[span(f, 1 - core, 32)], s1.at[f, other_kv], kv_send.at[f], kv_recv.at[f], to_core)

    for p in range(peers):
        uq[p * 96 : (p + 1) * 96, :] = up_ref[p, 0:96, :]
        ukv[p * 32 : (p + 1) * 32, :] = up_ref[p, 96:128, :]

    lane = lax.broadcasted_iota(jnp.int32, (1, 128), 1)
    block = lambda e: pl.ds(pl.multiple_of(e * SHARE, SHARE), SHARE)
    hand = lambda e: remote(away.at[block(e)], arrived.at[block(e)], lat_send.at[e], lat_recv.at[e], to_core)
    shares = rows // SHARE

    def share(at):
        here = pl.ds(pl.multiple_of(at, SHARE), SHARE)
        q = dot_nt(dq_ref[here, :], uq[...])
        kv = dot_nt(de_ref[here, :], ukv[...])
        rope = jnp.where(lane < ROPE, pltpu.roll(dkr_ref[here, :], NOPE, 1), 0.0)
        return q, kv, rope

    def send_away(e):
        q, kv, rope = share((1 - core) * rows + e * SHARE)
        away[block(e), 0:QR] = q.astype(BF)
        away[block(e), QR : QR + KVR] = kv.astype(BF)
        away[block(e), QR + KVR : LAT_WIDE] = rope.astype(BF)
        hand(e).start()

    each(shares, send_away)
    for f in range(4):
        out_copy(f).start()
        q_copy(f).start()
        kv_copy(f).start()

    def keep(e):
        q, kv, rope = share(core * rows + e * SHARE)
        hand(e).wait_recv()
        got = arrived[block(e), :].astype(F32)
        xb[block(e), 0:QR] = (q + got[:, 0:QR]).astype(BF)
        xb[block(e), QR : QR + KVR] = (kv + got[:, QR : QR + KVR]).astype(BF)
        xb[block(e), QR + KVR : LAT_WIDE] = (rope + got[:, QR + KVR :]).astype(BF)

        @pl.when(is_end)
        def _():
            each(SHARE // LAT_LINE, lambda n: to_mid(e * (SHARE // LAT_LINE) + n).start())

    each(shares, keep)

    small[...] = jnp.zeros_like(small)
    small[2:3, 0 : b2_ref.shape[1]] = b2_ref[...]
    stat_lane = lax.broadcasted_iota(jnp.int32, (1, LAT_WIDE), 1)
    stat_lane = jnp.logical_and(stat_lane >= LAT, stat_lane < LAT + 8)
    gain_q, gain_kv = gains[0:1, 0:QR], gains[0:1, QR : QR + KVR]

    def through(d, v, gain):
        factor = lax.rsqrt(jnp.mean(v * v, axis=1, keepdims=True) + EPS_NORM)
        scaled = d * gain
        gain_grad = jnp.sum(d * v * factor, axis=0, keepdims=True)
        return factor * scaled - v * (factor * factor * factor * jnp.mean(scaled * v, axis=1, keepdims=True)), gain_grad

    def finish_rows(e):
        v = sum_ref[piece(e), :].astype(F32)
        square = jnp.sum(jnp.where(stat_lane, v, 0.0), axis=1, keepdims=True)
        factor = lax.rsqrt(square / D + EPS_NORM)
        v = v * factor
        d = total[piece(e), :].astype(F32)
        ql, kl, raw = v[:, :QR], v[:, QR : QR + KVR], jnp.where(lane < ROPE, v[:, QR + KVR :], 0.0)
        dql, grad_q = through(d[:, :QR], ql, gain_q)
        dkl, grad_kv = through(d[:, QR : QR + KVR], kl, gain_kv)
        moved = pltpu.roll(d[:, QR + KVR :], NOPE, 1)
        turned = jnp.where(lane < NOPE + 16, pltpu.roll(moved, 128 - 16, 1), -pltpu.roll(moved, 16, 1))
        rope = pltpu.roll(moved * tcos[piece(e), :] + turned * tsin[piece(e), :], NOPE, 1)
        inner = (
            jnp.sum(dql * ql, axis=1, keepdims=True)
            + jnp.sum(dkl * kl, axis=1, keepdims=True)
            + jnp.sum(rope * raw, axis=1, keepdims=True)
        ) / D
        small[0:1, 0:QR] += grad_q
        small[0:1, QR : QR + KVR] += grad_kv
        dl[piece(e), 0:QR] = (dql * factor).astype(BF)
        dl[piece(e), QR : QR + KVR] = (dkl * factor).astype(BF)
        dl[piece(e), QR + KVR : LAT_WIDE] = (rope * factor).astype(BF)
        weight[piece(e), :] = jnp.broadcast_to(factor * factor * inner, (LAT_LINE, 128))

        @pl.when(e % 2 == 1)
        def _():
            pair = pl.ds(pl.multiple_of((e - 1) * LAT_LINE, 128), 128)
            d_in = dot_nn(dl[pair, :], w_ref[...])
            rows_in = x_ref[pair, :].astype(F32)
            gin_ref[pair, :] = (dh_ref[pair, :] + d_in * gain_ref[...] - rows_in * weight[pair, 0:1]).astype(BF)
            small[1:2, 0 : d_in.shape[1]] += jnp.sum(d_in * rows_in, axis=0, keepdims=True)
            xg[pair, :] = (rows_in * gain_ref[...]).astype(BF)
            dlt[:, pair] = dl[pair, :].astype(F32).T.astype(BF)

    def serve(n):
        @pl.when(jnp.logical_and(is_mid, n < count))
        def _():
            first(n)

        @pl.when(jnp.logical_and(is_mid, jnp.logical_and(n >= DEPTH, n < count + DEPTH)))
        def _():
            second(n - DEPTH)
            finish_rows(n - DEPTH)

        @pl.when(jnp.logical_and(is_end, jnp.logical_and(n >= 4, n < count + 4)))
        def _():
            to_mid(n - 4).wait_send()
            to_end(n - 4).wait_recv()
            finish_rows(n - 4)

    begin, middle, last, drain = torus(s1, xin, yin2, yin, xin2, pack_sems, x, y, to_x, to_y)
    begin_w, middle_w, last_w, drain_w = torus(s1w, xinw, yin2w, yinw, xin2w, w_sems, x, y, to_x, to_y)

    serve(0)
    for f in range(4):
        out_copy(f).wait_recv()
        s1[f, 0:320] = (gout_ref[span(f, core, 320), :].astype(F32) + cin[f].astype(F32)).astype(BF)
        s1[f, slot_q] = gq_ref[span(f, core, 96), :]
        s1[f, slot_kv] = gkv_ref[span(f, core, 32), :]
        q_got(f).wait_recv()
        kv_got(f).wait_recv()
    begin()
    each(6, lambda n: serve(n + 1))
    middle()
    each(4, lambda n: serve(n + 7))
    last(pack_out)
    lanes = pack_out.shape[1]
    gq_out[...] = dot_nn(pack_out[320:416, :], fold_ref[0:lanes, :]) + dot_nn(pack_out[416:512, :], fold_ref[lanes:, :])
    gkv_out[:, 0:lanes] = pack_out[512:544, :].astype(F32)
    gkv_out[:, lanes : 2 * lanes] = pack_out[544:576, :].astype(F32)
    each(count + 4 - 11, lambda n: serve(n + 11))

    both = dot_nn(dlt[0:QR, :], xg[...])
    for p in range(peers):
        w_pack[p, 0:96, :] = both[p * 96 : (p + 1) * 96].astype(BF)
    tail = dot_nn(dlt[QR:LAT, :], xg[...]).astype(BF)
    wide = lax.dot_general(sel_ref[...], tail, (((0,), (0,)), ((), ())), preferred_element_type=F32)
    for p in range(peers):
        w_pack[p, 96:144, :] = wide[p * 48 : (p + 1) * 48].astype(BF)
        w_pack[p, 144:160, :] = jnp.zeros((16, wide.shape[1]), BF)
    w_copy = lambda f: remote(w_pack.at[2 * f + 1 - core], cinw.at[f], w_send.at[f], w_recv.at[f], to_core)
    for f in range(4):
        w_copy(f).start()
    for f in range(4):
        w_copy(f).wait_recv()
        s1w[f] = (w_pack[2 * f + core].astype(F32) + cinw[f].astype(F32)).astype(BF)
    begin_w()
    middle_w()
    last_w(wd_out)

    squares = (
        total_square(wd_out[0:96, :]),
        total_square(wd_out[96:144, :]),
        total_square(pack_out[320:512, :]),
        total_square(pack_out[512:576, :]),
        total_square(pack_out[0:320, :]),
        square_ref[0:1, 0:1] + square_ref[1:2, 0:1],
        square_ref[2:3, 0:1],
    )
    line = jnp.zeros((1, 128), F32)
    for n, v in enumerate(squares):
        line = jnp.where(lane == n, v, line)
    small[3:4, 0:128] = line
    small_copy = lambda d, source: remote(small, small_in.at[source], small_send.at[d], small_recv.at[source], peer(d))
    for d in range(1, peers):
        small_copy(d, me).start()
    small_in[me] = small[...]
    for d in range(1, peers):
        small_copy(d, lax.rem(me + peers - d, peers)).wait_recv()
    whole = small_in[0]
    for p in range(1, peers):
        whole = whole + small_in[p]
    small_out[...] = whole
    norms = total_square(whole[1:2]) + total_square(whole[2:3])
    scal_in[z] = jnp.broadcast_to(jnp.where(lane == 7, norms, whole[3:4, 0:128]), (8, 128))
    scal_copy = lambda d, source: remote(
        scal_in.at[z], scal_in.at[source], scal_send.at[d], scal_recv.at[source], {"tp": lax.rem(z + d, 4)}
    )
    for d in range(1, 4):
        scal_copy(d, z).start()
    for d in range(1, 4):
        scal_copy(d, lax.rem(z + 4 - d, 4)).wait_recv()
    scalars = (scal_in[0] + scal_in[1]) + (scal_in[2] + scal_in[3])
    scalar_out[...] = jnp.where(lane == 8, total_square(whole[0:1]), scalars)

    for d in range(1, peers):
        small_copy(d, me).wait_send()
    for d in range(1, 4):
        scal_copy(d, z).wait_send()
    drain()
    drain_w()
    for f in range(4):
        out_copy(f).wait_send()
        q_copy(f).wait_send()
        kv_copy(f).wait_send()
        w_copy(f).wait_send()
    each(shares, lambda e: hand(e).wait_send())

    @pl.when(is_mid)
    def _():
        def sent(k):
            over(k).wait_send()
            to_end(k).wait_send()

        each(count, sent)


def latent_backward(*args):
    dq, up, x = args[0], args[3], args[6]
    rows, width = x.shape
    lanes = dq.shape[1]
    peers = up.shape[0]
    count = rows // LAT_LINE
    vmem = pl.BlockSpec(memory_space=pltpu.VMEM)
    dma = pltpu.SemaphoreType.DMA
    scratch = lambda *shape: pltpu.VMEM(shape, BF)
    halves = lambda half: [scratch(2, half, width), scratch(2, half, width), scratch(half, width), scratch(half, width)]
    torus_sems = [dma((2,))] * 4 + [dma((1,))] * 4
    return pl.pallas_call(
        latent_back_kernel,
        out_shape=[
            jax.ShapeDtypeStruct((rows, width), BF),
            jax.ShapeDtypeStruct((PACK, width), BF),
            jax.ShapeDtypeStruct((PIECE, width), BF),
            jax.ShapeDtypeStruct((8, QR + KVR), F32),
            jax.ShapeDtypeStruct((8, 128), F32),
            jax.ShapeDtypeStruct((QR // peers, args[-1].shape[1]), F32),
            jax.ShapeDtypeStruct((KVR // peers, args[-1].shape[0]), F32),
        ],
        in_specs=[vmem] * len(args),
        out_specs=[vmem] * 7,
        scratch_shapes=[scratch(QR, lanes), scratch(KVR, lanes)]
        + [scratch(rows, LAT_WIDE)] * 7
        + [
            scratch(LAT_WIDE, rows),
            scratch(rows, width),
            pltpu.VMEM((rows, 128), F32),
            scratch(peers, PIECE, width),
            pltpu.VMEM((8, QR + KVR), F32),
            pltpu.VMEM((peers, 8, QR + KVR), F32),
            pltpu.VMEM((4, 8, 128), F32),
            scratch(4, PACK, width),
            scratch(4, 320, width),
        ]
        + halves(HALF)
        + [scratch(4, PIECE, width), scratch(4, PIECE, width)]
        + halves(PIECE // 2)
        + [dma((rows // SHARE,))] * 2
        + [dma((4,))] * 8
        + [dma((peers,))] * 2
        + [dma((4,))] * 2
        + [dma((count,))] * 6
        + torus_sems * 2,
        compiler_params=pltpu.CompilerParams(collective_id=5, has_side_effects=True, vmem_limit_bytes=62 * MIB),
        cost_estimate=pl.CostEstimate(flops=rows * LAT_WIDE * width * 6, bytes_accessed=200 * MIB, transcendentals=0),
        name="latent_backward",
    )(*args)


def swap_cores(v):
    return lax.ppermute(v, "ctx", [(0, 1), (1, 0)])


def in_core_order(mine, other, core, axis):
    return jnp.where(
        core == 0, jnp.concatenate([mine, other], axis=axis), jnp.concatenate([other, mine], axis=axis)
    )


def gather_shards(v):
    return lax.all_gather(v, ("fsdp", "ctx"), axis=0, tiled=True)


X_SWAP = [(0, 1), (1, 0), (2, 3), (3, 2)]
Y_SWAP = [(0, 2), (2, 0), (1, 3), (3, 1)]


def take(v, which, axis):
    return lax.dynamic_index_in_dim(v, which, axis, keepdims=False)


def add_up(a, b):
    return (a.astype(F32) + b.astype(F32)).astype(BF)


def keep_half(v, axis, which, name, pairs):
    other = lax.ppermute(take(v, 1 - which, axis), name, pairs)
    return add_up(take(v, which, axis), other)


def scatter_fsdp(v):
    if lax.axis_size("fsdp") != 4:
        return lax.psum_scatter(v, "fsdp", scatter_dimension=0, tiled=False)
    place = lax.axis_index("fsdp")
    y, x = place // 2, place % 2
    _, rows, cols = v.shape
    v = v.reshape(2, 2, 2, rows // 2, cols)
    first = keep_half(v[:, :, 0], 1, x, "fsdp", X_SWAP)
    second = keep_half(v[:, :, 1], 0, y, "fsdp", Y_SWAP)
    first = keep_half(first, 0, y, "fsdp", Y_SWAP)
    second = keep_half(second, 0, x, "fsdp", X_SWAP)
    return jnp.concatenate([first, second], axis=0)


def scatter_grads(v):
    fsdp, ctx = lax.axis_size("fsdp"), lax.axis_size("ctx")
    rows, cols = v.shape
    v = v.reshape(fsdp, ctx, rows // (fsdp * ctx), cols)
    return scatter_fsdp(keep_half(v, 1, lax.axis_index("ctx"), "ctx", [(0, 1), (1, 0)]))


def split_two(v):
    high = v.astype(BF)
    return high, (v - high.astype(F32)).astype(BF)


def adamw_update(parameter, gradient, first_moment, second_moment, decay_rate):
    first_new = BETA_ONE * first_moment + (1.0 - BETA_ONE) * gradient
    second_new = BETA_TWO * second_moment + (1.0 - BETA_TWO) * gradient * gradient
    first_hat = first_new / (1.0 - BETA_ONE**STEP)
    second_hat = second_new / (1.0 - BETA_TWO**STEP)
    updated = parameter - LEARN_RATE * (
        first_hat / (jnp.sqrt(second_hat) + ADAM_EPS) + decay_rate * parameter
    )
    return (updated, first_new, second_new)


def norm_backward(incoming, values, factor, gain):
    scaled = incoming * gain
    gain_grad = jnp.sum(incoming * values * factor, axis=0)
    result = factor * scaled - values * factor**3 * jnp.mean(scaled * values, axis=1, keepdims=True)
    return (result, gain_grad)


def local(*args):
    tokens, cotangent, lengths = args[:3]
    params, firsts, seconds = args[3:12], args[12:21], args[21:30]
    w_qdown, w_kvdown, w_qup, w_kvup, w_out, w_gateup, w_down, g_norms, g_latent = params
    n_tp, n_ctx, n_fsdp = lax.axis_size("tp"), lax.axis_size("ctx"), lax.axis_size("fsdp")
    tp, core = lax.axis_index("tp"), lax.axis_index("ctx")
    rows, width = tokens.shape
    slot = rows * n_ctx
    heads_all = H // n_tp
    by_head = heads_all % n_ctx == 0
    heads = heads_all // n_ctx if by_head else heads_all

    fused = n_tp == 4 and n_fsdp == 4 and n_ctx == 2
    gains_norm = g_norms.astype(BF)
    gain_attn = gains_norm[0].astype(F32)
    inputs = tokens.astype(F32)
    seq_length = lengths[0, 0]
    own_index = core * rows + jnp.arange(rows, dtype=jnp.int32)
    own_segment = (own_index >= seq_length).astype(jnp.int32)
    live = (own_segment == 0).astype(F32)[:, None]

    q_shard = jnp.pad(
        w_qup.astype(BF).reshape(w_qup.shape[0], heads_all, HEAD), ((0, 0), (0, 0), (0, 128 - HEAD))
    ).reshape(w_qup.shape[0], heads_all * 128)
    up_shard = jnp.concatenate([q_shard, w_kvup.astype(BF)], axis=0)

    if fused:
        piece = jnp.concatenate(
            [
                w_qdown.T.astype(BF),
                jnp.pad(w_kvdown.T.astype(BF), ((0, 12), (0, 0))),
                jnp.broadcast_to(jnp.pad(g_latent.astype(BF), (0, width - g_latent.shape[0])), (16, width)),
            ],
            axis=0,
        )
        up_pair = jnp.stack([up_shard[:, : heads * 128], up_shard[:, heads * 128 :]])
        gain_wide = jnp.pad(gains_norm[1].astype(F32), (0, LAT_WIDE - width))[None]
        down_t, lat_sum, lat_all, cos_t, sin_t, seg_q, up, tcos, tsin, gains_lat, gate_up = latent_forward(
            tokens, gain_attn[None], gain_wide, piece, up_pair, lengths, w_gateup.astype(BF)
        )
        gain_mlp = lat_sum[rows : rows + n_tp, :width].reshape(D).astype(F32)
    else:
        out_t = gather_shards(w_out.T.astype(BF))
        gate_up = lax.all_gather(w_gateup.astype(BF), ("fsdp", "ctx"), axis=1, tiled=True)
        ff_down_t = gather_shards(w_down.T.astype(BF))
        index = jnp.arange(slot, dtype=jnp.int32)
        segment = (index >= seq_length).astype(jnp.int32)
        position = (index - segment * seq_length).astype(F32)
        frequency = ROPE_BASE ** (-2.0 * jnp.arange(ROPE // 2, dtype=F32) / ROPE)
        angles = frequency[:, None] * position[None, :]
        cos_t, sin_t = jnp.cos(angles), jnp.sin(angles)
        own_cos = lax.dynamic_slice_in_dim(cos_t, core * rows, rows, 1).T
        own_sin = lax.dynamic_slice_in_dim(sin_t, core * rows, rows, 1).T
        seg_f = segment.astype(F32)
        seg_q = jnp.concatenate([seg_f[None], 1.0 - seg_f[None], jnp.zeros((14, slot), F32)], axis=0).astype(BF)
        seg_k = (MASK_VALUE * jnp.concatenate([1.0 - seg_f[:, None], seg_f[:, None]], axis=1)).astype(BF)
        down_t = jnp.concatenate(
            [gather_shards(w_qdown.T.astype(BF)), gather_shards(w_kvdown.T.astype(BF)), jnp.zeros((LAT_WIDE - LAT, width), BF)]
        )
        gain_lat = lax.all_gather(g_latent.astype(BF), ("fsdp", "ctx"), axis=0, tiled=True).astype(F32)
        gain_mlp = lax.all_gather(gains_norm[1], "tp", axis=0, tiled=True).astype(F32)
        up = gather_shards(up_shard).reshape(n_fsdp * n_ctx, up_shard.shape[0], heads_all * 128)
        if by_head:
            up = lax.dynamic_slice_in_dim(up, core * heads * 128, heads * 128, 2)
        scaled_in = (inputs * gain_attn).astype(BF)
        lat_sum = lax.psum(dot_nt(scaled_in, down_t).astype(BF), "tp").astype(F32)
        square_sum = lax.psum(jnp.sum(inputs * inputs, axis=1), "tp")
    if not fused:
        factor_one = lax.rsqrt(square_sum / D + EPS_NORM)[:, None]
        latents = lat_sum[:, :LAT] * factor_one
        query_latent = latents[:, :QR]
        kv_latent = latents[:, QR : QR + KVR]
        gain_query, gain_kv = gain_lat[:QR], gain_lat[QR:]
        factor_query = lax.rsqrt(jnp.mean(query_latent * query_latent, axis=1, keepdims=True) + EPS_NORM)
        factor_kv = lax.rsqrt(jnp.mean(kv_latent * kv_latent, axis=1, keepdims=True) + EPS_NORM)
        rope_raw = latents[:, QR + KVR :]
        query_normed = (query_latent * factor_query * gain_query).astype(BF)
        kv_normed = (kv_latent * factor_kv * gain_kv).astype(BF)
        r_one, r_two = rope_raw[:, : ROPE // 2], rope_raw[:, ROPE // 2 :]
        rope_key = jnp.concatenate(
            [r_one * own_cos - r_two * own_sin, r_two * own_cos + r_one * own_sin], axis=1
        ).astype(BF)
        normed_lat = jnp.concatenate([query_normed, kv_normed, jnp.zeros((rows, NOPE), BF), rope_key], axis=1)
        lat_both = in_core_order(normed_lat, swap_cores(normed_lat), core, 0)
        lat_all = jnp.concatenate([lat_both, seg_k, jnp.zeros((slot, 128 - HEAD - 2), BF)], axis=1)
    qn, kn = lat_all[:, :QR], lat_all[:, QR : QR + KVR]

    if fused:
        att_heads, lse, q_t, k_rows, v_t, att_t, ff_down_t, out_t = attend_forward(
            lat_all, cos_t, sin_t, seg_q, up, w_down.T.astype(BF)[None], w_out.T.astype(BF)[None]
        )
        ff_down_t, out_t = ff_down_t.reshape(D, -1), out_t.reshape(D, -1)
    else:
        att_heads, lse, q_t, k_rows, v_t = attend_forward(lat_all, cos_t, sin_t, seg_q, up)
        att_flat = att_heads.reshape(heads * VD, slot)
        own_cols = lambda v: lax.dynamic_slice_in_dim(v, core * rows, rows, 1)
        if by_head:
            other = swap_cores(lax.dynamic_slice_in_dim(att_flat, (1 - core) * rows, rows, 1))
            att_t = in_core_order(own_cols(att_flat), other, core, 0)
        else:
            att_t = own_cols(att_flat)

    feature_owner = jnp.arange(D) // width
    own_features = lambda v: lax.dynamic_slice_in_dim(v, tp * width, width, 1)
    if fused:
        hidden, d_normed_part, mlp_part, normed_two_t, activation, d_gate, d_up = block_forward(
            att_t, tokens, out_t, gain_mlp[None], live, cotangent, gate_up, ff_down_t
        )
        attn_seed, d_hidden, grad_gain_mlp, grads, grad_squares = grad_reduce(
            live, gain_mlp[None], d_normed_part, hidden, cotangent, normed_two_t, d_gate, d_up, activation
        )
    else:
        dy = cotangent.astype(F32) * live
        mlp_seed = (RESIDUAL_SCALE * dy).astype(BF)
        h_part = RESIDUAL_SCALE * dot_nt(att_t.T, out_t)
        h_part = h_part + jnp.where(
            (feature_owner == tp)[None], jnp.concatenate([inputs] * n_tp, axis=1), 0.0
        )
        hidden = lax.psum(h_part.astype(BF), "tp")
        hidden_f = hidden.astype(F32)
        factor_two = lax.rsqrt(jnp.mean(hidden_f * hidden_f, axis=1, keepdims=True) + EPS_NORM)
        normed_two = (hidden_f * factor_two * gain_mlp).astype(BF)
        gate_proj = dot_nn(normed_two, gate_up[0])
        up_proj = dot_nn(normed_two, gate_up[1])
        sigmoid_gate = jax.nn.sigmoid(gate_proj)
        activation = (gate_proj * sigmoid_gate * up_proj).astype(BF)
        mlp_part = dot_nt(activation, ff_down_t).astype(BF)
        d_activation = dot_nn(mlp_seed, ff_down_t)
        d_gate = (
            d_activation * up_proj * sigmoid_gate * (1.0 + gate_proj * (1.0 - sigmoid_gate))
        ).astype(BF)
        d_up = (d_activation * gate_proj * sigmoid_gate).astype(BF)
        d_normed_part = (dot_nt(d_gate, gate_up[0]) + dot_nt(d_up, gate_up[1])).astype(BF)
        grad_down = scatter_grads(dot_tn(mlp_seed, activation).astype(BF))
        grad_gate = scatter_grads(dot_tn(normed_two, d_gate).astype(BF))
        grad_up = scatter_grads(dot_tn(normed_two, d_up).astype(BF))
        d_normed = lax.psum(d_normed_part, "tp").astype(F32)
        row_inner = jnp.mean(d_normed * gain_mlp * hidden_f, axis=1, keepdims=True)
        d_hidden_full = dy + factor_two * d_normed * gain_mlp - hidden_f * (factor_two**3 * row_inner)
        attn_seed = (RESIDUAL_SCALE * d_hidden_full).astype(BF)
        d_hidden = own_features(d_hidden_full)
        grad_gain_mlp = jnp.sum(own_features(d_normed * hidden_f) * factor_two, axis=0)
    mlp_part, attn_seed = lax.optimization_barrier((mlp_part, attn_seed))
    if fused:
        mlp_out = lax.psum_scatter(mlp_part, "tp", scatter_dimension=0, tiled=False).astype(F32)
    else:
        mlp_out = lax.psum_scatter(mlp_part, "tp", scatter_dimension=1, tiled=True).astype(F32)
    layer_out = (own_features(hidden).astype(F32) + RESIDUAL_SCALE * mlp_out).astype(BF)
    d_att_t = lax.dot_general(out_t, attn_seed, (((0,), (1,)), ((), ())), preferred_element_type=F32).astype(BF)
    grad_out = dot_tn(attn_seed, att_t.T).astype(BF)

    if by_head:
        pick = lambda v, which: lax.dynamic_slice_in_dim(v, which * heads * VD, heads * VD, 0)
        d_att = in_core_order(pick(d_att_t, core), swap_cores(pick(d_att_t, 1 - core)), core, 1)
    else:
        d_att = lax.dynamic_update_slice(jnp.zeros((heads * VD, slot), BF), d_att_t, (0, core * rows))
    d_q, d_e, d_kr = attend_backward(
        q_t, k_rows, v_t, att_heads, d_att.reshape(heads, VD, slot), lse, cos_t, sin_t
    )
    grad_qup = dot_tn(qn, d_q).astype(BF)
    grad_kvup = dot_tn(kn, d_e).astype(BF)

    def heads_only(g):
        return g.reshape(g.shape[0], heads_all, 128)[:, :, :HEAD].reshape(g.shape[0], heads_all * HEAD)

    share = g_latent.shape[0]
    my_share = (lax.axis_index("fsdp") * n_ctx + core) * share
    if fused:
        head_row = jnp.arange(heads_all * 128)
        fold = jnp.equal(
            jnp.where(head_row % 128 < HEAD, head_row // 128 * HEAD + head_row % 128, -1)[:, None],
            jnp.arange(heads_all * HEAD)[None],
        ).astype(BF)
        grad_input, pack, wd_grad, small, scalars, grad_qup, grad_kvup = latent_backward(
            d_q, d_e, d_kr, up, lat_sum, down_t, tokens, gain_attn[None], d_hidden, tcos, tsin, gains_lat,
            grad_out, grad_qup, grad_kvup, spread(n_fsdp * n_ctx), grad_gain_mlp, grad_squares, fold,
        )
        owned = [
            wd_grad[:96].astype(F32).T,
            wd_grad[96:132].astype(F32).T,
            grad_qup,
            grad_kvup,
            pack[:320].astype(F32).T,
            grads[:2].astype(F32),
            grads[2].astype(F32).T,
            small[1:3, :width],
            lax.dynamic_slice_in_dim(small[0], my_share, share, 0),
        ]
        totals = [scalars[0, n] for n in range(9)]
    else:
        q_up_here = up[:, : w_qup.shape[0]].reshape(QR, heads * 128)
        kv_up_here = up[:, w_qup.shape[0] :].reshape(KVR, heads * 128)
        d_lat_part = jnp.concatenate([dot_nt(d_q, q_up_here), dot_nt(d_e, kv_up_here), d_kr[:, NOPE:HEAD]], axis=1)
        own_rows = lambda v, which: lax.dynamic_slice_in_dim(v, which * rows, rows, 0)
        from_other = swap_cores(own_rows(d_lat_part, 1 - core).astype(BF)).astype(F32)
        d_lat = lax.psum((own_rows(d_lat_part, core) + from_other).astype(BF), "tp").astype(F32)
        d_rope = d_lat[:, QR + KVR : LAT]
        k_one, k_two = d_rope[:, : ROPE // 2], d_rope[:, ROPE // 2 :]
        d_rope_raw = jnp.concatenate([k_one * own_cos + k_two * own_sin, k_two * own_cos - k_one * own_sin], axis=1)
        d_query_latent, grad_gain_query = norm_backward(d_lat[:, :QR], query_latent, factor_query, gain_query)
        d_kv_latent, grad_gain_kv = norm_backward(d_lat[:, QR : QR + KVR], kv_latent, factor_kv, gain_kv)
        d_latents = jnp.concatenate([d_query_latent, d_kv_latent, d_rope_raw], axis=1)
        in_inner = jnp.sum(d_latents * latents, axis=1, keepdims=True) / D
        d_latents = (d_latents * factor_one).astype(BF)
        grad_both = dot_tn(d_latents, scaled_in).astype(BF)
        d_in = dot_nn(d_latents, down_t[:LAT])
        grad_gain_attn = jnp.sum(d_in * inputs, axis=0)
        grad_input = (d_hidden + d_in * gain_attn - inputs * (factor_one**2 * in_inner)).astype(BF)

        def scatter_up(g):
            if not by_head:
                return scatter_grads(g)
            n_rows, n_cols = g.shape
            g = g.reshape(n_fsdp, n_ctx, n_rows // (n_fsdp * n_ctx), n_cols)
            other = swap_cores(take(g, 1 - core, 1))
            return scatter_fsdp(in_core_order(take(g, core, 1), other, core, 2))

        owned = [
            scatter_grads(grad_both[:QR]).astype(F32).T,
            scatter_grads(grad_both[QR:]).astype(F32).T,
            heads_only(scatter_up(grad_qup)).astype(F32),
            scatter_up(grad_kvup).astype(F32),
            scatter_grads(grad_out).astype(F32).T,
            jnp.stack([grad_gate, grad_up]).astype(F32),
            grad_down.astype(F32).T,
        ]
        both_gains = jnp.stack([grad_gain_attn, grad_gain_mlp])
        placed_gains = jnp.where((feature_owner == tp)[None], jnp.concatenate([both_gains] * n_tp, axis=1), 0.0)
        latent_gains = jnp.concatenate([grad_gain_query, grad_gain_kv]) * (tp == 0)
        squares = jnp.stack([jnp.sum(g * g) for g in owned])
        small = lax.psum(
            jnp.concatenate([placed_gains.reshape(-1), latent_gains, squares]), ("fsdp", "ctx", "tp")
        )
        all_gains = small[: 2 * D].reshape(2, D)
        all_latent = small[2 * D : 2 * D + QR + KVR]
        owned.append(own_features(all_gains))
        owned.append(lax.dynamic_slice_in_dim(all_latent, my_share, share, 0))
        totals = [small[2 * D + QR + KVR + n] for n in range(7)]
        totals += [jnp.sum(all_gains * all_gains), jnp.sum(all_latent * all_latent)]
    entry_counts = (
        D * QR,
        D * (KVR + ROPE),
        QR * H * HEAD,
        KVR * H * (NOPE + VD),
        H * VD * D,
        2 * D * FF,
        FF * D,
        2 * D,
        QR + KVR,
    )
    new_params, new_firsts, new_seconds = [], [], []
    for n in range(9):
        limit = CLIP_RMS * entry_counts[n] ** 0.5
        clipped = owned[n] * (limit / jnp.maximum(jnp.sqrt(totals[n]), limit))
        updated, first_new, second_new = adamw_update(
            params[n], clipped, firsts[n], seconds[n], WEIGHT_DECAY if n < 7 else 0.0
        )
        new_params.append(updated)
        new_firsts.append(first_new)
        new_seconds.append(second_new)
    return (layer_out, grad_input, *owned, *new_params[:7], *new_firsts, *new_seconds)


def solution(mesh):
    sharded = ("fsdp", "ctx")
    weights = (
        P("tp", sharded),
        P("tp", sharded),
        P(sharded, "tp"),
        P(sharded, "tp"),
        P("tp", sharded),
        P(None, sharded, "tp"),
        P("tp", sharded),
    )
    gains = (P(None, "tp"), P(sharded))
    tokens = P(sharded, "tp")
    return jax.shard_map(
        local,
        mesh=mesh,
        in_specs=(tokens, P(sharded, None), P("fsdp", None)) + (weights + gains) * 3,
        out_specs=(tokens, tokens) + weights + gains + weights + (weights + gains) * 2,
        check_vma=False,
    )
```

```python
import functools

import jax
import jax.numpy as jnp
import numpy as np
from jax import lax
from jax.experimental import pallas as pl
from jax.experimental.pallas import tpu as pltpu
from jax.sharding import PartitionSpec as P

D = 2560
H = 40
NOPE = 64
ROPE = 32
VD = 64
QR = 768
KVR = 256
FF = 6400
STEP = 3
HEAD = NOPE + ROPE
LAT = QR + KVR + ROPE
LAT_WIDE = 1152

EPS_NORM = 1e-05
RESIDUAL_SCALE = 1.4 / 62**0.5
ROPE_BASE = 10000.0
MASK_VALUE = -1e30
BETA_ONE = 0.9
BETA_TWO = 0.95
ADAM_EPS = 1e-08
LEARN_RATE = 0.1
WEIGHT_DECAY = 0.1
CLIP_RMS = 0.0002
LOG2E = 1.4426950408889634
LN2 = 0.6931471805599453

BF = jnp.bfloat16
F32 = jnp.float32
MESH = pl.DeviceIdType.MESH
MIB = 1024 * 1024


def dot_nn(a, b):
    return lax.dot_general(a, b, (((1,), (0,)), ((), ())), preferred_element_type=F32)


def dot_nt(a, b):
    return lax.dot_general(a, b, (((1,), (1,)), ((), ())), preferred_element_type=F32)


def dot_tn(a, b):
    return lax.dot_general(a, b, (((0,), (0,)), ((), ())), preferred_element_type=F32)


def torus_gather(piece, whole, sems, place, core):
    x1s, x1r, y1s, y1r, c1s, c1r, x2s, x2r, y2s, y2r, cxs, cxr, cys, cyr, cds, cdr, own = sems
    y, x = place // 2, place % 2
    half = piece.shape[1] // 2
    upper, lower = pl.ds(0, half), pl.ds(half, half)
    to_core, to_x, to_y = {"ctx": 1 - core}, {"fsdp": y * 2 + 1 - x}, {"fsdp": (1 - y) * 2 + x}

    def owner(yy, xx, cc):
        return (yy * 2 + xx) * 2 + cc

    me, px, py = owner(y, x, core), owner(y, 1 - x, core), owner(1 - y, x, core)
    pd = owner(1 - y, 1 - x, core)

    def remote(src, dst, send, recv, i, to):
        return pltpu.make_async_remote_copy(
            src_ref=src, dst_ref=dst, send_sem=send.at[i], recv_sem=recv.at[i], device_id=to, device_id_type=MESH
        )

    first = lambda i, p, send, recv, to: remote(piece.at[i], whole.at[p, i], send, recv, i, to)
    part = lambda i, p, rows, send, recv, to: remote(whole.at[p, i, rows], whole.at[p, i, rows], send, recv, i, to)
    full = lambda i, p, send, recv: remote(whole.at[p, i], whole.at[p, i], send, recv, i, to_core)
    keep = lambda i: pltpu.make_async_copy(piece.at[i], whole.at[me, i], own.at[i])

    def begin(i):
        first(i, me, x1s, x1r, to_x).start()
        first(i, me, y1s, y1r, to_y).start()
        first(i, me, c1s, c1r, to_core).start()
        keep(i).start()

    def forward(i):
        first(i, px, x1s, x1r, to_x).wait_recv()
        part(i, px, upper, y2s, y2r, to_y).start()
        full(i, px, cxs, cxr).start()
        first(i, py, y1s, y1r, to_y).wait_recv()
        part(i, py, lower, x2s, x2r, to_x).start()
        full(i, py, cys, cyr).start()

    def final(i):
        part(i, pd, upper, y2s, y2r, to_y).wait_recv()
        part(i, pd, lower, x2s, x2r, to_x).wait_recv()
        full(i, pd, cds, cdr).start()

    def drain(i):
        first(i, owner(y, x, 1 - core), c1s, c1r, to_core).wait_recv()
        full(i, owner(y, 1 - x, 1 - core), cxs, cxr).wait_recv()
        full(i, owner(1 - y, x, 1 - core), cys, cyr).wait_recv()
        full(i, owner(1 - y, 1 - x, 1 - core), cds, cdr).wait_recv()
        first(i, me, x1s, x1r, to_x).wait_send()
        first(i, me, y1s, y1r, to_y).wait_send()
        first(i, me, c1s, c1r, to_core).wait_send()
        part(i, px, upper, y2s, y2r, to_y).wait_send()
        part(i, py, lower, x2s, x2r, to_x).wait_send()
        full(i, px, cxs, cxr).wait_send()
        full(i, py, cys, cyr).wait_send()
        full(i, pd, cds, cdr).wait_send()
        keep(i).wait()

    return begin, forward, final, drain


GATHER_SEMS = 17


BQ = 512


def attend_forward_kernel(fused, *refs):
    lat_ref, cos_ref, sin_ref, segq_ref, up_ref, *refs = refs
    if fused:
        down_any, out_any, *refs = refs
    o_ref, lse_ref, q_ref, k_ref, v_ref, *refs = refs
    if fused:
        att_any, down_all, out_all, *refs = refs
    stack_q, stack_kv, wq_t, *refs = refs
    h, i = pl.program_id(0), pl.program_id(1)
    rows = lat_ref.shape[0]
    heads, blocks = pl.num_programs(0), rows // BQ
    if fused:
        place, core = lax.axis_index("fsdp"), lax.axis_index("ctx")
        stage, att_send, att_recv, *sems = refs
        at = h * blocks + i
        gathers = (
            torus_gather(down_any, down_all, sems[:GATHER_SEMS], place, core),
            torus_gather(out_any, out_all, sems[GATHER_SEMS:], place, core),
        )

        @pl.when(at == 0)
        def _():
            y, x = place // 2, place % 2
            barrier = pltpu.get_barrier_semaphore()
            for to in ({"ctx": 1 - core}, {"fsdp": y * 2 + 1 - x}, {"fsdp": (1 - y) * 2 + x}):
                pl.semaphore_signal(barrier, inc=1, device_id=to, device_id_type=MESH)
            pl.semaphore_wait(barrier, 3)
            for begin, _, _, _ in gathers:
                begin(0)

        for n in range(2):

            @pl.when(at == (heads * blocks * (13 + 4 * n)) // 20)
            def _():
                gathers[n][1](0)
    pieces = up_ref.shape[0]
    nq, nk = QR // pieces, KVR // pieces

    @pl.when(i == 0)
    def _():
        for p in range(pieces):
            stack_q[p * nq : (p + 1) * nq, :] = up_ref[p, 0:nq, :].astype(F32)
            stack_kv[p * nk : (p + 1) * nk, :] = up_ref[p, nq : nq + nk, :].astype(F32)
        wq_t[...] = stack_q[...].T.astype(BF)
        kv = stack_kv[...]
        wk = jnp.where(lax.broadcasted_iota(jnp.int32, kv.shape, 1) < NOPE, kv, 0.0).astype(BF)
        wv_t = kv.T[NOPE:128].astype(BF)
        for r in range(rows // BQ):
            part = pl.ds(r * BQ, BQ)
            kn = lat_ref[part, QR : QR + KVR]
            qf = dot_nt(wq_t[...], lat_ref[part, 0:QR]) * (LOG2E * HEAD**-0.5)
            cos = cos_ref[:, part]
            sin = sin_ref[:, part]
            one, two = qf[NOPE : NOPE + 16], qf[NOPE + 16 : HEAD]
            q_ref[0, 0:NOPE, part] = qf[:NOPE].astype(BF)
            q_ref[0, NOPE : NOPE + 16, part] = (one * cos - two * sin).astype(BF)
            q_ref[0, NOPE + 16 : HEAD, part] = (two * cos + one * sin).astype(BF)
            q_ref[0, HEAD : HEAD + 16, part] = segq_ref[:, part]
            q_ref[0, HEAD + 16 : 128, part] = jnp.zeros((16, BQ), BF)
            k_ref[0, part, :] = (dot_nn(kn, wk) + lat_ref[part, QR + KVR : LAT_WIDE].astype(F32)).astype(BF)
            v_ref[0, 0:VD, part] = dot_nt(wv_t, kn).astype(BF)
            ones = lax.broadcasted_iota(jnp.int32, (16, BQ), 0) == 0
            v_ref[0, VD : VD + 16, part] = ones.astype(F32).astype(BF)

    here = pl.ds(pl.multiple_of(i * BQ, BQ), BQ)
    q = q_ref[0, :, here]

    def block(j, carried, masked):
        m, acc = carried
        there = pl.ds(pl.multiple_of(j * BQ, BQ), BQ)
        s = dot_nn(k_ref[0, there, :], q)
        if masked:
            krow = lax.broadcasted_iota(jnp.int32, s.shape, 0)
            qcol = lax.broadcasted_iota(jnp.int32, s.shape, 1)
            s = jnp.where(krow <= qcol, s, MASK_VALUE)
        top = jnp.maximum(m, jnp.max(s, axis=0, keepdims=True))
        p = jnp.exp2(s - top).astype(BF)
        acc = acc * jnp.exp2(m - top) + dot_nn(v_ref[0, :, there], p)
        return top, acc

    start = (jnp.full((1, BQ), -3e38, F32), jnp.zeros((80, BQ), F32))
    carried = lax.fori_loop(0, i, lambda j, c: block(j, c, False), start)
    m, acc = block(i, carried, True)
    total = acc[VD : VD + 1]
    o = (acc[:VD] / total).astype(BF)
    o_ref[0, :, here] = o
    lse_ref[0, :, here] = m + jnp.log2(total)
    if fused:
        count = blocks // 2

        def spot(owner, hh, b):
            return (
                pl.ds(pl.multiple_of((owner * heads + hh) * VD, VD), VD),
                pl.ds(pl.multiple_of(lax.rem(b, count) * BQ, BQ), BQ),
            )

        stage[h, i] = o
        keep = lambda hh, b: pltpu.make_async_copy(stage.at[hh, b], att_any.at[spot(core, hh, b)], att_send.at[hh, b])
        give = lambda hh, b, owner: pltpu.make_async_remote_copy(
            src_ref=stage.at[hh, b], dst_ref=att_any.at[spot(owner, hh, b)], send_sem=att_send.at[hh, b],
            recv_sem=att_recv.at[hh, lax.rem(b, count)], device_id={"ctx": 1 - core}, device_id_type=MESH,
        )

        @pl.when(i // count == core)
        def _():
            keep(h, i).start()

        @pl.when(i // count != core)
        def _():
            give(h, i, core).start()

        @pl.when(at == heads * blocks - 1)
        def _():
            def done(n):
                hh, b = n // count, lax.rem(n, count)
                keep(hh, core * count + b).wait()
                give(hh, (1 - core) * count + b, core).wait_send()
                give(hh, core * count + b, 1 - core).wait_recv()

            each(heads * count, done)
            for _, _, final, _ in gathers:
                final(0)
            for _, _, _, drain in gathers:
                drain(0)


def attend_forward(lat, cos, sin, segq, up, *pieces):
    heads = up.shape[2] // 128
    rows = lat.shape[0]
    fused = len(pieces) > 0
    anywhere = pl.BlockSpec(memory_space=pl.ANY)
    dma = pltpu.SemaphoreType.DMA
    more_out, more_scratch, params = [], [], {}
    if fused:
        more_out = [jax.ShapeDtypeStruct((2 * heads * VD, rows // 2), BF)]
        more_out += [jax.ShapeDtypeStruct((up.shape[0],) + p.shape, BF) for p in pieces]
        more_scratch = [pltpu.VMEM((heads, rows // BQ, VD, BQ), BF), dma((heads, rows // BQ)), dma((heads, rows // BQ // 2))]
        more_scratch += [dma((1,))] * (2 * GATHER_SEMS)
        params = {"collective_id": 6, "has_side_effects": True}
    whole = lambda a: pl.BlockSpec(a.shape, lambda h, i: (0,) * a.ndim)
    per_head = lambda a, b: pl.BlockSpec((1, a, b), lambda h, i: (h, 0, 0))
    return pl.pallas_call(
        functools.partial(attend_forward_kernel, fused),
        grid=(heads, rows // BQ),
        in_specs=[whole(lat), whole(cos), whole(sin), whole(segq)]
        + [pl.BlockSpec((up.shape[0], up.shape[1], 128), lambda h, i: (0, 0, h))]
        + [anywhere] * len(pieces),
        out_specs=[per_head(VD, rows), per_head(1, rows), per_head(128, rows), per_head(rows, 128), per_head(80, rows)]
        + [anywhere] * len(more_out),
        out_shape=[
            jax.ShapeDtypeStruct((heads, VD, rows), BF),
            jax.ShapeDtypeStruct((heads, 1, rows), F32),
            jax.ShapeDtypeStruct((heads, 128, rows), BF),
            jax.ShapeDtypeStruct((heads, rows, 128), BF),
            jax.ShapeDtypeStruct((heads, 80, rows), BF),
        ]
        + more_out,
        scratch_shapes=[pltpu.VMEM((QR, 128), F32), pltpu.VMEM((KVR, 128), F32), pltpu.VMEM((128, QR), BF)] + more_scratch,
        compiler_params=pltpu.CompilerParams(vmem_limit_bytes=(62 if fused else 40) * MIB, **params),
        cost_estimate=pl.CostEstimate(flops=heads * rows * rows * 320, bytes_accessed=30 * MIB, transcendentals=0),
        name="attend_forward",
    )(lat, cos, sin, segq, up, *pieces)


def attend_backward_kernel(q_ref, k_ref, v_ref, o_ref, do_ref, lse_ref, cos_ref, sin_ref, dq_ref, de_ref, dkr_ref, dq_acc, delta):
    h, j = pl.program_id(0), pl.program_id(1)
    rows = k_ref.shape[1]
    blocks = rows // BQ

    @pl.when(j == 0)
    def _():
        dq_acc[...] = jnp.zeros_like(dq_acc)
        delta[...] = jnp.sum(o_ref[0].astype(F32) * do_ref[0].astype(F32), axis=0, keepdims=True)

    there = pl.ds(pl.multiple_of(j * BQ, BQ), BQ)
    k = k_ref[0, there, :]
    kt = k.astype(F32).T.astype(BF)
    v = v_ref[0, 0:VD, there].astype(F32).T.astype(BF)

    def block(i, carried, masked):
        dk, dv = carried
        here = pl.ds(pl.multiple_of(i * BQ, BQ), BQ)
        q = q_ref[0, :, here]
        do = do_ref[0, :, here]
        s = dot_nn(k, q)
        if masked:
            krow = lax.broadcasted_iota(jnp.int32, s.shape, 0)
            qcol = lax.broadcasted_iota(jnp.int32, s.shape, 1)
            s = jnp.where(krow <= qcol, s, MASK_VALUE)
        p = jnp.exp2(s - lse_ref[0, :, here])
        dp = dot_nn(v, do)
        ds = (p * (dp - delta[:, here])).astype(BF)
        dv = dv + dot_nt(p.astype(BF), do)
        dk = dk + dot_nt(ds, q)
        dq_acc[:, here] = dq_acc[:, here] + dot_nn(kt, ds)
        return dk, dv

    start = (jnp.zeros((BQ, 128), F32), jnp.zeros((BQ, VD), F32))
    carried = block(j, start, True)
    dk, dv = lax.fori_loop(j + 1, blocks, lambda i, c: block(i, c, False), carried)
    dk = dk * LN2
    de_ref[there, 0:NOPE] = dk[:, :NOPE].astype(BF)
    de_ref[there, NOPE:128] = dv.astype(BF)

    @pl.when(h == 0)
    def _():
        dkr_ref[there, :] = dk

    @pl.when(h > 0)
    def _():
        dkr_ref[there, :] = dkr_ref[there, :] + dk

    @pl.when(j == blocks - 1)
    def _():
        for r in range(blocks):
            part = pl.ds(r * BQ, BQ)
            dq = dq_acc[:, part] * HEAD**-0.5
            cos, sin = cos_ref[:, part], sin_ref[:, part]
            one, two = dq[NOPE : NOPE + 16], dq[NOPE + 16 : HEAD]
            dq = jnp.concatenate(
                [dq[:NOPE], one * cos + two * sin, two * cos - one * sin, jnp.zeros((128 - HEAD, BQ), F32)], axis=0
            )
            dq_ref[part, :] = dq.T.astype(BF)


def attend_backward(q, k, v, o, do, lse, cos, sin):
    heads = q.shape[0]
    rows = k.shape[1]
    whole = lambda a: pl.BlockSpec(a.shape, lambda h, i: (0,) * a.ndim)
    per_head = lambda a: pl.BlockSpec((1,) + a.shape[1:], lambda h, i: (h, 0, 0))
    return pl.pallas_call(
        attend_backward_kernel,
        grid=(heads, rows // BQ),
        in_specs=[per_head(a) for a in (q, k, v, o, do, lse)] + [whole(cos), whole(sin)],
        out_specs=[
            pl.BlockSpec((rows, 128), lambda h, i: (0, h)),
            pl.BlockSpec((rows, 128), lambda h, i: (0, h)),
            pl.BlockSpec((rows, 128), lambda h, i: (0, 0)),
        ],
        out_shape=[
            jax.ShapeDtypeStruct((rows, heads * 128), BF),
            jax.ShapeDtypeStruct((rows, heads * 128), BF),
            jax.ShapeDtypeStruct((rows, 128), F32),
        ],
        scratch_shapes=[pltpu.VMEM((128, rows), F32), pltpu.VMEM((1, rows), F32)],
        compiler_params=pltpu.CompilerParams(vmem_limit_bytes=40 * MIB),
        cost_estimate=pl.CostEstimate(flops=heads * rows * rows * 900, bytes_accessed=30 * MIB, transcendentals=0),
        name="attend_backward",
    )(q, k, v, o, do, lse, cos, sin)


LAT_LINE = 64
LAT_DEPTH = 2
PIECE = 160


def latent_kernel(
    x_ref, gain_ref, gain2_ref, piece_ref, up_ref, sel_ref, freq_col, freq_lane, len_ref, gu_any,
    w_ref, total, lat_ref, cos_ref, sin_ref, segq_ref, upg_ref, tcos, tsin, gains, gu_all,
    gat, up_all, xb, near, cross, kvg,
    c_send, c_recv, *sems,
):
    gather_sems, w_sems, u_sems, sems = sems[40:], sems[6:23], sems[23:40], sems[:6]
    z, core, place = lax.axis_index("tp"), lax.axis_index("ctx"), lax.axis_index("fsdp")
    is_end, is_mid, partner, across = line_places(z)
    to_mid, over, to_end, first, second = line_copies(xb, near, cross, total, sems, partner, across, LAT_LINE)
    count = xb.shape[0] // LAT_LINE
    rows = x_ref.shape[0]
    peers = gat.shape[0]
    me = place * 2 + core

    def remote(src, dst, send, recv, to):
        return pltpu.make_async_remote_copy(
            src_ref=src, dst_ref=dst, send_sem=send, recv_sem=recv, device_id=to, device_id_type=MESH
        )

    y, x = place // 2, place % 2
    barrier = pltpu.get_barrier_semaphore()
    for to in ({"ctx": 1 - core}, {"fsdp": y * 2 + 1 - x}, {"fsdp": (1 - y) * 2 + x}, {"tp": partner}):
        pl.semaphore_signal(barrier, inc=1, device_id=to, device_id_type=MESH)

    @pl.when(is_mid)
    def _():
        pl.semaphore_signal(barrier, inc=1, device_id={"tp": across}, device_id_type=MESH)
        pl.semaphore_wait(barrier, 5)

    @pl.when(is_end)
    def _():
        pl.semaphore_wait(barrier, 4)

    begin, forward, final, drain = torus_gather(gu_any, gu_all, gather_sems, place, core)
    begin_w, forward_w, final_w, drain_w = torus_gather(piece_ref, gat, w_sems, place, core)
    begin_u, forward_u, final_u, drain_u = torus_gather(up_ref, up_all, u_sems, place, core)
    begin_w(0)

    length = len_ref[0, 0]
    slot = cos_ref.shape[1]
    index = lax.broadcasted_iota(jnp.int32, (1, slot), 1)
    segment = (index >= length).astype(jnp.int32)
    angle = freq_col[...] * (index - segment * length).astype(F32)
    cos_ref[...] = jnp.cos(angle)
    sin_ref[...] = jnp.sin(angle)
    row16 = lax.broadcasted_iota(jnp.int32, (16, slot), 0)
    seg_f = segment.astype(F32)
    segq_ref[...] = jnp.where(row16 == 0, seg_f, jnp.where(row16 == 1, 1.0 - seg_f, 0.0)).astype(BF)
    lane = lax.broadcasted_iota(jnp.int32, (1, 128), 1)
    in_rope = jnp.logical_and(lane >= NOPE, lane < HEAD)

    def own_index(e):
        at = core * rows + e * LAT_LINE
        return at + lax.broadcasted_iota(jnp.int32, (LAT_LINE, 1), 0)

    def table(e):
        here = pl.ds(pl.multiple_of(e * LAT_LINE, LAT_LINE), LAT_LINE)
        at = own_index(e)
        seg = (at >= length).astype(jnp.int32)
        turn = (at - seg * length).astype(F32) * freq_lane[...]
        tcos[here, :] = jnp.where(in_rope, jnp.cos(turn), 0.0)
        tsin[here, :] = jnp.where(in_rope, jnp.sin(turn), 0.0)

    each(rows // LAT_LINE, table)

    forward_w(0)
    begin_u(0)
    begin(0)
    begin(1)
    final_w(0)
    drain_w(0)
    for p in range(peers):
        w_ref[p * 96 : (p + 1) * 96, :] = gat[p, 0, 0:96, :]
        kvg[p * 48 : (p + 1) * 48, :] = gat[p, 0, 96:144, :]
        gains[:, p * 128 : (p + 1) * 128] = gat[p, 0, 144:160, 0:128].astype(F32)
    w_ref[QR:LAT, :] = dot_nn(sel_ref[...], kvg[...]).astype(BF)
    w_ref[LAT:LAT_WIDE, :] = jnp.zeros((LAT_WIDE - LAT, w_ref.shape[1]), BF)

    wide_lane = lax.broadcasted_iota(jnp.int32, (1, LAT_WIDE), 1)
    per = 128

    def project(r):
        here = pl.ds(pl.multiple_of(r * per, per), per)
        x = x_ref[here, :].astype(F32)
        square = jnp.sum(x * x, axis=1, keepdims=True)
        high = square.astype(BF).astype(F32)
        part = dot_nt((x * gain_ref[...]).astype(BF), w_ref[...])
        part = jnp.where(wide_lane == LAT + 2 * z, high, jnp.where(wide_lane == LAT + 2 * z + 1, square - high, part))
        xb[here, :] = part.astype(BF)

        @pl.when(is_end)
        def _():
            for n in range(per // LAT_LINE):
                to_mid(r * (per // LAT_LINE) + n).start()

    each(rows // per, project)
    gain_row = lax.broadcasted_iota(jnp.int32, (LAT_LINE, LAT_WIDE), 0) == z
    xb[rows : rows + LAT_LINE, :] = jnp.where(gain_row, gain2_ref[...], 0.0).astype(BF)

    @pl.when(is_end)
    def _():
        to_mid(count - 1).start()

    def handover(e):
        here = pl.ds(pl.multiple_of(core * rows + e * LAT_LINE, LAT_LINE), LAT_LINE)
        return remote(lat_ref.at[here], lat_ref.at[here], c_send.at[e], c_recv.at[e], {"ctx": 1 - core})

    stat_lane = jnp.logical_and(wide_lane >= LAT, wide_lane < LAT + 8)

    def finish_rows(e):
        @pl.when(e < rows // LAT_LINE)
        def _():
            here = pl.ds(pl.multiple_of(e * LAT_LINE, LAT_LINE), LAT_LINE)
            there = pl.ds(pl.multiple_of(core * rows + e * LAT_LINE, LAT_LINE), LAT_LINE)
            v = total[here, :].astype(F32)
            square = jnp.sum(jnp.where(stat_lane, v, 0.0), axis=1, keepdims=True)
            v = v * lax.rsqrt(square / D + EPS_NORM)
            ql, kl, raw = v[:, :QR], v[:, QR : QR + KVR], v[:, QR + KVR :]
            ql = ql * lax.rsqrt(jnp.mean(ql * ql, axis=1, keepdims=True) + EPS_NORM)
            kl = kl * lax.rsqrt(jnp.mean(kl * kl, axis=1, keepdims=True) + EPS_NORM)
            lat_ref[there, 0:QR] = (ql * gains[0:1, 0:QR]).astype(BF)
            lat_ref[there, QR : QR + KVR] = (kl * gains[0:1, QR : QR + KVR]).astype(BF)
            moved = pltpu.roll(jnp.where(lane < ROPE, raw, 0.0), NOPE, 1)
            turned = jnp.where(lane < NOPE + 16, -pltpu.roll(moved, 128 - 16, 1), pltpu.roll(moved, 16, 1))
            seg = (own_index(e) >= length).astype(F32)
            mask = jnp.where(lane == HEAD, 1.0 - seg, jnp.where(lane == HEAD + 1, seg, 0.0)) * MASK_VALUE
            lat_ref[there, QR + KVR : LAT_WIDE] = (moved * tcos[here, :] + turned * tsin[here, :] + mask).astype(BF)
            handover(e).start()

    def serve(n):
        @pl.when(jnp.logical_and(is_mid, n < count))
        def _():
            first(n)

        @pl.when(jnp.logical_and(is_mid, jnp.logical_and(n >= LAT_DEPTH, n < count + LAT_DEPTH)))
        def _():
            second(n - LAT_DEPTH)
            finish_rows(n - LAT_DEPTH)

        @pl.when(jnp.logical_and(is_end, n < count))
        def _():
            to_mid(n).wait_send()
            to_end(n).wait_recv()
            finish_rows(n)

    each(2, serve)
    forward_u(0)
    each(4, lambda n: serve(n + 2))
    forward(0)
    each(4, lambda n: serve(n + 6))
    forward(1)
    final_u(0)
    each(count + LAT_DEPTH - 10, lambda n: serve(n + 10))
    drain_u(0)
    for p in range(peers):
        upg_ref[p] = up_all[p, 0, pl.ds(pl.multiple_of(core * 128, 128), 128), :]
    final(0)
    final(1)

    @pl.when(is_mid)
    def _():
        def sent(k):
            over(k).wait_send()
            to_end(k).wait_send()

        each(count, sent)

    drain(0)
    drain(1)

    def passed(e):
        handover(e).wait_send()
        here = pl.ds(pl.multiple_of((1 - core) * rows + e * LAT_LINE, LAT_LINE), LAT_LINE)
        remote(lat_ref.at[here], lat_ref.at[here], c_send.at[e], c_recv.at[e], {"ctx": 1 - core}).wait_recv()

    each(rows // LAT_LINE, passed)


def spread(peers):
    index = np.arange(KVR + ROPE)
    return jnp.asarray((index // 36 * 48 + index % 36)[:, None] == np.arange(peers * 48)[None], BF)


def latent_forward(x, gain, gain2, piece, up, length, gate_up):
    rows, width = x.shape
    peers = lax.axis_size("fsdp") * lax.axis_size("ctx")
    slot = rows * lax.axis_size("ctx")
    wide = rows + LAT_LINE
    count = wide // LAT_LINE
    sel = spread(peers)
    frequency = (ROPE_BASE ** (-2.0 * np.arange(ROPE // 2) / ROPE)).astype(np.float32)
    vmem = pl.BlockSpec(memory_space=pltpu.VMEM)
    dma = pltpu.SemaphoreType.DMA
    return pl.pallas_call(
        latent_kernel,
        out_shape=[
            jax.ShapeDtypeStruct((LAT_WIDE, width), BF),
            jax.ShapeDtypeStruct((wide, LAT_WIDE), BF),
            jax.ShapeDtypeStruct((slot, LAT_WIDE), BF),
            jax.ShapeDtypeStruct((ROPE // 2, slot), F32),
            jax.ShapeDtypeStruct((ROPE // 2, slot), F32),
            jax.ShapeDtypeStruct((16, slot), BF),
            jax.ShapeDtypeStruct((peers, up.shape[1] // 2, up.shape[2]), BF),
            jax.ShapeDtypeStruct((rows, 128), F32),
            jax.ShapeDtypeStruct((rows, 128), F32),
            jax.ShapeDtypeStruct((16, QR + KVR), F32),
            jax.ShapeDtypeStruct((peers,) + gate_up.shape, BF),
        ],
        in_specs=[vmem] * 8 + [pl.BlockSpec(memory_space=pltpu.SMEM), pl.BlockSpec(memory_space=pl.ANY)],
        out_specs=[vmem] * 10 + [pl.BlockSpec(memory_space=pl.ANY)],
        scratch_shapes=[
            pltpu.VMEM((peers, 1, PIECE, width), BF),
            pltpu.VMEM((peers,) + up.shape, BF),
            pltpu.VMEM((wide, LAT_WIDE), BF),
            pltpu.VMEM((wide, LAT_WIDE), BF),
            pltpu.VMEM((wide, LAT_WIDE), BF),
            pltpu.VMEM((peers * 48, width), BF),
        ]
        + [dma((rows // LAT_LINE,))] * 2
        + [dma((count,))] * 6
        + [dma((1,))] * (2 * GATHER_SEMS)
        + [dma((2,))] * GATHER_SEMS,
        compiler_params=pltpu.CompilerParams(collective_id=0, has_side_effects=True, vmem_limit_bytes=62 * MIB),
        cost_estimate=pl.CostEstimate(flops=rows * LAT_WIDE * width * 2, bytes_accessed=150 * MIB, transcendentals=0),
        name="latent_forward",
    )(x, gain, gain2, piece, up, sel, jnp.asarray(frequency[:, None]), jnp.asarray(np.tile(frequency, 8)[None]), length, gate_up)


LINE = 16
DEPTH = 4
MLP_ROWS = 256
TILES = ((0, 384), (384, 384), (768, 384), (1152, 448))


def line_places(z):
    is_end = jnp.logical_or(z == 0, z == 3)
    partner = jnp.where(z == 0, 1, jnp.where(z == 3, 2, jnp.where(z == 1, 0, 3)))
    return is_end, jnp.logical_not(is_end), partner, jnp.where(z == 1, 2, 1)


def line_barrier(is_mid, is_end, partner, across):
    barrier = pltpu.get_barrier_semaphore()
    pl.semaphore_signal(barrier, inc=1, device_id={"tp": partner}, device_id_type=MESH)

    @pl.when(is_mid)
    def _():
        pl.semaphore_signal(barrier, inc=1, device_id={"tp": across}, device_id_type=MESH)
        pl.semaphore_wait(barrier, 2)

    @pl.when(is_end)
    def _():
        pl.semaphore_wait(barrier, 1)


def line_copies(source, near, cross, total, sems, partner, across, line=LINE):
    in_send, in_recv, mid_send, mid_recv, out_send, out_recv = sems

    def piece(k):
        return pl.ds(pl.multiple_of(k * line, line), line)

    def copy(src, dst, send, recv, k, to):
        return pltpu.make_async_remote_copy(
            src_ref=src.at[piece(k)], dst_ref=dst.at[piece(k)], send_sem=send.at[k], recv_sem=recv.at[k],
            device_id={"tp": to}, device_id_type=MESH,
        )

    to_mid = lambda k: copy(source, near, in_send, in_recv, k, partner)
    over = lambda k: copy(near, cross, mid_send, mid_recv, k, across)
    to_end = lambda k: copy(total, total, out_send, out_recv, k, partner)

    def first(k):
        to_mid(k).wait_recv()
        near[piece(k)] = source[piece(k)] + near[piece(k)]
        over(k).start()

    def second(k):
        over(k).wait_recv()
        total[piece(k)] = near[piece(k)] + cross[piece(k)]
        to_end(k).start()

    return to_mid, over, to_end, first, second


def each(count, body):
    def step(k, carry):
        body(k)
        return carry

    lax.fori_loop(0, count, step, 0)


def block_kernel(
    att_ref, x_ref, out_ref, gain_ref, live_ref, seed_any, gu_any, down_any,
    hid_any, dn_any, mo_any, n2t_any, act_any, dg_any, du_any,
    xb, near, cross, total, gu, down, n2, n2t, seed, d_all, act, dg, du,
    load_sem, down_sem, seed_sem, hid_sem, dn_sem, mo_sem, n2t_sem, act_sem, dg_sem, du_sem, *sems,
):
    z = lax.axis_index("tp")
    is_end, is_mid, partner, across = line_places(z)
    to_mid, over, to_end, first, second = line_copies(xb, near, cross, total, sems, partner, across)
    count = xb.shape[0] // LINE
    group = MLP_ROWS // LINE
    groups = count // group
    width = x_ref.shape[1]

    def rows_of(m):
        return pl.ds(pl.multiple_of(m * MLP_ROWS, MLP_ROWS), MLP_ROWS)

    peers, shard = gu_any.shape[0], gu_any.shape[2]
    load_gu = lambda p, i: pltpu.make_async_copy(gu_any.at[p, i], gu.at[i, pl.ds(p * shard, shard)], load_sem.at[p, i])
    load_down = pltpu.make_async_copy(down_any, down, down_sem)
    load_seed = lambda m: pltpu.make_async_copy(seed_any.at[rows_of(m)], seed, seed_sem.at[m])
    save_hid = lambda m: pltpu.make_async_copy(total.at[rows_of(m)], hid_any.at[rows_of(m)], hid_sem.at[m])
    save_dn = lambda m: pltpu.make_async_copy(xb.at[rows_of(m)], dn_any.at[rows_of(m)], dn_sem.at[m])
    save_mo = lambda m, n: pltpu.make_async_copy(
        cross.at[rows_of(m), pl.ds(n * width, width)], mo_any.at[n, rows_of(m)], mo_sem.at[m, n]
    )
    save_n2t = lambda m: pltpu.make_async_copy(n2t, n2t_any.at[:, rows_of(m)], n2t_sem.at[m])
    save_act = lambda m: pltpu.make_async_copy(act, act_any.at[rows_of(m)], act_sem.at[m])
    save_dg = lambda m: pltpu.make_async_copy(dg, dg_any.at[rows_of(m)], dg_sem.at[m])
    save_du = lambda m: pltpu.make_async_copy(du, du_any.at[rows_of(m)], du_sem.at[m])

    load_seed(0).start()
    load_down.start()
    for p in range(peers):
        load_gu(p, 0).start()
        load_gu(p, 1).start()
    line_barrier(is_mid, is_end, partner, across)

    mine = pl.ds(pl.multiple_of(z * width, 128), width)
    per = 128

    def project(p):
        rows = pl.ds(pl.multiple_of(p * per, per), per)
        part = dot_nt(att_ref[:, rows].astype(F32).T.astype(BF), out_ref[...]) * RESIDUAL_SCALE
        xb[rows, :] = part.astype(BF)
        xb[rows, mine] = (xb[rows, mine].astype(F32) + x_ref[rows, :].astype(F32)).astype(BF)

        @pl.when(is_end)
        def _():
            each(per // LINE, lambda n: to_mid(p * (per // LINE) + n).start())

    each(xb.shape[0] // per, project)

    @pl.when(is_mid)
    def _():
        each(DEPTH, first)

    load_down.wait()
    ahead = group // len(TILES) // groups

    def seed_product(m):
        load_seed(m).wait()

        def weigh(r):
            here = pl.ds(pl.multiple_of(r * 32, 32), 32)
            live = live_ref[pl.ds(pl.multiple_of(m * MLP_ROWS + r * 32, 32), 32), :]
            seed[here, :] = (seed[here, :].astype(F32) * (live * RESIDUAL_SCALE)).astype(BF)

        each(MLP_ROWS // 32, weigh)
        for t, (at, size) in enumerate(TILES):
            d_all[rows_of(m), pl.ds(at, size)] = dot_nn(seed[...], down[:, pl.ds(at, size)]).astype(BF)

            @pl.when(is_mid)
            def _():
                def both(v):
                    k = (m * len(TILES) + t) * ahead + v
                    first(k + DEPTH)
                    second(k)

                each(ahead, both)

        @pl.when(m + 1 < groups)
        def _():
            load_seed(m + 1).start()

    each(groups, seed_product)

    def mlp(m):
        rows = rows_of(m)

        @pl.when(is_end)
        def _():
            def arrive(n):
                to_mid(m * group + n).wait_send()
                to_end(m * group + n).wait_recv()

            each(group, arrive)

        def serve(n):
            def one(v):
                k = (m + 1) * group + DEPTH + n * (group // 8) + v

                @pl.when(jnp.logical_and(is_mid, k < count))
                def _():
                    first(k)

                @pl.when(jnp.logical_and(is_mid, k < count + DEPTH))
                def _():
                    second(k - DEPTH)

            each(group // 8, one)

        save_hid(m).start()

        @pl.when(m > 0)
        def _():
            save_n2t(m - 1).wait()
            save_act(m - 1).wait()
            save_dg(m - 1).wait()
            save_du(m - 1).wait()

        def normalize(r):
            here = pl.ds(pl.multiple_of(r * 32, 32), 32)
            h = total[pl.ds(pl.multiple_of(m * MLP_ROWS + r * 32, 32), 32), :].astype(F32)
            factor = lax.rsqrt(jnp.mean(h * h, axis=1, keepdims=True) + EPS_NORM)
            n2[here, :] = (h * factor * gain_ref[...]).astype(BF)

        each(MLP_ROWS // 32, normalize)

        def turn(c):
            cols = pl.ds(pl.multiple_of(c * 256, 256), 256)
            n2t[cols, :] = n2[:, cols].astype(F32).T.astype(BF)

        each(D // 256, turn)
        save_n2t(m).start()
        @pl.when(m == 0)
        def _():
            for p in range(peers):
                load_gu(p, 0).wait()
                load_gu(p, 1).wait()

        for t, (at, size) in enumerate(TILES):
            cols = pl.ds(at, size)
            g = dot_nn(n2[...], gu[0, :, cols])
            u = dot_nn(n2[...], gu[1, :, cols])
            d = d_all[rows, cols].astype(F32)
            sig = jax.nn.sigmoid(g)
            act[:, cols] = (g * sig * u).astype(BF)
            dg[:, cols] = (d * u * sig * (1.0 + g * (1.0 - sig))).astype(BF)
            du[:, cols] = (d * g * sig).astype(BF)
            serve(t)
        save_act(m).start()
        save_dg(m).start()
        save_du(m).start()

        for n in range(4):
            cols = pl.ds(n * 640, 640)
            xb[rows, cols] = (dot_nt(dg[...], gu[0, cols, :]) + dot_nt(du[...], gu[1, cols, :])).astype(BF)
            cross[rows, cols] = dot_nt(act[...], down[cols, :]).astype(BF)
            serve(4 + n)
        save_dn(m).start()
        for n in range(4):
            save_mo(m, n).start()

    each(groups, mlp)

    def finish(m):
        save_hid(m).wait()
        save_dn(m).wait()
        for n in range(4):
            save_mo(m, n).wait()

    each(groups, finish)
    save_n2t(groups - 1).wait()
    save_act(groups - 1).wait()
    save_dg(groups - 1).wait()
    save_du(groups - 1).wait()

    @pl.when(is_mid)
    def _():
        def sent(k):
            over(k).wait_send()
            to_end(k).wait_send()

        each(count, sent)


def block_forward(att, x, out_t, gain, live, seed, gate_up, down_t):
    rows, width = x.shape
    hidden_units = down_t.shape[1]
    count, groups = rows // LINE, rows // MLP_ROWS
    vmem = pl.BlockSpec(memory_space=pltpu.VMEM)
    anywhere = pl.BlockSpec(memory_space=pl.ANY)
    wide = jax.ShapeDtypeStruct((rows, D), BF)
    units = jax.ShapeDtypeStruct((rows, hidden_units), BF)
    dma = pltpu.SemaphoreType.DMA
    return pl.pallas_call(
        block_kernel,
        out_shape=[wide, wide, jax.ShapeDtypeStruct((4, rows, width), BF), jax.ShapeDtypeStruct((D, rows), BF), units, units, units],
        in_specs=[vmem] * 5 + [anywhere] * 3,
        out_specs=[anywhere] * 7,
        scratch_shapes=[pltpu.VMEM((rows, D), BF)] * 4
        + [
            pltpu.VMEM((2, D, hidden_units), BF),
            pltpu.VMEM(down_t.shape, BF),
            pltpu.VMEM((MLP_ROWS, D), BF),
            pltpu.VMEM((D, MLP_ROWS), BF),
            pltpu.VMEM((MLP_ROWS, D), BF),
            pltpu.VMEM((rows, hidden_units), BF),
        ]
        + [pltpu.VMEM((MLP_ROWS, hidden_units), BF)] * 3
        + [dma(gate_up.shape[:2]), dma]
        + [dma((groups,))] * 3
        + [dma((groups, 4))]
        + [dma((groups,))] * 4
        + [dma((count,))] * 6,
        compiler_params=pltpu.CompilerParams(collective_id=3, has_side_effects=True, vmem_limit_bytes=63 * MIB),
        cost_estimate=pl.CostEstimate(flops=rows * D * hidden_units * 12, bytes_accessed=400 * MIB, transcendentals=0),
        name="block_forward",
    )(att, x, out_t, gain, live, seed, gate_up, down_t)


LAG = 8
ROWS = 32
LOAD = 128


def total_square(v):
    v = v.astype(F32)
    return jnp.sum(jnp.sum(v * v, axis=0, keepdims=True), axis=1, keepdims=True)


def grad_kernel(
    live_ref, gain_ref, dnp_any, hid_any, cot_any, n2t_any, dg_any, du_any, act_any,
    sa_any, dh_any, gain_out, grad_any, square_out,
    near, cross, total, cin, stage, xin, yin2, yin, xin2, lhs, rhs, hbuf, cbuf, sbuf, dbuf, prep,
    total_sem, lhs_sem, rhs_sem, h_sem, c_sem, sa_sem, dh_sem, prep_sem, out_sem,
    core_send, core_recv, x_send, x_recv, y2_send, y2_recv, y_send, y_recv, x2_send, x2_recv, *sems,
):
    z, core, place = lax.axis_index("tp"), lax.axis_index("ctx"), lax.axis_index("fsdp")
    y, x = place // 2, place % 2
    is_end, is_mid, partner, across = line_places(z)
    to_mid, over, to_end, _, _ = line_copies(dnp_any, near, cross, total, sems, partner, across)
    count = total.shape[0] // LINE
    width = dh_any.shape[1]
    half = yin.shape[1]
    block = 2 * half
    mine = pl.ds(pl.multiple_of(z * width, 128), width)
    to_core, to_x, to_y = {"ctx": 1 - core}, {"fsdp": y * 2 + 1 - x}, {"fsdp": (1 - y) * 2 + x}

    def piece(k):
        return pl.ds(pl.multiple_of(k * LINE, LINE), LINE)

    def band(e):
        return pl.ds(pl.multiple_of(e * ROWS, ROWS), ROWS)

    bands = total.shape[0] // ROWS
    twice = ROWS // LINE

    def remote(src, dst, send, recv, to):
        return pltpu.make_async_remote_copy(
            src_ref=src, dst_ref=dst, send_sem=send, recv_sem=recv, device_id=to, device_id_type=MESH
        )

    local = pltpu.make_async_copy
    load_total = local(dnp_any, total, total_sem)
    load_lhs = local(n2t_any, lhs, lhs_sem)
    right = (dg_any, du_any, act_any)
    load_rhs = lambda i: local(right[i], rhs.at[i % 2], rhs_sem.at[i])
    rows_of = lambda g: pl.ds(pl.multiple_of(g * LOAD, LOAD), LOAD)
    load_h = lambda g: local(hid_any.at[rows_of(g)], hbuf.at[g % 2], h_sem.at[g])
    load_c = lambda g: local(cot_any.at[rows_of(g)], cbuf.at[g % 2], c_sem.at[g])
    save_sa = lambda e: local(sbuf.at[e % 2], sa_any.at[band(e)], sa_sem.at[e])
    save_dh = lambda e: local(dbuf.at[e % 2], dh_any.at[band(e)], dh_sem.at[e])

    load_lhs.start()
    load_rhs(0).start()
    load_rhs(1).start()
    load_h(0).start()
    load_c(0).start()

    @pl.when(is_mid)
    def _():
        load_total.start()

    barrier = pltpu.get_barrier_semaphore()
    for to in (to_core, to_x, to_y, {"tp": partner}):
        pl.semaphore_signal(barrier, inc=1, device_id=to, device_id_type=MESH)

    @pl.when(is_mid)
    def _():
        pl.semaphore_signal(barrier, inc=1, device_id={"tp": across}, device_id_type=MESH)
        pl.semaphore_wait(barrier, 5)

    @pl.when(is_end)
    def _():
        pl.semaphore_wait(barrier, 4)
        each(count, lambda k: to_mid(k).start())

    gain_out[...] = jnp.zeros_like(gain_out)

    @pl.when(is_mid)
    def _():
        load_total.wait()

    def finish_rows(e):
        per = LOAD // ROWS
        g = e // per

        @pl.when(e % per == 0)
        def _():
            load_h(g).wait()
            load_c(g).wait()

            @pl.when(g + 1 < bands // per)
            def _():
                load_h(g + 1).start()
                load_c(g + 1).start()

        @pl.when(e >= 2)
        def _():
            save_sa(e - 2).wait()
            save_dh(e - 2).wait()

        here = pl.ds(pl.multiple_of((e % per) * ROWS, ROWS), ROWS)
        live = live_ref[band(e), :]

        def grads_of(dn, h, dy, gain, factor, inner):
            return dy * live + factor * (dn * gain) - h * (factor * factor * factor * inner)

        dn = total[band(e), :].astype(F32)
        h = hbuf[g % 2, here, :].astype(F32)
        factor = lax.rsqrt(jnp.mean(h * h, axis=1, keepdims=True) + EPS_NORM)
        inner = jnp.mean(dn * gain_ref[...] * h, axis=1, keepdims=True)
        dy = cbuf[g % 2, here, :].astype(F32)
        sbuf[e % 2] = (RESIDUAL_SCALE * grads_of(dn, h, dy, gain_ref[...], factor, inner)).astype(BF)
        own_dn = total[band(e), mine].astype(F32)
        own_h = hbuf[g % 2, here, mine].astype(F32)
        own_dy = cbuf[g % 2, here, mine].astype(F32)
        dbuf[e % 2] = grads_of(own_dn, own_h, own_dy, gain_ref[:, mine], factor, inner)
        gain_out[...] += jnp.sum(own_dn * own_h * factor, axis=0, keepdims=True)
        save_sa(e).start()
        save_dh(e).start()

    def serve(n):
        @pl.when(jnp.logical_and(is_mid, n < count))
        def _():
            to_mid(n).wait_recv()
            near[piece(n)] = total[piece(n)] + near[piece(n)]
            over(n).start()

        @pl.when(jnp.logical_and(is_mid, jnp.logical_and(n >= DEPTH, n < count + DEPTH)))
        def _():
            k = n - DEPTH
            over(k).wait_recv()
            total[piece(k)] = near[piece(k)] + cross[piece(k)]
            to_end(k).start()

            @pl.when(k % twice == twice - 1)
            def _():
                finish_rows(k // twice)

        @pl.when(jnp.logical_and(is_end, jnp.logical_and(n >= LAG, n < count + LAG)))
        def _():
            k = n - LAG
            to_mid(k).wait_send()
            to_end(k).wait_recv()

            @pl.when(k % twice == twice - 1)
            def _():
                finish_rows(k // twice)

    def flip(v, by):
        return v + by - 2 * v * by

    def spot(j):
        down, over_x = 1 - j // 2, 1 - j % 2
        return down, over_x, flip(y, down), flip(x, over_x)

    def tile(i, f, parity):
        rows = pl.ds(pl.multiple_of((2 * f + parity) * block, 16), block)
        return dot_nn(lhs[rows, :], rhs[i % 2])

    upper, lower = pl.ds(0, half), pl.ds(half, half)
    core_copy = lambda i, j, f: remote(stage.at[j % 2], cin.at[i, f], core_send.at[i, j], core_recv.at[i, f], to_core)
    x_copy = lambda i, f, yy: remote(cin.at[i, f, upper], xin.at[i, yy], x_send.at[i, yy], x_recv.at[i, yy], to_x)
    y2_copy = lambda i, f, xx: remote(cin.at[i, f, lower], yin2.at[i, xx], y2_send.at[i, xx], y2_recv.at[i, xx], to_y)
    y_copy = lambda i: remote(xin.at[i, 1 - y], yin.at[i], y_send.at[i], y_recv.at[i], to_y)
    x2_copy = lambda i: remote(yin2.at[i, 1 - x], xin2.at[i], x2_send.at[i], x2_recv.at[i], to_x)
    save_upper = lambda i: local(yin.at[i], grad_any.at[i, upper], out_sem.at[i, 0])
    save_lower = lambda i: local(xin2.at[i], grad_any.at[i, lower], out_sem.at[i, 1])

    def plus(a, b):
        return (a.astype(F32) + b.astype(F32)).astype(BF)

    def products(i, n0):
        def for_other(j):
            _, _, yy, xx = spot(j)
            f = yy * 2 + xx

            @pl.when(j >= 2)
            def _():
                core_copy(i, j - 2, f).wait_send()

            stage[j % 2] = tile(i, f, 1 - core).astype(BF)
            core_copy(i, j, f).start()
            serve(n0 + j)

        each(4, for_other)

        def for_own(j):
            down, over_x, yy, xx = spot(j)
            f = yy * 2 + xx
            own = tile(i, f, core)
            core_copy(i, j, f).wait_recv()
            cin[i, f] = (own + cin[i, f].astype(F32)).astype(BF)

            @pl.when(over_x == 1)
            def _():
                x_copy(i, f, yy).start()

            @pl.when(down == 1)
            def _():
                y2_copy(i, f, xx).start()

            serve(n0 + 4 + j)

        each(4, for_own)
        for j in (2, 3):
            core_copy(i, j, 0).wait_send()

    def first_stage(i):
        x_copy(i, 0, 1 - y).wait_recv()
        xin[i, 1 - y] = plus(xin[i, 1 - y], cin[i, (1 - y) * 2 + x, upper])
        y_copy(i).start()
        y2_copy(i, 0, 1 - x).wait_recv()
        yin2[i, 1 - x] = plus(yin2[i, 1 - x], cin[i, y * 2 + 1 - x, lower])
        x2_copy(i).start()
        x_copy(i, 0, y).wait_recv()
        xin[i, y] = plus(xin[i, y], cin[i, y * 2 + x, upper])
        y2_copy(i, 0, x).wait_recv()
        yin2[i, x] = plus(yin2[i, x], cin[i, y * 2 + x, lower])

    def second_stage(i):
        y_copy(i).wait_recv()
        yin[i] = plus(yin[i], xin[i, y])
        save_upper(i).start()
        x2_copy(i).wait_recv()
        xin2[i] = plus(xin2[i], yin2[i, x])
        save_lower(i).start()
        square = total_square(yin[i]) + total_square(xin2[i])
        square_out[i : i + 1, :] = jnp.broadcast_to(square, (1, 128))

    square_out[...] = jnp.zeros_like(square_out)
    load_lhs.wait()
    load_rhs(0).wait()
    products(0, 0)
    load_rhs(2).start()
    load_rhs(1).wait()
    products(1, 8)

    cols_of = lambda c: pl.ds(pl.multiple_of(c * 256, 256), 256)
    load_prep = lambda c: local(cot_any.at[:, cols_of(c)], prep.at[c % 2], prep_sem.at[c])
    load_prep(0).start()
    groups = D // 256

    def turn(c):
        load_prep(c).wait()

        @pl.when(c + 1 < groups)
        def _():
            load_prep(c + 1).start()

        seed = prep[c % 2].astype(F32) * (live_ref[...] * RESIDUAL_SCALE)
        lhs[cols_of(c), :] = seed.T.astype(BF)
        serve(16 + c)

    each(groups, turn)
    first_stage(0)
    load_rhs(2).wait()
    products(2, 16 + groups)
    served = 24 + groups

    def serve_until(stop, served):
        each(stop - served, lambda n: serve(n + served))
        return stop

    first_stage(1)
    served = serve_until(42, served)
    second_stage(0)
    served = serve_until(50, served)
    first_stage(2)
    served = serve_until(58, served)
    second_stage(1)
    serve_until(count + LAG, served)
    second_stage(2)
    for i in range(3):
        for v in range(2):
            x_copy(i, 0, v).wait_send()
            y2_copy(i, 0, v).wait_send()
        y_copy(i).wait_send()
        x2_copy(i).wait_send()
        save_upper(i).wait()
        save_lower(i).wait()
    for e in (bands - 2, bands - 1):
        save_sa(e).wait()
        save_dh(e).wait()

    @pl.when(is_mid)
    def _():
        def sent(k):
            over(k).wait_send()
            to_end(k).wait_send()

        each(count, sent)


def grad_reduce(live, gain, d_normed_part, hidden, cotangent, normed_t, d_gate, d_up, activation):
    rows = hidden.shape[0]
    units = d_gate.shape[1]
    width = D // lax.axis_size("tp")
    shard = D // (lax.axis_size("fsdp") * lax.axis_size("ctx"))
    count = rows // LINE
    vmem = pl.BlockSpec(memory_space=pltpu.VMEM)
    anywhere = pl.BlockSpec(memory_space=pl.ANY)
    dma = pltpu.SemaphoreType.DMA
    scratch = lambda *shape: pltpu.VMEM(shape, BF)
    return pl.pallas_call(
        grad_kernel,
        out_shape=[
            jax.ShapeDtypeStruct((rows, D), BF),
            jax.ShapeDtypeStruct((rows, width), F32),
            jax.ShapeDtypeStruct((1, width), F32),
            jax.ShapeDtypeStruct((3, shard, units), BF),
            jax.ShapeDtypeStruct((8, 128), F32),
        ],
        in_specs=[vmem] * 2 + [anywhere] * 7,
        out_specs=[anywhere, anywhere, vmem, anywhere, vmem],
        scratch_shapes=[scratch(rows, D)] * 3
        + [
            scratch(3, 4, shard, units),
            scratch(2, shard, units),
            scratch(3, 2, shard // 2, units),
            scratch(3, 2, shard // 2, units),
            scratch(3, shard // 2, units),
            scratch(3, shard // 2, units),
            scratch(D, rows),
            scratch(2, rows, units),
            scratch(2, LOAD, D),
            scratch(2, LOAD, D),
            scratch(2, ROWS, D),
            pltpu.VMEM((2, ROWS, width), F32),
            scratch(2, rows, 256),
        ]
        + [dma, dma, dma((3,)), dma((rows // LOAD,)), dma((rows // LOAD,)), dma((rows // ROWS,)), dma((rows // ROWS,)), dma((D // 256,)), dma((3, 2))]
        + [dma((3, 4))] * 2
        + [dma((3, 2))] * 4
        + [dma((3,))] * 4
        + [dma((count,))] * 6,
        compiler_params=pltpu.CompilerParams(collective_id=4, has_side_effects=True, vmem_limit_bytes=63 * MIB),
        cost_estimate=pl.CostEstimate(flops=rows * D * units * 6, bytes_accessed=400 * MIB, transcendentals=0),
        name="grad_reduce",
    )(live, gain, d_normed_part, hidden, cotangent, normed_t, d_gate, d_up, activation)


PACK = 576
HALF = PACK // 2
SHARE = 256


def torus(s1, xin, yin2, yin, xin2, sems, x, y, to_x, to_y):
    x_send, x_recv, y2_send, y2_recv, y_send, y_recv, x2_send, x2_recv = sems
    half = yin.shape[0]
    upper, lower = pl.ds(0, half), pl.ds(half, half)

    def remote(src, dst, send, recv, to):
        return pltpu.make_async_remote_copy(
            src_ref=src, dst_ref=dst, send_sem=send, recv_sem=recv, device_id=to, device_id_type=MESH
        )

    def plus(a, b):
        return (a.astype(F32) + b.astype(F32)).astype(BF)

    x_copy = lambda v: remote(s1.at[v * 2 + 1 - x, upper], xin.at[v], x_send.at[v], x_recv.at[v], to_x)
    y2_copy = lambda v: remote(s1.at[(1 - y) * 2 + v, lower], yin2.at[v], y2_send.at[v], y2_recv.at[v], to_y)
    y_copy = remote(xin.at[1 - y], yin, y_send.at[0], y_recv.at[0], to_y)
    x2_copy = remote(yin2.at[1 - x], xin2, x2_send.at[0], x2_recv.at[0], to_x)

    def begin():
        x_copy(1 - y).start()
        y2_copy(1 - x).start()
        x_copy(y).start()
        y2_copy(x).start()

    def middle():
        x_copy(1 - y).wait_recv()
        xin[1 - y] = plus(xin[1 - y], s1[(1 - y) * 2 + x, upper])
        y_copy.start()
        y2_copy(1 - x).wait_recv()
        yin2[1 - x] = plus(yin2[1 - x], s1[y * 2 + 1 - x, lower])
        x2_copy.start()
        x_copy(y).wait_recv()
        xin[y] = plus(xin[y], s1[y * 2 + x, upper])
        y2_copy(x).wait_recv()
        yin2[x] = plus(yin2[x], s1[y * 2 + x, lower])

    def last(out):
        y_copy.wait_recv()
        out[upper, :] = plus(yin[...], xin[y])
        x2_copy.wait_recv()
        out[lower, :] = plus(xin2[...], yin2[x])

    def drain():
        for v in range(2):
            x_copy(v).wait_send()
            y2_copy(v).wait_send()
        y_copy.wait_send()
        x2_copy.wait_send()

    return begin, middle, last, drain


def latent_back_kernel(
    dq_ref, de_ref, dkr_ref, up_ref, sum_ref, w_ref, x_ref, gain_ref, dh_ref, tcos, tsin, gains, gout_ref, gq_ref, gkv_ref,
    sel_ref, b2_ref, square_ref, limit_ref, fold_ref,
    gin_ref, pack_out, wd_out, small_out, scalar_out, gq_out, gkv_out,
    uq, ukv, away, arrived, xb, near, cross, total, dl, dlt, xg, weight, w_pack, small, small_in, scal_in,
    s1, cin, xin, yin2, yin, xin2, s1w, cinw, xinw, yin2w, yinw, xin2w,
    lat_send, lat_recv, out_send, out_recv, q_send, q_recv, kv_send, kv_recv, w_send, w_recv,
    small_send, small_recv, scal_send, scal_recv, *sems,
):
    z, core, place = lax.axis_index("tp"), lax.axis_index("ctx"), lax.axis_index("fsdp")
    y, x = place // 2, place % 2
    is_end, is_mid, partner, across = line_places(z)
    line_sems, pack_sems, w_sems = sems[:6], sems[6:14], sems[14:22]
    to_mid, over, to_end, first, second = line_copies(xb, near, cross, total, line_sems, partner, across, LAT_LINE)
    count = xb.shape[0] // LAT_LINE
    rows = xb.shape[0]
    peers = up_ref.shape[0]
    me = place * 2 + core
    to_core, to_x, to_y = {"ctx": 1 - core}, {"fsdp": y * 2 + 1 - x}, {"fsdp": (1 - y) * 2 + x}

    def remote(src, dst, send, recv, to):
        return pltpu.make_async_remote_copy(
            src_ref=src, dst_ref=dst, send_sem=send, recv_sem=recv, device_id=to, device_id_type=MESH
        )

    def peer(d):
        to = lax.rem(me + d, peers)
        return {"fsdp": to // 2, "ctx": lax.rem(to, 2)}

    barrier = pltpu.get_barrier_semaphore()
    for d in range(1, peers):
        pl.semaphore_signal(barrier, inc=1, device_id=peer(d), device_id_type=MESH)
    for d in range(1, 4):
        pl.semaphore_signal(barrier, inc=1, device_id={"tp": lax.rem(z + d, 4)}, device_id_type=MESH)
    pl.semaphore_wait(barrier, peers + 2)

    def piece(e):
        return pl.ds(pl.multiple_of(e * LAT_LINE, LAT_LINE), LAT_LINE)

    def span(f, parity, size):
        return pl.ds(pl.multiple_of((2 * f + parity) * size, size), size)

    slot_q, slot_kv = pl.ds(320 + 96 * core, 96), pl.ds(512 + 32 * core, 32)
    other_q, other_kv = pl.ds(320 + 96 * (1 - core), 96), pl.ds(512 + 32 * (1 - core), 32)
    out_copy = lambda f: remote(gout_ref.at[span(f, 1 - core, 320)], cin.at[f], out_send.at[f], out_recv.at[f], to_core)
    q_copy = lambda f: remote(gq_ref.at[span(f, 1 - core, 96)], s1.at[f, slot_q], q_send.at[f], q_recv.at[f], to_core)
    kv_copy = lambda f: remote(gkv_ref.at[span(f, 1 - core, 32)], s1.at[f, slot_kv], kv_send.at[f], kv_recv.at[f], to_core)
    q_got = lambda f: remote(gq_ref.at[span(f, 1 - core, 96)], s1.at[f, other_q], q_send.at[f], q_recv.at[f], to_core)
    kv_got = lambda f: remote(gkv_ref.at[span(f, 1 - core, 32)], s1.at[f, other_kv], kv_send.at[f], kv_recv.at[f], to_core)

    for p in range(peers):
        uq[p * 96 : (p + 1) * 96, :] = up_ref[p, 0:96, :]
        ukv[p * 32 : (p + 1) * 32, :] = up_ref[p, 96:128, :]

    lane = lax.broadcasted_iota(jnp.int32, (1, 128), 1)
    block = lambda e: pl.ds(pl.multiple_of(e * SHARE, SHARE), SHARE)
    hand = lambda e: remote(away.at[block(e)], arrived.at[block(e)], lat_send.at[e], lat_recv.at[e], to_core)
    shares = rows // SHARE

    def share(at):
        here = pl.ds(pl.multiple_of(at, SHARE), SHARE)
        q = dot_nt(dq_ref[here, :], uq[...])
        kv = dot_nt(de_ref[here, :], ukv[...])
        rope = jnp.where(lane < ROPE, pltpu.roll(dkr_ref[here, :], NOPE, 1), 0.0)
        return q, kv, rope

    def send_away(e):
        q, kv, rope = share((1 - core) * rows + e * SHARE)
        away[block(e), 0:QR] = q.astype(BF)
        away[block(e), QR : QR + KVR] = kv.astype(BF)
        away[block(e), QR + KVR : LAT_WIDE] = rope.astype(BF)
        hand(e).start()

    each(shares, send_away)
    for f in range(4):
        out_copy(f).start()
        q_copy(f).start()
        kv_copy(f).start()

    def keep(e):
        q, kv, rope = share(core * rows + e * SHARE)
        hand(e).wait_recv()
        got = arrived[block(e), :].astype(F32)
        xb[block(e), 0:QR] = (q + got[:, 0:QR]).astype(BF)
        xb[block(e), QR : QR + KVR] = (kv + got[:, QR : QR + KVR]).astype(BF)
        xb[block(e), QR + KVR : LAT_WIDE] = (rope + got[:, QR + KVR :]).astype(BF)

        @pl.when(is_end)
        def _():
            each(SHARE // LAT_LINE, lambda n: to_mid(e * (SHARE // LAT_LINE) + n).start())

    each(shares, keep)

    small[...] = jnp.zeros_like(small)
    small[2:3, 0 : b2_ref.shape[1]] = b2_ref[...]
    stat_lane = lax.broadcasted_iota(jnp.int32, (1, LAT_WIDE), 1)
    stat_lane = jnp.logical_and(stat_lane >= LAT, stat_lane < LAT + 8)
    gain_q, gain_kv = gains[0:1, 0:QR], gains[0:1, QR : QR + KVR]

    def through(d, v, gain):
        factor = lax.rsqrt(jnp.mean(v * v, axis=1, keepdims=True) + EPS_NORM)
        scaled = d * gain
        gain_grad = jnp.sum(d * v * factor, axis=0, keepdims=True)
        return factor * scaled - v * (factor * factor * factor * jnp.mean(scaled * v, axis=1, keepdims=True)), gain_grad

    def finish_rows(e):
        v = sum_ref[piece(e), :].astype(F32)
        square = jnp.sum(jnp.where(stat_lane, v, 0.0), axis=1, keepdims=True)
        factor = lax.rsqrt(square / D + EPS_NORM)
        v = v * factor
        d = total[piece(e), :].astype(F32)
        ql, kl, raw = v[:, :QR], v[:, QR : QR + KVR], jnp.where(lane < ROPE, v[:, QR + KVR :], 0.0)
        dql, grad_q = through(d[:, :QR], ql, gain_q)
        dkl, grad_kv = through(d[:, QR : QR + KVR], kl, gain_kv)
        moved = pltpu.roll(d[:, QR + KVR :], NOPE, 1)
        turned = jnp.where(lane < NOPE + 16, pltpu.roll(moved, 128 - 16, 1), -pltpu.roll(moved, 16, 1))
        rope = pltpu.roll(moved * tcos[piece(e), :] + turned * tsin[piece(e), :], NOPE, 1)
        inner = (
            jnp.sum(dql * ql, axis=1, keepdims=True)
            + jnp.sum(dkl * kl, axis=1, keepdims=True)
            + jnp.sum(rope * raw, axis=1, keepdims=True)
        ) / D
        small[0:1, 0:QR] += grad_q
        small[0:1, QR : QR + KVR] += grad_kv
        dl[piece(e), 0:QR] = (dql * factor).astype(BF)
        dl[piece(e), QR : QR + KVR] = (dkl * factor).astype(BF)
        dl[piece(e), QR + KVR : LAT_WIDE] = (rope * factor).astype(BF)
        weight[piece(e), :] = jnp.broadcast_to(factor * factor * inner, (LAT_LINE, 128))

        @pl.when(e % 2 == 1)
        def _():
            pair = pl.ds(pl.multiple_of((e - 1) * LAT_LINE, 128), 128)
            d_in = dot_nn(dl[pair, :], w_ref[...])
            rows_in = x_ref[pair, :].astype(F32)
            gin_ref[pair, :] = (dh_ref[pair, :] + d_in * gain_ref[...] - rows_in * weight[pair, 0:1]).astype(BF)
            small[1:2, 0 : d_in.shape[1]] += jnp.sum(d_in * rows_in, axis=0, keepdims=True)
            xg[pair, :] = (rows_in * gain_ref[...]).astype(BF)
            dlt[:, pair] = dl[pair, :].astype(F32).T.astype(BF)

    def serve(n):
        @pl.when(jnp.logical_and(is_mid, n < count))
        def _():
            first(n)

        @pl.when(jnp.logical_and(is_mid, jnp.logical_and(n >= LAT_DEPTH, n < count + LAT_DEPTH)))
        def _():
            second(n - LAT_DEPTH)
            finish_rows(n - LAT_DEPTH)

        @pl.when(jnp.logical_and(is_end, jnp.logical_and(n >= 3, n < count + 3)))
        def _():
            to_mid(n - 3).wait_send()
            to_end(n - 3).wait_recv()
            finish_rows(n - 3)

    begin, middle, last, drain = torus(s1, xin, yin2, yin, xin2, pack_sems, x, y, to_x, to_y)
    begin_w, middle_w, last_w, drain_w = torus(s1w, xinw, yin2w, yinw, xin2w, w_sems, x, y, to_x, to_y)

    serve(0)
    for f in range(4):
        out_copy(f).wait_recv()
        s1[f, 0:320] = (gout_ref[span(f, core, 320), :].astype(F32) + cin[f].astype(F32)).astype(BF)
        s1[f, slot_q] = gq_ref[span(f, core, 96), :]
        s1[f, slot_kv] = gkv_ref[span(f, core, 32), :]
        q_got(f).wait_recv()
        kv_got(f).wait_recv()
    begin()
    each(6, lambda n: serve(n + 1))
    middle()
    each(4, lambda n: serve(n + 7))
    last(pack_out)
    lanes = pack_out.shape[1]
    gq_out[...] = dot_nn(pack_out[320:416, :], fold_ref[0:lanes, :]) + dot_nn(pack_out[416:512, :], fold_ref[lanes:, :])
    gkv_out[:, 0:lanes] = pack_out[512:544, :].astype(F32)
    gkv_out[:, lanes : 2 * lanes] = pack_out[544:576, :].astype(F32)
    each(count + 3 - 11, lambda n: serve(n + 11))

    both = dot_nn(dlt[0:QR, :], xg[...])
    for p in range(peers):
        w_pack[p, 0:96, :] = both[p * 96 : (p + 1) * 96].astype(BF)
    tail = dot_nn(dlt[QR:LAT, :], xg[...]).astype(BF)
    wide = lax.dot_general(sel_ref[...], tail, (((0,), (0,)), ((), ())), preferred_element_type=F32)
    for p in range(peers):
        w_pack[p, 96:144, :] = wide[p * 48 : (p + 1) * 48].astype(BF)
        w_pack[p, 144:160, :] = jnp.zeros((16, wide.shape[1]), BF)
    w_copy = lambda f: remote(w_pack.at[2 * f + 1 - core], cinw.at[f], w_send.at[f], w_recv.at[f], to_core)
    for f in range(4):
        w_copy(f).start()
    for f in range(4):
        w_copy(f).wait_recv()
        s1w[f] = (w_pack[2 * f + core].astype(F32) + cinw[f].astype(F32)).astype(BF)
    begin_w()
    middle_w()
    last_w(wd_out)

    squares = (
        total_square(wd_out[0:96, :]),
        total_square(wd_out[96:144, :]),
        total_square(pack_out[320:512, :]),
        total_square(pack_out[512:576, :]),
        total_square(pack_out[0:320, :]),
        square_ref[0:1, 0:1] + square_ref[1:2, 0:1],
        square_ref[2:3, 0:1],
    )
    line = jnp.zeros((1, 128), F32)
    for n, v in enumerate(squares):
        line = jnp.where(lane == n, v, line)
    small[3:4, 0:128] = line
    small_copy = lambda d, source: remote(small, small_in.at[source], small_send.at[d], small_recv.at[source], peer(d))
    for d in range(1, peers):
        small_copy(d, me).start()
    small_in[me] = small[...]
    for d in range(1, peers):
        small_copy(d, lax.rem(me + peers - d, peers)).wait_recv()
    whole = small_in[0]
    for p in range(1, peers):
        whole = whole + small_in[p]
    small_out[...] = whole
    norms = total_square(whole[1:2]) + total_square(whole[2:3])
    scal_in[z] = jnp.broadcast_to(jnp.where(lane == 7, norms, whole[3:4, 0:128]), (8, 128))
    scal_copy = lambda d, source: remote(
        scal_in.at[z], scal_in.at[source], scal_send.at[d], scal_recv.at[source], {"tp": lax.rem(z + d, 4)}
    )
    for d in range(1, 4):
        scal_copy(d, z).start()
    for d in range(1, 4):
        scal_copy(d, lax.rem(z + 4 - d, 4)).wait_recv()
    scalars = (scal_in[0] + scal_in[1]) + (scal_in[2] + scal_in[3])
    scalars = jnp.where(lane == 8, total_square(whole[0:1]), scalars)
    scalar_out[...] = limit_ref[...] / jnp.maximum(jnp.sqrt(scalars), limit_ref[...])

    for d in range(1, peers):
        small_copy(d, me).wait_send()
    for d in range(1, 4):
        scal_copy(d, z).wait_send()
    drain()
    drain_w()
    for f in range(4):
        out_copy(f).wait_send()
        q_copy(f).wait_send()
        kv_copy(f).wait_send()
        w_copy(f).wait_send()
    each(shares, lambda e: hand(e).wait_send())

    @pl.when(is_mid)
    def _():
        def sent(k):
            over(k).wait_send()
            to_end(k).wait_send()

        each(count, sent)


def latent_backward(*args):
    dq, up, x = args[0], args[3], args[6]
    rows, width = x.shape
    lanes = dq.shape[1]
    peers = up.shape[0]
    count = rows // LAT_LINE
    vmem = pl.BlockSpec(memory_space=pltpu.VMEM)
    dma = pltpu.SemaphoreType.DMA
    scratch = lambda *shape: pltpu.VMEM(shape, BF)
    halves = lambda half: [scratch(2, half, width), scratch(2, half, width), scratch(half, width), scratch(half, width)]
    torus_sems = [dma((2,))] * 4 + [dma((1,))] * 4
    return pl.pallas_call(
        latent_back_kernel,
        out_shape=[
            jax.ShapeDtypeStruct((rows, width), BF),
            jax.ShapeDtypeStruct((PACK, width), BF),
            jax.ShapeDtypeStruct((PIECE, width), BF),
            jax.ShapeDtypeStruct((8, QR + KVR), F32),
            jax.ShapeDtypeStruct((8, 128), F32),
            jax.ShapeDtypeStruct((QR // peers, args[-1].shape[1]), F32),
            jax.ShapeDtypeStruct((KVR // peers, args[-1].shape[0]), F32),
        ],
        in_specs=[vmem] * len(args),
        out_specs=[vmem] * 7,
        scratch_shapes=[scratch(QR, lanes), scratch(KVR, lanes)]
        + [scratch(rows, LAT_WIDE)] * 7
        + [
            scratch(LAT_WIDE, rows),
            scratch(rows, width),
            pltpu.VMEM((rows, 128), F32),
            scratch(peers, PIECE, width),
            pltpu.VMEM((8, QR + KVR), F32),
            pltpu.VMEM((peers, 8, QR + KVR), F32),
            pltpu.VMEM((4, 8, 128), F32),
            scratch(4, PACK, width),
            scratch(4, 320, width),
        ]
        + halves(HALF)
        + [scratch(4, PIECE, width), scratch(4, PIECE, width)]
        + halves(PIECE // 2)
        + [dma((rows // SHARE,))] * 2
        + [dma((4,))] * 8
        + [dma((peers,))] * 2
        + [dma((4,))] * 2
        + [dma((count,))] * 6
        + torus_sems * 2,
        compiler_params=pltpu.CompilerParams(collective_id=5, has_side_effects=True, vmem_limit_bytes=62 * MIB),
        cost_estimate=pl.CostEstimate(flops=rows * LAT_WIDE * width * 6, bytes_accessed=200 * MIB, transcendentals=0),
        name="latent_backward",
    )(*args)


def swap_cores(v):
    return lax.ppermute(v, "ctx", [(0, 1), (1, 0)])


def in_core_order(mine, other, core, axis):
    return jnp.where(
        core == 0, jnp.concatenate([mine, other], axis=axis), jnp.concatenate([other, mine], axis=axis)
    )


def gather_shards(v):
    return lax.all_gather(v, ("fsdp", "ctx"), axis=0, tiled=True)


X_SWAP = [(0, 1), (1, 0), (2, 3), (3, 2)]
Y_SWAP = [(0, 2), (2, 0), (1, 3), (3, 1)]


def take(v, which, axis):
    return lax.dynamic_index_in_dim(v, which, axis, keepdims=False)


def add_up(a, b):
    return (a.astype(F32) + b.astype(F32)).astype(BF)


def keep_half(v, axis, which, name, pairs):
    other = lax.ppermute(take(v, 1 - which, axis), name, pairs)
    return add_up(take(v, which, axis), other)


def scatter_fsdp(v):
    if lax.axis_size("fsdp") != 4:
        return lax.psum_scatter(v, "fsdp", scatter_dimension=0, tiled=False)
    place = lax.axis_index("fsdp")
    y, x = place // 2, place % 2
    _, rows, cols = v.shape
    v = v.reshape(2, 2, 2, rows // 2, cols)
    first = keep_half(v[:, :, 0], 1, x, "fsdp", X_SWAP)
    second = keep_half(v[:, :, 1], 0, y, "fsdp", Y_SWAP)
    first = keep_half(first, 0, y, "fsdp", Y_SWAP)
    second = keep_half(second, 0, x, "fsdp", X_SWAP)
    return jnp.concatenate([first, second], axis=0)


def scatter_grads(v):
    fsdp, ctx = lax.axis_size("fsdp"), lax.axis_size("ctx")
    rows, cols = v.shape
    v = v.reshape(fsdp, ctx, rows // (fsdp * ctx), cols)
    return scatter_fsdp(keep_half(v, 1, lax.axis_index("ctx"), "ctx", [(0, 1), (1, 0)]))


def split_two(v):
    high = v.astype(BF)
    return high, (v - high.astype(F32)).astype(BF)


def adamw_update(parameter, gradient, first_moment, second_moment, decay_rate):
    first_new = BETA_ONE * first_moment + (1.0 - BETA_ONE) * gradient
    second_new = BETA_TWO * second_moment + (1.0 - BETA_TWO) * gradient * gradient
    first_hat = first_new / (1.0 - BETA_ONE**STEP)
    second_hat = second_new / (1.0 - BETA_TWO**STEP)
    updated = parameter - LEARN_RATE * (
        first_hat / (jnp.sqrt(second_hat) + ADAM_EPS) + decay_rate * parameter
    )
    return (updated, first_new, second_new)


def norm_backward(incoming, values, factor, gain):
    scaled = incoming * gain
    gain_grad = jnp.sum(incoming * values * factor, axis=0)
    result = factor * scaled - values * factor**3 * jnp.mean(scaled * values, axis=1, keepdims=True)
    return (result, gain_grad)


def local(*args):
    tokens, cotangent, lengths = args[:3]
    params, firsts, seconds = args[3:12], args[12:21], args[21:30]
    w_qdown, w_kvdown, w_qup, w_kvup, w_out, w_gateup, w_down, g_norms, g_latent = params
    n_tp, n_ctx, n_fsdp = lax.axis_size("tp"), lax.axis_size("ctx"), lax.axis_size("fsdp")
    tp, core = lax.axis_index("tp"), lax.axis_index("ctx")
    rows, width = tokens.shape
    slot = rows * n_ctx
    heads_all = H // n_tp
    by_head = heads_all % n_ctx == 0
    heads = heads_all // n_ctx if by_head else heads_all

    fused = n_tp == 4 and n_fsdp == 4 and n_ctx == 2
    gains_norm = g_norms.astype(BF)
    gain_attn = gains_norm[0].astype(F32)
    inputs = tokens.astype(F32)
    seq_length = lengths[0, 0]
    own_index = core * rows + jnp.arange(rows, dtype=jnp.int32)
    own_segment = (own_index >= seq_length).astype(jnp.int32)
    live = (own_segment == 0).astype(F32)[:, None]

    q_shard = jnp.pad(
        w_qup.astype(BF).reshape(w_qup.shape[0], heads_all, HEAD), ((0, 0), (0, 0), (0, 128 - HEAD))
    ).reshape(w_qup.shape[0], heads_all * 128)
    up_shard = jnp.concatenate([q_shard, w_kvup.astype(BF)], axis=0)

    if fused:
        piece = jnp.concatenate(
            [
                w_qdown.T.astype(BF),
                jnp.pad(w_kvdown.T.astype(BF), ((0, 12), (0, 0))),
                jnp.broadcast_to(jnp.pad(g_latent.astype(BF), (0, width - g_latent.shape[0])), (16, width)),
            ],
            axis=0,
        )
        up_pair = jnp.concatenate([up_shard[:, : heads * 128], up_shard[:, heads * 128 :]])[None]
        gain_wide = jnp.pad(gains_norm[1].astype(F32), (0, LAT_WIDE - width))[None]
        down_t, lat_sum, lat_all, cos_t, sin_t, seg_q, up, tcos, tsin, gains_lat, gate_up = latent_forward(
            tokens, gain_attn[None], gain_wide, piece[None], up_pair, lengths, w_gateup.astype(BF)
        )
        gain_mlp = lat_sum[rows : rows + n_tp, :width].reshape(D).astype(F32)
    else:
        out_t = gather_shards(w_out.T.astype(BF))
        gate_up = lax.all_gather(w_gateup.astype(BF), ("fsdp", "ctx"), axis=1, tiled=True)
        ff_down_t = gather_shards(w_down.T.astype(BF))
        index = jnp.arange(slot, dtype=jnp.int32)
        segment = (index >= seq_length).astype(jnp.int32)
        position = (index - segment * seq_length).astype(F32)
        frequency = ROPE_BASE ** (-2.0 * jnp.arange(ROPE // 2, dtype=F32) / ROPE)
        angles = frequency[:, None] * position[None, :]
        cos_t, sin_t = jnp.cos(angles), jnp.sin(angles)
        own_cos = lax.dynamic_slice_in_dim(cos_t, core * rows, rows, 1).T
        own_sin = lax.dynamic_slice_in_dim(sin_t, core * rows, rows, 1).T
        seg_f = segment.astype(F32)
        seg_q = jnp.concatenate([seg_f[None], 1.0 - seg_f[None], jnp.zeros((14, slot), F32)], axis=0).astype(BF)
        seg_k = (MASK_VALUE * jnp.concatenate([1.0 - seg_f[:, None], seg_f[:, None]], axis=1)).astype(BF)
        down_t = jnp.concatenate(
            [gather_shards(w_qdown.T.astype(BF)), gather_shards(w_kvdown.T.astype(BF)), jnp.zeros((LAT_WIDE - LAT, width), BF)]
        )
        gain_lat = lax.all_gather(g_latent.astype(BF), ("fsdp", "ctx"), axis=0, tiled=True).astype(F32)
        gain_mlp = lax.all_gather(gains_norm[1], "tp", axis=0, tiled=True).astype(F32)
        up = gather_shards(up_shard).reshape(n_fsdp * n_ctx, up_shard.shape[0], heads_all * 128)
        if by_head:
            up = lax.dynamic_slice_in_dim(up, core * heads * 128, heads * 128, 2)
        scaled_in = (inputs * gain_attn).astype(BF)
        lat_sum = lax.psum(dot_nt(scaled_in, down_t).astype(BF), "tp").astype(F32)
        square_sum = lax.psum(jnp.sum(inputs * inputs, axis=1), "tp")
    if not fused:
        factor_one = lax.rsqrt(square_sum / D + EPS_NORM)[:, None]
        latents = lat_sum[:, :LAT] * factor_one
        query_latent = latents[:, :QR]
        kv_latent = latents[:, QR : QR + KVR]
        gain_query, gain_kv = gain_lat[:QR], gain_lat[QR:]
        factor_query = lax.rsqrt(jnp.mean(query_latent * query_latent, axis=1, keepdims=True) + EPS_NORM)
        factor_kv = lax.rsqrt(jnp.mean(kv_latent * kv_latent, axis=1, keepdims=True) + EPS_NORM)
        rope_raw = latents[:, QR + KVR :]
        query_normed = (query_latent * factor_query * gain_query).astype(BF)
        kv_normed = (kv_latent * factor_kv * gain_kv).astype(BF)
        r_one, r_two = rope_raw[:, : ROPE // 2], rope_raw[:, ROPE // 2 :]
        rope_key = jnp.concatenate(
            [r_one * own_cos - r_two * own_sin, r_two * own_cos + r_one * own_sin], axis=1
        ).astype(BF)
        normed_lat = jnp.concatenate([query_normed, kv_normed, jnp.zeros((rows, NOPE), BF), rope_key], axis=1)
        lat_both = in_core_order(normed_lat, swap_cores(normed_lat), core, 0)
        lat_all = jnp.concatenate([lat_both, seg_k, jnp.zeros((slot, 128 - HEAD - 2), BF)], axis=1)
    qn, kn = lat_all[:, :QR], lat_all[:, QR : QR + KVR]

    if fused:
        att_heads, lse, q_t, k_rows, v_t, att_t, ff_down_t, out_t = attend_forward(
            lat_all, cos_t, sin_t, seg_q, up, w_down.T.astype(BF)[None], w_out.T.astype(BF)[None]
        )
        ff_down_t, out_t = ff_down_t.reshape(D, -1), out_t.reshape(D, -1)
    else:
        att_heads, lse, q_t, k_rows, v_t = attend_forward(lat_all, cos_t, sin_t, seg_q, up)
        att_flat = att_heads.reshape(heads * VD, slot)
        own_cols = lambda v: lax.dynamic_slice_in_dim(v, core * rows, rows, 1)
        if by_head:
            other = swap_cores(lax.dynamic_slice_in_dim(att_flat, (1 - core) * rows, rows, 1))
            att_t = in_core_order(own_cols(att_flat), other, core, 0)
        else:
            att_t = own_cols(att_flat)

    feature_owner = jnp.arange(D) // width
    own_features = lambda v: lax.dynamic_slice_in_dim(v, tp * width, width, 1)
    if fused:
        hidden, d_normed_part, mlp_part, normed_two_t, activation, d_gate, d_up = block_forward(
            att_t, tokens, out_t, gain_mlp[None], live, cotangent, gate_up, ff_down_t
        )
        attn_seed, d_hidden, grad_gain_mlp, grads, grad_squares = grad_reduce(
            live, gain_mlp[None], d_normed_part, hidden, cotangent, normed_two_t, d_gate, d_up, activation
        )
    else:
        dy = cotangent.astype(F32) * live
        mlp_seed = (RESIDUAL_SCALE * dy).astype(BF)
        h_part = RESIDUAL_SCALE * dot_nt(att_t.T, out_t)
        h_part = h_part + jnp.where(
            (feature_owner == tp)[None], jnp.concatenate([inputs] * n_tp, axis=1), 0.0
        )
        hidden = lax.psum(h_part.astype(BF), "tp")
        hidden_f = hidden.astype(F32)
        factor_two = lax.rsqrt(jnp.mean(hidden_f * hidden_f, axis=1, keepdims=True) + EPS_NORM)
        normed_two = (hidden_f * factor_two * gain_mlp).astype(BF)
        gate_proj = dot_nn(normed_two, gate_up[0])
        up_proj = dot_nn(normed_two, gate_up[1])
        sigmoid_gate = jax.nn.sigmoid(gate_proj)
        activation = (gate_proj * sigmoid_gate * up_proj).astype(BF)
        mlp_part = dot_nt(activation, ff_down_t).astype(BF)
        d_activation = dot_nn(mlp_seed, ff_down_t)
        d_gate = (
            d_activation * up_proj * sigmoid_gate * (1.0 + gate_proj * (1.0 - sigmoid_gate))
        ).astype(BF)
        d_up = (d_activation * gate_proj * sigmoid_gate).astype(BF)
        d_normed_part = (dot_nt(d_gate, gate_up[0]) + dot_nt(d_up, gate_up[1])).astype(BF)
        grad_down = scatter_grads(dot_tn(mlp_seed, activation).astype(BF))
        grad_gate = scatter_grads(dot_tn(normed_two, d_gate).astype(BF))
        grad_up = scatter_grads(dot_tn(normed_two, d_up).astype(BF))
        d_normed = lax.psum(d_normed_part, "tp").astype(F32)
        row_inner = jnp.mean(d_normed * gain_mlp * hidden_f, axis=1, keepdims=True)
        d_hidden_full = dy + factor_two * d_normed * gain_mlp - hidden_f * (factor_two**3 * row_inner)
        attn_seed = (RESIDUAL_SCALE * d_hidden_full).astype(BF)
        d_hidden = own_features(d_hidden_full)
        grad_gain_mlp = jnp.sum(own_features(d_normed * hidden_f) * factor_two, axis=0)
    mlp_part, attn_seed = lax.optimization_barrier((mlp_part, attn_seed))
    if fused:
        mlp_out = lax.psum_scatter(mlp_part, "tp", scatter_dimension=0, tiled=False).astype(F32)
    else:
        mlp_out = lax.psum_scatter(mlp_part, "tp", scatter_dimension=1, tiled=True).astype(F32)
    layer_out = (own_features(hidden).astype(F32) + RESIDUAL_SCALE * mlp_out).astype(BF)
    d_att_t = lax.dot_general(out_t, attn_seed, (((0,), (1,)), ((), ())), preferred_element_type=F32).astype(BF)
    grad_out = dot_tn(attn_seed, att_t.T).astype(BF)

    if by_head:
        pick = lambda v, which: lax.dynamic_slice_in_dim(v, which * heads * VD, heads * VD, 0)
        d_att = in_core_order(pick(d_att_t, core), swap_cores(pick(d_att_t, 1 - core)), core, 1)
    else:
        d_att = lax.dynamic_update_slice(jnp.zeros((heads * VD, slot), BF), d_att_t, (0, core * rows))
    d_q, d_e, d_kr = attend_backward(
        q_t, k_rows, v_t, att_heads, d_att.reshape(heads, VD, slot), lse, cos_t, sin_t
    )
    grad_qup = dot_tn(qn, d_q).astype(BF)
    grad_kvup = dot_tn(kn, d_e).astype(BF)

    def heads_only(g):
        return g.reshape(g.shape[0], heads_all, 128)[:, :, :HEAD].reshape(g.shape[0], heads_all * HEAD)

    entry_counts = (
        D * QR,
        D * (KVR + ROPE),
        QR * H * HEAD,
        KVR * H * (NOPE + VD),
        H * VD * D,
        2 * D * FF,
        FF * D,
        2 * D,
        QR + KVR,
    )
    limits = [CLIP_RMS * n**0.5 for n in entry_counts]
    share = g_latent.shape[0]
    my_share = (lax.axis_index("fsdp") * n_ctx + core) * share
    if fused:
        fold = jnp.asarray(np.kron(np.eye(heads_all), np.eye(128, HEAD)), BF)
        grad_input, pack, wd_grad, small, scalars, grad_qup, grad_kvup = latent_backward(
            d_q, d_e, d_kr, up, lat_sum, down_t, tokens, gain_attn[None], d_hidden, tcos, tsin, gains_lat,
            grad_out, grad_qup, grad_kvup, spread(n_fsdp * n_ctx), grad_gain_mlp, grad_squares, jnp.array([limits + [1.0] * 119], F32), fold,
        )
        owned = [
            wd_grad[:96].astype(F32).T,
            wd_grad[96:132].astype(F32).T,
            grad_qup,
            grad_kvup,
            pack[:320].astype(F32).T,
            grads[:2].astype(F32),
            grads[2].astype(F32).T,
            small[1:3, :width],
            lax.dynamic_slice_in_dim(small[0], my_share, share, 0),
        ]
        factors = [scalars[0, n] for n in range(9)]
    else:
        q_up_here = up[:, : w_qup.shape[0]].reshape(QR, heads * 128)
        kv_up_here = up[:, w_qup.shape[0] :].reshape(KVR, heads * 128)
        d_lat_part = jnp.concatenate([dot_nt(d_q, q_up_here), dot_nt(d_e, kv_up_here), d_kr[:, NOPE:HEAD]], axis=1)
        own_rows = lambda v, which: lax.dynamic_slice_in_dim(v, which * rows, rows, 0)
        from_other = swap_cores(own_rows(d_lat_part, 1 - core).astype(BF)).astype(F32)
        d_lat = lax.psum((own_rows(d_lat_part, core) + from_other).astype(BF), "tp").astype(F32)
        d_rope = d_lat[:, QR + KVR : LAT]
        k_one, k_two = d_rope[:, : ROPE // 2], d_rope[:, ROPE // 2 :]
        d_rope_raw = jnp.concatenate([k_one * own_cos + k_two * own_sin, k_two * own_cos - k_one * own_sin], axis=1)
        d_query_latent, grad_gain_query = norm_backward(d_lat[:, :QR], query_latent, factor_query, gain_query)
        d_kv_latent, grad_gain_kv = norm_backward(d_lat[:, QR : QR + KVR], kv_latent, factor_kv, gain_kv)
        d_latents = jnp.concatenate([d_query_latent, d_kv_latent, d_rope_raw], axis=1)
        in_inner = jnp.sum(d_latents * latents, axis=1, keepdims=True) / D
        d_latents = (d_latents * factor_one).astype(BF)
        grad_both = dot_tn(d_latents, scaled_in).astype(BF)
        d_in = dot_nn(d_latents, down_t[:LAT])
        grad_gain_attn = jnp.sum(d_in * inputs, axis=0)
        grad_input = (d_hidden + d_in * gain_attn - inputs * (factor_one**2 * in_inner)).astype(BF)

        def scatter_up(g):
            if not by_head:
                return scatter_grads(g)
            n_rows, n_cols = g.shape
            g = g.reshape(n_fsdp, n_ctx, n_rows // (n_fsdp * n_ctx), n_cols)
            other = swap_cores(take(g, 1 - core, 1))
            return scatter_fsdp(in_core_order(take(g, core, 1), other, core, 2))

        owned = [
            scatter_grads(grad_both[:QR]).astype(F32).T,
            scatter_grads(grad_both[QR:]).astype(F32).T,
            heads_only(scatter_up(grad_qup)).astype(F32),
            scatter_up(grad_kvup).astype(F32),
            scatter_grads(grad_out).astype(F32).T,
            jnp.stack([grad_gate, grad_up]).astype(F32),
            grad_down.astype(F32).T,
        ]
        both_gains = jnp.stack([grad_gain_attn, grad_gain_mlp])
        placed_gains = jnp.where((feature_owner == tp)[None], jnp.concatenate([both_gains] * n_tp, axis=1), 0.0)
        latent_gains = jnp.concatenate([grad_gain_query, grad_gain_kv]) * (tp == 0)
        squares = jnp.stack([jnp.sum(g * g) for g in owned])
        small = lax.psum(
            jnp.concatenate([placed_gains.reshape(-1), latent_gains, squares]), ("fsdp", "ctx", "tp")
        )
        all_gains = small[: 2 * D].reshape(2, D)
        all_latent = small[2 * D : 2 * D + QR + KVR]
        owned.append(own_features(all_gains))
        owned.append(lax.dynamic_slice_in_dim(all_latent, my_share, share, 0))
        totals = [small[2 * D + QR + KVR + n] for n in range(7)]
        totals += [jnp.sum(all_gains * all_gains), jnp.sum(all_latent * all_latent)]
        factors = [limit / jnp.maximum(jnp.sqrt(total), limit) for limit, total in zip(limits, totals)]
    new_params, new_firsts, new_seconds = [], [], []
    for n in range(9):
        clipped = owned[n] * factors[n]
        updated, first_new, second_new = adamw_update(
            params[n], clipped, firsts[n], seconds[n], WEIGHT_DECAY if n < 7 else 0.0
        )
        new_params.append(updated)
        new_firsts.append(first_new)
        new_seconds.append(second_new)
    return (layer_out, grad_input, *owned, *new_params[:7], *new_firsts, *new_seconds)


def solution(mesh):
    sharded = ("fsdp", "ctx")
    weights = (
        P("tp", sharded),
        P("tp", sharded),
        P(sharded, "tp"),
        P(sharded, "tp"),
        P("tp", sharded),
        P(None, sharded, "tp"),
        P("tp", sharded),
    )
    gains = (P(None, "tp"), P(sharded))
    tokens = P(sharded, "tp")
    return jax.shard_map(
        local,
        mesh=mesh,
        in_specs=(tokens, P(sharded, None), P("fsdp", None)) + (weights + gains) * 3,
        out_specs=(tokens, tokens) + weights + gains + weights + (weights + gains) * 2,
        check_vma=False,
    )
```

```python
import functools

import jax
import jax.numpy as jnp
import numpy as np
from jax import lax
from jax.experimental import pallas as pl
from jax.experimental.pallas import tpu as pltpu
from jax.sharding import PartitionSpec as P

D = 2560
H = 40
NOPE = 64
ROPE = 32
VD = 64
QR = 768
KVR = 256
FF = 6400
STEP = 3
HEAD = NOPE + ROPE
LAT = QR + KVR + ROPE
LAT_WIDE = 1152

EPS_NORM = 1e-05
RESIDUAL_SCALE = 1.4 / 62**0.5
ROPE_BASE = 10000.0
MASK_VALUE = -1e30
BETA_ONE = 0.9
BETA_TWO = 0.95
ADAM_EPS = 1e-08
LEARN_RATE = 0.1
WEIGHT_DECAY = 0.1
CLIP_RMS = 0.0002
LOG2E = 1.4426950408889634
LN2 = 0.6931471805599453

BF = jnp.bfloat16
F32 = jnp.float32
MESH = pl.DeviceIdType.MESH
MIB = 1024 * 1024


def dot_nn(a, b):
    return lax.dot_general(a, b, (((1,), (0,)), ((), ())), preferred_element_type=F32)


def dot_nt(a, b):
    return lax.dot_general(a, b, (((1,), (1,)), ((), ())), preferred_element_type=F32)


def dot_tn(a, b):
    return lax.dot_general(a, b, (((0,), (0,)), ((), ())), preferred_element_type=F32)


def torus_gather(piece, whole, sems, place, core):
    x1s, x1r, y1s, y1r, c1s, c1r, x2s, x2r, y2s, y2r, cxs, cxr, cys, cyr, cds, cdr, own = sems
    y, x = place // 2, place % 2
    half = piece.shape[1] // 2
    upper, lower = pl.ds(0, half), pl.ds(half, half)
    to_core, to_x, to_y = {"ctx": 1 - core}, {"fsdp": y * 2 + 1 - x}, {"fsdp": (1 - y) * 2 + x}

    def owner(yy, xx, cc):
        return (yy * 2 + xx) * 2 + cc

    me, px, py = owner(y, x, core), owner(y, 1 - x, core), owner(1 - y, x, core)
    pd = owner(1 - y, 1 - x, core)

    def remote(src, dst, send, recv, i, to):
        return pltpu.make_async_remote_copy(
            src_ref=src, dst_ref=dst, send_sem=send.at[i], recv_sem=recv.at[i], device_id=to, device_id_type=MESH
        )

    first = lambda i, p, send, recv, to: remote(piece.at[i], whole.at[p, i], send, recv, i, to)
    part = lambda i, p, rows, send, recv, to: remote(whole.at[p, i, rows], whole.at[p, i, rows], send, recv, i, to)
    full = lambda i, p, send, recv: remote(whole.at[p, i], whole.at[p, i], send, recv, i, to_core)
    keep = lambda i: pltpu.make_async_copy(piece.at[i], whole.at[me, i], own.at[i])

    def begin(i):
        first(i, me, x1s, x1r, to_x).start()
        first(i, me, y1s, y1r, to_y).start()
        first(i, me, c1s, c1r, to_core).start()
        keep(i).start()

    def forward(i):
        first(i, px, x1s, x1r, to_x).wait_recv()
        part(i, px, upper, y2s, y2r, to_y).start()
        full(i, px, cxs, cxr).start()
        first(i, py, y1s, y1r, to_y).wait_recv()
        part(i, py, lower, x2s, x2r, to_x).start()
        full(i, py, cys, cyr).start()

    def final(i):
        part(i, pd, upper, y2s, y2r, to_y).wait_recv()
        part(i, pd, lower, x2s, x2r, to_x).wait_recv()
        full(i, pd, cds, cdr).start()

    def drain(i):
        first(i, owner(y, x, 1 - core), c1s, c1r, to_core).wait_recv()
        full(i, owner(y, 1 - x, 1 - core), cxs, cxr).wait_recv()
        full(i, owner(1 - y, x, 1 - core), cys, cyr).wait_recv()
        full(i, owner(1 - y, 1 - x, 1 - core), cds, cdr).wait_recv()
        first(i, me, x1s, x1r, to_x).wait_send()
        first(i, me, y1s, y1r, to_y).wait_send()
        first(i, me, c1s, c1r, to_core).wait_send()
        part(i, px, upper, y2s, y2r, to_y).wait_send()
        part(i, py, lower, x2s, x2r, to_x).wait_send()
        full(i, px, cxs, cxr).wait_send()
        full(i, py, cys, cyr).wait_send()
        full(i, pd, cds, cdr).wait_send()
        keep(i).wait()

    return begin, forward, final, drain


GATHER_SEMS = 17


BQ = 512


def attend_forward_kernel(fused, *refs):
    lat_ref, cos_ref, sin_ref, segq_ref, up_ref, *refs = refs
    if fused:
        down_any, out_any, *refs = refs
    o_ref, lse_ref, q_ref, k_ref, v_ref, *refs = refs
    if fused:
        att_any, down_all, out_all, *refs = refs
    stack_q, stack_kv, wq_t, *refs = refs
    h, i = pl.program_id(0), pl.program_id(1)
    rows = lat_ref.shape[0]
    heads, blocks = pl.num_programs(0), rows // BQ
    if fused:
        place, core = lax.axis_index("fsdp"), lax.axis_index("ctx")
        stage, att_send, att_recv, *sems = refs
        at = h * blocks + i
        gathers = (
            torus_gather(down_any, down_all, sems[:GATHER_SEMS], place, core),
            torus_gather(out_any, out_all, sems[GATHER_SEMS:], place, core),
        )

        @pl.when(at == 0)
        def _():
            y, x = place // 2, place % 2
            barrier = pltpu.get_barrier_semaphore()
            for to in ({"ctx": 1 - core}, {"fsdp": y * 2 + 1 - x}, {"fsdp": (1 - y) * 2 + x}):
                pl.semaphore_signal(barrier, inc=1, device_id=to, device_id_type=MESH)
            pl.semaphore_wait(barrier, 3)
            for begin, _, _, _ in gathers:
                begin(0)

        for n in range(2):

            @pl.when(at == (heads * blocks * (13 + 4 * n)) // 20)
            def _():
                gathers[n][1](0)
    pieces = up_ref.shape[0]
    nq, nk = QR // pieces, KVR // pieces

    @pl.when(i == 0)
    def _():
        for p in range(pieces):
            stack_q[p * nq : (p + 1) * nq, :] = up_ref[p, 0:nq, :].astype(F32)
            stack_kv[p * nk : (p + 1) * nk, :] = up_ref[p, nq : nq + nk, :].astype(F32)
        wq_t[...] = stack_q[...].T.astype(BF)
        kv = stack_kv[...]
        wk = jnp.where(lax.broadcasted_iota(jnp.int32, kv.shape, 1) < NOPE, kv, 0.0).astype(BF)
        wv_t = kv.T[NOPE:128].astype(BF)
        for r in range(rows // BQ):
            part = pl.ds(r * BQ, BQ)
            kn = lat_ref[part, QR : QR + KVR]
            qf = dot_nt(wq_t[...], lat_ref[part, 0:QR]) * (LOG2E * HEAD**-0.5)
            cos = cos_ref[:, part]
            sin = sin_ref[:, part]
            one, two = qf[NOPE : NOPE + 16], qf[NOPE + 16 : HEAD]
            q_ref[0, 0:NOPE, part] = qf[:NOPE].astype(BF)
            q_ref[0, NOPE : NOPE + 16, part] = (one * cos - two * sin).astype(BF)
            q_ref[0, NOPE + 16 : HEAD, part] = (two * cos + one * sin).astype(BF)
            q_ref[0, HEAD : HEAD + 16, part] = segq_ref[:, part]
            q_ref[0, HEAD + 16 : 128, part] = jnp.zeros((16, BQ), BF)
            k_ref[0, part, :] = (dot_nn(kn, wk) + lat_ref[part, QR + KVR : LAT_WIDE].astype(F32)).astype(BF)
            v_ref[0, 0:VD, part] = dot_nt(wv_t, kn).astype(BF)
            ones = lax.broadcasted_iota(jnp.int32, (16, BQ), 0) == 0
            v_ref[0, VD : VD + 16, part] = ones.astype(F32).astype(BF)

    here = pl.ds(pl.multiple_of(i * BQ, BQ), BQ)
    q = q_ref[0, :, here]

    def block(j, carried, masked):
        m, acc = carried
        there = pl.ds(pl.multiple_of(j * BQ, BQ), BQ)
        s = dot_nn(k_ref[0, there, :], q)
        if masked:
            krow = lax.broadcasted_iota(jnp.int32, s.shape, 0)
            qcol = lax.broadcasted_iota(jnp.int32, s.shape, 1)
            s = jnp.where(krow <= qcol, s, MASK_VALUE)
        top = jnp.maximum(m, jnp.max(s, axis=0, keepdims=True))
        p = jnp.exp2(s - top).astype(BF)
        acc = acc * jnp.exp2(m - top) + dot_nn(v_ref[0, :, there], p)
        return top, acc

    start = (jnp.full((1, BQ), -3e38, F32), jnp.zeros((80, BQ), F32))
    carried = lax.fori_loop(0, i, lambda j, c: block(j, c, False), start)
    m, acc = block(i, carried, True)
    total = acc[VD : VD + 1]
    o = (acc[:VD] / total).astype(BF)
    o_ref[0, :, here] = o
    lse_ref[0, :, here] = m + jnp.log2(total)
    if fused:
        count = blocks // 2

        def spot(owner, hh, b):
            return (
                pl.ds(pl.multiple_of((owner * heads + hh) * VD, VD), VD),
                pl.ds(pl.multiple_of(lax.rem(b, count) * BQ, BQ), BQ),
            )

        stage[h, i] = o
        keep = lambda hh, b: pltpu.make_async_copy(stage.at[hh, b], att_any.at[spot(core, hh, b)], att_send.at[hh, b])
        give = lambda hh, b, owner: pltpu.make_async_remote_copy(
            src_ref=stage.at[hh, b], dst_ref=att_any.at[spot(owner, hh, b)], send_sem=att_send.at[hh, b],
            recv_sem=att_recv.at[hh, lax.rem(b, count)], device_id={"ctx": 1 - core}, device_id_type=MESH,
        )

        @pl.when(i // count == core)
        def _():
            keep(h, i).start()

        @pl.when(i // count != core)
        def _():
            give(h, i, core).start()

        @pl.when(at == heads * blocks - 1)
        def _():
            def done(n):
                hh, b = n // count, lax.rem(n, count)
                keep(hh, core * count + b).wait()
                give(hh, (1 - core) * count + b, core).wait_send()
                give(hh, core * count + b, 1 - core).wait_recv()

            each(heads * count, done)
            for _, _, final, _ in gathers:
                final(0)
            for _, _, _, drain in gathers:
                drain(0)


def attend_forward(lat, cos, sin, segq, up, *pieces):
    heads = up.shape[2] // 128
    rows = lat.shape[0]
    fused = len(pieces) > 0
    anywhere = pl.BlockSpec(memory_space=pl.ANY)
    dma = pltpu.SemaphoreType.DMA
    more_out, more_scratch, params = [], [], {}
    if fused:
        more_out = [jax.ShapeDtypeStruct((2 * heads * VD, rows // 2), BF)]
        more_out += [jax.ShapeDtypeStruct((up.shape[0],) + p.shape, BF) for p in pieces]
        more_scratch = [pltpu.VMEM((heads, rows // BQ, VD, BQ), BF), dma((heads, rows // BQ)), dma((heads, rows // BQ // 2))]
        more_scratch += [dma((1,))] * (2 * GATHER_SEMS)
        params = {"collective_id": 6, "has_side_effects": True}
    whole = lambda a: pl.BlockSpec(a.shape, lambda h, i: (0,) * a.ndim)
    per_head = lambda a, b: pl.BlockSpec((1, a, b), lambda h, i: (h, 0, 0))
    return pl.pallas_call(
        functools.partial(attend_forward_kernel, fused),
        grid=(heads, rows // BQ),
        in_specs=[whole(lat), whole(cos), whole(sin), whole(segq)]
        + [pl.BlockSpec((up.shape[0], up.shape[1], 128), lambda h, i: (0, 0, h))]
        + [anywhere] * len(pieces),
        out_specs=[per_head(VD, rows), per_head(1, rows), per_head(128, rows), per_head(rows, 128), per_head(80, rows)]
        + [anywhere] * len(more_out),
        out_shape=[
            jax.ShapeDtypeStruct((heads, VD, rows), BF),
            jax.ShapeDtypeStruct((heads, 1, rows), F32),
            jax.ShapeDtypeStruct((heads, 128, rows), BF),
            jax.ShapeDtypeStruct((heads, rows, 128), BF),
            jax.ShapeDtypeStruct((heads, 80, rows), BF),
        ]
        + more_out,
        scratch_shapes=[pltpu.VMEM((QR, 128), F32), pltpu.VMEM((KVR, 128), F32), pltpu.VMEM((128, QR), BF)] + more_scratch,
        compiler_params=pltpu.CompilerParams(vmem_limit_bytes=(62 if fused else 40) * MIB, **params),
        cost_estimate=pl.CostEstimate(flops=heads * rows * rows * 320, bytes_accessed=30 * MIB, transcendentals=0),
        name="attend_forward",
    )(lat, cos, sin, segq, up, *pieces)


def attend_backward_kernel(q_ref, k_ref, v_ref, o_ref, do_ref, lse_ref, cos_ref, sin_ref, dq_ref, de_ref, dkr_ref, dq_acc, delta):
    h, j = pl.program_id(0), pl.program_id(1)
    rows = k_ref.shape[1]
    blocks = rows // BQ

    @pl.when(j == 0)
    def _():
        dq_acc[...] = jnp.zeros_like(dq_acc)
        delta[...] = jnp.sum(o_ref[0].astype(F32) * do_ref[0].astype(F32), axis=0, keepdims=True)

    there = pl.ds(pl.multiple_of(j * BQ, BQ), BQ)
    k = k_ref[0, there, :]
    kt = k.astype(F32).T.astype(BF)
    v = v_ref[0, 0:VD, there].astype(F32).T.astype(BF)

    def block(i, carried, masked):
        dk, dv = carried
        here = pl.ds(pl.multiple_of(i * BQ, BQ), BQ)
        q = q_ref[0, :, here]
        do = do_ref[0, :, here]
        s = dot_nn(k, q)
        if masked:
            krow = lax.broadcasted_iota(jnp.int32, s.shape, 0)
            qcol = lax.broadcasted_iota(jnp.int32, s.shape, 1)
            s = jnp.where(krow <= qcol, s, MASK_VALUE)
        p = jnp.exp2(s - lse_ref[0, :, here])
        dp = dot_nn(v, do)
        ds = (p * (dp - delta[:, here])).astype(BF)
        dv = dv + dot_nt(p.astype(BF), do)
        dk = dk + dot_nt(ds, q)
        dq_acc[:, here] = dq_acc[:, here] + dot_nn(kt, ds)
        return dk, dv

    start = (jnp.zeros((BQ, 128), F32), jnp.zeros((BQ, VD), F32))
    carried = block(j, start, True)
    dk, dv = lax.fori_loop(j + 1, blocks, lambda i, c: block(i, c, False), carried)
    dk = dk * LN2
    de_ref[there, 0:NOPE] = dk[:, :NOPE].astype(BF)
    de_ref[there, NOPE:128] = dv.astype(BF)

    @pl.when(h == 0)
    def _():
        dkr_ref[there, :] = dk

    @pl.when(h > 0)
    def _():
        dkr_ref[there, :] = dkr_ref[there, :] + dk

    @pl.when(j == blocks - 1)
    def _():
        for r in range(blocks):
            part = pl.ds(r * BQ, BQ)
            dq = dq_acc[:, part] * HEAD**-0.5
            cos, sin = cos_ref[:, part], sin_ref[:, part]
            one, two = dq[NOPE : NOPE + 16], dq[NOPE + 16 : HEAD]
            dq = jnp.concatenate(
                [dq[:NOPE], one * cos + two * sin, two * cos - one * sin, jnp.zeros((128 - HEAD, BQ), F32)], axis=0
            )
            dq_ref[part, :] = dq.T.astype(BF)


def attend_backward(q, k, v, o, do, lse, cos, sin):
    heads = q.shape[0]
    rows = k.shape[1]
    whole = lambda a: pl.BlockSpec(a.shape, lambda h, i: (0,) * a.ndim)
    per_head = lambda a: pl.BlockSpec((1,) + a.shape[1:], lambda h, i: (h, 0, 0))
    return pl.pallas_call(
        attend_backward_kernel,
        grid=(heads, rows // BQ),
        in_specs=[per_head(a) for a in (q, k, v, o, do, lse)] + [whole(cos), whole(sin)],
        out_specs=[
            pl.BlockSpec((rows, 128), lambda h, i: (0, h)),
            pl.BlockSpec((rows, 128), lambda h, i: (0, h)),
            pl.BlockSpec((rows, 128), lambda h, i: (0, 0)),
        ],
        out_shape=[
            jax.ShapeDtypeStruct((rows, heads * 128), BF),
            jax.ShapeDtypeStruct((rows, heads * 128), BF),
            jax.ShapeDtypeStruct((rows, 128), F32),
        ],
        scratch_shapes=[pltpu.VMEM((128, rows), F32), pltpu.VMEM((1, rows), F32)],
        compiler_params=pltpu.CompilerParams(vmem_limit_bytes=40 * MIB),
        cost_estimate=pl.CostEstimate(flops=heads * rows * rows * 900, bytes_accessed=30 * MIB, transcendentals=0),
        name="attend_backward",
    )(q, k, v, o, do, lse, cos, sin)


LAT_LINE = 64
LAT_DEPTH = 2
PIECE = 160


def latent_kernel(
    x_ref, gain_ref, gain2_ref, piece_ref, up_ref, sel_ref, freq_col, freq_lane, len_ref, gu_any,
    w_ref, total, lat_ref, cos_ref, sin_ref, segq_ref, upg_ref, tcos, tsin, gains, gu_all,
    gat, up_all, xb, near, cross, kvg,
    c_send, c_recv, *sems,
):
    gather_sems, w_sems, u_sems, sems = sems[40:], sems[6:23], sems[23:40], sems[:6]
    z, core, place = lax.axis_index("tp"), lax.axis_index("ctx"), lax.axis_index("fsdp")
    is_end, is_mid, partner, across = line_places(z)
    to_mid, over, to_end, first, second = line_copies(xb, near, cross, total, sems, partner, across, LAT_LINE)
    count = xb.shape[0] // LAT_LINE
    rows = x_ref.shape[0]
    peers = gat.shape[0]
    me = place * 2 + core

    def remote(src, dst, send, recv, to):
        return pltpu.make_async_remote_copy(
            src_ref=src, dst_ref=dst, send_sem=send, recv_sem=recv, device_id=to, device_id_type=MESH
        )

    y, x = place // 2, place % 2
    barrier = pltpu.get_barrier_semaphore()
    for to in ({"ctx": 1 - core}, {"fsdp": y * 2 + 1 - x}, {"fsdp": (1 - y) * 2 + x}, {"tp": partner}):
        pl.semaphore_signal(barrier, inc=1, device_id=to, device_id_type=MESH)

    @pl.when(is_mid)
    def _():
        pl.semaphore_signal(barrier, inc=1, device_id={"tp": across}, device_id_type=MESH)
        pl.semaphore_wait(barrier, 5)

    @pl.when(is_end)
    def _():
        pl.semaphore_wait(barrier, 4)

    begin, forward, final, drain = torus_gather(gu_any, gu_all, gather_sems, place, core)
    begin_w, forward_w, final_w, drain_w = torus_gather(piece_ref, gat, w_sems, place, core)
    begin_u, forward_u, final_u, drain_u = torus_gather(up_ref, up_all, u_sems, place, core)
    begin_w(0)

    length = len_ref[0, 0]
    slot = cos_ref.shape[1]
    index = lax.broadcasted_iota(jnp.int32, (1, slot), 1)
    segment = (index >= length).astype(jnp.int32)
    angle = freq_col[...] * (index - segment * length).astype(F32)
    cos_ref[...] = jnp.cos(angle)
    sin_ref[...] = jnp.sin(angle)
    row16 = lax.broadcasted_iota(jnp.int32, (16, slot), 0)
    seg_f = segment.astype(F32)
    segq_ref[...] = jnp.where(row16 == 0, seg_f, jnp.where(row16 == 1, 1.0 - seg_f, 0.0)).astype(BF)
    lane = lax.broadcasted_iota(jnp.int32, (1, 128), 1)
    in_rope = jnp.logical_and(lane >= NOPE, lane < HEAD)

    def own_index(e):
        at = core * rows + e * LAT_LINE
        return at + lax.broadcasted_iota(jnp.int32, (LAT_LINE, 1), 0)

    def table(e):
        here = pl.ds(pl.multiple_of(e * LAT_LINE, LAT_LINE), LAT_LINE)
        at = own_index(e)
        seg = (at >= length).astype(jnp.int32)
        turn = (at - seg * length).astype(F32) * freq_lane[...]
        tcos[here, :] = jnp.where(in_rope, jnp.cos(turn), 0.0)
        tsin[here, :] = jnp.where(in_rope, jnp.sin(turn), 0.0)

    each(rows // LAT_LINE, table)

    forward_w(0)
    begin_u(0)
    begin(0)
    begin(1)
    final_w(0)
    drain_w(0)
    for p in range(peers):
        w_ref[p * 96 : (p + 1) * 96, :] = gat[p, 0, 0:96, :]
        kvg[p * 48 : (p + 1) * 48, :] = gat[p, 0, 96:144, :]
        gains[:, p * 128 : (p + 1) * 128] = gat[p, 0, 144:160, 0:128].astype(F32)
    w_ref[QR:LAT, :] = dot_nn(sel_ref[...], kvg[...]).astype(BF)
    w_ref[LAT:LAT_WIDE, :] = jnp.zeros((LAT_WIDE - LAT, w_ref.shape[1]), BF)

    wide_lane = lax.broadcasted_iota(jnp.int32, (1, LAT_WIDE), 1)
    per = 128

    def project(r):
        here = pl.ds(pl.multiple_of(r * per, per), per)
        x = x_ref[here, :].astype(F32)
        square = jnp.sum(x * x, axis=1, keepdims=True)
        high = square.astype(BF).astype(F32)
        part = dot_nt((x * gain_ref[...]).astype(BF), w_ref[...])
        part = jnp.where(wide_lane == LAT + 2 * z, high, jnp.where(wide_lane == LAT + 2 * z + 1, square - high, part))
        xb[here, :] = part.astype(BF)

        @pl.when(is_end)
        def _():
            for n in range(per // LAT_LINE):
                to_mid(r * (per // LAT_LINE) + n).start()

    each(rows // per, project)
    gain_row = lax.broadcasted_iota(jnp.int32, (LAT_LINE, LAT_WIDE), 0) == z
    xb[rows : rows + LAT_LINE, :] = jnp.where(gain_row, gain2_ref[...], 0.0).astype(BF)

    @pl.when(is_end)
    def _():
        to_mid(count - 1).start()

    def handover(e):
        here = pl.ds(pl.multiple_of(core * rows + e * LAT_LINE, LAT_LINE), LAT_LINE)
        return remote(lat_ref.at[here], lat_ref.at[here], c_send.at[e], c_recv.at[e], {"ctx": 1 - core})

    stat_lane = jnp.logical_and(wide_lane >= LAT, wide_lane < LAT + 8)

    def finish_rows(e):
        @pl.when(e < rows // LAT_LINE)
        def _():
            here = pl.ds(pl.multiple_of(e * LAT_LINE, LAT_LINE), LAT_LINE)
            there = pl.ds(pl.multiple_of(core * rows + e * LAT_LINE, LAT_LINE), LAT_LINE)
            v = total[here, :].astype(F32)
            square = jnp.sum(jnp.where(stat_lane, v, 0.0), axis=1, keepdims=True)
            v = v * lax.rsqrt(square / D + EPS_NORM)
            ql, kl, raw = v[:, :QR], v[:, QR : QR + KVR], v[:, QR + KVR :]
            ql = ql * lax.rsqrt(jnp.mean(ql * ql, axis=1, keepdims=True) + EPS_NORM)
            kl = kl * lax.rsqrt(jnp.mean(kl * kl, axis=1, keepdims=True) + EPS_NORM)
            lat_ref[there, 0:QR] = (ql * gains[0:1, 0:QR]).astype(BF)
            lat_ref[there, QR : QR + KVR] = (kl * gains[0:1, QR : QR + KVR]).astype(BF)
            moved = pltpu.roll(jnp.where(lane < ROPE, raw, 0.0), NOPE, 1)
            turned = jnp.where(lane < NOPE + 16, -pltpu.roll(moved, 128 - 16, 1), pltpu.roll(moved, 16, 1))
            seg = (own_index(e) >= length).astype(F32)
            mask = jnp.where(lane == HEAD, 1.0 - seg, jnp.where(lane == HEAD + 1, seg, 0.0)) * MASK_VALUE
            lat_ref[there, QR + KVR : LAT_WIDE] = (moved * tcos[here, :] + turned * tsin[here, :] + mask).astype(BF)
            handover(e).start()

    def serve(n):
        @pl.when(jnp.logical_and(is_mid, n < count))
        def _():
            first(n)

        @pl.when(jnp.logical_and(is_mid, jnp.logical_and(n >= LAT_DEPTH, n < count + LAT_DEPTH)))
        def _():
            second(n - LAT_DEPTH)
            finish_rows(n - LAT_DEPTH)

        @pl.when(jnp.logical_and(is_end, n < count))
        def _():
            to_mid(n).wait_send()
            to_end(n).wait_recv()
            finish_rows(n)

    each(2, serve)
    forward_u(0)
    each(4, lambda n: serve(n + 2))
    forward(0)
    each(4, lambda n: serve(n + 6))
    forward(1)
    final_u(0)
    each(count + LAT_DEPTH - 10, lambda n: serve(n + 10))
    drain_u(0)
    for p in range(peers):
        upg_ref[p] = up_all[p, 0, pl.ds(pl.multiple_of(core * 128, 128), 128), :]
    final(0)
    final(1)

    @pl.when(is_mid)
    def _():
        def sent(k):
            over(k).wait_send()
            to_end(k).wait_send()

        each(count, sent)

    drain(0)
    drain(1)

    def passed(e):
        handover(e).wait_send()
        here = pl.ds(pl.multiple_of((1 - core) * rows + e * LAT_LINE, LAT_LINE), LAT_LINE)
        remote(lat_ref.at[here], lat_ref.at[here], c_send.at[e], c_recv.at[e], {"ctx": 1 - core}).wait_recv()

    each(rows // LAT_LINE, passed)


def spread(peers):
    index = np.arange(KVR + ROPE)
    return jnp.asarray((index // 36 * 48 + index % 36)[:, None] == np.arange(peers * 48)[None], BF)


def latent_forward(x, gain, gain2, piece, up, length, gate_up):
    rows, width = x.shape
    peers = lax.axis_size("fsdp") * lax.axis_size("ctx")
    slot = rows * lax.axis_size("ctx")
    wide = rows + LAT_LINE
    count = wide // LAT_LINE
    sel = spread(peers)
    frequency = (ROPE_BASE ** (-2.0 * np.arange(ROPE // 2) / ROPE)).astype(np.float32)
    vmem = pl.BlockSpec(memory_space=pltpu.VMEM)
    dma = pltpu.SemaphoreType.DMA
    return pl.pallas_call(
        latent_kernel,
        out_shape=[
            jax.ShapeDtypeStruct((LAT_WIDE, width), BF),
            jax.ShapeDtypeStruct((wide, LAT_WIDE), BF),
            jax.ShapeDtypeStruct((slot, LAT_WIDE), BF),
            jax.ShapeDtypeStruct((ROPE // 2, slot), F32),
            jax.ShapeDtypeStruct((ROPE // 2, slot), F32),
            jax.ShapeDtypeStruct((16, slot), BF),
            jax.ShapeDtypeStruct((peers, up.shape[1] // 2, up.shape[2]), BF),
            jax.ShapeDtypeStruct((rows, 128), F32),
            jax.ShapeDtypeStruct((rows, 128), F32),
            jax.ShapeDtypeStruct((16, QR + KVR), F32),
            jax.ShapeDtypeStruct((peers,) + gate_up.shape, BF),
        ],
        in_specs=[vmem] * 8 + [pl.BlockSpec(memory_space=pltpu.SMEM), pl.BlockSpec(memory_space=pl.ANY)],
        out_specs=[vmem] * 10 + [pl.BlockSpec(memory_space=pl.ANY)],
        scratch_shapes=[
            pltpu.VMEM((peers, 1, PIECE, width), BF),
            pltpu.VMEM((peers,) + up.shape, BF),
            pltpu.VMEM((wide, LAT_WIDE), BF),
            pltpu.VMEM((wide, LAT_WIDE), BF),
            pltpu.VMEM((wide, LAT_WIDE), BF),
            pltpu.VMEM((peers * 48, width), BF),
        ]
        + [dma((rows // LAT_LINE,))] * 2
        + [dma((count,))] * 6
        + [dma((1,))] * (2 * GATHER_SEMS)
        + [dma((2,))] * GATHER_SEMS,
        compiler_params=pltpu.CompilerParams(collective_id=0, has_side_effects=True, vmem_limit_bytes=62 * MIB),
        cost_estimate=pl.CostEstimate(flops=rows * LAT_WIDE * width * 2, bytes_accessed=150 * MIB, transcendentals=0),
        name="latent_forward",
    )(x, gain, gain2, piece, up, sel, jnp.asarray(frequency[:, None]), jnp.asarray(np.tile(frequency, 8)[None]), length, gate_up)


LINE = 16
DEPTH = 4
MLP_ROWS = 256
TILES = ((0, 384), (384, 384), (768, 384), (1152, 448))


def line_places(z):
    is_end = jnp.logical_or(z == 0, z == 3)
    partner = jnp.where(z == 0, 1, jnp.where(z == 3, 2, jnp.where(z == 1, 0, 3)))
    return is_end, jnp.logical_not(is_end), partner, jnp.where(z == 1, 2, 1)


def line_barrier(is_mid, is_end, partner, across):
    barrier = pltpu.get_barrier_semaphore()
    pl.semaphore_signal(barrier, inc=1, device_id={"tp": partner}, device_id_type=MESH)

    @pl.when(is_mid)
    def _():
        pl.semaphore_signal(barrier, inc=1, device_id={"tp": across}, device_id_type=MESH)
        pl.semaphore_wait(barrier, 2)

    @pl.when(is_end)
    def _():
        pl.semaphore_wait(barrier, 1)


def line_copies(source, near, cross, total, sems, partner, across, line=LINE):
    in_send, in_recv, mid_send, mid_recv, out_send, out_recv = sems

    def piece(k):
        return pl.ds(pl.multiple_of(k * line, line), line)

    def copy(src, dst, send, recv, k, to):
        return pltpu.make_async_remote_copy(
            src_ref=src.at[piece(k)], dst_ref=dst.at[piece(k)], send_sem=send.at[k], recv_sem=recv.at[k],
            device_id={"tp": to}, device_id_type=MESH,
        )

    to_mid = lambda k: copy(source, near, in_send, in_recv, k, partner)
    over = lambda k: copy(near, cross, mid_send, mid_recv, k, across)
    to_end = lambda k: copy(total, total, out_send, out_recv, k, partner)

    def first(k):
        to_mid(k).wait_recv()
        near[piece(k)] = source[piece(k)] + near[piece(k)]
        over(k).start()

    def second(k):
        over(k).wait_recv()
        total[piece(k)] = near[piece(k)] + cross[piece(k)]
        to_end(k).start()

    return to_mid, over, to_end, first, second


def each(count, body):
    def step(k, carry):
        body(k)
        return carry

    lax.fori_loop(0, count, step, 0)


def block_kernel(
    att_ref, x_ref, out_ref, gain_ref, live_ref, seed_any, gu_any, down_any,
    hid_any, dn_any, mo_any, n2t_any, act_any, dg_any, du_any,
    xb, near, cross, total, gu, down, n2, n2t, seed, d_all, act, dg, du,
    load_sem, down_sem, seed_sem, hid_sem, dn_sem, mo_sem, n2t_sem, act_sem, dg_sem, du_sem, *sems,
):
    z = lax.axis_index("tp")
    is_end, is_mid, partner, across = line_places(z)
    to_mid, over, to_end, first, second = line_copies(xb, near, cross, total, sems, partner, across)
    count = xb.shape[0] // LINE
    group = MLP_ROWS // LINE
    groups = count // group
    width = x_ref.shape[1]

    def rows_of(m):
        return pl.ds(pl.multiple_of(m * MLP_ROWS, MLP_ROWS), MLP_ROWS)

    peers, shard = gu_any.shape[0], gu_any.shape[2]
    load_gu = lambda p, i: pltpu.make_async_copy(gu_any.at[p, i], gu.at[i, pl.ds(p * shard, shard)], load_sem.at[p, i])
    load_down = pltpu.make_async_copy(down_any, down, down_sem)
    load_seed = lambda m: pltpu.make_async_copy(seed_any.at[rows_of(m)], seed, seed_sem.at[m])
    save_hid = lambda m: pltpu.make_async_copy(total.at[rows_of(m)], hid_any.at[rows_of(m)], hid_sem.at[m])
    save_dn = lambda m: pltpu.make_async_copy(xb.at[rows_of(m)], dn_any.at[rows_of(m)], dn_sem.at[m])
    save_mo = lambda m, n: pltpu.make_async_copy(
        cross.at[rows_of(m), pl.ds(n * width, width)], mo_any.at[n, rows_of(m)], mo_sem.at[m, n]
    )
    save_n2t = lambda m: pltpu.make_async_copy(n2t, n2t_any.at[:, rows_of(m)], n2t_sem.at[m])
    save_act = lambda m: pltpu.make_async_copy(act, act_any.at[rows_of(m)], act_sem.at[m])
    save_dg = lambda m: pltpu.make_async_copy(dg, dg_any.at[rows_of(m)], dg_sem.at[m])
    save_du = lambda m: pltpu.make_async_copy(du, du_any.at[rows_of(m)], du_sem.at[m])

    load_seed(0).start()
    load_down.start()
    for p in range(peers):
        load_gu(p, 0).start()
        load_gu(p, 1).start()
    line_barrier(is_mid, is_end, partner, across)

    mine = pl.ds(pl.multiple_of(z * width, 128), width)
    per = 128

    def project(p):
        rows = pl.ds(pl.multiple_of(p * per, per), per)
        part = dot_nt(att_ref[:, rows].astype(F32).T.astype(BF), out_ref[...]) * RESIDUAL_SCALE
        xb[rows, :] = part.astype(BF)
        xb[rows, mine] = (xb[rows, mine].astype(F32) + x_ref[rows, :].astype(F32)).astype(BF)

        @pl.when(is_end)
        def _():
            each(per // LINE, lambda n: to_mid(p * (per // LINE) + n).start())

    each(xb.shape[0] // per, project)

    @pl.when(is_mid)
    def _():
        each(DEPTH, first)

    load_down.wait()
    ahead = group // len(TILES) // groups

    def seed_product(m):
        load_seed(m).wait()

        def weigh(r):
            here = pl.ds(pl.multiple_of(r * 32, 32), 32)
            live = live_ref[pl.ds(pl.multiple_of(m * MLP_ROWS + r * 32, 32), 32), :]
            seed[here, :] = (seed[here, :].astype(F32) * (live * RESIDUAL_SCALE)).astype(BF)

        each(MLP_ROWS // 32, weigh)
        for t, (at, size) in enumerate(TILES):
            d_all[rows_of(m), pl.ds(at, size)] = dot_nn(seed[...], down[:, pl.ds(at, size)]).astype(BF)

            @pl.when(is_mid)
            def _():
                def both(v):
                    k = (m * len(TILES) + t) * ahead + v
                    first(k + DEPTH)
                    second(k)

                each(ahead, both)

        @pl.when(m + 1 < groups)
        def _():
            load_seed(m + 1).start()

    each(groups, seed_product)

    def mlp(m):
        rows = rows_of(m)

        @pl.when(is_end)
        def _():
            def arrive(n):
                to_mid(m * group + n).wait_send()
                to_end(m * group + n).wait_recv()

            each(group, arrive)

        def serve(n):
            def one(v):
                k = (m + 1) * group + DEPTH + n * (group // 8) + v

                @pl.when(jnp.logical_and(is_mid, k < count))
                def _():
                    first(k)

                @pl.when(jnp.logical_and(is_mid, k < count + DEPTH))
                def _():
                    second(k - DEPTH)

            each(group // 8, one)

        save_hid(m).start()

        @pl.when(m > 0)
        def _():
            save_n2t(m - 1).wait()
            save_act(m - 1).wait()
            save_dg(m - 1).wait()
            save_du(m - 1).wait()

        def normalize(r):
            here = pl.ds(pl.multiple_of(r * 32, 32), 32)
            h = total[pl.ds(pl.multiple_of(m * MLP_ROWS + r * 32, 32), 32), :].astype(F32)
            factor = lax.rsqrt(jnp.mean(h * h, axis=1, keepdims=True) + EPS_NORM)
            n2[here, :] = (h * factor * gain_ref[...]).astype(BF)

        each(MLP_ROWS // 32, normalize)

        def turn(c):
            cols = pl.ds(pl.multiple_of(c * 256, 256), 256)
            n2t[cols, :] = n2[:, cols].astype(F32).T.astype(BF)

        each(D // 256, turn)
        save_n2t(m).start()
        @pl.when(m == 0)
        def _():
            for p in range(peers):
                load_gu(p, 0).wait()
                load_gu(p, 1).wait()

        for t, (at, size) in enumerate(TILES):
            cols = pl.ds(at, size)
            g = dot_nn(n2[...], gu[0, :, cols])
            u = dot_nn(n2[...], gu[1, :, cols])
            d = d_all[rows, cols].astype(F32)
            sig = jax.nn.sigmoid(g)
            act[:, cols] = (g * sig * u).astype(BF)
            dg[:, cols] = (d * u * sig * (1.0 + g * (1.0 - sig))).astype(BF)
            du[:, cols] = (d * g * sig).astype(BF)
            serve(t)
        save_act(m).start()
        save_dg(m).start()
        save_du(m).start()

        for n in range(4):
            cols = pl.ds(n * 640, 640)
            xb[rows, cols] = (dot_nt(dg[...], gu[0, cols, :]) + dot_nt(du[...], gu[1, cols, :])).astype(BF)
            cross[rows, cols] = dot_nt(act[...], down[cols, :]).astype(BF)
            serve(4 + n)
        save_dn(m).start()
        for n in range(4):
            save_mo(m, n).start()

    each(groups, mlp)

    def finish(m):
        save_hid(m).wait()
        save_dn(m).wait()
        for n in range(4):
            save_mo(m, n).wait()

    each(groups, finish)
    save_n2t(groups - 1).wait()
    save_act(groups - 1).wait()
    save_dg(groups - 1).wait()
    save_du(groups - 1).wait()

    @pl.when(is_mid)
    def _():
        def sent(k):
            over(k).wait_send()
            to_end(k).wait_send()

        each(count, sent)


def block_forward(att, x, out_t, gain, live, seed, gate_up, down_t):
    rows, width = x.shape
    hidden_units = down_t.shape[1]
    count, groups = rows // LINE, rows // MLP_ROWS
    vmem = pl.BlockSpec(memory_space=pltpu.VMEM)
    anywhere = pl.BlockSpec(memory_space=pl.ANY)
    wide = jax.ShapeDtypeStruct((rows, D), BF)
    units = jax.ShapeDtypeStruct((rows, hidden_units), BF)
    dma = pltpu.SemaphoreType.DMA
    return pl.pallas_call(
        block_kernel,
        out_shape=[wide, wide, jax.ShapeDtypeStruct((4, rows, width), BF), jax.ShapeDtypeStruct((D, rows), BF), units, units, units],
        in_specs=[vmem] * 5 + [anywhere] * 3,
        out_specs=[anywhere] * 7,
        scratch_shapes=[pltpu.VMEM((rows, D), BF)] * 4
        + [
            pltpu.VMEM((2, D, hidden_units), BF),
            pltpu.VMEM(down_t.shape, BF),
            pltpu.VMEM((MLP_ROWS, D), BF),
            pltpu.VMEM((D, MLP_ROWS), BF),
            pltpu.VMEM((MLP_ROWS, D), BF),
            pltpu.VMEM((rows, hidden_units), BF),
        ]
        + [pltpu.VMEM((MLP_ROWS, hidden_units), BF)] * 3
        + [dma(gate_up.shape[:2]), dma]
        + [dma((groups,))] * 3
        + [dma((groups, 4))]
        + [dma((groups,))] * 4
        + [dma((count,))] * 6,
        compiler_params=pltpu.CompilerParams(collective_id=3, has_side_effects=True, vmem_limit_bytes=63 * MIB),
        cost_estimate=pl.CostEstimate(flops=rows * D * hidden_units * 12, bytes_accessed=400 * MIB, transcendentals=0),
        name="block_forward",
    )(att, x, out_t, gain, live, seed, gate_up, down_t)


LAG = 8
ROWS = 32
LOAD = 128


def total_square(v):
    v = v.astype(F32)
    return jnp.sum(jnp.sum(v * v, axis=0, keepdims=True), axis=1, keepdims=True)


def grad_kernel(
    live_ref, gain_ref, dnp_any, hid_any, cot_any, n2t_any, dg_any, du_any, act_any,
    sa_any, dh_any, gain_out, grad_any, square_out,
    near, cross, total, cin, stage, xin, yin2, yin, xin2, lhs, rhs, hbuf, cbuf, sbuf, dbuf, prep,
    total_sem, lhs_sem, rhs_sem, h_sem, c_sem, sa_sem, dh_sem, prep_sem, out_sem,
    core_send, core_recv, x_send, x_recv, y2_send, y2_recv, y_send, y_recv, x2_send, x2_recv, *sems,
):
    z, core, place = lax.axis_index("tp"), lax.axis_index("ctx"), lax.axis_index("fsdp")
    y, x = place // 2, place % 2
    is_end, is_mid, partner, across = line_places(z)
    to_mid, over, to_end, _, _ = line_copies(dnp_any, near, cross, total, sems, partner, across)
    count = total.shape[0] // LINE
    width = dh_any.shape[1]
    half = yin.shape[1]
    block = 2 * half
    mine = pl.ds(pl.multiple_of(z * width, 128), width)
    to_core, to_x, to_y = {"ctx": 1 - core}, {"fsdp": y * 2 + 1 - x}, {"fsdp": (1 - y) * 2 + x}

    def piece(k):
        return pl.ds(pl.multiple_of(k * LINE, LINE), LINE)

    def band(e):
        return pl.ds(pl.multiple_of(e * ROWS, ROWS), ROWS)

    bands = total.shape[0] // ROWS
    twice = ROWS // LINE

    def remote(src, dst, send, recv, to):
        return pltpu.make_async_remote_copy(
            src_ref=src, dst_ref=dst, send_sem=send, recv_sem=recv, device_id=to, device_id_type=MESH
        )

    local = pltpu.make_async_copy
    load_total = local(dnp_any, total, total_sem)
    load_lhs = local(n2t_any, lhs, lhs_sem)
    right = (dg_any, du_any, act_any)
    load_rhs = lambda i: local(right[i], rhs.at[i % 2], rhs_sem.at[i])
    rows_of = lambda g: pl.ds(pl.multiple_of(g * LOAD, LOAD), LOAD)
    load_h = lambda g: local(hid_any.at[rows_of(g)], hbuf.at[g % 2], h_sem.at[g])
    load_c = lambda g: local(cot_any.at[rows_of(g)], cbuf.at[g % 2], c_sem.at[g])
    save_sa = lambda e: local(sbuf.at[e % 2], sa_any.at[band(e)], sa_sem.at[e])
    save_dh = lambda e: local(dbuf.at[e % 2], dh_any.at[band(e)], dh_sem.at[e])

    load_lhs.start()
    load_rhs(0).start()
    load_rhs(1).start()
    load_h(0).start()
    load_c(0).start()

    @pl.when(is_mid)
    def _():
        load_total.start()

    barrier = pltpu.get_barrier_semaphore()
    for to in (to_core, to_x, to_y, {"tp": partner}):
        pl.semaphore_signal(barrier, inc=1, device_id=to, device_id_type=MESH)

    @pl.when(is_mid)
    def _():
        pl.semaphore_signal(barrier, inc=1, device_id={"tp": across}, device_id_type=MESH)
        pl.semaphore_wait(barrier, 5)

    @pl.when(is_end)
    def _():
        pl.semaphore_wait(barrier, 4)
        each(count, lambda k: to_mid(k).start())

    gain_out[...] = jnp.zeros_like(gain_out)

    @pl.when(is_mid)
    def _():
        load_total.wait()

    def finish_rows(e):
        per = LOAD // ROWS
        g = e // per

        @pl.when(e % per == 0)
        def _():
            load_h(g).wait()
            load_c(g).wait()

            @pl.when(g + 1 < bands // per)
            def _():
                load_h(g + 1).start()
                load_c(g + 1).start()

        @pl.when(e >= 2)
        def _():
            save_sa(e - 2).wait()
            save_dh(e - 2).wait()

        here = pl.ds(pl.multiple_of((e % per) * ROWS, ROWS), ROWS)
        live = live_ref[band(e), :]

        def grads_of(dn, h, dy, gain, factor, inner):
            return dy * live + factor * (dn * gain) - h * (factor * factor * factor * inner)

        dn = total[band(e), :].astype(F32)
        h = hbuf[g % 2, here, :].astype(F32)
        factor = lax.rsqrt(jnp.mean(h * h, axis=1, keepdims=True) + EPS_NORM)
        inner = jnp.mean(dn * gain_ref[...] * h, axis=1, keepdims=True)
        dy = cbuf[g % 2, here, :].astype(F32)
        sbuf[e % 2] = (RESIDUAL_SCALE * grads_of(dn, h, dy, gain_ref[...], factor, inner)).astype(BF)
        own_dn = total[band(e), mine].astype(F32)
        own_h = hbuf[g % 2, here, mine].astype(F32)
        own_dy = cbuf[g % 2, here, mine].astype(F32)
        dbuf[e % 2] = grads_of(own_dn, own_h, own_dy, gain_ref[:, mine], factor, inner)
        gain_out[...] += jnp.sum(own_dn * own_h * factor, axis=0, keepdims=True)
        save_sa(e).start()
        save_dh(e).start()

    def serve(n):
        @pl.when(jnp.logical_and(is_mid, n < count))
        def _():
            to_mid(n).wait_recv()
            near[piece(n)] = total[piece(n)] + near[piece(n)]
            over(n).start()

        @pl.when(jnp.logical_and(is_mid, jnp.logical_and(n >= DEPTH, n < count + DEPTH)))
        def _():
            k = n - DEPTH
            over(k).wait_recv()
            total[piece(k)] = near[piece(k)] + cross[piece(k)]
            to_end(k).start()

            @pl.when(k % twice == twice - 1)
            def _():
                finish_rows(k // twice)

        @pl.when(jnp.logical_and(is_end, jnp.logical_and(n >= LAG, n < count + LAG)))
        def _():
            k = n - LAG
            to_mid(k).wait_send()
            to_end(k).wait_recv()

            @pl.when(k % twice == twice - 1)
            def _():
                finish_rows(k // twice)

    def flip(v, by):
        return v + by - 2 * v * by

    def spot(j):
        down, over_x = 1 - j // 2, 1 - j % 2
        return down, over_x, flip(y, down), flip(x, over_x)

    def tile(i, f, parity):
        rows = pl.ds(pl.multiple_of((2 * f + parity) * block, 16), block)
        return dot_nn(lhs[rows, :], rhs[i % 2])

    upper, lower = pl.ds(0, half), pl.ds(half, half)
    core_copy = lambda i, j, f: remote(stage.at[j % 2], cin.at[i, f], core_send.at[i, j], core_recv.at[i, f], to_core)
    x_copy = lambda i, f, yy: remote(cin.at[i, f, upper], xin.at[i, yy], x_send.at[i, yy], x_recv.at[i, yy], to_x)
    y2_copy = lambda i, f, xx: remote(cin.at[i, f, lower], yin2.at[i, xx], y2_send.at[i, xx], y2_recv.at[i, xx], to_y)
    y_copy = lambda i: remote(xin.at[i, 1 - y], yin.at[i], y_send.at[i], y_recv.at[i], to_y)
    x2_copy = lambda i: remote(yin2.at[i, 1 - x], xin2.at[i], x2_send.at[i], x2_recv.at[i], to_x)
    save_upper = lambda i: local(yin.at[i], grad_any.at[i, upper], out_sem.at[i, 0])
    save_lower = lambda i: local(xin2.at[i], grad_any.at[i, lower], out_sem.at[i, 1])

    def plus(a, b):
        return a + b

    def products(i, n0):
        def for_other(j):
            _, _, yy, xx = spot(j)
            f = yy * 2 + xx

            @pl.when(j >= 2)
            def _():
                core_copy(i, j - 2, f).wait_send()

            stage[j % 2] = tile(i, f, 1 - core).astype(BF)
            core_copy(i, j, f).start()
            serve(n0 + j)

        each(4, for_other)

        def for_own(j):
            down, over_x, yy, xx = spot(j)
            f = yy * 2 + xx
            own = tile(i, f, core)
            core_copy(i, j, f).wait_recv()
            cin[i, f] = (own + cin[i, f].astype(F32)).astype(BF)

            @pl.when(over_x == 1)
            def _():
                x_copy(i, f, yy).start()

            @pl.when(down == 1)
            def _():
                y2_copy(i, f, xx).start()

            serve(n0 + 4 + j)

        each(4, for_own)
        for j in (2, 3):
            core_copy(i, j, 0).wait_send()

    def first_stage(i):
        x_copy(i, 0, 1 - y).wait_recv()
        xin[i, 1 - y] = plus(xin[i, 1 - y], cin[i, (1 - y) * 2 + x, upper])
        y_copy(i).start()
        y2_copy(i, 0, 1 - x).wait_recv()
        yin2[i, 1 - x] = plus(yin2[i, 1 - x], cin[i, y * 2 + 1 - x, lower])
        x2_copy(i).start()
        x_copy(i, 0, y).wait_recv()
        xin[i, y] = plus(xin[i, y], cin[i, y * 2 + x, upper])
        y2_copy(i, 0, x).wait_recv()
        yin2[i, x] = plus(yin2[i, x], cin[i, y * 2 + x, lower])

    def second_stage(i):
        y_copy(i).wait_recv()
        yin[i] = plus(yin[i], xin[i, y])
        save_upper(i).start()
        x2_copy(i).wait_recv()
        xin2[i] = plus(xin2[i], yin2[i, x])
        save_lower(i).start()
        square = total_square(yin[i]) + total_square(xin2[i])
        square_out[i : i + 1, :] = jnp.broadcast_to(square, (1, 128))

    square_out[...] = jnp.zeros_like(square_out)
    load_lhs.wait()
    load_rhs(0).wait()
    products(0, 0)
    load_rhs(2).start()
    load_rhs(1).wait()
    products(1, 8)

    cols_of = lambda c: pl.ds(pl.multiple_of(c * 256, 256), 256)
    load_prep = lambda c: local(cot_any.at[:, cols_of(c)], prep.at[c % 2], prep_sem.at[c])
    load_prep(0).start()
    groups = D // 256

    def turn(c):
        load_prep(c).wait()

        @pl.when(c + 1 < groups)
        def _():
            load_prep(c + 1).start()

        seed = prep[c % 2].astype(F32) * (live_ref[...] * RESIDUAL_SCALE)
        lhs[cols_of(c), :] = seed.T.astype(BF)
        serve(16 + c)

    each(groups, turn)
    first_stage(0)
    load_rhs(2).wait()
    products(2, 16 + groups)
    served = 24 + groups

    def serve_until(stop, served):
        each(stop - served, lambda n: serve(n + served))
        return stop

    first_stage(1)
    served = serve_until(42, served)
    second_stage(0)
    served = serve_until(50, served)
    first_stage(2)
    served = serve_until(58, served)
    second_stage(1)
    serve_until(count + LAG, served)
    second_stage(2)
    for i in range(3):
        for v in range(2):
            x_copy(i, 0, v).wait_send()
            y2_copy(i, 0, v).wait_send()
        y_copy(i).wait_send()
        x2_copy(i).wait_send()
        save_upper(i).wait()
        save_lower(i).wait()
    for e in (bands - 2, bands - 1):
        save_sa(e).wait()
        save_dh(e).wait()

    @pl.when(is_mid)
    def _():
        def sent(k):
            over(k).wait_send()
            to_end(k).wait_send()

        each(count, sent)


def grad_reduce(live, gain, d_normed_part, hidden, cotangent, normed_t, d_gate, d_up, activation):
    rows = hidden.shape[0]
    units = d_gate.shape[1]
    width = D // lax.axis_size("tp")
    shard = D // (lax.axis_size("fsdp") * lax.axis_size("ctx"))
    count = rows // LINE
    vmem = pl.BlockSpec(memory_space=pltpu.VMEM)
    anywhere = pl.BlockSpec(memory_space=pl.ANY)
    dma = pltpu.SemaphoreType.DMA
    scratch = lambda *shape: pltpu.VMEM(shape, BF)
    return pl.pallas_call(
        grad_kernel,
        out_shape=[
            jax.ShapeDtypeStruct((rows, D), BF),
            jax.ShapeDtypeStruct((rows, width), F32),
            jax.ShapeDtypeStruct((1, width), F32),
            jax.ShapeDtypeStruct((3, shard, units), BF),
            jax.ShapeDtypeStruct((8, 128), F32),
        ],
        in_specs=[vmem] * 2 + [anywhere] * 7,
        out_specs=[anywhere, anywhere, vmem, anywhere, vmem],
        scratch_shapes=[scratch(rows, D)] * 3
        + [
            scratch(3, 4, shard, units),
            scratch(2, shard, units),
            scratch(3, 2, shard // 2, units),
            scratch(3, 2, shard // 2, units),
            scratch(3, shard // 2, units),
            scratch(3, shard // 2, units),
            scratch(D, rows),
            scratch(2, rows, units),
            scratch(2, LOAD, D),
            scratch(2, LOAD, D),
            scratch(2, ROWS, D),
            pltpu.VMEM((2, ROWS, width), F32),
            scratch(2, rows, 256),
        ]
        + [dma, dma, dma((3,)), dma((rows // LOAD,)), dma((rows // LOAD,)), dma((rows // ROWS,)), dma((rows // ROWS,)), dma((D // 256,)), dma((3, 2))]
        + [dma((3, 4))] * 2
        + [dma((3, 2))] * 4
        + [dma((3,))] * 4
        + [dma((count,))] * 6,
        compiler_params=pltpu.CompilerParams(collective_id=4, has_side_effects=True, vmem_limit_bytes=63 * MIB),
        cost_estimate=pl.CostEstimate(flops=rows * D * units * 6, bytes_accessed=400 * MIB, transcendentals=0),
        name="grad_reduce",
    )(live, gain, d_normed_part, hidden, cotangent, normed_t, d_gate, d_up, activation)


PACK = 576
HALF = PACK // 2
SHARE = 256


def torus(s1, xin, yin2, yin, xin2, sems, x, y, to_x, to_y):
    x_send, x_recv, y2_send, y2_recv, y_send, y_recv, x2_send, x2_recv = sems
    half = yin.shape[0]
    upper, lower = pl.ds(0, half), pl.ds(half, half)

    def remote(src, dst, send, recv, to):
        return pltpu.make_async_remote_copy(
            src_ref=src, dst_ref=dst, send_sem=send, recv_sem=recv, device_id=to, device_id_type=MESH
        )

    def plus(a, b):
        return a + b

    x_copy = lambda v: remote(s1.at[v * 2 + 1 - x, upper], xin.at[v], x_send.at[v], x_recv.at[v], to_x)
    y2_copy = lambda v: remote(s1.at[(1 - y) * 2 + v, lower], yin2.at[v], y2_send.at[v], y2_recv.at[v], to_y)
    y_copy = remote(xin.at[1 - y], yin, y_send.at[0], y_recv.at[0], to_y)
    x2_copy = remote(yin2.at[1 - x], xin2, x2_send.at[0], x2_recv.at[0], to_x)

    def begin():
        x_copy(1 - y).start()
        y2_copy(1 - x).start()
        x_copy(y).start()
        y2_copy(x).start()

    def middle():
        x_copy(1 - y).wait_recv()
        xin[1 - y] = plus(xin[1 - y], s1[(1 - y) * 2 + x, upper])
        y_copy.start()
        y2_copy(1 - x).wait_recv()
        yin2[1 - x] = plus(yin2[1 - x], s1[y * 2 + 1 - x, lower])
        x2_copy.start()
        x_copy(y).wait_recv()
        xin[y] = plus(xin[y], s1[y * 2 + x, upper])
        y2_copy(x).wait_recv()
        yin2[x] = plus(yin2[x], s1[y * 2 + x, lower])

    def last(out):
        y_copy.wait_recv()
        out[upper, :] = plus(yin[...], xin[y])
        x2_copy.wait_recv()
        out[lower, :] = plus(xin2[...], yin2[x])

    def drain():
        for v in range(2):
            x_copy(v).wait_send()
            y2_copy(v).wait_send()
        y_copy.wait_send()
        x2_copy.wait_send()

    return begin, middle, last, drain


def latent_back_kernel(
    dq_ref, de_ref, dkr_ref, up_ref, sum_ref, w_ref, x_ref, gain_ref, dh_ref, tcos, tsin, gains, gout_ref, gq_ref, gkv_ref,
    sel_ref, b2_ref, square_ref, limit_ref, fold_ref,
    gin_ref, pack_out, wd_out, small_out, scalar_out, gq_out, gkv_out,
    uq, ukv, away, arrived, xb, near, cross, total, dl, dlt, xg, weight, w_pack, small, small_in, scal_in,
    s1, cin, xin, yin2, yin, xin2, s1w, cinw, xinw, yin2w, yinw, xin2w,
    lat_send, lat_recv, out_send, out_recv, q_send, q_recv, kv_send, kv_recv, w_send, w_recv,
    small_send, small_recv, scal_send, scal_recv, *sems,
):
    z, core, place = lax.axis_index("tp"), lax.axis_index("ctx"), lax.axis_index("fsdp")
    y, x = place // 2, place % 2
    is_end, is_mid, partner, across = line_places(z)
    line_sems, pack_sems, w_sems = sems[:6], sems[6:14], sems[14:22]
    to_mid, over, to_end, first, second = line_copies(xb, near, cross, total, line_sems, partner, across, LAT_LINE)
    count = xb.shape[0] // LAT_LINE
    rows = xb.shape[0]
    peers = up_ref.shape[0]
    me = place * 2 + core
    to_core, to_x, to_y = {"ctx": 1 - core}, {"fsdp": y * 2 + 1 - x}, {"fsdp": (1 - y) * 2 + x}

    def remote(src, dst, send, recv, to):
        return pltpu.make_async_remote_copy(
            src_ref=src, dst_ref=dst, send_sem=send, recv_sem=recv, device_id=to, device_id_type=MESH
        )

    def peer(d):
        to = lax.rem(me + d, peers)
        return {"fsdp": to // 2, "ctx": lax.rem(to, 2)}

    barrier = pltpu.get_barrier_semaphore()
    for d in range(1, peers):
        pl.semaphore_signal(barrier, inc=1, device_id=peer(d), device_id_type=MESH)
    for d in range(1, 4):
        pl.semaphore_signal(barrier, inc=1, device_id={"tp": lax.rem(z + d, 4)}, device_id_type=MESH)
    pl.semaphore_wait(barrier, peers + 2)

    def piece(e):
        return pl.ds(pl.multiple_of(e * LAT_LINE, LAT_LINE), LAT_LINE)

    def span(f, parity, size):
        return pl.ds(pl.multiple_of((2 * f + parity) * size, size), size)

    slot_q, slot_kv = pl.ds(320 + 96 * core, 96), pl.ds(512 + 32 * core, 32)
    other_q, other_kv = pl.ds(320 + 96 * (1 - core), 96), pl.ds(512 + 32 * (1 - core), 32)
    out_copy = lambda f: remote(gout_ref.at[span(f, 1 - core, 320)], cin.at[f], out_send.at[f], out_recv.at[f], to_core)
    q_copy = lambda f: remote(gq_ref.at[span(f, 1 - core, 96)], s1.at[f, slot_q], q_send.at[f], q_recv.at[f], to_core)
    kv_copy = lambda f: remote(gkv_ref.at[span(f, 1 - core, 32)], s1.at[f, slot_kv], kv_send.at[f], kv_recv.at[f], to_core)
    q_got = lambda f: remote(gq_ref.at[span(f, 1 - core, 96)], s1.at[f, other_q], q_send.at[f], q_recv.at[f], to_core)
    kv_got = lambda f: remote(gkv_ref.at[span(f, 1 - core, 32)], s1.at[f, other_kv], kv_send.at[f], kv_recv.at[f], to_core)

    for p in range(peers):
        uq[p * 96 : (p + 1) * 96, :] = up_ref[p, 0:96, :]
        ukv[p * 32 : (p + 1) * 32, :] = up_ref[p, 96:128, :]

    lane = lax.broadcasted_iota(jnp.int32, (1, 128), 1)
    block = lambda e: pl.ds(pl.multiple_of(e * SHARE, SHARE), SHARE)
    hand = lambda e: remote(away.at[block(e)], arrived.at[block(e)], lat_send.at[e], lat_recv.at[e], to_core)
    shares = rows // SHARE

    def share(at):
        here = pl.ds(pl.multiple_of(at, SHARE), SHARE)
        q = dot_nt(dq_ref[here, :], uq[...])
        kv = dot_nt(de_ref[here, :], ukv[...])
        rope = jnp.where(lane < ROPE, pltpu.roll(dkr_ref[here, :], NOPE, 1), 0.0)
        return q, kv, rope

    def send_away(e):
        q, kv, rope = share((1 - core) * rows + e * SHARE)
        away[block(e), 0:QR] = q.astype(BF)
        away[block(e), QR : QR + KVR] = kv.astype(BF)
        away[block(e), QR + KVR : LAT_WIDE] = rope.astype(BF)
        hand(e).start()

    each(shares, send_away)
    for f in range(4):
        out_copy(f).start()
        q_copy(f).start()
        kv_copy(f).start()

    def keep(e):
        q, kv, rope = share(core * rows + e * SHARE)
        hand(e).wait_recv()
        got = arrived[block(e), :].astype(F32)
        xb[block(e), 0:QR] = (q + got[:, 0:QR]).astype(BF)
        xb[block(e), QR : QR + KVR] = (kv + got[:, QR : QR + KVR]).astype(BF)
        xb[block(e), QR + KVR : LAT_WIDE] = (rope + got[:, QR + KVR :]).astype(BF)

        @pl.when(is_end)
        def _():
            each(SHARE // LAT_LINE, lambda n: to_mid(e * (SHARE // LAT_LINE) + n).start())

    each(shares, keep)

    small[...] = jnp.zeros_like(small)
    small[2:3, 0 : b2_ref.shape[1]] = b2_ref[...]
    stat_lane = lax.broadcasted_iota(jnp.int32, (1, LAT_WIDE), 1)
    stat_lane = jnp.logical_and(stat_lane >= LAT, stat_lane < LAT + 8)
    gain_q, gain_kv = gains[0:1, 0:QR], gains[0:1, QR : QR + KVR]

    def through(d, v, gain):
        factor = lax.rsqrt(jnp.mean(v * v, axis=1, keepdims=True) + EPS_NORM)
        scaled = d * gain
        gain_grad = jnp.sum(d * v * factor, axis=0, keepdims=True)
        return factor * scaled - v * (factor * factor * factor * jnp.mean(scaled * v, axis=1, keepdims=True)), gain_grad

    def finish_rows(e):
        v = sum_ref[piece(e), :].astype(F32)
        square = jnp.sum(jnp.where(stat_lane, v, 0.0), axis=1, keepdims=True)
        factor = lax.rsqrt(square / D + EPS_NORM)
        v = v * factor
        d = total[piece(e), :].astype(F32)
        ql, kl, raw = v[:, :QR], v[:, QR : QR + KVR], jnp.where(lane < ROPE, v[:, QR + KVR :], 0.0)
        dql, grad_q = through(d[:, :QR], ql, gain_q)
        dkl, grad_kv = through(d[:, QR : QR + KVR], kl, gain_kv)
        moved = pltpu.roll(d[:, QR + KVR :], NOPE, 1)
        turned = jnp.where(lane < NOPE + 16, pltpu.roll(moved, 128 - 16, 1), -pltpu.roll(moved, 16, 1))
        rope = pltpu.roll(moved * tcos[piece(e), :] + turned * tsin[piece(e), :], NOPE, 1)
        inner = (
            jnp.sum(dql * ql, axis=1, keepdims=True)
            + jnp.sum(dkl * kl, axis=1, keepdims=True)
            + jnp.sum(rope * raw, axis=1, keepdims=True)
        ) / D
        small[0:1, 0:QR] += grad_q
        small[0:1, QR : QR + KVR] += grad_kv
        dl[piece(e), 0:QR] = (dql * factor).astype(BF)
        dl[piece(e), QR : QR + KVR] = (dkl * factor).astype(BF)
        dl[piece(e), QR + KVR : LAT_WIDE] = (rope * factor).astype(BF)
        weight[piece(e), :] = jnp.broadcast_to(factor * factor * inner, (LAT_LINE, 128))

        @pl.when(e % 2 == 1)
        def _():
            pair = pl.ds(pl.multiple_of((e - 1) * LAT_LINE, 128), 128)
            d_in = dot_nn(dl[pair, :], w_ref[...])
            rows_in = x_ref[pair, :].astype(F32)
            gin_ref[pair, :] = (dh_ref[pair, :] + d_in * gain_ref[...] - rows_in * weight[pair, 0:1]).astype(BF)
            small[1:2, 0 : d_in.shape[1]] += jnp.sum(d_in * rows_in, axis=0, keepdims=True)
            xg[pair, :] = (rows_in * gain_ref[...]).astype(BF)
            dlt[:, pair] = dl[pair, :].astype(F32).T.astype(BF)

    def serve(n):
        @pl.when(jnp.logical_and(is_mid, n < count))
        def _():
            first(n)

        @pl.when(jnp.logical_and(is_mid, jnp.logical_and(n >= LAT_DEPTH, n < count + LAT_DEPTH)))
        def _():
            second(n - LAT_DEPTH)
            finish_rows(n - LAT_DEPTH)

        @pl.when(jnp.logical_and(is_end, jnp.logical_and(n >= 3, n < count + 3)))
        def _():
            to_mid(n - 3).wait_send()
            to_end(n - 3).wait_recv()
            finish_rows(n - 3)

    begin, middle, last, drain = torus(s1, xin, yin2, yin, xin2, pack_sems, x, y, to_x, to_y)
    begin_w, middle_w, last_w, drain_w = torus(s1w, xinw, yin2w, yinw, xin2w, w_sems, x, y, to_x, to_y)

    serve(0)
    for f in range(4):
        out_copy(f).wait_recv()
        s1[f, 0:320] = (gout_ref[span(f, core, 320), :].astype(F32) + cin[f].astype(F32)).astype(BF)
        s1[f, slot_q] = gq_ref[span(f, core, 96), :]
        s1[f, slot_kv] = gkv_ref[span(f, core, 32), :]
        q_got(f).wait_recv()
        kv_got(f).wait_recv()
    begin()
    each(6, lambda n: serve(n + 1))
    middle()
    each(4, lambda n: serve(n + 7))
    last(pack_out)
    lanes = pack_out.shape[1]
    gq_out[...] = dot_nn(pack_out[320:416, :], fold_ref[0:lanes, :]) + dot_nn(pack_out[416:512, :], fold_ref[lanes:, :])
    gkv_out[:, 0:lanes] = pack_out[512:544, :].astype(F32)
    gkv_out[:, lanes : 2 * lanes] = pack_out[544:576, :].astype(F32)
    each(count + 3 - 11, lambda n: serve(n + 11))

    both = dot_nn(dlt[0:QR, :], xg[...])
    for p in range(peers):
        w_pack[p, 0:96, :] = both[p * 96 : (p + 1) * 96].astype(BF)
    tail = dot_nn(dlt[QR:LAT, :], xg[...]).astype(BF)
    wide = lax.dot_general(sel_ref[...], tail, (((0,), (0,)), ((), ())), preferred_element_type=F32)
    for p in range(peers):
        w_pack[p, 96:144, :] = wide[p * 48 : (p + 1) * 48].astype(BF)
        w_pack[p, 144:160, :] = jnp.zeros((16, wide.shape[1]), BF)
    w_copy = lambda f: remote(w_pack.at[2 * f + 1 - core], cinw.at[f], w_send.at[f], w_recv.at[f], to_core)
    for f in range(4):
        w_copy(f).start()
    for f in range(4):
        w_copy(f).wait_recv()
        s1w[f] = (w_pack[2 * f + core].astype(F32) + cinw[f].astype(F32)).astype(BF)
    begin_w()
    middle_w()
    last_w(wd_out)

    squares = (
        total_square(wd_out[0:96, :]),
        total_square(wd_out[96:144, :]),
        total_square(pack_out[320:512, :]),
        total_square(pack_out[512:576, :]),
        total_square(pack_out[0:320, :]),
        square_ref[0:1, 0:1] + square_ref[1:2, 0:1],
        square_ref[2:3, 0:1],
    )
    line = jnp.zeros((1, 128), F32)
    for n, v in enumerate(squares):
        line = jnp.where(lane == n, v, line)
    small[3:4, 0:128] = line
    small_copy = lambda d, source: remote(small, small_in.at[source], small_send.at[d], small_recv.at[source], peer(d))
    for d in range(1, peers):
        small_copy(d, me).start()
    small_in[me] = small[...]
    for d in range(1, peers):
        small_copy(d, lax.rem(me + peers - d, peers)).wait_recv()
    whole = small_in[0]
    for p in range(1, peers):
        whole = whole + small_in[p]
    small_out[...] = whole
    norms = total_square(whole[1:2]) + total_square(whole[2:3])
    scal_in[z] = jnp.broadcast_to(jnp.where(lane == 7, norms, whole[3:4, 0:128]), (8, 128))
    scal_copy = lambda d, source: remote(
        scal_in.at[z], scal_in.at[source], scal_send.at[d], scal_recv.at[source], {"tp": lax.rem(z + d, 4)}
    )
    for d in range(1, 4):
        scal_copy(d, z).start()
    for d in range(1, 4):
        scal_copy(d, lax.rem(z + 4 - d, 4)).wait_recv()
    scalars = (scal_in[0] + scal_in[1]) + (scal_in[2] + scal_in[3])
    scalars = jnp.where(lane == 8, total_square(whole[0:1]), scalars)
    scalar_out[...] = limit_ref[...] / jnp.maximum(jnp.sqrt(scalars), limit_ref[...])

    for d in range(1, peers):
        small_copy(d, me).wait_send()
    for d in range(1, 4):
        scal_copy(d, z).wait_send()
    drain()
    drain_w()
    for f in range(4):
        out_copy(f).wait_send()
        q_copy(f).wait_send()
        kv_copy(f).wait_send()
        w_copy(f).wait_send()
    each(shares, lambda e: hand(e).wait_send())

    @pl.when(is_mid)
    def _():
        def sent(k):
            over(k).wait_send()
            to_end(k).wait_send()

        each(count, sent)


def latent_backward(*args):
    dq, up, x = args[0], args[3], args[6]
    rows, width = x.shape
    lanes = dq.shape[1]
    peers = up.shape[0]
    count = rows // LAT_LINE
    vmem = pl.BlockSpec(memory_space=pltpu.VMEM)
    dma = pltpu.SemaphoreType.DMA
    scratch = lambda *shape: pltpu.VMEM(shape, BF)
    halves = lambda half: [scratch(2, half, width), scratch(2, half, width), scratch(half, width), scratch(half, width)]
    torus_sems = [dma((2,))] * 4 + [dma((1,))] * 4
    return pl.pallas_call(
        latent_back_kernel,
        out_shape=[
            jax.ShapeDtypeStruct((rows, width), BF),
            jax.ShapeDtypeStruct((PACK, width), BF),
            jax.ShapeDtypeStruct((PIECE, width), BF),
            jax.ShapeDtypeStruct((8, QR + KVR), F32),
            jax.ShapeDtypeStruct((8, 128), F32),
            jax.ShapeDtypeStruct((QR // peers, args[-1].shape[1]), F32),
            jax.ShapeDtypeStruct((KVR // peers, args[-1].shape[0]), F32),
        ],
        in_specs=[vmem] * len(args),
        out_specs=[vmem] * 7,
        scratch_shapes=[scratch(QR, lanes), scratch(KVR, lanes)]
        + [scratch(rows, LAT_WIDE)] * 7
        + [
            scratch(LAT_WIDE, rows),
            scratch(rows, width),
            pltpu.VMEM((rows, 128), F32),
            scratch(peers, PIECE, width),
            pltpu.VMEM((8, QR + KVR), F32),
            pltpu.VMEM((peers, 8, QR + KVR), F32),
            pltpu.VMEM((4, 8, 128), F32),
            scratch(4, PACK, width),
            scratch(4, 320, width),
        ]
        + halves(HALF)
        + [scratch(4, PIECE, width), scratch(4, PIECE, width)]
        + halves(PIECE // 2)
        + [dma((rows // SHARE,))] * 2
        + [dma((4,))] * 8
        + [dma((peers,))] * 2
        + [dma((4,))] * 2
        + [dma((count,))] * 6
        + torus_sems * 2,
        compiler_params=pltpu.CompilerParams(collective_id=5, has_side_effects=True, vmem_limit_bytes=62 * MIB),
        cost_estimate=pl.CostEstimate(flops=rows * LAT_WIDE * width * 6, bytes_accessed=200 * MIB, transcendentals=0),
        name="latent_backward",
    )(*args)


def swap_cores(v):
    return lax.ppermute(v, "ctx", [(0, 1), (1, 0)])


def in_core_order(mine, other, core, axis):
    return jnp.where(
        core == 0, jnp.concatenate([mine, other], axis=axis), jnp.concatenate([other, mine], axis=axis)
    )


def gather_shards(v):
    return lax.all_gather(v, ("fsdp", "ctx"), axis=0, tiled=True)


X_SWAP = [(0, 1), (1, 0), (2, 3), (3, 2)]
Y_SWAP = [(0, 2), (2, 0), (1, 3), (3, 1)]


def take(v, which, axis):
    return lax.dynamic_index_in_dim(v, which, axis, keepdims=False)


def add_up(a, b):
    return (a.astype(F32) + b.astype(F32)).astype(BF)


def keep_half(v, axis, which, name, pairs):
    other = lax.ppermute(take(v, 1 - which, axis), name, pairs)
    return add_up(take(v, which, axis), other)


def scatter_fsdp(v):
    if lax.axis_size("fsdp") != 4:
        return lax.psum_scatter(v, "fsdp", scatter_dimension=0, tiled=False)
    place = lax.axis_index("fsdp")
    y, x = place // 2, place % 2
    _, rows, cols = v.shape
    v = v.reshape(2, 2, 2, rows // 2, cols)
    first = keep_half(v[:, :, 0], 1, x, "fsdp", X_SWAP)
    second = keep_half(v[:, :, 1], 0, y, "fsdp", Y_SWAP)
    first = keep_half(first, 0, y, "fsdp", Y_SWAP)
    second = keep_half(second, 0, x, "fsdp", X_SWAP)
    return jnp.concatenate([first, second], axis=0)


def scatter_grads(v):
    fsdp, ctx = lax.axis_size("fsdp"), lax.axis_size("ctx")
    rows, cols = v.shape
    v = v.reshape(fsdp, ctx, rows // (fsdp * ctx), cols)
    return scatter_fsdp(keep_half(v, 1, lax.axis_index("ctx"), "ctx", [(0, 1), (1, 0)]))


def split_two(v):
    high = v.astype(BF)
    return high, (v - high.astype(F32)).astype(BF)


def adamw_update(parameter, gradient, first_moment, second_moment, decay_rate):
    first_new = BETA_ONE * first_moment + (1.0 - BETA_ONE) * gradient
    second_new = BETA_TWO * second_moment + (1.0 - BETA_TWO) * gradient * gradient
    first_hat = first_new / (1.0 - BETA_ONE**STEP)
    second_hat = second_new / (1.0 - BETA_TWO**STEP)
    updated = parameter - LEARN_RATE * (
        first_hat / (jnp.sqrt(second_hat) + ADAM_EPS) + decay_rate * parameter
    )
    return (updated, first_new, second_new)


def norm_backward(incoming, values, factor, gain):
    scaled = incoming * gain
    gain_grad = jnp.sum(incoming * values * factor, axis=0)
    result = factor * scaled - values * factor**3 * jnp.mean(scaled * values, axis=1, keepdims=True)
    return (result, gain_grad)


def local(*args):
    tokens, cotangent, lengths = args[:3]
    params, firsts, seconds = args[3:12], args[12:21], args[21:30]
    w_qdown, w_kvdown, w_qup, w_kvup, w_out, w_gateup, w_down, g_norms, g_latent = params
    n_tp, n_ctx, n_fsdp = lax.axis_size("tp"), lax.axis_size("ctx"), lax.axis_size("fsdp")
    tp, core = lax.axis_index("tp"), lax.axis_index("ctx")
    rows, width = tokens.shape
    slot = rows * n_ctx
    heads_all = H // n_tp
    by_head = heads_all % n_ctx == 0
    heads = heads_all // n_ctx if by_head else heads_all

    fused = n_tp == 4 and n_fsdp == 4 and n_ctx == 2
    gains_norm = g_norms.astype(BF)
    gain_attn = gains_norm[0].astype(F32)
    inputs = tokens.astype(F32)
    seq_length = lengths[0, 0]
    own_index = core * rows + jnp.arange(rows, dtype=jnp.int32)
    own_segment = (own_index >= seq_length).astype(jnp.int32)
    live = (own_segment == 0).astype(F32)[:, None]

    q_shard = jnp.pad(
        w_qup.astype(BF).reshape(w_qup.shape[0], heads_all, HEAD), ((0, 0), (0, 0), (0, 128 - HEAD))
    ).reshape(w_qup.shape[0], heads_all * 128)
    up_shard = jnp.concatenate([q_shard, w_kvup.astype(BF)], axis=0)

    if fused:
        piece = jnp.concatenate(
            [
                w_qdown.T.astype(BF),
                jnp.pad(w_kvdown.T.astype(BF), ((0, 12), (0, 0))),
                jnp.broadcast_to(jnp.pad(g_latent.astype(BF), (0, width - g_latent.shape[0])), (16, width)),
            ],
            axis=0,
        )
        up_pair = jnp.concatenate([up_shard[:, : heads * 128], up_shard[:, heads * 128 :]])[None]
        gain_wide = jnp.pad(gains_norm[1].astype(F32), (0, LAT_WIDE - width))[None]
        down_t, lat_sum, lat_all, cos_t, sin_t, seg_q, up, tcos, tsin, gains_lat, gate_up = latent_forward(
            tokens, gain_attn[None], gain_wide, piece[None], up_pair, lengths, w_gateup.astype(BF)
        )
        gain_mlp = lat_sum[rows : rows + n_tp, :width].reshape(D).astype(F32)
    else:
        out_t = gather_shards(w_out.T.astype(BF))
        gate_up = lax.all_gather(w_gateup.astype(BF), ("fsdp", "ctx"), axis=1, tiled=True)
        ff_down_t = gather_shards(w_down.T.astype(BF))
        index = jnp.arange(slot, dtype=jnp.int32)
        segment = (index >= seq_length).astype(jnp.int32)
        position = (index - segment * seq_length).astype(F32)
        frequency = ROPE_BASE ** (-2.0 * jnp.arange(ROPE // 2, dtype=F32) / ROPE)
        angles = frequency[:, None] * position[None, :]
        cos_t, sin_t = jnp.cos(angles), jnp.sin(angles)
        own_cos = lax.dynamic_slice_in_dim(cos_t, core * rows, rows, 1).T
        own_sin = lax.dynamic_slice_in_dim(sin_t, core * rows, rows, 1).T
        seg_f = segment.astype(F32)
        seg_q = jnp.concatenate([seg_f[None], 1.0 - seg_f[None], jnp.zeros((14, slot), F32)], axis=0).astype(BF)
        seg_k = (MASK_VALUE * jnp.concatenate([1.0 - seg_f[:, None], seg_f[:, None]], axis=1)).astype(BF)
        down_t = jnp.concatenate(
            [gather_shards(w_qdown.T.astype(BF)), gather_shards(w_kvdown.T.astype(BF)), jnp.zeros((LAT_WIDE - LAT, width), BF)]
        )
        gain_lat = lax.all_gather(g_latent.astype(BF), ("fsdp", "ctx"), axis=0, tiled=True).astype(F32)
        gain_mlp = lax.all_gather(gains_norm[1], "tp", axis=0, tiled=True).astype(F32)
        up = gather_shards(up_shard).reshape(n_fsdp * n_ctx, up_shard.shape[0], heads_all * 128)
        if by_head:
            up = lax.dynamic_slice_in_dim(up, core * heads * 128, heads * 128, 2)
        scaled_in = (inputs * gain_attn).astype(BF)
        lat_sum = lax.psum(dot_nt(scaled_in, down_t).astype(BF), "tp").astype(F32)
        square_sum = lax.psum(jnp.sum(inputs * inputs, axis=1), "tp")
    if not fused:
        factor_one = lax.rsqrt(square_sum / D + EPS_NORM)[:, None]
        latents = lat_sum[:, :LAT] * factor_one
        query_latent = latents[:, :QR]
        kv_latent = latents[:, QR : QR + KVR]
        gain_query, gain_kv = gain_lat[:QR], gain_lat[QR:]
        factor_query = lax.rsqrt(jnp.mean(query_latent * query_latent, axis=1, keepdims=True) + EPS_NORM)
        factor_kv = lax.rsqrt(jnp.mean(kv_latent * kv_latent, axis=1, keepdims=True) + EPS_NORM)
        rope_raw = latents[:, QR + KVR :]
        query_normed = (query_latent * factor_query * gain_query).astype(BF)
        kv_normed = (kv_latent * factor_kv * gain_kv).astype(BF)
        r_one, r_two = rope_raw[:, : ROPE // 2], rope_raw[:, ROPE // 2 :]
        rope_key = jnp.concatenate(
            [r_one * own_cos - r_two * own_sin, r_two * own_cos + r_one * own_sin], axis=1
        ).astype(BF)
        normed_lat = jnp.concatenate([query_normed, kv_normed, jnp.zeros((rows, NOPE), BF), rope_key], axis=1)
        lat_both = in_core_order(normed_lat, swap_cores(normed_lat), core, 0)
        lat_all = jnp.concatenate([lat_both, seg_k, jnp.zeros((slot, 128 - HEAD - 2), BF)], axis=1)
    qn, kn = lat_all[:, :QR], lat_all[:, QR : QR + KVR]

    if fused:
        att_heads, lse, q_t, k_rows, v_t, att_t, ff_down_t, out_t = attend_forward(
            lat_all, cos_t, sin_t, seg_q, up, w_down.T.astype(BF)[None], w_out.T.astype(BF)[None]
        )
        ff_down_t, out_t = ff_down_t.reshape(D, -1), out_t.reshape(D, -1)
    else:
        att_heads, lse, q_t, k_rows, v_t = attend_forward(lat_all, cos_t, sin_t, seg_q, up)
        att_flat = att_heads.reshape(heads * VD, slot)
        own_cols = lambda v: lax.dynamic_slice_in_dim(v, core * rows, rows, 1)
        if by_head:
            other = swap_cores(lax.dynamic_slice_in_dim(att_flat, (1 - core) * rows, rows, 1))
            att_t = in_core_order(own_cols(att_flat), other, core, 0)
        else:
            att_t = own_cols(att_flat)

    feature_owner = jnp.arange(D) // width
    own_features = lambda v: lax.dynamic_slice_in_dim(v, tp * width, width, 1)
    if fused:
        hidden, d_normed_part, mlp_part, normed_two_t, activation, d_gate, d_up = block_forward(
            att_t, tokens, out_t, gain_mlp[None], live, cotangent, gate_up, ff_down_t
        )
        attn_seed, d_hidden, grad_gain_mlp, grads, grad_squares = grad_reduce(
            live, gain_mlp[None], d_normed_part, hidden, cotangent, normed_two_t, d_gate, d_up, activation
        )
    else:
        dy = cotangent.astype(F32) * live
        mlp_seed = (RESIDUAL_SCALE * dy).astype(BF)
        h_part = RESIDUAL_SCALE * dot_nt(att_t.T, out_t)
        h_part = h_part + jnp.where(
            (feature_owner == tp)[None], jnp.concatenate([inputs] * n_tp, axis=1), 0.0
        )
        hidden = lax.psum(h_part.astype(BF), "tp")
        hidden_f = hidden.astype(F32)
        factor_two = lax.rsqrt(jnp.mean(hidden_f * hidden_f, axis=1, keepdims=True) + EPS_NORM)
        normed_two = (hidden_f * factor_two * gain_mlp).astype(BF)
        gate_proj = dot_nn(normed_two, gate_up[0])
        up_proj = dot_nn(normed_two, gate_up[1])
        sigmoid_gate = jax.nn.sigmoid(gate_proj)
        activation = (gate_proj * sigmoid_gate * up_proj).astype(BF)
        mlp_part = dot_nt(activation, ff_down_t).astype(BF)
        d_activation = dot_nn(mlp_seed, ff_down_t)
        d_gate = (
            d_activation * up_proj * sigmoid_gate * (1.0 + gate_proj * (1.0 - sigmoid_gate))
        ).astype(BF)
        d_up = (d_activation * gate_proj * sigmoid_gate).astype(BF)
        d_normed_part = (dot_nt(d_gate, gate_up[0]) + dot_nt(d_up, gate_up[1])).astype(BF)
        grad_down = scatter_grads(dot_tn(mlp_seed, activation).astype(BF))
        grad_gate = scatter_grads(dot_tn(normed_two, d_gate).astype(BF))
        grad_up = scatter_grads(dot_tn(normed_two, d_up).astype(BF))
        d_normed = lax.psum(d_normed_part, "tp").astype(F32)
        row_inner = jnp.mean(d_normed * gain_mlp * hidden_f, axis=1, keepdims=True)
        d_hidden_full = dy + factor_two * d_normed * gain_mlp - hidden_f * (factor_two**3 * row_inner)
        attn_seed = (RESIDUAL_SCALE * d_hidden_full).astype(BF)
        d_hidden = own_features(d_hidden_full)
        grad_gain_mlp = jnp.sum(own_features(d_normed * hidden_f) * factor_two, axis=0)
    mlp_part, attn_seed = lax.optimization_barrier((mlp_part, attn_seed))
    if fused:
        mlp_out = lax.psum_scatter(mlp_part, "tp", scatter_dimension=0, tiled=False).astype(F32)
    else:
        mlp_out = lax.psum_scatter(mlp_part, "tp", scatter_dimension=1, tiled=True).astype(F32)
    layer_out = (own_features(hidden).astype(F32) + RESIDUAL_SCALE * mlp_out).astype(BF)
    d_att_t = lax.dot_general(out_t, attn_seed, (((0,), (1,)), ((), ())), preferred_element_type=F32).astype(BF)
    grad_out = dot_tn(attn_seed, att_t.T).astype(BF)

    if by_head:
        pick = lambda v, which: lax.dynamic_slice_in_dim(v, which * heads * VD, heads * VD, 0)
        d_att = in_core_order(pick(d_att_t, core), swap_cores(pick(d_att_t, 1 - core)), core, 1)
    else:
        d_att = lax.dynamic_update_slice(jnp.zeros((heads * VD, slot), BF), d_att_t, (0, core * rows))
    d_q, d_e, d_kr = attend_backward(
        q_t, k_rows, v_t, att_heads, d_att.reshape(heads, VD, slot), lse, cos_t, sin_t
    )
    grad_qup = dot_tn(qn, d_q).astype(BF)
    grad_kvup = dot_tn(kn, d_e).astype(BF)

    def heads_only(g):
        return g.reshape(g.shape[0], heads_all, 128)[:, :, :HEAD].reshape(g.shape[0], heads_all * HEAD)

    entry_counts = (
        D * QR,
        D * (KVR + ROPE),
        QR * H * HEAD,
        KVR * H * (NOPE + VD),
        H * VD * D,
        2 * D * FF,
        FF * D,
        2 * D,
        QR + KVR,
    )
    limits = [CLIP_RMS * n**0.5 for n in entry_counts]
    share = g_latent.shape[0]
    my_share = (lax.axis_index("fsdp") * n_ctx + core) * share
    if fused:
        fold = jnp.asarray(np.kron(np.eye(heads_all), np.eye(128, HEAD)), BF)
        grad_input, pack, wd_grad, small, scalars, grad_qup, grad_kvup = latent_backward(
            d_q, d_e, d_kr, up, lat_sum, down_t, tokens, gain_attn[None], d_hidden, tcos, tsin, gains_lat,
            grad_out, grad_qup, grad_kvup, spread(n_fsdp * n_ctx), grad_gain_mlp, grad_squares, jnp.array([limits + [1.0] * 119], F32), fold,
        )
        owned = [
            wd_grad[:96].astype(F32).T,
            wd_grad[96:132].astype(F32).T,
            grad_qup,
            grad_kvup,
            pack[:320].astype(F32).T,
            grads[:2].astype(F32),
            grads[2].astype(F32).T,
            small[1:3, :width],
            lax.dynamic_slice_in_dim(small[0], my_share, share, 0),
        ]
        factors = [scalars[0, n] for n in range(9)]
    else:
        q_up_here = up[:, : w_qup.shape[0]].reshape(QR, heads * 128)
        kv_up_here = up[:, w_qup.shape[0] :].reshape(KVR, heads * 128)
        d_lat_part = jnp.concatenate([dot_nt(d_q, q_up_here), dot_nt(d_e, kv_up_here), d_kr[:, NOPE:HEAD]], axis=1)
        own_rows = lambda v, which: lax.dynamic_slice_in_dim(v, which * rows, rows, 0)
        from_other = swap_cores(own_rows(d_lat_part, 1 - core).astype(BF)).astype(F32)
        d_lat = lax.psum((own_rows(d_lat_part, core) + from_other).astype(BF), "tp").astype(F32)
        d_rope = d_lat[:, QR + KVR : LAT]
        k_one, k_two = d_rope[:, : ROPE // 2], d_rope[:, ROPE // 2 :]
        d_rope_raw = jnp.concatenate([k_one * own_cos + k_two * own_sin, k_two * own_cos - k_one * own_sin], axis=1)
        d_query_latent, grad_gain_query = norm_backward(d_lat[:, :QR], query_latent, factor_query, gain_query)
        d_kv_latent, grad_gain_kv = norm_backward(d_lat[:, QR : QR + KVR], kv_latent, factor_kv, gain_kv)
        d_latents = jnp.concatenate([d_query_latent, d_kv_latent, d_rope_raw], axis=1)
        in_inner = jnp.sum(d_latents * latents, axis=1, keepdims=True) / D
        d_latents = (d_latents * factor_one).astype(BF)
        grad_both = dot_tn(d_latents, scaled_in).astype(BF)
        d_in = dot_nn(d_latents, down_t[:LAT])
        grad_gain_attn = jnp.sum(d_in * inputs, axis=0)
        grad_input = (d_hidden + d_in * gain_attn - inputs * (factor_one**2 * in_inner)).astype(BF)

        def scatter_up(g):
            if not by_head:
                return scatter_grads(g)
            n_rows, n_cols = g.shape
            g = g.reshape(n_fsdp, n_ctx, n_rows // (n_fsdp * n_ctx), n_cols)
            other = swap_cores(take(g, 1 - core, 1))
            return scatter_fsdp(in_core_order(take(g, core, 1), other, core, 2))

        owned = [
            scatter_grads(grad_both[:QR]).astype(F32).T,
            scatter_grads(grad_both[QR:]).astype(F32).T,
            heads_only(scatter_up(grad_qup)).astype(F32),
            scatter_up(grad_kvup).astype(F32),
            scatter_grads(grad_out).astype(F32).T,
            jnp.stack([grad_gate, grad_up]).astype(F32),
            grad_down.astype(F32).T,
        ]
        both_gains = jnp.stack([grad_gain_attn, grad_gain_mlp])
        placed_gains = jnp.where((feature_owner == tp)[None], jnp.concatenate([both_gains] * n_tp, axis=1), 0.0)
        latent_gains = jnp.concatenate([grad_gain_query, grad_gain_kv]) * (tp == 0)
        squares = jnp.stack([jnp.sum(g * g) for g in owned])
        small = lax.psum(
            jnp.concatenate([placed_gains.reshape(-1), latent_gains, squares]), ("fsdp", "ctx", "tp")
        )
        all_gains = small[: 2 * D].reshape(2, D)
        all_latent = small[2 * D : 2 * D + QR + KVR]
        owned.append(own_features(all_gains))
        owned.append(lax.dynamic_slice_in_dim(all_latent, my_share, share, 0))
        totals = [small[2 * D + QR + KVR + n] for n in range(7)]
        totals += [jnp.sum(all_gains * all_gains), jnp.sum(all_latent * all_latent)]
        factors = [limit / jnp.maximum(jnp.sqrt(total), limit) for limit, total in zip(limits, totals)]
    new_params, new_firsts, new_seconds = [], [], []
    for n in range(9):
        clipped = owned[n] * factors[n]
        updated, first_new, second_new = adamw_update(
            params[n], clipped, firsts[n], seconds[n], WEIGHT_DECAY if n < 7 else 0.0
        )
        new_params.append(updated)
        new_firsts.append(first_new)
        new_seconds.append(second_new)
    return (layer_out, grad_input, *owned, *new_params[:7], *new_firsts, *new_seconds)


def solution(mesh):
    sharded = ("fsdp", "ctx")
    weights = (
        P("tp", sharded),
        P("tp", sharded),
        P(sharded, "tp"),
        P(sharded, "tp"),
        P("tp", sharded),
        P(None, sharded, "tp"),
        P("tp", sharded),
    )
    gains = (P(None, "tp"), P(sharded))
    tokens = P(sharded, "tp")
    return jax.shard_map(
        local,
        mesh=mesh,
        in_specs=(tokens, P(sharded, None), P("fsdp", None)) + (weights + gains) * 3,
        out_specs=(tokens, tokens) + weights + gains + weights + (weights + gains) * 2,
        check_vma=False,
    )
```
